32 devices in a mesh: shard: 8 (over z, y), tensor: 4 (over x, core).
Axes of the slice: x: 2, y: 2, z: 4, core: 2. Of those that a mesh axis runs over, the one named last changes fastest.
Arguments:
- grads: float32 [16, 384, 384], P('tensor', 'shard'), may hold values from -0.3 to 0.3
- moment_one: float32 [32, 73728], P(('tensor', 'shard')), may hold values from -0.3 to 0.3
- moment_two: float32 [32, 73728], P(('tensor', 'shard')), may hold values from 0.0005 to 0.01
- left_stat: float32 [32, 73728], P(('tensor', 'shard')), may hold values from -1 to 9, as said below
- right_stat: float32 [32, 73728], P(('tensor', 'shard')), may hold values from -1 to 9, as said below
- left_basis: float32 [32, 73728], P(('tensor', 'shard')), may hold values from -1 to 2
- right_basis: float32 [32, 73728], P(('tensor', 'shard')), may hold values from -1 to 2
Outputs:
- update: float32 [16, 384, 384], P('tensor', 'shard')
- new_moment_one: float32 [32, 73728], P(('tensor', 'shard'))
- new_moment_two: float32 [32, 73728], P(('tensor', 'shard'))
- new_left_stat: float32 [32, 73728], P(('tensor', 'shard'))
- new_right_stat: float32 [32, 73728], P(('tensor', 'shard'))
- new_left_basis: float32 [32, 73728], P(('tensor', 'shard'))
- new_right_basis: float32 [32, 73728], P(('tensor', 'shard'))
The draws below stay inside these ranges and needn't reach their ends.
Inputs may be any that keep to these rules, and one draw needn't show every extreme that they name: `left_stat`: each tile of the statistics is symmetric. `right_stat`: each tile of the statistics is symmetric.
All inputs are finite; a program needn't handle non-finite values.
Results may differ from the reference program's by a relative error of at most 0.00024.
Values sent between devices are 32-bit elements; how exact they have to be, the bound alone decides.
No kernel may reach another device: no remote copies, remote signals or barrier semaphores. Data moves between devices by JAX's collectives and lax.ppermute only.
A program may use at most 64 MiB of HBM per device.

```python
import math
import jax
import jax.numpy as jnp
from jax import lax

B = 384
HALF = 192
NS_ITERS = 5
TILES = 16
HALVES = 32


def to_halves_drawn(tiles):
    count = tiles.shape[0]
    return tiles.reshape(count, B, 2, HALF).transpose(0, 2, 1, 3).reshape(2 * count, B * HALF)


def identity_tiles():
    return (jnp.arange(B)[:, None] == jnp.arange(B)[None, :]).astype(jnp.float32)


def statistic(key):
    diag_key, noise_key = jax.random.split(key)
    diagonal = jnp.exp(jax.random.uniform(diag_key, (TILES, B), jnp.float32, math.log(0.5), math.log(5.0)))
    noise = jnp.clip(jax.random.normal(noise_key, (TILES, B, B), jnp.float32), -4.0, 4.0) * 0.05
    symmetric = noise + jnp.transpose(noise, (0, 2, 1))
    return to_halves_drawn(symmetric + identity_tiles()[None, :, :] * diagonal[:, :, None])


def basis(key):
    noise = jnp.clip(jax.random.normal(key, (TILES, B, B), jnp.float32), -4.0, 4.0) * (0.5 / math.sqrt(B))
    return to_halves_drawn(identity_tiles()[None, :, :] + noise)


def draw_left_stat(key, part):
    return statistic(jax.random.fold_in(key, 11))


def draw_right_stat(key, part):
    return statistic(jax.random.fold_in(key, 12))


def draw_left_basis(key, part):
    return basis(jax.random.fold_in(key, 13))


def draw_right_basis(key, part):
    return basis(jax.random.fold_in(key, 14))


def steps_of(stream_key, dims, cuts, low, largest):
    gain = 1.0
    for dim, blocks in cuts:
        heights = jax.random.uniform(jax.random.fold_in(jax.random.fold_in(stream_key, 6), dim), (blocks,), jnp.float32, low / len(cuts), largest / len(cuts))
        gain = gain * jnp.repeat(jnp.exp(heights), dims[dim] // blocks).reshape((-1,) + (1,) * (len(dims) - 1 - dim))
    return gain


def centred(stream_key, dims, scale, most, pieces=(), dtype=jnp.bfloat16):
    gain = steps_of(stream_key, dims, pieces, -0.22, 0.18) if pieces else 1.0
    entries = jax.random.normal(stream_key, dims, jnp.float32) * scale * gain
    return jnp.minimum(jnp.maximum(entries, -most), most).astype(dtype)


def setup_inputs(seed: int = 0) -> dict:
    keys = jax.random.split(jax.random.key(seed), 8)
    return {
        "grads": centred(keys[0], (TILES, B, B), 0.05, 0.3, ((0, 4), (1, 8)), jnp.float32),
        "moment_one": centred(keys[1], (HALVES, B * HALF), 0.05, 0.3, ((0, 32),), jnp.float32),
        "moment_two": jnp.clip(jnp.exp(math.log(0.01) - 2.9957322 * jax.random.uniform(keys[2], (HALVES, B * HALF), jnp.float32) ** steps_of(keys[2], (HALVES, B * HALF), ((0, 32),), -0.2, 0.2)), 0.0005, 0.01),
        "left_stat": draw_left_stat(jax.random.fold_in(keys[7], 71), 0),
        "right_stat": draw_right_stat(jax.random.fold_in(keys[7], 71), 0),
        "left_basis": draw_left_basis(jax.random.fold_in(keys[7], 71), 0),
        "right_basis": draw_right_basis(jax.random.fold_in(keys[7], 71), 0),
    }


HIGHEST_PRECISION = lax.Precision.HIGHEST
BETA_ONE = 0.9
BETA_TWO = 0.95
ADAM_EPS = 1e-08
NORM_EPS = 1e-06
LINEAR_COEFF = 3.4445
CUBIC_COEFF = -4.775
QUINTIC_COEFF = 2.0315

def matmul(first_matrix, second_matrix):
    return jnp.dot(first_matrix, second_matrix, precision=HIGHEST_PRECISION, preferred_element_type=jnp.float32)

def to_tiles(halves):
    count = halves.shape[0]
    return halves.reshape(count // 2, 2, B, HALF).transpose(0, 2, 1, 3).reshape(count // 2, B, 2 * HALF)

def to_halves(tiles):
    count = tiles.shape[0]
    return tiles.reshape(count, B, 2, HALF).transpose(0, 2, 1, 3).reshape(2 * count, B * HALF)

def orthogonalize(power):
    frobenius = jnp.sqrt(jnp.sum(power * power) + NORM_EPS)
    iterate = power / frobenius
    for iteration in range(NS_ITERS):
        gram = matmul(iterate, iterate.T)
        poly = CUBIC_COEFF * gram + QUINTIC_COEFF * matmul(gram, gram)
        iterate = LINEAR_COEFF * iterate + matmul(poly, iterate)
    return iterate

def one_tile(inputs):
    gradient, moment_first, moment_second, stat_left, stat_right, basis_left, basis_right = inputs
    rotated = matmul(matmul(basis_left.T, gradient), basis_right)
    new_first = BETA_ONE * moment_first + (1.0 - BETA_ONE) * rotated
    new_second = BETA_TWO * moment_second + (1.0 - BETA_TWO) * rotated * rotated
    direction = new_first / (jnp.sqrt(new_second) + ADAM_EPS)
    update = matmul(basis_left, matmul(direction, basis_right.T))
    new_left = 0.5 * stat_left + 0.5 * matmul(gradient, gradient.T)
    new_right = 0.5 * stat_right + 0.5 * matmul(gradient.T, gradient)
    refreshed_left = orthogonalize(matmul(new_left, basis_left))
    refreshed_right = orthogonalize(matmul(new_right, basis_right))
    return (update, new_first, new_second, new_left, new_right, refreshed_left, refreshed_right)

def reference(grads, moment_one, moment_two, left_stat, right_stat, left_basis, right_basis):
    inputs = (grads, to_tiles(moment_one), to_tiles(moment_two), to_tiles(left_stat), to_tiles(right_stat), to_tiles(left_basis), to_tiles(right_basis))
    results = lax.map(one_tile, inputs)
    return (results[0], to_halves(results[1]), to_halves(results[2]), to_halves(results[3]), to_halves(results[4]), to_halves(results[5]), to_halves(results[6]))
```

```python
import jax
import jax.numpy as jnp
from jax import lax
from jax.experimental import pallas as pl
from jax.experimental.pallas import tpu as pltpu
from jax.sharding import PartitionSpec as P

NS_ITERS = 5
BETA_ONE = 0.9
BETA_TWO = 0.95
ADAM_EPS = 1e-08
NORM_EPS = 1e-06
LINEAR_COEFF = 3.4445
CUBIC_COEFF = -4.775
QUINTIC_COEFF = 2.0315
LANES = 128
F32 = jnp.float32


def split(x):
    high = x.astype(jnp.bfloat16)
    return high, (x - high.astype(F32)).astype(jnp.bfloat16)


def dot(a, b, dims=((1,), (0,))):
    return dot_parts(split(a), split(b), dims)


def dot_parts(a, b, dims=((1,), (0,))):
    (ka,), (kb,) = dims
    left = jnp.concatenate([a[0], a[0], a[1]], axis=ka)
    right = jnp.concatenate([b[0], b[1], b[0]], axis=kb)
    return lax.dot_general(left, right, (dims, ((), ())), preferred_element_type=F32)


def swap(x):
    return pltpu.roll(x, LANES // 2, 1)


def low_lanes(shape):
    return lax.broadcasted_iota(jnp.int32, shape, 1) < LANES // 2


def pick(flag, x, y):
    return [jnp.where(flag, u, v) for u, v in zip(x, y)]


def thirds(ref, start=0, rows=None):
    rows = ref.shape[0] if rows is None else rows
    return [ref[pl.ds(start + k, rows // 3, stride=3), :] for k in range(3)]


def put_thirds(ref, parts):
    for k in range(3):
        ref[pl.ds(k, parts[k].shape[0], stride=3), :] = parts[k]


def interleave(scratch, index, even, odd):
    scratch[index, pl.ds(0, even.shape[0], stride=2), :] = even
    scratch[index, pl.ds(1, odd.shape[0], stride=2), :] = odd


def whole_of(scratch, first, second):
    a, b, c = first
    d, e, f = second
    low = low_lanes(a.shape)
    sb, sc, sd, se = swap(b), swap(c), swap(d), swap(e)
    interleave(scratch, 0, a, jnp.where(low, sb, sc))
    interleave(scratch, 1, jnp.where(low, b, sd), jnp.where(low, sc, e))
    interleave(scratch, 2, jnp.where(low, sd, se), f)
    return jnp.concatenate([scratch[0], scratch[1], scratch[2]], axis=1)


def half_of(scratch, flat):
    a, b, c = flat
    low = low_lanes(a.shape)
    sb, sc = swap(b), swap(c)
    interleave(scratch, 0, a, jnp.where(low, sb, sc))
    interleave(scratch, 1, jnp.where(low, b, 0.0), jnp.where(low, sc, 0.0))
    return jnp.concatenate([scratch[0], scratch[1]], axis=1)


def flat_of(scratch, half):
    scratch[0] = half[:, :LANES]
    scratch[1] = half[:, LANES:]
    pairs = half.shape[0] // 2
    even0 = scratch[0, pl.ds(0, pairs, stride=2), :]
    odd0 = swap(scratch[0, pl.ds(1, pairs, stride=2), :])
    even1 = scratch[1, pl.ds(0, pairs, stride=2), :]
    odd1 = swap(scratch[1, pl.ds(1, pairs, stride=2), :])
    low = low_lanes(even0.shape)
    return [even0, jnp.where(low, even1, odd0), jnp.where(low, odd0, odd1)]


def take_half(whole, first):
    one, two, three = whole[:, :LANES], whole[:, LANES : 2 * LANES], whole[:, 2 * LANES :]
    low = low_lanes(one.shape)
    s2, s3 = swap(two), swap(three)
    head = jnp.where(first, one, jnp.where(low, s2, s3))
    tail = jnp.where(low, jnp.where(first, two, s3), 0.0)
    return jnp.concatenate([head, tail], axis=1)


def is_left():
    return lax.rem(lax.axis_index("shard"), 2) == 0


def stats_kernel(grad_ref, left_ref, right_ref, got_ref, new_left_ref, new_right_ref, stat_ref, scratch):
    left = is_left()
    flat_rows = left_ref.shape[0]
    l_flat, r_flat = thirds(left_ref), thirds(right_ref)
    own, other = pick(left, l_flat, r_flat), pick(left, r_flat, l_flat)
    corner = thirds(got_ref, flat_rows, flat_rows // 2)
    placed = [jnp.concatenate([jnp.where(left, 0.0, c), jnp.where(left, c, 0.0)], axis=0) for c in corner]
    known = whole_of(scratch, pick(left, own, placed), pick(left, placed, own))
    full = known.shape[0]
    row = lax.broadcasted_iota(jnp.int32, known.shape, 0)
    column = lax.broadcasted_iota(jnp.int32, known.shape, 1)
    missing = (jnp.where(left, row, column) < full // 2) & (jnp.where(left, column, row) >= full // 2)
    stat = jnp.where(missing, known.T, known)
    grad = grad_ref[...]
    turned = grad.T
    a = jnp.where(left, grad, turned)
    b = jnp.where(left, turned, grad)
    product = dot(a, b)
    stat_ref[...] = 0.5 * stat + 0.5 * product
    new_own = [0.5 * u + 0.5 * v for u, v in zip(own, flat_of(scratch, take_half(product, left)))]
    other_product = dot(b, take_half(a, left))
    new_other = [0.5 * u + 0.5 * v for u, v in zip(other, flat_of(scratch, other_product))]
    put_thirds(new_left_ref, pick(left, new_own, new_other))
    put_thirds(new_right_ref, pick(left, new_other, new_own))


def refresh_kernel(stat_ref, left_ref, right_ref, got_ref, keep_ref, send_ref, scratch, x_ref):
    left = is_left()
    own = pick(left, thirds(left_ref), thirds(right_ref))
    got = thirds(got_ref, 0, left_ref.shape[0])
    basis = whole_of(scratch, pick(left, own, got), pick(left, got, own))
    power = dot(stat_ref[...], basis)
    x_ref[...] = power * (1.0 / jnp.sqrt(jnp.sum(power * power) + NORM_EPS))

    @pl.loop(0, NS_ITERS)
    def _(step):
        x = x_ref[...]
        parts = split(x)
        gram = dot_parts(parts, parts, ((1,), (1,)))
        gram_parts = split(gram)
        poly = CUBIC_COEFF * gram + QUINTIC_COEFF * dot_parts(gram_parts, gram_parts)
        x_ref[...] = LINEAR_COEFF * x + dot_parts(split(poly), parts)

    x = x_ref[...]
    put_thirds(send_ref, flat_of(scratch, take_half(x, jnp.logical_not(left))))
    put_thirds(keep_ref, flat_of(scratch, take_half(x, left)))


def update_kernel(
    grad_ref, left_ref, right_ref, got_ref, first_left_ref, one_ref, two_ref, new_one_ref, new_two_ref, update_ref, scratch
):
    left = is_left()
    own = thirds(left_ref)
    got = thirds(got_ref, 0, left_ref.shape[0])
    basis_left = whole_of(scratch, pick(left, own, thirds(first_left_ref)), pick(left, got, own))
    left_parts = split(basis_left)
    basis_right = split(half_of(scratch, thirds(right_ref)))
    inner = dot_parts(split(grad_ref[...]), basis_right)
    rotated = flat_of(scratch, dot(basis_left.T, inner))
    ones = thirds(one_ref)
    twos = thirds(two_ref)
    new_one = [BETA_ONE * m + (1.0 - BETA_ONE) * r for m, r in zip(ones, rotated)]
    new_two = [BETA_TWO * v + (1.0 - BETA_TWO) * r * r for v, r in zip(twos, rotated)]
    put_thirds(new_one_ref, new_one)
    put_thirds(new_two_ref, new_two)
    direction = [m / (jnp.sqrt(v) + ADAM_EPS) for m, v in zip(new_one, new_two)]
    outer = dot_parts(left_parts, split(half_of(scratch, direction)))
    update_ref[...] = dot_parts(split(outer), basis_right, ((1,), (1,)))


def call(kernel, outs, scratch, flops, nbytes):
    return pl.pallas_call(
        kernel,
        out_shape=[jax.ShapeDtypeStruct(s, F32) for s in outs],
        scratch_shapes=[pltpu.VMEM(s, F32) for s in scratch],
        compiler_params=pltpu.CompilerParams(vmem_limit_bytes=40 * 1024 * 1024),
        cost_estimate=pl.CostEstimate(flops=flops, bytes_accessed=nbytes, transcendentals=0),
    )


def local(grads, moment_one, moment_two, left_stat, right_stat, left_basis, right_basis):
    tiles_here, rows_here, full = grads.shape
    half = full // 2
    size = lax.axis_size("shard")
    flat_rows = full * half // LANES
    flat_shape = (flat_rows, LANES)
    parity = lax.axis_index("shard") % 2

    def flat(x):
        return x.reshape(flat_shape)

    one, two, l_stat, r_stat, l_basis, r_basis = map(
        flat, (moment_one, moment_two, left_stat, right_stat, left_basis, right_basis)
    )
    pieces = jnp.broadcast_to(grads[:, None], (tiles_here, 2, rows_here, full)).reshape(size, rows_here, full)
    grad = lax.all_to_all(pieces, "shard", split_axis=0, concat_axis=0, tiled=True).reshape(full, full)
    outgoing = jnp.where(
        parity == 0,
        jnp.concatenate([r_basis, r_stat[: flat_rows // 2]], axis=0),
        jnp.concatenate([l_basis, l_stat[flat_rows // 2 :]], axis=0),
    )
    got = lax.ppermute(outgoing, "shard", [(i, i ^ 1) for i in range(size)])
    first_left = lax.ppermute(l_basis, "shard", [(i, i + 1) for i in range(0, size, 2)])

    cube = 2 * full**3 * 3
    new_left, new_right, stat = call(
        stats_kernel, [flat_shape, flat_shape, (full, full)], [(3, full, LANES)], 2 * cube, 8 * full * full * 4
    )(grad, l_stat, r_stat, got)
    new_one, new_two, partial = call(
        update_kernel, [flat_shape, flat_shape, (full, full)], [(3, full, LANES)], 2 * cube, 8 * full * full * 4
    )(grad, l_basis, r_basis, got, first_left, one, two)
    returned = lax.all_to_all(
        partial.reshape(size, rows_here, full), "shard", split_axis=0, concat_axis=0, tiled=True
    )
    keep, send = call(
        refresh_kernel, [flat_shape, flat_shape], [(3, full, LANES), (full, full)], 16 * cube, 4 * full * full * 4
    )(stat, l_basis, r_basis, got)
    back = lax.ppermute(send, "shard", [(i, i ^ 1) for i in range(size)])
    new_l_basis = jnp.where(parity == 0, keep, back)
    new_r_basis = jnp.where(parity == 0, back, keep)
    update = returned.reshape(tiles_here, 2, rows_here, full).sum(axis=1)

    def unflat(x):
        return x.reshape(1, full * half)

    return (update, *map(unflat, (new_one, new_two, new_left, new_right, new_l_basis, new_r_basis)))


def solution(mesh):
    halves = P(("tensor", "shard"), None)
    rows = P("tensor", "shard", None)
    return jax.shard_map(
        local, mesh=mesh, in_specs=(rows,) + (halves,) * 6, out_specs=(rows,) + (halves,) * 6, check_vma=False
    )
```

```python
import functools

import jax
import jax.numpy as jnp
from jax import lax
from jax.experimental import pallas as pl
from jax.experimental.pallas import tpu as pltpu
from jax.sharding import PartitionSpec as P

NS_ITERS = 5
BETA_ONE = 0.9
BETA_TWO = 0.95
ADAM_EPS = 1e-08
NORM_EPS = 1e-06
LINEAR_COEFF = 3.4445
CUBIC_COEFF = -4.775
QUINTIC_COEFF = 2.0315
LANES = 128
F32 = jnp.float32


def split(x):
    high = x.astype(jnp.bfloat16)
    return high, (x - high.astype(F32)).astype(jnp.bfloat16)


def dot(a, b, dims=((1,), (0,))):
    return dot_parts(split(a), split(b), dims)


def dot_parts(a, b, dims=((1,), (0,))):
    (ka,), (kb,) = dims
    left = jnp.concatenate([a[0], a[0], a[1]], axis=ka)
    right = jnp.concatenate([b[0], b[1], b[0]], axis=kb)
    return lax.dot_general(left, right, (dims, ((), ())), preferred_element_type=F32)


def swap(x):
    return pltpu.roll(x, LANES // 2, 1)


def low_lanes(shape):
    return lax.broadcasted_iota(jnp.int32, shape, 1) < LANES // 2


def pick(flag, x, y):
    return [jnp.where(flag, u, v) for u, v in zip(x, y)]


def thirds(ref, start=0, rows=None):
    rows = ref.shape[0] if rows is None else rows
    return [ref[pl.ds(start + k, rows // 3, stride=3), :] for k in range(3)]


def put_thirds(ref, parts):
    for k in range(3):
        ref[pl.ds(k, parts[k].shape[0], stride=3), :] = parts[k]


def interleave(scratch, index, even, odd):
    scratch[index, pl.ds(0, even.shape[0], stride=2), :] = even
    scratch[index, pl.ds(1, odd.shape[0], stride=2), :] = odd


def whole_of(scratch, first, second):
    a, b, c = first
    d, e, f = second
    low = low_lanes(a.shape)
    sb, sc, sd, se = swap(b), swap(c), swap(d), swap(e)
    interleave(scratch, 0, a, jnp.where(low, sb, sc))
    interleave(scratch, 1, jnp.where(low, b, sd), jnp.where(low, sc, e))
    interleave(scratch, 2, jnp.where(low, sd, se), f)
    return jnp.concatenate([scratch[0], scratch[1], scratch[2]], axis=1)


def half_of(scratch, flat):
    a, b, c = flat
    low = low_lanes(a.shape)
    sb, sc = swap(b), swap(c)
    interleave(scratch, 0, a, jnp.where(low, sb, sc))
    interleave(scratch, 1, jnp.where(low, b, 0.0), jnp.where(low, sc, 0.0))
    return jnp.concatenate([scratch[0], scratch[1]], axis=1)


def flat_of(scratch, half):
    scratch[0] = half[:, :LANES]
    scratch[1] = half[:, LANES:]
    pairs = half.shape[0] // 2
    even0 = scratch[0, pl.ds(0, pairs, stride=2), :]
    odd0 = swap(scratch[0, pl.ds(1, pairs, stride=2), :])
    even1 = scratch[1, pl.ds(0, pairs, stride=2), :]
    odd1 = swap(scratch[1, pl.ds(1, pairs, stride=2), :])
    low = low_lanes(even0.shape)
    return [even0, jnp.where(low, even1, odd0), jnp.where(low, odd0, odd1)]


def take_half(whole, first):
    one, two, three = whole[:, :LANES], whole[:, LANES : 2 * LANES], whole[:, 2 * LANES :]
    low = low_lanes(one.shape)
    s2, s3 = swap(two), swap(three)
    head = jnp.where(first, one, jnp.where(low, s2, s3))
    tail = jnp.where(low, jnp.where(first, two, s3), 0.0)
    return jnp.concatenate([head, tail], axis=1)


def is_left():
    return lax.rem(lax.axis_index("shard"), 2) == 0


def gather_rows(left, mine_ref, theirs_ref):
    blocks = []
    for k in range(mine_ref.shape[0]):
        mine, theirs = mine_ref[k], theirs_ref[k]
        blocks += [jnp.where(left, mine, theirs), jnp.where(left, theirs, mine)]
    return jnp.concatenate(blocks, axis=0)


def prepare_kernel(l_stat_ref, r_stat_ref, l_basis_ref, r_basis_ref, got_ref, stat_ref, basis_ref, scratch):
    left = is_left()
    flat_rows = l_stat_ref.shape[0]
    own = pick(left, thirds(l_basis_ref), thirds(r_basis_ref))
    got = thirds(got_ref, 0, flat_rows)
    basis_ref[...] = whole_of(scratch, pick(left, own, got), pick(left, got, own))
    own = pick(left, thirds(l_stat_ref), thirds(r_stat_ref))
    corner = thirds(got_ref, flat_rows, flat_rows // 2)
    placed = [jnp.concatenate([jnp.where(left, 0.0, c), jnp.where(left, c, 0.0)], axis=0) for c in corner]
    known = whole_of(scratch, pick(left, own, placed), pick(left, placed, own))
    half = known.shape[0] // 2
    row = lax.broadcasted_iota(jnp.int32, known.shape, 0)
    column = lax.broadcasted_iota(jnp.int32, known.shape, 1)
    missing = (jnp.where(left, row, column) < half) & (jnp.where(left, column, row) >= half)
    stat_ref[...] = 0.5 * jnp.where(missing, known.T, known)


def iterate(x_ref, steps):
    @pl.loop(0, steps)
    def _(step):
        x = x_ref[...]
        parts = split(x)
        gram = dot_parts(parts, parts, ((1,), (1,)))
        gram_parts = split(gram)
        poly = CUBIC_COEFF * gram + QUINTIC_COEFF * dot_parts(gram_parts, gram_parts)
        x_ref[...] = LINEAR_COEFF * x + dot_parts(split(poly), parts)


def begin_kernel(steps, mine_ref, theirs_ref, stat_ref, basis_ref, grad_ref, new_stat_ref, x_ref):
    left = is_left()
    grad = gather_rows(left, mine_ref, theirs_ref)
    grad_ref[...] = grad
    turned = grad.T
    new_stat = stat_ref[...] + 0.5 * dot(jnp.where(left, grad, turned), jnp.where(left, turned, grad))
    new_stat_ref[...] = new_stat
    power = dot(new_stat, basis_ref[...])
    x_ref[...] = power * (1.0 / jnp.sqrt(jnp.sum(power * power) + NORM_EPS))
    iterate(x_ref, steps)


def end_kernel(steps, start_ref, keep_ref, send_ref, scratch, x_ref):
    left = is_left()
    x_ref[...] = start_ref[...]
    iterate(x_ref, steps)
    x = x_ref[...]
    put_thirds(send_ref, flat_of(scratch, take_half(x, jnp.logical_not(left))))
    put_thirds(keep_ref, flat_of(scratch, take_half(x, left)))


def update_kernel(
    grad_ref, basis_ref, left_ref, right_ref, first_left_ref, one_ref, two_ref, new_one_ref, new_two_ref, mine_ref, theirs_ref, scratch
):
    left = is_left()
    basis_left = jnp.where(left, basis_ref[...], whole_of(scratch, thirds(first_left_ref), thirds(left_ref)))
    left_parts = split(basis_left)
    basis_right = split(half_of(scratch, thirds(right_ref)))
    inner = dot_parts(split(grad_ref[...]), basis_right)
    rotated = flat_of(scratch, dot(basis_left.T, inner))
    ones = thirds(one_ref)
    twos = thirds(two_ref)
    new_one = [BETA_ONE * m + (1.0 - BETA_ONE) * r for m, r in zip(ones, rotated)]
    new_two = [BETA_TWO * v + (1.0 - BETA_TWO) * r * r for v, r in zip(twos, rotated)]
    put_thirds(new_one_ref, new_one)
    put_thirds(new_two_ref, new_two)
    direction = [m / (jnp.sqrt(v) + ADAM_EPS) for m, v in zip(new_one, new_two)]
    outer = dot_parts(left_parts, split(half_of(scratch, direction)))
    partial = dot_parts(split(outer), basis_right, ((1,), (1,)))
    rows = mine_ref.shape[1]
    for k in range(mine_ref.shape[0]):
        even = partial[2 * k * rows : (2 * k + 1) * rows]
        odd = partial[(2 * k + 1) * rows : (2 * k + 2) * rows]
        mine_ref[k] = jnp.where(left, even, odd)
        theirs_ref[k] = jnp.where(left, odd, even)


def stats_kernel(grad_ref, new_stat_ref, left_ref, right_ref, new_left_ref, new_right_ref, scratch):
    left = is_left()
    other = pick(left, thirds(right_ref), thirds(left_ref))
    grad = grad_ref[...]
    turned = grad.T
    a = jnp.where(left, grad, turned)
    b = jnp.where(left, turned, grad)
    new_own = flat_of(scratch, take_half(new_stat_ref[...], left))
    product = flat_of(scratch, dot(b, take_half(a, left)))
    new_other = [0.5 * u + 0.5 * v for u, v in zip(other, product)]
    put_thirds(new_left_ref, pick(left, new_own, new_other))
    put_thirds(new_right_ref, pick(left, new_other, new_own))


def call(kernel, outs, scratch, products, full, name):
    size = full * full
    return pl.pallas_call(
        kernel,
        out_shape=[jax.ShapeDtypeStruct(s, F32) for s in outs],
        scratch_shapes=[pltpu.VMEM(s, F32) for s in scratch],
        compiler_params=pltpu.CompilerParams(vmem_limit_bytes=40 * 1024 * 1024),
        cost_estimate=pl.CostEstimate(flops=int(products * 6 * full * size), bytes_accessed=16 * size, transcendentals=0),
        name=name,
    )


def after(x, *others):
    return lax.optimization_barrier((x, *others))[0]


def local(grads, moment_one, moment_two, left_stat, right_stat, left_basis, right_basis):
    tiles_here, rows_here, full = grads.shape
    size = lax.axis_size("shard")
    flat_rows = full * (full // 2) // LANES
    flat = (flat_rows, LANES)
    square = (full, full)
    blocks = (tiles_here, rows_here, full)
    parity = lax.axis_index("shard") % 2
    pairs = [(i, i ^ 1) for i in range(size)]
    sides = [list(range(k, size, 2)) for k in range(2)]
    aligned = rows_here % 8 == 0
    strips = blocks if aligned else (1, full // 2, full)

    def exchange(x):
        return lax.all_to_all(x, "shard", split_axis=0, concat_axis=0, axis_index_groups=sides, tiled=True)

    one, two, l_stat, r_stat, l_basis, r_basis = (
        x.reshape(flat) for x in (moment_one, moment_two, left_stat, right_stat, left_basis, right_basis)
    )
    outgoing = jnp.where(
        parity == 0,
        jnp.concatenate([r_basis, r_stat[: flat_rows // 2]], axis=0),
        jnp.concatenate([l_basis, l_stat[flat_rows // 2 :]], axis=0),
    )
    got = lax.ppermute(outgoing, "shard", pairs)
    mine = exchange(after(grads, outgoing))
    theirs = lax.ppermute(mine, "shard", pairs)
    first_left = lax.ppermute(after(l_basis, theirs), "shard", [(i, i + 1) for i in range(0, size, 2)])
    stat, basis = call(prepare_kernel, [square, square], [(3, full, LANES)], 0.1, full, "prepare")(
        l_stat, r_stat, l_basis, r_basis, got
    )
    if not aligned:
        mine, theirs = jnp.where(parity == 0, mine, theirs), jnp.where(parity == 0, theirs, mine)
        merged = jnp.stack([mine, theirs], axis=1).reshape(2, full // 2, full)
        mine = lax.dynamic_slice_in_dim(merged, parity, 1, 0)
        theirs = lax.dynamic_slice_in_dim(merged, 1 - parity, 1, 0)
    grad, new_stat, x = call(functools.partial(begin_kernel, 2), [square] * 3, [], 8, full, "begin")(
        mine, theirs, stat, basis
    )
    new_one, new_two, own_rows, other_rows = call(
        update_kernel, [flat, flat, strips, strips], [(3, full, LANES)], 2, full, "update"
    )(after(grad, x), basis, l_basis, r_basis, first_left, one, two)
    if not aligned:
        top = jnp.where(parity == 0, own_rows, other_rows)
        bottom = jnp.where(parity == 0, other_rows, own_rows)
        merged = jnp.concatenate([top, bottom], axis=1).reshape(tiles_here, 2, rows_here, full)
        own_rows = lax.dynamic_index_in_dim(merged, parity, 1, keepdims=False)
        other_rows = lax.dynamic_index_in_dim(merged, 1 - parity, 1, keepdims=False)
    got_rows = lax.ppermute(other_rows, "shard", pairs)
    keep, send = call(
        functools.partial(end_kernel, NS_ITERS - 2), [flat, flat], [(3, full, LANES), square], 9, full, "end"
    )(after(x, other_rows))
    back = lax.ppermute(send, "shard", pairs)
    update = exchange(after(own_rows, send) + after(got_rows, send))
    new_left, new_right = call(stats_kernel, [flat, flat], [(3, full, LANES)], 1, full, "stats")(
        after(grad, send), new_stat, l_stat, r_stat
    )
    new_l_basis = jnp.where(parity == 0, keep, back)
    new_r_basis = jnp.where(parity == 0, back, keep)
    halves = (new_one, new_two, new_left, new_right, new_l_basis, new_r_basis)
    return (update, *(x.reshape(1, flat_rows * LANES) for x in halves))


def solution(mesh):
    halves = P(("tensor", "shard"), None)
    rows = P("tensor", "shard", None)
    return jax.shard_map(
        local, mesh=mesh, in_specs=(rows,) + (halves,) * 6, out_specs=(rows,) + (halves,) * 6, check_vma=False
    )
```

```python
import functools

import jax
import jax.numpy as jnp
from jax import lax
from jax.experimental import pallas as pl
from jax.experimental.pallas import tpu as pltpu
from jax.sharding import PartitionSpec as P

NS_ITERS = 5
BETA_ONE = 0.9
BETA_TWO = 0.95
ADAM_EPS = 1e-08
NORM_EPS = 1e-06
LINEAR_COEFF = 3.4445
CUBIC_COEFF = -4.775
QUINTIC_COEFF = 2.0315
LANES = 128
F32 = jnp.float32


def split(x):
    high = x.astype(jnp.bfloat16)
    return high, (x - high.astype(F32)).astype(jnp.bfloat16)


def dot(a, b, dims=((1,), (0,))):
    return dot_parts(split(a), split(b), dims)


def dot_parts(a, b, dims=((1,), (0,))):
    (ka,), (kb,) = dims
    left = jnp.concatenate([a[0], a[0], a[1]], axis=ka)
    right = jnp.concatenate([b[0], b[1], b[0]], axis=kb)
    return lax.dot_general(left, right, (dims, ((), ())), preferred_element_type=F32)


def swap(x):
    return pltpu.roll(x, LANES // 2, 1)


def low_lanes(shape):
    return lax.broadcasted_iota(jnp.int32, shape, 1) < LANES // 2


def pick(flag, x, y):
    return [jnp.where(flag, u, v) for u, v in zip(x, y)]


def thirds(ref, start=0, rows=None):
    rows = ref.shape[0] if rows is None else rows
    return [ref[pl.ds(start + k, rows // 3, stride=3), :] for k in range(3)]


def put_thirds(ref, parts):
    for k in range(3):
        ref[pl.ds(k, parts[k].shape[0], stride=3), :] = parts[k]


def interleave(scratch, index, even, odd):
    scratch[index, pl.ds(0, even.shape[0], stride=2), :] = even
    scratch[index, pl.ds(1, odd.shape[0], stride=2), :] = odd


def whole_of(scratch, first, second):
    a, b, c = first
    d, e, f = second
    low = low_lanes(a.shape)
    sb, sc, sd, se = swap(b), swap(c), swap(d), swap(e)
    interleave(scratch, 0, a, jnp.where(low, sb, sc))
    interleave(scratch, 1, jnp.where(low, b, sd), jnp.where(low, sc, e))
    interleave(scratch, 2, jnp.where(low, sd, se), f)
    return jnp.concatenate([scratch[0], scratch[1], scratch[2]], axis=1)


def half_of(scratch, flat):
    a, b, c = flat
    low = low_lanes(a.shape)
    sb, sc = swap(b), swap(c)
    interleave(scratch, 0, a, jnp.where(low, sb, sc))
    interleave(scratch, 1, jnp.where(low, b, 0.0), jnp.where(low, sc, 0.0))
    return jnp.concatenate([scratch[0], scratch[1]], axis=1)


def flat_of(scratch, half):
    scratch[0] = half[:, :LANES]
    scratch[1] = half[:, LANES:]
    pairs = half.shape[0] // 2
    even0 = scratch[0, pl.ds(0, pairs, stride=2), :]
    odd0 = swap(scratch[0, pl.ds(1, pairs, stride=2), :])
    even1 = scratch[1, pl.ds(0, pairs, stride=2), :]
    odd1 = swap(scratch[1, pl.ds(1, pairs, stride=2), :])
    low = low_lanes(even0.shape)
    return [even0, jnp.where(low, even1, odd0), jnp.where(low, odd0, odd1)]


def take_half(whole, first):
    one, two, three = whole[:, :LANES], whole[:, LANES : 2 * LANES], whole[:, 2 * LANES :]
    low = low_lanes(one.shape)
    s2, s3 = swap(two), swap(three)
    head = jnp.where(first, one, jnp.where(low, s2, s3))
    tail = jnp.where(low, jnp.where(first, two, s3), 0.0)
    return jnp.concatenate([head, tail], axis=1)


def is_left():
    return lax.rem(lax.axis_index("shard"), 2) == 0


def pack_kernel(hops, l_stat_ref, r_stat_ref, l_basis_ref, r_basis_ref, grads_ref, *refs):
    out_ref, piece_refs, (corner, small, sems) = refs[0], refs[1 : 1 + len(hops)], refs[1 + len(hops) :]
    left = is_left()
    flat_rows = l_basis_ref.shape[0]
    half_rows = flat_rows // 2
    rows = grads_ref.shape[1]
    here = lax.axis_index("shard") // 2

    def copies(basis_ref, stat_ref, start):
        return [
            pltpu.make_async_copy(stat_ref.at[pl.ds(start, half_rows)], corner, sems.at[0]),
            pltpu.make_async_copy(basis_ref, out_ref.at[pl.ds(0, flat_rows)], sems.at[1]),
        ]

    @pl.when(left)
    def _():
        for copy in copies(r_basis_ref, r_stat_ref, 0):
            copy.start()

    @pl.when(jnp.logical_not(left))
    def _():
        for copy in copies(l_basis_ref, l_stat_ref, half_rows):
            copy.start()

    more = []
    for number, (hop, piece_ref) in enumerate(zip(hops, piece_refs)):
        more.append(pltpu.make_async_copy(grads_ref.at[here ^ hop], piece_ref, sems.at[2 + number]))
    if hops:
        start = flat_rows + corner_rows(flat_rows)
        for k in range(grads_ref.shape[2] // LANES):
            source = grads_ref.at[here, :, pl.ds(k * LANES, LANES)]
            more.append(
                pltpu.make_async_copy(source, out_ref.at[pl.ds(start + k * rows, rows)], sems.at[2 + len(hops) + k])
            )
    for copy in more:
        copy.start()
    first, second = copies(l_basis_ref, l_stat_ref, half_rows)
    first.wait()
    third = half_rows // 9
    a, b, c = thirds(corner)
    low = low_lanes((third, LANES))
    middle = slice(third, 2 * third)
    small[pl.ds(0, third)] = jnp.where(low, a[:third], b[:third])
    small[pl.ds(third, third)] = a[middle]
    small[pl.ds(2 * third, third)] = jnp.where(low, swap(b[middle]), swap(c[middle]))
    small[pl.ds(3 * third, 3 * third)] = corner[pl.ds(6 * third, 3 * third)]
    last = pltpu.make_async_copy(small, out_ref.at[pl.ds(flat_rows, corner_rows(flat_rows))], sems.at[0])
    last.start()
    for copy in [second, *more, last]:
        copy.wait()


def corner_rows(flat_rows):
    return flat_rows // 3


def unpack_corner(got_ref, start, count):
    third = count // 6
    small = got_ref[pl.ds(start, third), :]
    even = got_ref[pl.ds(start + third, third), :]
    odd = swap(got_ref[pl.ds(start + 2 * third, third), :])
    a, b, c = thirds(got_ref, start + 3 * third, 3 * third)
    low = low_lanes(small.shape)
    zero = jnp.zeros_like(small)
    return [
        jnp.concatenate([jnp.where(low, small, zero), even, a], axis=0),
        jnp.concatenate([jnp.where(low, zero, small), jnp.where(low, zero, odd), b], axis=0),
        jnp.concatenate([zero, jnp.where(low, odd, zero), c], axis=0),
    ]


def prepare_kernel(l_stat_ref, r_stat_ref, l_basis_ref, r_basis_ref, got_ref, stat_ref, basis_ref, scratch):
    left = is_left()
    flat_rows = l_stat_ref.shape[0]
    own = pick(left, thirds(l_basis_ref), thirds(r_basis_ref))
    got = thirds(got_ref, 0, flat_rows)
    basis_ref[...] = whole_of(scratch, pick(left, own, got), pick(left, got, own))
    own = pick(left, thirds(l_stat_ref), thirds(r_stat_ref))
    corner = unpack_corner(got_ref, flat_rows, corner_rows(flat_rows))
    placed = [jnp.concatenate([jnp.where(left, 0.0, c), jnp.where(left, c, 0.0)], axis=0) for c in corner]
    known = whole_of(scratch, pick(left, own, placed), pick(left, placed, own))
    half = known.shape[0] // 2
    part = half // 3
    row = lax.broadcasted_iota(jnp.int32, known.shape, 0)
    column = lax.broadcasted_iota(jnp.int32, known.shape, 1)
    missing = (jnp.where(left, row, column) < half) & (jnp.where(left, column, row) >= half)
    offset = jnp.where(left, half, 0)
    row, column = row - offset, column - offset
    limit = jnp.where(row < part, part, 2 * part)
    missing |= (row >= 0) & (row < 2 * part) & (column < half) & (column >= limit)
    stat_ref[...] = 0.5 * jnp.where(missing, known.T, known)


def place_rows(grad_ref, block, rows, value):
    grad_ref[pl.ds(pl.multiple_of(block * rows, 8), rows), :] = value


def iterate(x_ref, steps):
    @pl.loop(0, steps)
    def _(step):
        x = x_ref[...]
        parts = split(x)
        gram = dot_parts(parts, parts, ((1,), (1,)))
        gram_parts = split(gram)
        poly = CUBIC_COEFF * gram + QUINTIC_COEFF * dot_parts(gram_parts, gram_parts)
        x_ref[...] = LINEAR_COEFF * x + dot_parts(split(poly), parts)


def begin_kernel(steps, hops, *refs):
    left = is_left()
    if hops:
        grads_ref, got_ref, *rest = refs
        mine_refs, theirs_refs = rest[: len(hops)], rest[len(hops) : 2 * len(hops)]
        stat_ref, basis_ref, grad_ref, new_stat_ref, x_ref = rest[2 * len(hops) :]
        rows = grads_ref.shape[1]
        here = lax.axis_index("shard") // 2
        parity = lax.axis_index("shard") % 2
        start = got_ref.shape[0] - grad_ref.shape[1] // LANES * rows
        received = [got_ref[pl.ds(start + k * rows, rows), :] for k in range(grad_ref.shape[1] // LANES)]
        place_rows(grad_ref, 2 * here + parity, rows, grads_ref[here])
        place_rows(grad_ref, 2 * here + 1 - parity, rows, jnp.concatenate(received, axis=1))
        for hop, mine, theirs in zip(hops, mine_refs, theirs_refs):
            place_rows(grad_ref, 2 * (here ^ hop) + parity, rows, mine[...])
            place_rows(grad_ref, 2 * (here ^ hop) + 1 - parity, rows, theirs[...])
    else:
        whole_ref, stat_ref, basis_ref, grad_ref, new_stat_ref, x_ref = refs
        grad_ref[...] = whole_ref[...]
    grad = grad_ref[...]
    turned = grad.T
    new_stat = stat_ref[...] + 0.5 * dot(jnp.where(left, grad, turned), jnp.where(left, turned, grad))
    new_stat_ref[...] = new_stat
    power = dot(new_stat, basis_ref[...])
    x_ref[...] = power * (1.0 / jnp.sqrt(jnp.sum(power * power) + NORM_EPS))
    iterate(x_ref, steps)


def end_kernel(steps, start_ref, keep_ref, send_ref, scratch, x_ref):
    left = is_left()
    x_ref[...] = start_ref[...]
    iterate(x_ref, steps)
    x = x_ref[...]
    put_thirds(send_ref, flat_of(scratch, take_half(x, jnp.logical_not(left))))
    put_thirds(keep_ref, flat_of(scratch, take_half(x, left)))


def update_kernel(
    hops,
    grad_ref,
    basis_ref,
    left_ref,
    right_ref,
    first_left_ref,
    one_ref,
    two_ref,
    new_one_ref,
    new_two_ref,
    mine_ref,
    theirs_ref,
    scratch,
    partial_ref,
):
    left = is_left()
    basis_left = jnp.where(left, basis_ref[...], whole_of(scratch, thirds(first_left_ref), thirds(left_ref)))
    left_parts = split(basis_left)
    basis_right = split(half_of(scratch, thirds(right_ref)))
    inner = dot_parts(split(grad_ref[...]), basis_right)
    rotated = flat_of(scratch, dot(basis_left.T, inner))
    ones = thirds(one_ref)
    twos = thirds(two_ref)
    new_one = [BETA_ONE * m + (1.0 - BETA_ONE) * r for m, r in zip(ones, rotated)]
    new_two = [BETA_TWO * v + (1.0 - BETA_TWO) * r * r for v, r in zip(twos, rotated)]
    put_thirds(new_one_ref, new_one)
    put_thirds(new_two_ref, new_two)
    direction = [m / (jnp.sqrt(v) + ADAM_EPS) for m, v in zip(new_one, new_two)]
    outer = dot_parts(left_parts, split(half_of(scratch, direction)))
    partial_ref[...] = dot_parts(split(outer), basis_right, ((1,), (1,)))
    rows = mine_ref.shape[1]
    here = lax.axis_index("shard") // 2
    parity = lax.axis_index("shard") % 2
    for k, hop in enumerate((0, *hops)):
        block = 2 * (here ^ hop) if hops else 0
        mine_ref[k] = partial_ref[pl.ds(pl.multiple_of((block + parity) * rows, 8), rows), :]
        theirs_ref[k] = partial_ref[pl.ds(pl.multiple_of((block + 1 - parity) * rows, 8), rows), :]


def add_kernel(mine_ref, theirs_ref, *out_refs):
    for k, out_ref in enumerate(out_refs):
        out_ref[...] = mine_ref[k] + theirs_ref[k]


def finish_kernel(hops, keep_ref, back_ref, *refs):
    count = 1 + len(hops)
    rows_refs = refs[:count]
    update_ref, new_left_ref, new_right_ref, sems = refs[count:]
    left = is_left()
    here = lax.axis_index("shard") // 2

    def copies(own_ref, other_ref):
        return [
            pltpu.make_async_copy(keep_ref, own_ref, sems.at[0]),
            pltpu.make_async_copy(back_ref, other_ref, sems.at[1]),
        ]

    @pl.when(left)
    def _():
        for copy in copies(new_left_ref, new_right_ref):
            copy.start()

    @pl.when(jnp.logical_not(left))
    def _():
        for copy in copies(new_right_ref, new_left_ref):
            copy.start()

    rows = [
        pltpu.make_async_copy(rows_refs[k], update_ref.at[here ^ hop], sems.at[2 + k])
        for k, hop in enumerate((0, *hops))
    ]
    for copy in rows:
        copy.start()
    for copy in rows + copies(new_left_ref, new_right_ref):
        copy.wait()


def stats_kernel(grad_ref, new_stat_ref, left_ref, right_ref, new_left_ref, new_right_ref, scratch):
    left = is_left()
    other = pick(left, thirds(right_ref), thirds(left_ref))
    grad = grad_ref[...]
    turned = grad.T
    a = jnp.where(left, grad, turned)
    b = jnp.where(left, turned, grad)
    new_own = flat_of(scratch, take_half(new_stat_ref[...], left))
    product = flat_of(scratch, dot(b, take_half(a, left)))
    new_other = [0.5 * u + 0.5 * v for u, v in zip(other, product)]
    put_thirds(new_left_ref, pick(left, new_own, new_other))
    put_thirds(new_right_ref, pick(left, new_other, new_own))


def call(kernel, outs, scratch, products, full, name, copies=0, **specs):
    size = full * full
    scratch = [pltpu.VMEM(s, F32) for s in scratch]
    if copies:
        scratch.append(pltpu.SemaphoreType.DMA((copies,)))
    return pl.pallas_call(
        kernel,
        out_shape=[jax.ShapeDtypeStruct(s, F32) for s in outs],
        scratch_shapes=scratch,
        compiler_params=pltpu.CompilerParams(vmem_limit_bytes=40 * 1024 * 1024),
        cost_estimate=pl.CostEstimate(flops=int(products * 6 * full * size), bytes_accessed=16 * size, transcendentals=0),
        name=name,
        **specs,
    )


def anywhere(count):
    return [pl.BlockSpec(memory_space=pl.ANY)] * count


def after(x, *others):
    return lax.optimization_barrier((x, *others))[0]


def local(grads, moment_one, moment_two, left_stat, right_stat, left_basis, right_basis):
    tiles_here, rows_here, full = grads.shape
    size = lax.axis_size("shard")
    flat_rows = full * (full // 2) // LANES
    flat = (flat_rows, LANES)
    square = (full, full)
    block = (rows_here, full)
    parity = lax.axis_index("shard") % 2
    pairs = [(i, i ^ 1) for i in range(size)]
    sides = [list(range(k, size, 2)) for k in range(2)]
    near = size in (4, 8) and rows_here % 8 == 0
    hops = {4: (1,), 8: (2, 3, 1)}[size] if near else ()
    strips = (tiles_here, *block) if near else (1, full // 2, full)

    def exchange(x):
        return lax.all_to_all(x, "shard", split_axis=0, concat_axis=0, axis_index_groups=sides, tiled=True)

    def hop_by(x, hop):
        return lax.ppermute(x, "shard", [(i, i ^ (2 * hop)) for i in range(size)])

    def partner(x):
        return lax.ppermute(x, "shard", pairs)

    one, two, l_stat, r_stat, l_basis, r_basis = (
        x.reshape(flat) for x in (moment_one, moment_two, left_stat, right_stat, left_basis, right_basis)
    )
    count = corner_rows(flat_rows)
    outgoing_rows = flat_rows + count + (rows_here * (full // LANES) if near else 0)
    outgoing, *pieces = call(
        functools.partial(pack_kernel, hops),
        [(outgoing_rows, LANES)] + [block] * len(hops),
        [(flat_rows // 2, LANES), (count, LANES)],
        0.1,
        full,
        "pack",
        copies=2 + len(hops) + full // LANES,
        in_specs=anywhere(5),
        out_specs=anywhere(1 + len(hops)),
    )(l_stat, r_stat, l_basis, r_basis, grads)
    got = partner(outgoing)
    if near:
        mine = [hop_by(piece, hop) for hop, piece in zip(hops, pieces)]
        theirs = [partner(x) for x in mine]
        rows = (grads, got, *mine, *theirs)
        last = theirs
    else:
        mine = exchange(grads)
        theirs = partner(mine)
        mine, last = jnp.where(parity == 0, mine, theirs), [theirs]
        rows = (jnp.stack([mine, jnp.where(parity == 0, theirs, mine)], axis=1).reshape(square),)
    first_left = partner(after(l_basis, *last))
    stat, basis = call(prepare_kernel, [square, square], [(3, full, LANES)], 0.1, full, "prepare")(
        l_stat, r_stat, l_basis, r_basis, got
    )
    grad, new_stat, x = call(functools.partial(begin_kernel, 2, hops), [square] * 3, [], 8, full, "begin")(
        *rows, stat, basis
    )
    new_one, new_two, own_rows, other_rows = call(
        functools.partial(update_kernel, hops), [flat, flat, strips, strips], [(3, full, LANES), square], 2, full, "update"
    )(after(grad, x), basis, l_basis, r_basis, first_left, one, two)
    if not near:
        top = jnp.where(parity == 0, own_rows, other_rows)
        bottom = jnp.where(parity == 0, other_rows, own_rows)
        merged = jnp.concatenate([top, bottom], axis=1).reshape(tiles_here, 2, rows_here, full)
        own_rows = lax.dynamic_index_in_dim(merged, parity, 1, keepdims=False)
        other_rows = lax.dynamic_index_in_dim(merged, 1 - parity, 1, keepdims=False)
    got_rows = partner(other_rows)
    keep, send = call(
        functools.partial(end_kernel, NS_ITERS - 2), [flat, flat], [(3, full, LANES), square], 9, full, "end"
    )(after(x, other_rows))
    back = partner(send)
    if near:
        kept, *sums = call(add_kernel, [block] * (1 + len(hops)), [], 0.1, full, "add")(
            after(own_rows, send), after(got_rows, send)
        )
        returned = [hop_by(x, hop) for hop, x in zip(hops, sums)]
        update, new_l_basis, new_r_basis = call(
            functools.partial(finish_kernel, hops),
            [grads.shape, flat, flat],
            [],
            0.1,
            full,
            "finish",
            copies=3 + len(hops),
            in_specs=anywhere(3 + len(hops)),
            out_specs=anywhere(3),
        )(keep, back, kept, *returned)
    else:
        update = exchange(after(own_rows, send) + after(got_rows, send))
        new_l_basis = jnp.where(parity == 0, keep, back)
        new_r_basis = jnp.where(parity == 0, back, keep)
    new_left, new_right = call(stats_kernel, [flat, flat], [(3, full, LANES)], 1, full, "stats")(
        after(grad, send), new_stat, l_stat, r_stat
    )
    halves = (new_one, new_two, new_left, new_right, new_l_basis, new_r_basis)
    return (update, *(x.reshape(1, flat_rows * LANES) for x in halves))


def solution(mesh):
    halves = P(("tensor", "shard"), None)
    rows = P("tensor", "shard", None)
    return jax.shard_map(
        local, mesh=mesh, in_specs=(rows,) + (halves,) * 6, out_specs=(rows,) + (halves,) * 6, check_vma=False
    )
```

```python
import functools

import jax
import jax.numpy as jnp
from jax import lax
from jax.experimental import pallas as pl
from jax.experimental.pallas import tpu as pltpu
from jax.sharding import PartitionSpec as P

NS_ITERS = 5
BETA_ONE = 0.9
BETA_TWO = 0.95
ADAM_EPS = 1e-08
NORM_EPS = 1e-06
LINEAR_COEFF = 3.4445
CUBIC_COEFF = -4.775
QUINTIC_COEFF = 2.0315
LANES = 128
F32 = jnp.float32


def split(x):
    high = x.astype(jnp.bfloat16)
    return high, (x - high.astype(F32)).astype(jnp.bfloat16)


def dot(a, b, dims=((1,), (0,))):
    return dot_parts(split(a), split(b), dims)


def dot_parts(a, b, dims=((1,), (0,))):
    (ka,), (kb,) = dims
    left = jnp.concatenate([a[0], a[0], a[1]], axis=ka)
    right = jnp.concatenate([b[0], b[1], b[0]], axis=kb)
    return lax.dot_general(left, right, (dims, ((), ())), preferred_element_type=F32)


def swap(x):
    return pltpu.roll(x, LANES // 2, 1)


def low_lanes(shape):
    return lax.broadcasted_iota(jnp.int32, shape, 1) < LANES // 2


def pick(flag, x, y):
    return [jnp.where(flag, u, v) for u, v in zip(x, y)]


def thirds(ref, start=0, rows=None):
    rows = ref.shape[0] if rows is None else rows
    return [ref[pl.ds(start + k, rows // 3, stride=3), :] for k in range(3)]


def put_thirds(ref, parts):
    for k in range(3):
        ref[pl.ds(k, parts[k].shape[0], stride=3), :] = parts[k]


def interleave(scratch, index, even, odd):
    scratch[index, pl.ds(0, even.shape[0], stride=2), :] = even
    scratch[index, pl.ds(1, odd.shape[0], stride=2), :] = odd


def whole_of(scratch, first, second):
    a, b, c = first
    d, e, f = second
    low = low_lanes(a.shape)
    sb, sc, sd, se = swap(b), swap(c), swap(d), swap(e)
    interleave(scratch, 0, a, jnp.where(low, sb, sc))
    interleave(scratch, 1, jnp.where(low, b, sd), jnp.where(low, sc, e))
    interleave(scratch, 2, jnp.where(low, sd, se), f)
    return jnp.concatenate([scratch[0], scratch[1], scratch[2]], axis=1)


def half_of(scratch, flat):
    a, b, c = flat
    low = low_lanes(a.shape)
    sb, sc = swap(b), swap(c)
    interleave(scratch, 0, a, jnp.where(low, sb, sc))
    interleave(scratch, 1, jnp.where(low, b, 0.0), jnp.where(low, sc, 0.0))
    return jnp.concatenate([scratch[0], scratch[1]], axis=1)


def flat_of(scratch, half):
    scratch[0] = half[:, :LANES]
    scratch[1] = half[:, LANES:]
    pairs = half.shape[0] // 2
    even0 = scratch[0, pl.ds(0, pairs, stride=2), :]
    odd0 = swap(scratch[0, pl.ds(1, pairs, stride=2), :])
    even1 = scratch[1, pl.ds(0, pairs, stride=2), :]
    odd1 = swap(scratch[1, pl.ds(1, pairs, stride=2), :])
    low = low_lanes(even0.shape)
    return [even0, jnp.where(low, even1, odd0), jnp.where(low, odd0, odd1)]


def take_half(whole, first):
    one, two, three = whole[:, :LANES], whole[:, LANES : 2 * LANES], whole[:, 2 * LANES :]
    low = low_lanes(one.shape)
    s2, s3 = swap(two), swap(three)
    head = jnp.where(first, one, jnp.where(low, s2, s3))
    tail = jnp.where(low, jnp.where(first, two, s3), 0.0)
    return jnp.concatenate([head, tail], axis=1)


def is_left():
    return lax.rem(lax.axis_index("shard"), 2) == 0


def pack_kernel(hops, l_stat_ref, r_stat_ref, l_basis_ref, r_basis_ref, grads_ref, *refs):
    out_ref, small_ref, *refs = refs
    piece_refs, (corner, sems) = refs[: len(hops)], refs[len(hops) :]
    left = is_left()
    flat_rows = l_basis_ref.shape[0]
    half_rows = flat_rows // 2
    rows = grads_ref.shape[1]
    here = lax.axis_index("shard") // 2

    def copies(basis_ref, stat_ref, start):
        return [
            pltpu.make_async_copy(stat_ref.at[pl.ds(start, half_rows)], corner, sems.at[0]),
            pltpu.make_async_copy(basis_ref, out_ref.at[pl.ds(0, flat_rows)], sems.at[1]),
        ]

    @pl.when(left)
    def _():
        for copy in copies(r_basis_ref, r_stat_ref, 0):
            copy.start()

    @pl.when(jnp.logical_not(left))
    def _():
        for copy in copies(l_basis_ref, l_stat_ref, half_rows):
            copy.start()

    more = []
    for number, (hop, piece_ref) in enumerate(zip(hops, piece_refs)):
        more.append(pltpu.make_async_copy(grads_ref.at[here ^ hop], piece_ref, sems.at[2 + number]))
    if hops:
        for k in range(grads_ref.shape[2] // LANES):
            source = grads_ref.at[here, :, pl.ds(k * LANES, LANES)]
            target = out_ref.at[pl.ds(flat_rows + k * rows, rows)]
            more.append(pltpu.make_async_copy(source, target, sems.at[2 + len(hops) + k]))
    for copy in more:
        copy.start()
    first, second = copies(l_basis_ref, l_stat_ref, half_rows)
    first.wait()
    third = half_rows // 9
    a, b, c = thirds(corner)
    low = low_lanes((third, LANES))
    middle = slice(third, 2 * third)
    small_ref[pl.ds(0, third)] = jnp.where(low, a[:third], b[:third])
    small_ref[pl.ds(third, third)] = a[middle]
    small_ref[pl.ds(2 * third, third)] = jnp.where(low, swap(b[middle]), swap(c[middle]))
    small_ref[pl.ds(3 * third, 3 * third)] = corner[pl.ds(6 * third, 3 * third)]
    for copy in [second, *more]:
        copy.wait()


def corner_rows(flat_rows):
    return flat_rows // 3


def unpack_corner(got_ref):
    third = got_ref.shape[0] // 6
    small = got_ref[pl.ds(0, third), :]
    even = got_ref[pl.ds(third, third), :]
    odd = swap(got_ref[pl.ds(2 * third, third), :])
    a, b, c = thirds(got_ref, 3 * third, 3 * third)
    low = low_lanes(small.shape)
    zero = jnp.zeros_like(small)
    return [
        jnp.concatenate([jnp.where(low, small, zero), even, a], axis=0),
        jnp.concatenate([jnp.where(low, zero, small), jnp.where(low, zero, odd), b], axis=0),
        jnp.concatenate([zero, jnp.where(low, odd, zero), c], axis=0),
    ]


def statistic(left, own, got_ref, scratch):
    corner = unpack_corner(got_ref)
    placed = [jnp.concatenate([jnp.where(left, 0.0, c), jnp.where(left, c, 0.0)], axis=0) for c in corner]
    known = whole_of(scratch, pick(left, own, placed), pick(left, placed, own))
    half = known.shape[0] // 2
    part = half // 3
    row = lax.broadcasted_iota(jnp.int32, known.shape, 0)
    column = lax.broadcasted_iota(jnp.int32, known.shape, 1)
    missing = (jnp.where(left, row, column) < half) & (jnp.where(left, column, row) >= half)
    offset = jnp.where(left, half, 0)
    row, column = row - offset, column - offset
    limit = jnp.where(row < part, part, 2 * part)
    missing |= (row >= 0) & (row < 2 * part) & (column < half) & (column >= limit)
    return jnp.where(missing, known.T, known)


def place_rows(grad_ref, block, rows, value):
    grad_ref[pl.ds(pl.multiple_of(block * rows, 8), rows), :] = value


def iterate(x_ref, steps):
    @pl.loop(0, steps)
    def _(step):
        x = x_ref[...]
        parts = split(x)
        gram = dot_parts(parts, parts, ((1,), (1,)))
        gram_parts = split(gram)
        poly = CUBIC_COEFF * gram + QUINTIC_COEFF * dot_parts(gram_parts, gram_parts)
        x_ref[...] = LINEAR_COEFF * x + dot_parts(split(poly), parts)


def products_kernel(hops, l_stat_ref, r_stat_ref, l_basis_ref, r_basis_ref, got_ref, *refs):
    left = is_left()
    outs = refs[-9:]
    grad_ref, product_ref, basis_ref, right_ref, inner_ref, own_ref, other_ref, copy_ref, scratch = outs
    if hops:
        grads_ref, mine_refs, theirs_refs = refs[0], refs[1 : 1 + len(hops)], refs[1 + len(hops) : 1 + 2 * len(hops)]
        rows = grads_ref.shape[1]
        here = lax.axis_index("shard") // 2
        parity = lax.axis_index("shard") % 2
        start = l_basis_ref.shape[0]
        received = [got_ref[pl.ds(start + k * rows, rows), :] for k in range(grad_ref.shape[1] // LANES)]
        place_rows(grad_ref, 2 * here + parity, rows, grads_ref[here])
        place_rows(grad_ref, 2 * here + 1 - parity, rows, jnp.concatenate(received, axis=1))
        for hop, mine, theirs in zip(hops, mine_refs, theirs_refs):
            place_rows(grad_ref, 2 * (here ^ hop) + parity, rows, mine[...])
            place_rows(grad_ref, 2 * (here ^ hop) + 1 - parity, rows, theirs[...])
    else:
        grad_ref[...] = refs[0][...]
    own = pick(left, thirds(l_basis_ref), thirds(r_basis_ref))
    got = thirds(got_ref, 0, l_basis_ref.shape[0])
    basis_ref[...] = whole_of(scratch, pick(left, own, got), pick(left, got, own))
    own_ref[...] = jnp.where(left, l_stat_ref[...], r_stat_ref[...])
    other_ref[...] = jnp.where(left, r_stat_ref[...], l_stat_ref[...])
    copy_ref[...] = l_basis_ref[...]
    right = half_of(scratch, thirds(r_basis_ref))
    right_ref[...] = right
    grad = grad_ref[...]
    turned = grad.T
    product_ref[...] = dot(jnp.where(left, grad, turned), jnp.where(left, turned, grad))
    inner_ref[...] = dot(grad, right)


def begin_kernel(steps, own_ref, corner_ref, product_ref, basis_ref, new_stat_ref, x_ref, scratch):
    new_stat = 0.5 * statistic(is_left(), thirds(own_ref), corner_ref, scratch) + 0.5 * product_ref[...]
    new_stat_ref[...] = new_stat
    power = dot(new_stat, basis_ref[...])
    x_ref[...] = power * (1.0 / jnp.sqrt(jnp.sum(power * power) + NORM_EPS))
    iterate(x_ref, steps)


def end_kernel(steps, start_ref, keep_ref, send_ref, scratch, x_ref):
    left = is_left()
    x_ref[...] = start_ref[...]
    iterate(x_ref, steps)
    x = x_ref[...]
    put_thirds(send_ref, flat_of(scratch, take_half(x, jnp.logical_not(left))))
    put_thirds(keep_ref, flat_of(scratch, take_half(x, left)))


def update_kernel(
    hops,
    inner_ref,
    basis_ref,
    left_ref,
    right_ref,
    first_left_ref,
    one_ref,
    two_ref,
    new_one_ref,
    new_two_ref,
    mine_ref,
    theirs_ref,
    scratch,
    partial_ref,
):
    left = is_left()
    basis_left = jnp.where(left, basis_ref[...], whole_of(scratch, thirds(first_left_ref), thirds(left_ref)))
    left_parts = split(basis_left)
    basis_right = split(right_ref[...])
    rotated = flat_of(scratch, dot(basis_left.T, inner_ref[...]))
    ones = thirds(one_ref)
    twos = thirds(two_ref)
    new_one = [BETA_ONE * m + (1.0 - BETA_ONE) * r for m, r in zip(ones, rotated)]
    new_two = [BETA_TWO * v + (1.0 - BETA_TWO) * r * r for v, r in zip(twos, rotated)]
    put_thirds(new_one_ref, new_one)
    put_thirds(new_two_ref, new_two)
    direction = [m / (jnp.sqrt(v) + ADAM_EPS) for m, v in zip(new_one, new_two)]
    outer = dot_parts(left_parts, split(half_of(scratch, direction)))
    partial_ref[...] = dot_parts(split(outer), basis_right, ((1,), (1,)))
    rows = mine_ref.shape[1]
    here = lax.axis_index("shard") // 2
    parity = lax.axis_index("shard") % 2
    for k, hop in enumerate((0, *hops)):
        block = 2 * (here ^ hop) if hops else 0
        mine_ref[k] = partial_ref[pl.ds(pl.multiple_of((block + parity) * rows, 8), rows), :]
        theirs_ref[k] = partial_ref[pl.ds(pl.multiple_of((block + 1 - parity) * rows, 8), rows), :]


def add_kernel(mine_ref, theirs_ref, *out_refs):
    for k, out_ref in enumerate(out_refs):
        out_ref[...] = mine_ref[k] + theirs_ref[k]


def finish_kernel(hops, keep_ref, back_ref, *refs):
    count = 1 + len(hops)
    rows_refs = refs[:count]
    update_ref, new_left_ref, new_right_ref, sems = refs[count:]
    left = is_left()
    here = lax.axis_index("shard") // 2

    def copies(own_ref, other_ref):
        return [
            pltpu.make_async_copy(keep_ref, own_ref, sems.at[0]),
            pltpu.make_async_copy(back_ref, other_ref, sems.at[1]),
        ]

    @pl.when(left)
    def _():
        for copy in copies(new_left_ref, new_right_ref):
            copy.start()

    @pl.when(jnp.logical_not(left))
    def _():
        for copy in copies(new_right_ref, new_left_ref):
            copy.start()

    rows = [
        pltpu.make_async_copy(rows_refs[k], update_ref.at[here ^ hop], sems.at[2 + k])
        for k, hop in enumerate((0, *hops))
    ]
    for copy in rows:
        copy.start()
    for copy in rows + copies(new_left_ref, new_right_ref):
        copy.wait()


def stats_kernel(grad_ref, new_stat_ref, other_ref, new_left_ref, new_right_ref, scratch):
    left = is_left()
    grad = grad_ref[...]
    turned = grad.T
    a = jnp.where(left, grad, turned)
    b = jnp.where(left, turned, grad)
    new_own = flat_of(scratch, take_half(new_stat_ref[...], left))
    product = flat_of(scratch, dot(b, take_half(a, left)))
    new_other = [0.5 * u + 0.5 * v for u, v in zip(thirds(other_ref), product)]
    put_thirds(new_left_ref, pick(left, new_own, new_other))
    put_thirds(new_right_ref, pick(left, new_other, new_own))


def call(kernel, outs, scratch, products, full, name, copies=0, limit=40, **specs):
    size = full * full
    scratch = [pltpu.VMEM(s, F32) for s in scratch]
    if copies:
        scratch.append(pltpu.SemaphoreType.DMA((copies,)))
    return pl.pallas_call(
        kernel,
        out_shape=[jax.ShapeDtypeStruct(s, F32) for s in outs],
        scratch_shapes=scratch,
        compiler_params=pltpu.CompilerParams(vmem_limit_bytes=limit * 1024 * 1024),
        cost_estimate=pl.CostEstimate(flops=int(products * 6 * full * size), bytes_accessed=16 * size, transcendentals=0),
        name=name,
        **specs,
    )


def anywhere(count):
    return [pl.BlockSpec(memory_space=pl.ANY)] * count


def after(x, *others):
    return lax.optimization_barrier((x, *others))[0]


def local(grads, moment_one, moment_two, left_stat, right_stat, left_basis, right_basis):
    tiles_here, rows_here, full = grads.shape
    size = lax.axis_size("shard")
    flat_rows = full * (full // 2) // LANES
    flat = (flat_rows, LANES)
    square = (full, full)
    block = (rows_here, full)
    parity = lax.axis_index("shard") % 2
    pairs = [(i, i ^ 1) for i in range(size)]
    sides = [list(range(k, size, 2)) for k in range(2)]
    near = size in (4, 8) and rows_here % 8 == 0
    hops = {4: (1,), 8: (2, 3, 1)}[size] if near else ()
    strips = (tiles_here, *block) if near else (1, full // 2, full)

    def exchange(x):
        return lax.all_to_all(x, "shard", split_axis=0, concat_axis=0, axis_index_groups=sides, tiled=True)

    def hop_by(x, hop):
        return lax.ppermute(x, "shard", [(i, i ^ (2 * hop)) for i in range(size)])

    def partner(x):
        return lax.ppermute(x, "shard", pairs)

    one, two, l_stat, r_stat, l_basis, r_basis = (
        x.reshape(flat) for x in (moment_one, moment_two, left_stat, right_stat, left_basis, right_basis)
    )
    count = corner_rows(flat_rows)
    outgoing_rows = flat_rows + (rows_here * (full // LANES) if near else 0)
    outgoing, corner, *pieces = call(
        functools.partial(pack_kernel, hops),
        [(outgoing_rows, LANES), (count, LANES)] + [block] * len(hops),
        [(flat_rows // 2, LANES)],
        0.1,
        full,
        "pack",
        copies=2 + len(hops) + full // LANES,
        limit=63,
        in_specs=[pl.BlockSpec(memory_space=pltpu.HBM)] * 5,
        out_specs=anywhere(1) + [pl.BlockSpec(memory_space=pltpu.VMEM)] + anywhere(len(hops)),
    )(l_stat, r_stat, l_basis, r_basis, grads)
    got = partner(outgoing)
    if near:
        mine = [hop_by(piece, hop) for hop, piece in zip(hops, pieces)]
        theirs = [partner(x) for x in mine]
        rows = (grads, *mine, *theirs)
    else:
        mine = exchange(grads)
        theirs = partner(mine)
        even, odd = jnp.where(parity == 0, mine, theirs), jnp.where(parity == 0, theirs, mine)
        rows = (jnp.stack([even, odd], axis=1).reshape(square),)
        mine = [mine]
    got_corner = partner(after(corner, *mine))
    grad, product, basis, right, inner, own, other, left = call(
        functools.partial(products_kernel, hops),
        [square, square, square, (full, 2 * LANES), (full, 2 * LANES), flat, flat, flat],
        [(3, full, LANES)],
        2,
        full,
        "products",
    )(l_stat, r_stat, l_basis, r_basis, got, *rows)
    first_left = partner(after(l_basis, product))
    new_stat, x = call(functools.partial(begin_kernel, 2), [square] * 2, [(3, full, LANES)], 7, full, "begin")(
        own, got_corner, product, basis
    )
    new_one, new_two, own_rows, other_rows = call(
        functools.partial(update_kernel, hops), [flat, flat, strips, strips], [(3, full, LANES), square], 2, full, "update"
    )(after(inner, x), basis, left, right, first_left, one, two)
    if not near:
        top = jnp.where(parity == 0, own_rows, other_rows)
        bottom = jnp.where(parity == 0, other_rows, own_rows)
        merged = jnp.concatenate([top, bottom], axis=1).reshape(tiles_here, 2, rows_here, full)
        own_rows = lax.dynamic_index_in_dim(merged, parity, 1, keepdims=False)
        other_rows = lax.dynamic_index_in_dim(merged, 1 - parity, 1, keepdims=False)
    got_rows = partner(other_rows)
    keep, send = call(
        functools.partial(end_kernel, NS_ITERS - 2), [flat, flat], [(3, full, LANES), square], 9, full, "end"
    )(after(x, other_rows))
    back = partner(send)
    if near:
        kept, *sums = call(add_kernel, [block] * (1 + len(hops)), [], 0.1, full, "add")(
            after(own_rows, send), after(got_rows, send)
        )
        returned = [hop_by(x, hop) for hop, x in zip(hops, sums)]
        update, new_l_basis, new_r_basis = call(
            functools.partial(finish_kernel, hops),
            [grads.shape, flat, flat],
            [],
            0.1,
            full,
            "finish",
            copies=3 + len(hops),
            in_specs=anywhere(3 + len(hops)),
            out_specs=anywhere(3),
        )(keep, back, kept, *returned)
    else:
        update = exchange(after(own_rows, send) + after(got_rows, send))
        new_l_basis = jnp.where(parity == 0, keep, back)
        new_r_basis = jnp.where(parity == 0, back, keep)
    new_left, new_right = call(stats_kernel, [flat, flat], [(3, full, LANES)], 1, full, "stats")(
        after(grad, send), new_stat, other
    )
    halves = (new_one, new_two, new_left, new_right, new_l_basis, new_r_basis)
    return (update, *(x.reshape(1, flat_rows * LANES) for x in halves))


def solution(mesh):
    halves = P(("tensor", "shard"), None)
    rows = P("tensor", "shard", None)
    return jax.shard_map(
        local, mesh=mesh, in_specs=(rows,) + (halves,) * 6, out_specs=(rows,) + (halves,) * 6, check_vma=False
    )
```

```python
import functools

import jax
import jax.numpy as jnp
from jax import lax
from jax.experimental import pallas as pl
from jax.experimental.pallas import tpu as pltpu
from jax.sharding import PartitionSpec as P

NS_ITERS = 5
BETA_ONE = 0.9
BETA_TWO = 0.95
ADAM_EPS = 1e-08
NORM_EPS = 1e-06
LINEAR_COEFF = 3.4445
CUBIC_COEFF = -4.775
QUINTIC_COEFF = 2.0315
LANES = 128
F32 = jnp.float32


def split(x):
    high = x.astype(jnp.bfloat16)
    return high, (x - high.astype(F32)).astype(jnp.bfloat16)


def dot(a, b, dims=((1,), (0,))):
    return dot_parts(split(a), split(b), dims)


def dot_parts(a, b, dims=((1,), (0,))):
    (ka,), (kb,) = dims
    left = jnp.concatenate([a[0], a[0], a[1]], axis=ka)
    right = jnp.concatenate([b[0], b[1], b[0]], axis=kb)
    return lax.dot_general(left, right, (dims, ((), ())), preferred_element_type=F32)


def swap(x):
    return pltpu.roll(x, LANES // 2, 1)


def low_lanes(shape):
    return lax.broadcasted_iota(jnp.int32, shape, 1) < LANES // 2


def pick(flag, x, y):
    return [jnp.where(flag, u, v) for u, v in zip(x, y)]


def thirds(ref, start=0, rows=None):
    rows = ref.shape[0] if rows is None else rows
    return [ref[pl.ds(start + k, rows // 3, stride=3), :] for k in range(3)]


def put_thirds(ref, parts):
    for k in range(3):
        ref[pl.ds(k, parts[k].shape[0], stride=3), :] = parts[k]


def interleave(scratch, index, even, odd):
    scratch[index, pl.ds(0, even.shape[0], stride=2), :] = even
    scratch[index, pl.ds(1, odd.shape[0], stride=2), :] = odd


def whole_of(scratch, first, second):
    a, b, c = first
    d, e, f = second
    low = low_lanes(a.shape)
    sb, sc, sd, se = swap(b), swap(c), swap(d), swap(e)
    interleave(scratch, 0, a, jnp.where(low, sb, sc))
    interleave(scratch, 1, jnp.where(low, b, sd), jnp.where(low, sc, e))
    interleave(scratch, 2, jnp.where(low, sd, se), f)
    return jnp.concatenate([scratch[0], scratch[1], scratch[2]], axis=1)


def half_of(scratch, flat):
    a, b, c = flat
    low = low_lanes(a.shape)
    sb, sc = swap(b), swap(c)
    interleave(scratch, 0, a, jnp.where(low, sb, sc))
    interleave(scratch, 1, jnp.where(low, b, 0.0), jnp.where(low, sc, 0.0))
    return jnp.concatenate([scratch[0], scratch[1]], axis=1)


def flat_of(scratch, half):
    scratch[0] = half[:, :LANES]
    scratch[1] = half[:, LANES:]
    pairs = half.shape[0] // 2
    even0 = scratch[0, pl.ds(0, pairs, stride=2), :]
    odd0 = swap(scratch[0, pl.ds(1, pairs, stride=2), :])
    even1 = scratch[1, pl.ds(0, pairs, stride=2), :]
    odd1 = swap(scratch[1, pl.ds(1, pairs, stride=2), :])
    low = low_lanes(even0.shape)
    return [even0, jnp.where(low, even1, odd0), jnp.where(low, odd0, odd1)]


def take_half(whole, first):
    one, two, three = whole[:, :LANES], whole[:, LANES : 2 * LANES], whole[:, 2 * LANES :]
    low = low_lanes(one.shape)
    s2, s3 = swap(two), swap(three)
    head = jnp.where(first, one, jnp.where(low, s2, s3))
    tail = jnp.where(low, jnp.where(first, two, s3), 0.0)
    return jnp.concatenate([head, tail], axis=1)


def is_left():
    return lax.rem(lax.axis_index("shard"), 2) == 0


def pack_kernel(hops, l_stat_ref, r_stat_ref, l_basis_ref, r_basis_ref, grads_ref, *refs):
    out_ref, small_ref, *refs = refs
    piece_refs, (corner, sems) = refs[: len(hops)], refs[len(hops) :]
    left = is_left()
    flat_rows = l_basis_ref.shape[0]
    half_rows = flat_rows // 2
    rows = grads_ref.shape[1]
    here = lax.axis_index("shard") // 2

    def copies(basis_ref, stat_ref, start):
        return [
            pltpu.make_async_copy(stat_ref.at[pl.ds(start, half_rows)], corner, sems.at[0]),
            pltpu.make_async_copy(basis_ref, out_ref.at[pl.ds(0, flat_rows)], sems.at[1]),
        ]

    @pl.when(left)
    def _():
        for copy in copies(r_basis_ref, r_stat_ref, 0):
            copy.start()

    @pl.when(jnp.logical_not(left))
    def _():
        for copy in copies(l_basis_ref, l_stat_ref, half_rows):
            copy.start()

    more = []
    for number, (hop, piece_ref) in enumerate(zip(hops, piece_refs)):
        more.append(pltpu.make_async_copy(grads_ref.at[here ^ hop], piece_ref, sems.at[2 + number]))
    if hops:
        for k in range(grads_ref.shape[2] // LANES):
            source = grads_ref.at[here, :, pl.ds(k * LANES, LANES)]
            target = out_ref.at[pl.ds(flat_rows + k * rows, rows)]
            more.append(pltpu.make_async_copy(source, target, sems.at[2 + len(hops) + k]))
    for copy in more:
        copy.start()
    first, second = copies(l_basis_ref, l_stat_ref, half_rows)
    first.wait()
    third = half_rows // 9
    a, b, c = thirds(corner)
    low = low_lanes((third, LANES))
    middle = slice(third, 2 * third)
    small_ref[pl.ds(0, third)] = jnp.where(low, a[:third], b[:third])
    small_ref[pl.ds(third, third)] = a[middle]
    small_ref[pl.ds(2 * third, third)] = jnp.where(low, swap(b[middle]), swap(c[middle]))
    small_ref[pl.ds(3 * third, 3 * third)] = corner[pl.ds(6 * third, 3 * third)]
    for copy in [second, *more]:
        copy.wait()


def corner_rows(flat_rows):
    return flat_rows // 3


def unpack_corner(got_ref):
    third = got_ref.shape[0] // 6
    small = got_ref[pl.ds(0, third), :]
    even = got_ref[pl.ds(third, third), :]
    odd = swap(got_ref[pl.ds(2 * third, third), :])
    a, b, c = thirds(got_ref, 3 * third, 3 * third)
    low = low_lanes(small.shape)
    zero = jnp.zeros_like(small)
    return [
        jnp.concatenate([jnp.where(low, small, zero), even, a], axis=0),
        jnp.concatenate([jnp.where(low, zero, small), jnp.where(low, zero, odd), b], axis=0),
        jnp.concatenate([zero, jnp.where(low, odd, zero), c], axis=0),
    ]


def statistic(left, own, got_ref, scratch):
    corner = unpack_corner(got_ref)
    placed = [jnp.concatenate([jnp.where(left, 0.0, c), jnp.where(left, c, 0.0)], axis=0) for c in corner]
    known = whole_of(scratch, pick(left, own, placed), pick(left, placed, own))
    half = known.shape[0] // 2
    part = half // 3
    row = lax.broadcasted_iota(jnp.int32, known.shape, 0)
    column = lax.broadcasted_iota(jnp.int32, known.shape, 1)
    missing = (jnp.where(left, row, column) < half) & (jnp.where(left, column, row) >= half)
    offset = jnp.where(left, half, 0)
    row, column = row - offset, column - offset
    limit = jnp.where(row < part, part, 2 * part)
    missing |= (row >= 0) & (row < 2 * part) & (column < half) & (column >= limit)
    return jnp.where(missing, known.T, known)


def place_rows(grad_ref, block, rows, value):
    grad_ref[pl.ds(pl.multiple_of(block * rows, 8), rows), :] = value


def iterate(x_ref, steps):
    @pl.loop(0, steps)
    def _(step):
        x = x_ref[...]
        parts = split(x)
        gram = dot_parts(parts, parts, ((1,), (1,)))
        gram_parts = split(gram)
        poly = CUBIC_COEFF * gram + QUINTIC_COEFF * dot_parts(gram_parts, gram_parts)
        x_ref[...] = LINEAR_COEFF * x + dot_parts(split(poly), parts)


def products_kernel(hops, l_stat_ref, r_stat_ref, l_basis_ref, r_basis_ref, got_ref, *refs):
    left = is_left()
    outs = refs[-9:]
    grad_ref, product_ref, basis_ref, right_ref, inner_ref, own_ref, other_ref, copy_ref, scratch = outs
    if hops:
        grads_ref, mine_refs, theirs_refs = refs[0], refs[1 : 1 + len(hops)], refs[1 + len(hops) : 1 + 2 * len(hops)]
        rows = grads_ref.shape[1]
        here = lax.axis_index("shard") // 2
        parity = lax.axis_index("shard") % 2
        start = l_basis_ref.shape[0]
        received = [got_ref[pl.ds(start + k * rows, rows), :] for k in range(grad_ref.shape[1] // LANES)]
        place_rows(grad_ref, 2 * here + parity, rows, grads_ref[here])
        place_rows(grad_ref, 2 * here + 1 - parity, rows, jnp.concatenate(received, axis=1))
        for hop, mine, theirs in zip(hops, mine_refs, theirs_refs):
            place_rows(grad_ref, 2 * (here ^ hop) + parity, rows, mine[...])
            place_rows(grad_ref, 2 * (here ^ hop) + 1 - parity, rows, theirs[...])
    else:
        grad_ref[...] = refs[0][...]
    own = pick(left, thirds(l_basis_ref), thirds(r_basis_ref))
    got = thirds(got_ref, 0, l_basis_ref.shape[0])
    basis_ref[...] = whole_of(scratch, pick(left, own, got), pick(left, got, own))
    own_ref[...] = jnp.where(left, l_stat_ref[...], r_stat_ref[...])
    other_ref[...] = jnp.where(left, r_stat_ref[...], l_stat_ref[...])
    copy_ref[...] = l_basis_ref[...]
    right = half_of(scratch, thirds(r_basis_ref))
    right_ref[...] = right
    grad = grad_ref[...]
    turned = grad.T
    product_ref[...] = dot(jnp.where(left, grad, turned), jnp.where(left, turned, grad))
    inner_ref[...] = dot(grad, right)


def begin_kernel(steps, own_ref, corner_ref, product_ref, basis_ref, new_stat_ref, x_ref, scratch):
    new_stat = 0.5 * statistic(is_left(), thirds(own_ref), corner_ref, scratch) + 0.5 * product_ref[...]
    new_stat_ref[...] = new_stat
    power = dot(new_stat, basis_ref[...])
    x_ref[...] = power * (1.0 / jnp.sqrt(jnp.sum(power * power) + NORM_EPS))
    iterate(x_ref, steps)


def end_kernel(steps, start_ref, keep_ref, send_ref, scratch, x_ref):
    left = is_left()
    x_ref[...] = start_ref[...]
    iterate(x_ref, steps)
    x = x_ref[...]
    put_thirds(send_ref, flat_of(scratch, take_half(x, jnp.logical_not(left))))
    put_thirds(keep_ref, flat_of(scratch, take_half(x, left)))


def update_kernel(
    hops,
    inner_ref,
    basis_ref,
    left_ref,
    right_ref,
    first_left_ref,
    one_ref,
    two_ref,
    new_one_ref,
    new_two_ref,
    mine_ref,
    theirs_ref,
    scratch,
    partial_ref,
):
    left = is_left()
    basis_left = jnp.where(left, basis_ref[...], whole_of(scratch, thirds(first_left_ref), thirds(left_ref)))
    left_parts = split(basis_left)
    basis_right = split(right_ref[...])
    rotated = flat_of(scratch, dot(basis_left.T, inner_ref[...]))
    ones = thirds(one_ref)
    twos = thirds(two_ref)
    new_one = [BETA_ONE * m + (1.0 - BETA_ONE) * r for m, r in zip(ones, rotated)]
    new_two = [BETA_TWO * v + (1.0 - BETA_TWO) * r * r for v, r in zip(twos, rotated)]
    put_thirds(new_one_ref, new_one)
    put_thirds(new_two_ref, new_two)
    direction = [m / (jnp.sqrt(v) + ADAM_EPS) for m, v in zip(new_one, new_two)]
    outer = dot_parts(left_parts, split(half_of(scratch, direction)))
    partial_ref[...] = dot_parts(split(outer), basis_right, ((1,), (1,)))
    rows = mine_ref.shape[1]
    here = lax.axis_index("shard") // 2
    parity = lax.axis_index("shard") % 2
    for k, hop in enumerate((0, *hops)):
        block = 2 * (here ^ hop) if hops else 0
        mine_ref[k] = partial_ref[pl.ds(pl.multiple_of((block + parity) * rows, 8), rows), :]
        theirs_ref[k] = partial_ref[pl.ds(pl.multiple_of((block + 1 - parity) * rows, 8), rows), :]


def add_kernel(mine_ref, theirs_ref, *out_refs):
    for k, out_ref in enumerate(out_refs):
        out_ref[...] = mine_ref[k] + theirs_ref[k]


def finish_kernel(hops, keep_ref, back_ref, *refs):
    count = 1 + len(hops)
    rows_refs = refs[:count]
    update_ref, new_left_ref, new_right_ref, sems = refs[count:]
    left = is_left()
    here = lax.axis_index("shard") // 2

    def copies(own_ref, other_ref):
        return [
            pltpu.make_async_copy(keep_ref, own_ref, sems.at[0]),
            pltpu.make_async_copy(back_ref, other_ref, sems.at[1]),
        ]

    @pl.when(left)
    def _():
        for copy in copies(new_left_ref, new_right_ref):
            copy.start()

    @pl.when(jnp.logical_not(left))
    def _():
        for copy in copies(new_right_ref, new_left_ref):
            copy.start()

    rows = [
        pltpu.make_async_copy(rows_refs[k], update_ref.at[here ^ hop], sems.at[2 + k])
        for k, hop in enumerate((0, *hops))
    ]
    for copy in rows:
        copy.start()
    for copy in rows + copies(new_left_ref, new_right_ref):
        copy.wait()


def stats_kernel(grad_ref, new_stat_ref, other_ref, new_left_ref, new_right_ref, scratch):
    left = is_left()
    grad = grad_ref[...]
    turned = grad.T
    a = jnp.where(left, grad, turned)
    b = jnp.where(left, turned, grad)
    new_own = flat_of(scratch, take_half(new_stat_ref[...], left))
    product = flat_of(scratch, dot(b, take_half(a, left)))
    new_other = [0.5 * u + 0.5 * v for u, v in zip(thirds(other_ref), product)]
    put_thirds(new_left_ref, pick(left, new_own, new_other))
    put_thirds(new_right_ref, pick(left, new_other, new_own))


def call(kernel, outs, scratch, products, full, name, copies=0, kind=jax.ShapeDtypeStruct, **specs):
    size = full * full
    scratch = [pltpu.VMEM(s, F32) for s in scratch]
    if copies:
        scratch.append(pltpu.SemaphoreType.DMA((copies,)))
    return pl.pallas_call(
        kernel,
        out_shape=[kind(s, F32) for s in outs],
        scratch_shapes=scratch,
        compiler_params=pltpu.CompilerParams(vmem_limit_bytes=40 * 1024 * 1024),
        cost_estimate=pl.CostEstimate(flops=int(products * 6 * full * size), bytes_accessed=16 * size, transcendentals=0),
        name=name,
        **specs,
    )


def anywhere(count):
    return [pl.BlockSpec(memory_space=pl.ANY)] * count


def after(x, *others):
    return lax.optimization_barrier((x, *others))[0]


def local(grads, moment_one, moment_two, left_stat, right_stat, left_basis, right_basis):
    tiles_here, rows_here, full = grads.shape
    size = lax.axis_size("shard")
    flat_rows = full * (full // 2) // LANES
    flat = (flat_rows, LANES)
    square = (full, full)
    block = (rows_here, full)
    parity = lax.axis_index("shard") % 2
    pairs = [(i, i ^ 1) for i in range(size)]
    sides = [list(range(k, size, 2)) for k in range(2)]
    near = size in (4, 8) and rows_here % 8 == 0
    hops = {4: (1,), 8: (2, 3, 1)}[size] if near else ()
    strips = (tiles_here, *block) if near else (1, full // 2, full)

    def exchange(x):
        return lax.all_to_all(x, "shard", split_axis=0, concat_axis=0, axis_index_groups=sides, tiled=True)

    def hop_by(x, hop):
        return lax.ppermute(x, "shard", [(i, i ^ (2 * hop)) for i in range(size)])

    def partner(x):
        return lax.ppermute(x, "shard", pairs)

    one, two, l_stat, r_stat, l_basis, r_basis = (
        x.reshape(flat) for x in (moment_one, moment_two, left_stat, right_stat, left_basis, right_basis)
    )
    count = corner_rows(flat_rows)
    outgoing_rows = flat_rows + (rows_here * (full // LANES) if near else 0)
    outgoing, corner, *pieces = call(
        functools.partial(pack_kernel, hops),
        [(outgoing_rows, LANES), (count, LANES)] + [block] * len(hops),
        [(flat_rows // 2, LANES)],
        0.1,
        full,
        "pack",
        copies=2 + len(hops) + full // LANES,
        kind=pltpu.VMEM,
        in_specs=anywhere(5),
        out_specs=anywhere(1) + [pl.BlockSpec(memory_space=pltpu.VMEM)] + anywhere(len(hops)),
    )(*(pltpu.with_memory_space_constraint(x, pltpu.HBM) for x in (l_stat, r_stat, l_basis, r_basis, grads)))
    got = partner(outgoing)
    if near:
        mine = [hop_by(piece, hop) for hop, piece in zip(hops, pieces)]
        theirs = [partner(x) for x in mine]
        rows = (grads, *mine, *theirs)
    else:
        mine = exchange(grads)
        theirs = partner(mine)
        even, odd = jnp.where(parity == 0, mine, theirs), jnp.where(parity == 0, theirs, mine)
        rows = (jnp.stack([even, odd], axis=1).reshape(square),)
        mine = [mine]
    got_corner = partner(after(corner, *mine))
    grad, product, basis, right, inner, own, other, left = call(
        functools.partial(products_kernel, hops),
        [square, square, square, (full, 2 * LANES), (full, 2 * LANES), flat, flat, flat],
        [(3, full, LANES)],
        2,
        full,
        "products",
    )(l_stat, r_stat, l_basis, r_basis, got, *rows)
    first_left = partner(after(l_basis, product))
    new_stat, x = call(functools.partial(begin_kernel, 2), [square] * 2, [(3, full, LANES)], 7, full, "begin")(
        own, got_corner, product, basis
    )
    new_one, new_two, own_rows, other_rows = call(
        functools.partial(update_kernel, hops), [flat, flat, strips, strips], [(3, full, LANES), square], 2, full, "update"
    )(after(inner, x), basis, left, right, first_left, one, two)
    if not near:
        top = jnp.where(parity == 0, own_rows, other_rows)
        bottom = jnp.where(parity == 0, other_rows, own_rows)
        merged = jnp.concatenate([top, bottom], axis=1).reshape(tiles_here, 2, rows_here, full)
        own_rows = lax.dynamic_index_in_dim(merged, parity, 1, keepdims=False)
        other_rows = lax.dynamic_index_in_dim(merged, 1 - parity, 1, keepdims=False)
    got_rows = partner(other_rows)
    keep, send = call(
        functools.partial(end_kernel, NS_ITERS - 2), [flat, flat], [(3, full, LANES), square], 9, full, "end"
    )(after(x, other_rows))
    back = partner(send)
    if near:
        kept, *sums = call(add_kernel, [block] * (1 + len(hops)), [], 0.1, full, "add")(
            after(own_rows, send), after(got_rows, send)
        )
        returned = [hop_by(x, hop) for hop, x in zip(hops, sums)]
        update, new_l_basis, new_r_basis = call(
            functools.partial(finish_kernel, hops),
            [grads.shape, flat, flat],
            [],
            0.1,
            full,
            "finish",
            copies=3 + len(hops),
            in_specs=anywhere(3 + len(hops)),
            out_specs=anywhere(3),
        )(keep, back, kept, *returned)
    else:
        update = exchange(after(own_rows, send) + after(got_rows, send))
        new_l_basis = jnp.where(parity == 0, keep, back)
        new_r_basis = jnp.where(parity == 0, back, keep)
    new_left, new_right = call(stats_kernel, [flat, flat], [(3, full, LANES)], 1, full, "stats")(
        after(grad, send), new_stat, other
    )
    halves = (new_one, new_two, new_left, new_right, new_l_basis, new_r_basis)
    return (update, *(x.reshape(1, flat_rows * LANES) for x in halves))


def solution(mesh):
    halves = P(("tensor", "shard"), None)
    rows = P("tensor", "shard", None)
    return jax.shard_map(
        local, mesh=mesh, in_specs=(rows,) + (halves,) * 6, out_specs=(rows,) + (halves,) * 6, check_vma=False
    )
```

```python
import functools

import jax
import jax.numpy as jnp
from jax import lax
from jax.experimental import pallas as pl
from jax.experimental.pallas import tpu as pltpu
from jax.sharding import PartitionSpec as P

NS_ITERS = 5
BETA_ONE = 0.9
BETA_TWO = 0.95
ADAM_EPS = 1e-08
NORM_EPS = 1e-06
LINEAR_COEFF = 3.4445
CUBIC_COEFF = -4.775
QUINTIC_COEFF = 2.0315
LANES = 128
F32 = jnp.float32


def split(x):
    high = x.astype(jnp.bfloat16)
    return high, (x - high.astype(F32)).astype(jnp.bfloat16)


def dot(a, b, dims=((1,), (0,))):
    return dot_parts(split(a), split(b), dims)


def dot_parts(a, b, dims=((1,), (0,))):
    (ka,), (kb,) = dims
    left = jnp.concatenate([a[0], a[0], a[1]], axis=ka)
    right = jnp.concatenate([b[0], b[1], b[0]], axis=kb)
    return lax.dot_general(left, right, (dims, ((), ())), preferred_element_type=F32)


def symmetric_dot(a, b, dims=((1,), (0,))):
    (ka,), (kb,) = dims
    cut = a[0].shape[0] - LANES
    head = lambda x, axis: lax.slice_in_dim(x, 0, cut, axis=axis)
    tail = lambda x, axis: lax.slice_in_dim(x, cut, cut + LANES, axis=axis)
    left = dot_parts(a, [head(x, 1 - kb) for x in b], dims)
    corner = dot_parts([tail(x, 1 - ka) for x in a], [tail(x, 1 - kb) for x in b], dims)
    right = jnp.concatenate([left[cut:].T, corner], axis=0)
    return jnp.concatenate([left, right], axis=1)


def swap(x):
    return pltpu.roll(x, LANES // 2, 1)


def low_lanes(shape):
    return lax.broadcasted_iota(jnp.int32, shape, 1) < LANES // 2


def pick(flag, x, y):
    return [jnp.where(flag, u, v) for u, v in zip(x, y)]


def thirds(ref, start=0, rows=None):
    rows = ref.shape[0] if rows is None else rows
    return [ref[pl.ds(start + k, rows // 3, stride=3), :] for k in range(3)]


def put_thirds(ref, parts):
    for k in range(3):
        ref[pl.ds(k, parts[k].shape[0], stride=3), :] = parts[k]


def interleave(scratch, index, even, odd):
    scratch[index, pl.ds(0, even.shape[0], stride=2), :] = even
    scratch[index, pl.ds(1, odd.shape[0], stride=2), :] = odd


def whole_of(scratch, first, second):
    a, b, c = first
    d, e, f = second
    low = low_lanes(a.shape)
    sb, sc, sd, se = swap(b), swap(c), swap(d), swap(e)
    interleave(scratch, 0, a, jnp.where(low, sb, sc))
    interleave(scratch, 1, jnp.where(low, b, sd), jnp.where(low, sc, e))
    interleave(scratch, 2, jnp.where(low, sd, se), f)
    return jnp.concatenate([scratch[0], scratch[1], scratch[2]], axis=1)


def half_of(scratch, flat):
    a, b, c = flat
    low = low_lanes(a.shape)
    sb, sc = swap(b), swap(c)
    interleave(scratch, 0, a, jnp.where(low, sb, sc))
    interleave(scratch, 1, jnp.where(low, b, 0.0), jnp.where(low, sc, 0.0))
    return jnp.concatenate([scratch[0], scratch[1]], axis=1)


def flat_of(scratch, half):
    scratch[0] = half[:, :LANES]
    scratch[1] = half[:, LANES:]
    pairs = half.shape[0] // 2
    even0 = scratch[0, pl.ds(0, pairs, stride=2), :]
    odd0 = swap(scratch[0, pl.ds(1, pairs, stride=2), :])
    even1 = scratch[1, pl.ds(0, pairs, stride=2), :]
    odd1 = swap(scratch[1, pl.ds(1, pairs, stride=2), :])
    low = low_lanes(even0.shape)
    return [even0, jnp.where(low, even1, odd0), jnp.where(low, odd0, odd1)]


def take_half(whole, first):
    one, two, three = whole[:, :LANES], whole[:, LANES : 2 * LANES], whole[:, 2 * LANES :]
    low = low_lanes(one.shape)
    s2, s3 = swap(two), swap(three)
    head = jnp.where(first, one, jnp.where(low, s2, s3))
    tail = jnp.where(low, jnp.where(first, two, s3), 0.0)
    return jnp.concatenate([head, tail], axis=1)


def is_left():
    return lax.rem(lax.axis_index("shard"), 2) == 0


def pack_kernel(hops, l_stat_ref, r_stat_ref, l_basis_ref, r_basis_ref, grads_ref, *refs):
    out_ref, small_ref, *refs = refs
    piece_refs, (corner, sems) = refs[: len(hops)], refs[len(hops) :]
    left = is_left()
    flat_rows = l_basis_ref.shape[0]
    half_rows = flat_rows // 2
    rows = grads_ref.shape[1]
    here = lax.axis_index("shard") // 2

    def copies(basis_ref, stat_ref, start):
        return [
            pltpu.make_async_copy(stat_ref.at[pl.ds(start, half_rows)], corner, sems.at[0]),
            pltpu.make_async_copy(basis_ref, out_ref.at[pl.ds(0, flat_rows)], sems.at[1]),
        ]

    @pl.when(left)
    def _():
        for copy in copies(r_basis_ref, r_stat_ref, 0):
            copy.start()

    @pl.when(jnp.logical_not(left))
    def _():
        for copy in copies(l_basis_ref, l_stat_ref, half_rows):
            copy.start()

    more = []
    for number, (hop, piece_ref) in enumerate(zip(hops, piece_refs)):
        more.append(pltpu.make_async_copy(grads_ref.at[here ^ hop], piece_ref, sems.at[2 + number]))
    if hops:
        for k in range(grads_ref.shape[2] // LANES):
            source = grads_ref.at[here, :, pl.ds(k * LANES, LANES)]
            target = out_ref.at[pl.ds(flat_rows + k * rows, rows)]
            more.append(pltpu.make_async_copy(source, target, sems.at[2 + len(hops) + k]))
    for copy in more:
        copy.start()
    first, second = copies(l_basis_ref, l_stat_ref, half_rows)
    first.wait()
    third = half_rows // 9
    a, b, c = thirds(corner)
    low = low_lanes((third, LANES))
    middle = slice(third, 2 * third)
    small_ref[pl.ds(0, third)] = jnp.where(low, a[:third], b[:third])
    small_ref[pl.ds(third, third)] = a[middle]
    small_ref[pl.ds(2 * third, third)] = jnp.where(low, swap(b[middle]), swap(c[middle]))
    small_ref[pl.ds(3 * third, 3 * third)] = corner[pl.ds(6 * third, 3 * third)]
    for copy in [second, *more]:
        copy.wait()


def corner_rows(flat_rows):
    return flat_rows // 3


def unpack_corner(got_ref):
    third = got_ref.shape[0] // 6
    small = got_ref[pl.ds(0, third), :]
    even = got_ref[pl.ds(third, third), :]
    odd = swap(got_ref[pl.ds(2 * third, third), :])
    a, b, c = thirds(got_ref, 3 * third, 3 * third)
    low = low_lanes(small.shape)
    zero = jnp.zeros_like(small)
    return [
        jnp.concatenate([jnp.where(low, small, zero), even, a], axis=0),
        jnp.concatenate([jnp.where(low, zero, small), jnp.where(low, zero, odd), b], axis=0),
        jnp.concatenate([zero, jnp.where(low, odd, zero), c], axis=0),
    ]


def statistic(left, own, got_ref, scratch):
    corner = unpack_corner(got_ref)
    placed = [jnp.concatenate([jnp.where(left, 0.0, c), jnp.where(left, c, 0.0)], axis=0) for c in corner]
    known = whole_of(scratch, pick(left, own, placed), pick(left, placed, own))
    half = known.shape[0] // 2
    part = half // 3
    row = lax.broadcasted_iota(jnp.int32, known.shape, 0)
    column = lax.broadcasted_iota(jnp.int32, known.shape, 1)
    missing = (jnp.where(left, row, column) < half) & (jnp.where(left, column, row) >= half)
    offset = jnp.where(left, half, 0)
    row, column = row - offset, column - offset
    limit = jnp.where(row < part, part, 2 * part)
    missing |= (row >= 0) & (row < 2 * part) & (column < half) & (column >= limit)
    return jnp.where(missing, known.T, known)


def place_rows(grad_ref, block, rows, value):
    grad_ref[pl.ds(pl.multiple_of(block * rows, 8), rows), :] = value


def polynomial(parts):
    gram = symmetric_dot(parts, parts, ((1,), (1,)))
    gram_parts = split(gram)
    return CUBIC_COEFF * gram + QUINTIC_COEFF * symmetric_dot(gram_parts, gram_parts)


def iterate(x_ref, steps):
    @pl.loop(0, steps)
    def _(step):
        x = x_ref[...]
        parts = split(x)
        x_ref[...] = LINEAR_COEFF * x + dot_parts(split(polynomial(parts)), parts)


def products_kernel(hops, l_stat_ref, r_stat_ref, l_basis_ref, r_basis_ref, got_ref, *refs):
    left = is_left()
    outs = refs[-9:]
    grad_ref, product_ref, basis_ref, right_ref, inner_ref, own_ref, other_ref, copy_ref, scratch = outs
    if hops:
        grads_ref, mine_refs, theirs_refs = refs[0], refs[1 : 1 + len(hops)], refs[1 + len(hops) : 1 + 2 * len(hops)]
        rows = grads_ref.shape[1]
        here = lax.axis_index("shard") // 2
        parity = lax.axis_index("shard") % 2
        start = l_basis_ref.shape[0]
        received = [got_ref[pl.ds(start + k * rows, rows), :] for k in range(grad_ref.shape[1] // LANES)]
        place_rows(grad_ref, 2 * here + parity, rows, grads_ref[here])
        place_rows(grad_ref, 2 * here + 1 - parity, rows, jnp.concatenate(received, axis=1))
        for hop, mine, theirs in zip(hops, mine_refs, theirs_refs):
            place_rows(grad_ref, 2 * (here ^ hop) + parity, rows, mine[...])
            place_rows(grad_ref, 2 * (here ^ hop) + 1 - parity, rows, theirs[...])
    else:
        grad_ref[...] = refs[0][...]
    own = pick(left, thirds(l_basis_ref), thirds(r_basis_ref))
    got = thirds(got_ref, 0, l_basis_ref.shape[0])
    basis_ref[...] = whole_of(scratch, pick(left, own, got), pick(left, got, own))
    own_ref[...] = jnp.where(left, l_stat_ref[...], r_stat_ref[...])
    other_ref[...] = jnp.where(left, r_stat_ref[...], l_stat_ref[...])
    copy_ref[...] = l_basis_ref[...]
    right = half_of(scratch, thirds(r_basis_ref))
    right_ref[...] = right
    grad = grad_ref[...]
    parts = split(jnp.where(left, grad, grad.T))
    product_ref[...] = symmetric_dot(parts, parts, ((1,), (1,)))
    inner_ref[...] = dot(grad, right)


def begin_kernel(steps, own_ref, corner_ref, product_ref, basis_ref, new_stat_ref, x_ref, scratch):
    new_stat = 0.5 * statistic(is_left(), thirds(own_ref), corner_ref, scratch) + 0.5 * product_ref[...]
    new_stat_ref[...] = new_stat
    power = dot(new_stat, basis_ref[...])
    x_ref[...] = power * (1.0 / jnp.sqrt(jnp.sum(power * power) + NORM_EPS))
    iterate(x_ref, steps)


def end_kernel(steps, start_ref, x_ref, poly_ref, send_ref, scratch):
    x_ref[...] = start_ref[...]
    iterate(x_ref, steps - 1)
    x = x_ref[...]
    poly = polynomial(split(x))
    poly_ref[...] = poly
    half = take_half(x, jnp.logical_not(is_left()))
    put_thirds(send_ref, flat_of(scratch, LINEAR_COEFF * half + dot(poly, half)))


def update_kernel(
    hops,
    inner_ref,
    basis_ref,
    left_ref,
    right_ref,
    first_left_ref,
    one_ref,
    two_ref,
    new_one_ref,
    new_two_ref,
    mine_ref,
    theirs_ref,
    scratch,
    partial_ref,
):
    left = is_left()
    basis_left = jnp.where(left, basis_ref[...], whole_of(scratch, thirds(first_left_ref), thirds(left_ref)))
    left_parts = split(basis_left)
    basis_right = split(right_ref[...])
    rotated = flat_of(scratch, dot(basis_left.T, inner_ref[...]))
    ones = thirds(one_ref)
    twos = thirds(two_ref)
    new_one = [BETA_ONE * m + (1.0 - BETA_ONE) * r for m, r in zip(ones, rotated)]
    new_two = [BETA_TWO * v + (1.0 - BETA_TWO) * r * r for v, r in zip(twos, rotated)]
    put_thirds(new_one_ref, new_one)
    put_thirds(new_two_ref, new_two)
    direction = [m / (jnp.sqrt(v) + ADAM_EPS) for m, v in zip(new_one, new_two)]
    outer = dot_parts(left_parts, split(half_of(scratch, direction)))
    partial_ref[...] = dot_parts(split(outer), basis_right, ((1,), (1,)))
    rows = mine_ref.shape[1]
    here = lax.axis_index("shard") // 2
    parity = lax.axis_index("shard") % 2
    for k, hop in enumerate((0, *hops)):
        block = 2 * (here ^ hop) if hops else 0
        mine_ref[k] = partial_ref[pl.ds(pl.multiple_of((block + parity) * rows, 8), rows), :]
        theirs_ref[k] = partial_ref[pl.ds(pl.multiple_of((block + 1 - parity) * rows, 8), rows), :]


def add_kernel(mine_ref, theirs_ref, *out_refs):
    for k, out_ref in enumerate(out_refs):
        out_ref[...] = mine_ref[k] + theirs_ref[k]


def finish_kernel(hops, keep_ref, back_ref, *refs):
    count = 1 + len(hops)
    rows_refs = refs[:count]
    update_ref, new_left_ref, new_right_ref, sems = refs[count:]
    left = is_left()
    here = lax.axis_index("shard") // 2

    def copies(own_ref, other_ref):
        return [
            pltpu.make_async_copy(keep_ref, own_ref, sems.at[0]),
            pltpu.make_async_copy(back_ref, other_ref, sems.at[1]),
        ]

    @pl.when(left)
    def _():
        for copy in copies(new_left_ref, new_right_ref):
            copy.start()

    @pl.when(jnp.logical_not(left))
    def _():
        for copy in copies(new_right_ref, new_left_ref):
            copy.start()

    rows = [
        pltpu.make_async_copy(rows_refs[k], update_ref.at[here ^ hop], sems.at[2 + k])
        for k, hop in enumerate((0, *hops))
    ]
    for copy in rows:
        copy.start()
    for copy in rows + copies(new_left_ref, new_right_ref):
        copy.wait()


def rest_kernel(x_ref, poly_ref, grad_ref, new_stat_ref, other_ref, keep_ref, new_left_ref, new_right_ref, scratch):
    left = is_left()
    half = take_half(x_ref[...], left)
    put_thirds(keep_ref, flat_of(scratch, LINEAR_COEFF * half + dot(poly_ref[...], half)))
    grad = grad_ref[...]
    turned = grad.T
    a = jnp.where(left, grad, turned)
    b = jnp.where(left, turned, grad)
    new_own = flat_of(scratch, take_half(new_stat_ref[...], left))
    product = flat_of(scratch, dot(b, take_half(a, left)))
    new_other = [0.5 * u + 0.5 * v for u, v in zip(thirds(other_ref), product)]
    put_thirds(new_left_ref, pick(left, new_own, new_other))
    put_thirds(new_right_ref, pick(left, new_other, new_own))


def call(kernel, outs, scratch, products, full, name, copies=0, kind=jax.ShapeDtypeStruct, **specs):
    size = full * full
    scratch = [pltpu.VMEM(s, F32) for s in scratch]
    if copies:
        scratch.append(pltpu.SemaphoreType.DMA((copies,)))
    return pl.pallas_call(
        kernel,
        out_shape=[kind(s, F32) for s in outs],
        scratch_shapes=scratch,
        compiler_params=pltpu.CompilerParams(vmem_limit_bytes=40 * 1024 * 1024),
        cost_estimate=pl.CostEstimate(flops=int(products * 6 * full * size), bytes_accessed=16 * size, transcendentals=0),
        name=name,
        **specs,
    )


def anywhere(count):
    return [pl.BlockSpec(memory_space=pl.ANY)] * count


def after(x, *others):
    return lax.optimization_barrier((x, *others))[0]


def local(grads, moment_one, moment_two, left_stat, right_stat, left_basis, right_basis):
    tiles_here, rows_here, full = grads.shape
    size = lax.axis_size("shard")
    flat_rows = full * (full // 2) // LANES
    flat = (flat_rows, LANES)
    square = (full, full)
    block = (rows_here, full)
    parity = lax.axis_index("shard") % 2
    pairs = [(i, i ^ 1) for i in range(size)]
    sides = [list(range(k, size, 2)) for k in range(2)]
    near = size in (4, 8) and rows_here % 8 == 0
    hops = {4: (1,), 8: (2, 3, 1)}[size] if near else ()
    strips = (tiles_here, *block) if near else (1, full // 2, full)

    def exchange(x):
        return lax.all_to_all(x, "shard", split_axis=0, concat_axis=0, axis_index_groups=sides, tiled=True)

    def hop_by(x, hop):
        return lax.ppermute(x, "shard", [(i, i ^ (2 * hop)) for i in range(size)])

    def partner(x):
        return lax.ppermute(x, "shard", pairs)

    one, two, l_stat, r_stat, l_basis, r_basis = (
        x.reshape(flat) for x in (moment_one, moment_two, left_stat, right_stat, left_basis, right_basis)
    )
    count = corner_rows(flat_rows)
    outgoing_rows = flat_rows + (rows_here * (full // LANES) if near else 0)
    outgoing, corner, *pieces = call(
        functools.partial(pack_kernel, hops),
        [(outgoing_rows, LANES), (count, LANES)] + [block] * len(hops),
        [(flat_rows // 2, LANES)],
        0.1,
        full,
        "pack",
        copies=2 + len(hops) + full // LANES,
        kind=pltpu.VMEM,
        in_specs=anywhere(5),
        out_specs=anywhere(1) + [pl.BlockSpec(memory_space=pltpu.VMEM)] + anywhere(len(hops)),
    )(*(pltpu.with_memory_space_constraint(x, pltpu.HBM) for x in (l_stat, r_stat, l_basis, r_basis, grads)))
    got = partner(outgoing)
    if near:
        mine = [hop_by(piece, hop) for hop, piece in zip(hops, pieces)]
        theirs = [partner(x) for x in mine]
        rows = (grads, *mine, *theirs)
    else:
        mine = exchange(grads)
        theirs = partner(mine)
        even, odd = jnp.where(parity == 0, mine, theirs), jnp.where(parity == 0, theirs, mine)
        rows = (jnp.stack([even, odd], axis=1).reshape(square),)
        mine = [mine]
    got_corner = partner(after(corner, *mine))
    grad, product, basis, right, inner, own, other, left = call(
        functools.partial(products_kernel, hops),
        [square, square, square, (full, 2 * LANES), (full, 2 * LANES), flat, flat, flat],
        [(3, full, LANES)],
        2,
        full,
        "products",
    )(l_stat, r_stat, l_basis, r_basis, got, *rows)
    first_left = partner(after(l_basis, product))
    new_stat, x = call(functools.partial(begin_kernel, 2), [square] * 2, [(3, full, LANES)], 7, full, "begin")(
        own, got_corner, product, basis
    )
    new_one, new_two, own_rows, other_rows = call(
        functools.partial(update_kernel, hops), [flat, flat, strips, strips], [(3, full, LANES), square], 2, full, "update"
    )(after(inner, x), basis, left, right, first_left, one, two)
    if not near:
        top = jnp.where(parity == 0, own_rows, other_rows)
        bottom = jnp.where(parity == 0, other_rows, own_rows)
        merged = jnp.concatenate([top, bottom], axis=1).reshape(tiles_here, 2, rows_here, full)
        own_rows = lax.dynamic_index_in_dim(merged, parity, 1, keepdims=False)
        other_rows = lax.dynamic_index_in_dim(merged, 1 - parity, 1, keepdims=False)
    got_rows = partner(other_rows)
    x, poly, send = call(
        functools.partial(end_kernel, NS_ITERS - 2), [square, square, flat], [(3, full, LANES)], 9, full, "end"
    )(after(x, other_rows))
    back = partner(send)
    keep, new_left, new_right = call(rest_kernel, [flat, flat, flat], [(3, full, LANES)], 1.5, full, "rest")(
        x, poly, grad, new_stat, other
    )
    if near:
        kept, *sums = call(add_kernel, [block] * (1 + len(hops)), [], 0.1, full, "add")(
            after(own_rows, send), after(got_rows, send)
        )
        returned = [hop_by(x, hop) for hop, x in zip(hops, sums)]
        update, new_l_basis, new_r_basis = call(
            functools.partial(finish_kernel, hops),
            [grads.shape, flat, flat],
            [],
            0.1,
            full,
            "finish",
            copies=3 + len(hops),
            in_specs=anywhere(3 + len(hops)),
            out_specs=anywhere(3),
        )(keep, back, kept, *returned)
    else:
        update = exchange(after(own_rows, send) + after(got_rows, send))
        new_l_basis = jnp.where(parity == 0, keep, back)
        new_r_basis = jnp.where(parity == 0, back, keep)
    halves = (new_one, new_two, new_left, new_right, new_l_basis, new_r_basis)
    return (update, *(x.reshape(1, flat_rows * LANES) for x in halves))


def solution(mesh):
    halves = P(("tensor", "shard"), None)
    rows = P("tensor", "shard", None)
    return jax.shard_map(
        local, mesh=mesh, in_specs=(rows,) + (halves,) * 6, out_specs=(rows,) + (halves,) * 6, check_vma=False
    )
```

```python
import functools

import jax
import jax.numpy as jnp
from jax import lax
from jax.experimental import pallas as pl
from jax.experimental.pallas import tpu as pltpu
from jax.sharding import PartitionSpec as P

NS_ITERS = 5
BETA_ONE = 0.9
BETA_TWO = 0.95
ADAM_EPS = 1e-08
NORM_EPS = 1e-06
LINEAR_COEFF = 3.4445
CUBIC_COEFF = -4.775
QUINTIC_COEFF = 2.0315
LANES = 128
F32 = jnp.float32


def split(x):
    high = x.astype(jnp.bfloat16)
    return high, (x - high.astype(F32)).astype(jnp.bfloat16)


def dot(a, b, dims=((1,), (0,))):
    return dot_parts(split(a), split(b), dims)


def dot_parts(a, b, dims=((1,), (0,))):
    (ka,), (kb,) = dims
    left = jnp.concatenate([a[0], a[0], a[1]], axis=ka)
    right = jnp.concatenate([b[0], b[1], b[0]], axis=kb)
    return lax.dot_general(left, right, (dims, ((), ())), preferred_element_type=F32)


def symmetric_dot(a, b, dims=((1,), (0,))):
    (ka,), (kb,) = dims
    cut = a[0].shape[0] - LANES
    head = lambda x, axis: lax.slice_in_dim(x, 0, cut, axis=axis)
    tail = lambda x, axis: lax.slice_in_dim(x, cut, cut + LANES, axis=axis)
    left = dot_parts(a, [head(x, 1 - kb) for x in b], dims)
    corner = dot_parts([tail(x, 1 - ka) for x in a], [tail(x, 1 - kb) for x in b], dims)
    right = jnp.concatenate([left[cut:].T, corner], axis=0)
    return jnp.concatenate([left, right], axis=1)


def swap(x):
    return pltpu.roll(x, LANES // 2, 1)


def low_lanes(shape):
    return lax.broadcasted_iota(jnp.int32, shape, 1) < LANES // 2


def pick(flag, x, y):
    return [jnp.where(flag, u, v) for u, v in zip(x, y)]


def thirds(ref, start=0, rows=None):
    rows = ref.shape[0] if rows is None else rows
    return [ref[pl.ds(start + k, rows // 3, stride=3), :] for k in range(3)]


def put_thirds(ref, parts):
    for k in range(3):
        ref[pl.ds(k, parts[k].shape[0], stride=3), :] = parts[k]


def interleave(scratch, index, even, odd):
    scratch[index, pl.ds(0, even.shape[0], stride=2), :] = even
    scratch[index, pl.ds(1, odd.shape[0], stride=2), :] = odd


def whole_of(scratch, first, second):
    a, b, c = first
    d, e, f = second
    low = low_lanes(a.shape)
    sb, sc, sd, se = swap(b), swap(c), swap(d), swap(e)
    interleave(scratch, 0, a, jnp.where(low, sb, sc))
    interleave(scratch, 1, jnp.where(low, b, sd), jnp.where(low, sc, e))
    interleave(scratch, 2, jnp.where(low, sd, se), f)
    return jnp.concatenate([scratch[0], scratch[1], scratch[2]], axis=1)


def half_of(scratch, flat):
    a, b, c = flat
    low = low_lanes(a.shape)
    sb, sc = swap(b), swap(c)
    interleave(scratch, 0, a, jnp.where(low, sb, sc))
    interleave(scratch, 1, jnp.where(low, b, 0.0), jnp.where(low, sc, 0.0))
    return jnp.concatenate([scratch[0], scratch[1]], axis=1)


def flat_of(scratch, half):
    scratch[0] = half[:, :LANES]
    scratch[1] = half[:, LANES:]
    pairs = half.shape[0] // 2
    even0 = scratch[0, pl.ds(0, pairs, stride=2), :]
    odd0 = swap(scratch[0, pl.ds(1, pairs, stride=2), :])
    even1 = scratch[1, pl.ds(0, pairs, stride=2), :]
    odd1 = swap(scratch[1, pl.ds(1, pairs, stride=2), :])
    low = low_lanes(even0.shape)
    return [even0, jnp.where(low, even1, odd0), jnp.where(low, odd0, odd1)]


def take_half(whole, first):
    one, two, three = whole[:, :LANES], whole[:, LANES : 2 * LANES], whole[:, 2 * LANES :]
    low = low_lanes(one.shape)
    s2, s3 = swap(two), swap(three)
    head = jnp.where(first, one, jnp.where(low, s2, s3))
    tail = jnp.where(low, jnp.where(first, two, s3), 0.0)
    return jnp.concatenate([head, tail], axis=1)


def is_left():
    return lax.rem(lax.axis_index("shard"), 2) == 0


def pack_kernel(hops, l_stat_ref, r_stat_ref, l_basis_ref, r_basis_ref, grads_ref, *refs):
    out_ref, small_ref, *refs = refs
    piece_refs, (corner, sems) = refs[: len(hops)], refs[len(hops) :]
    left = is_left()
    flat_rows = l_basis_ref.shape[0]
    half_rows = flat_rows // 2
    rows = grads_ref.shape[1]
    here = lax.axis_index("shard") // 2

    def copies(basis_ref, stat_ref, start):
        return [
            pltpu.make_async_copy(stat_ref.at[pl.ds(start, half_rows)], corner, sems.at[0]),
            pltpu.make_async_copy(basis_ref, out_ref.at[pl.ds(0, flat_rows)], sems.at[1]),
        ]

    @pl.when(left)
    def _():
        for copy in copies(r_basis_ref, r_stat_ref, 0):
            copy.start()

    @pl.when(jnp.logical_not(left))
    def _():
        for copy in copies(l_basis_ref, l_stat_ref, half_rows):
            copy.start()

    more = []
    for number, (hop, piece_ref) in enumerate(zip(hops, piece_refs)):
        more.append(pltpu.make_async_copy(grads_ref.at[here ^ hop], piece_ref, sems.at[2 + number]))
    if hops:
        for k in range(grads_ref.shape[2] // LANES):
            source = grads_ref.at[here, :, pl.ds(k * LANES, LANES)]
            target = out_ref.at[pl.ds(flat_rows + k * rows, rows)]
            more.append(pltpu.make_async_copy(source, target, sems.at[2 + len(hops) + k]))
    for copy in more:
        copy.start()
    first, second = copies(l_basis_ref, l_stat_ref, half_rows)
    first.wait()
    third = half_rows // 9
    a, b, c = thirds(corner)
    low = low_lanes((third, LANES))
    middle = slice(third, 2 * third)
    small_ref[pl.ds(0, third)] = jnp.where(low, a[:third], b[:third])
    small_ref[pl.ds(third, third)] = a[middle]
    small_ref[pl.ds(2 * third, third)] = jnp.where(low, swap(b[middle]), swap(c[middle]))
    small_ref[pl.ds(3 * third, 3 * third)] = corner[pl.ds(6 * third, 3 * third)]
    for copy in [second, *more]:
        copy.wait()


def corner_rows(flat_rows):
    return flat_rows // 3


def unpack_corner(got_ref):
    third = got_ref.shape[0] // 6
    small = got_ref[pl.ds(0, third), :]
    even = got_ref[pl.ds(third, third), :]
    odd = swap(got_ref[pl.ds(2 * third, third), :])
    a, b, c = thirds(got_ref, 3 * third, 3 * third)
    low = low_lanes(small.shape)
    zero = jnp.zeros_like(small)
    return [
        jnp.concatenate([jnp.where(low, small, zero), even, a], axis=0),
        jnp.concatenate([jnp.where(low, zero, small), jnp.where(low, zero, odd), b], axis=0),
        jnp.concatenate([zero, jnp.where(low, odd, zero), c], axis=0),
    ]


def statistic(left, own, got_ref, scratch):
    corner = unpack_corner(got_ref)
    placed = [jnp.concatenate([jnp.where(left, 0.0, c), jnp.where(left, c, 0.0)], axis=0) for c in corner]
    known = whole_of(scratch, pick(left, own, placed), pick(left, placed, own))
    half = known.shape[0] // 2
    part = half // 3
    row = lax.broadcasted_iota(jnp.int32, known.shape, 0)
    column = lax.broadcasted_iota(jnp.int32, known.shape, 1)
    missing = (jnp.where(left, row, column) < half) & (jnp.where(left, column, row) >= half)
    offset = jnp.where(left, half, 0)
    row, column = row - offset, column - offset
    limit = jnp.where(row < part, part, 2 * part)
    missing |= (row >= 0) & (row < 2 * part) & (column < half) & (column >= limit)
    return jnp.where(missing, known.T, known)


def place_rows(grad_ref, block, rows, value):
    grad_ref[pl.ds(pl.multiple_of(block * rows, 8), rows), :] = value


def polynomial(parts):
    gram = dot_parts(parts, parts, ((1,), (1,)))
    gram_parts = split(gram)
    return CUBIC_COEFF * gram + QUINTIC_COEFF * dot_parts(gram_parts, gram_parts)


def iterate(x, steps):
    for _ in range(steps):
        parts = split(x)
        x = LINEAR_COEFF * x + dot_parts(split(polynomial(parts)), parts)
    return x


def products_kernel(hops, l_stat_ref, r_stat_ref, l_basis_ref, r_basis_ref, got_ref, *refs):
    left = is_left()
    outs = refs[-9:]
    grad_ref, product_ref, basis_ref, right_ref, inner_ref, own_ref, other_ref, copy_ref, scratch = outs
    if hops:
        grads_ref, mine_refs, theirs_refs = refs[0], refs[1 : 1 + len(hops)], refs[1 + len(hops) : 1 + 2 * len(hops)]
        rows = grads_ref.shape[1]
        here = lax.axis_index("shard") // 2
        parity = lax.axis_index("shard") % 2
        start = l_basis_ref.shape[0]
        received = [got_ref[pl.ds(start + k * rows, rows), :] for k in range(grad_ref.shape[1] // LANES)]
        place_rows(grad_ref, 2 * here + parity, rows, grads_ref[here])
        place_rows(grad_ref, 2 * here + 1 - parity, rows, jnp.concatenate(received, axis=1))
        for hop, mine, theirs in zip(hops, mine_refs, theirs_refs):
            place_rows(grad_ref, 2 * (here ^ hop) + parity, rows, mine[...])
            place_rows(grad_ref, 2 * (here ^ hop) + 1 - parity, rows, theirs[...])
    else:
        grad_ref[...] = refs[0][...]
    own = pick(left, thirds(l_basis_ref), thirds(r_basis_ref))
    got = thirds(got_ref, 0, l_basis_ref.shape[0])
    basis_ref[...] = whole_of(scratch, pick(left, own, got), pick(left, got, own))
    own_ref[...] = jnp.where(left, l_stat_ref[...], r_stat_ref[...])
    other_ref[...] = jnp.where(left, r_stat_ref[...], l_stat_ref[...])
    copy_ref[...] = l_basis_ref[...]
    right = half_of(scratch, thirds(r_basis_ref))
    right_ref[...] = right
    grad = grad_ref[...]
    parts = split(jnp.where(left, grad, grad.T))
    product_ref[...] = symmetric_dot(parts, parts, ((1,), (1,)))
    inner_ref[...] = dot(grad, right)


def begin_kernel(steps, own_ref, corner_ref, product_ref, basis_ref, new_stat_ref, x_ref, scratch):
    new_stat = 0.5 * statistic(is_left(), thirds(own_ref), corner_ref, scratch) + 0.5 * product_ref[...]
    new_stat_ref[...] = new_stat
    power = dot(new_stat, basis_ref[...])
    x_ref[...] = iterate(power * (1.0 / jnp.sqrt(jnp.sum(power * power) + NORM_EPS)), steps)


def end_kernel(steps, start_ref, x_ref, poly_ref, send_ref, scratch):
    x = iterate(start_ref[...], steps - 1)
    x_ref[...] = x
    poly = polynomial(split(x))
    poly_ref[...] = poly
    half = take_half(x, jnp.logical_not(is_left()))
    put_thirds(send_ref, flat_of(scratch, LINEAR_COEFF * half + dot(poly, half)))


def update_kernel(
    hops,
    inner_ref,
    basis_ref,
    left_ref,
    right_ref,
    first_left_ref,
    one_ref,
    two_ref,
    new_one_ref,
    new_two_ref,
    mine_ref,
    theirs_ref,
    scratch,
    partial_ref,
):
    left = is_left()
    basis_left = jnp.where(left, basis_ref[...], whole_of(scratch, thirds(first_left_ref), thirds(left_ref)))
    left_parts = split(basis_left)
    basis_right = split(right_ref[...])
    rotated = flat_of(scratch, dot(basis_left.T, inner_ref[...]))
    ones = thirds(one_ref)
    twos = thirds(two_ref)
    new_one = [BETA_ONE * m + (1.0 - BETA_ONE) * r for m, r in zip(ones, rotated)]
    new_two = [BETA_TWO * v + (1.0 - BETA_TWO) * r * r for v, r in zip(twos, rotated)]
    put_thirds(new_one_ref, new_one)
    put_thirds(new_two_ref, new_two)
    direction = [m / (jnp.sqrt(v) + ADAM_EPS) for m, v in zip(new_one, new_two)]
    outer = dot_parts(left_parts, split(half_of(scratch, direction)))
    partial_ref[...] = dot_parts(split(outer), basis_right, ((1,), (1,)))
    rows = mine_ref.shape[1]
    here = lax.axis_index("shard") // 2
    parity = lax.axis_index("shard") % 2
    for k, hop in enumerate((0, *hops)):
        block = 2 * (here ^ hop) if hops else 0
        mine_ref[k] = partial_ref[pl.ds(pl.multiple_of((block + parity) * rows, 8), rows), :]
        theirs_ref[k] = partial_ref[pl.ds(pl.multiple_of((block + 1 - parity) * rows, 8), rows), :]


def add_kernel(mine_ref, theirs_ref, *out_refs):
    for k, out_ref in enumerate(out_refs):
        out_ref[...] = mine_ref[k] + theirs_ref[k]


def bases_kernel(keep_ref, back_ref, new_left_ref, new_right_ref, sems):
    left = is_left()

    def copies(own_ref, other_ref):
        return [
            pltpu.make_async_copy(keep_ref, own_ref, sems.at[0]),
            pltpu.make_async_copy(back_ref, other_ref, sems.at[1]),
        ]

    @pl.when(left)
    def _():
        for copy in copies(new_left_ref, new_right_ref):
            copy.start()

    @pl.when(jnp.logical_not(left))
    def _():
        for copy in copies(new_right_ref, new_left_ref):
            copy.start()

    for copy in copies(new_left_ref, new_right_ref):
        copy.wait()


def rows_kernel(hops, *refs):
    rows_refs, (update_ref, sems) = refs[:-2], refs[-2:]
    here = lax.axis_index("shard") // 2
    copies = [
        pltpu.make_async_copy(rows_refs[k], update_ref.at[here ^ hop], sems.at[k]) for k, hop in enumerate((0, *hops))
    ]
    for copy in copies:
        copy.start()
    for copy in copies:
        copy.wait()


def rest_kernel(x_ref, poly_ref, grad_ref, new_stat_ref, other_ref, keep_ref, new_left_ref, new_right_ref, scratch):
    left = is_left()
    half = take_half(x_ref[...], left)
    put_thirds(keep_ref, flat_of(scratch, LINEAR_COEFF * half + dot(poly_ref[...], half)))
    grad = grad_ref[...]
    turned = grad.T
    a = jnp.where(left, grad, turned)
    b = jnp.where(left, turned, grad)
    new_own = flat_of(scratch, take_half(new_stat_ref[...], left))
    product = flat_of(scratch, dot(b, take_half(a, left)))
    new_other = [0.5 * u + 0.5 * v for u, v in zip(thirds(other_ref), product)]
    put_thirds(new_left_ref, pick(left, new_own, new_other))
    put_thirds(new_right_ref, pick(left, new_other, new_own))


def call(kernel, outs, scratch, products, full, name, copies=0, kind=jax.ShapeDtypeStruct, **specs):
    size = full * full
    scratch = [pltpu.VMEM(s, F32) for s in scratch]
    if copies:
        scratch.append(pltpu.SemaphoreType.DMA((copies,)))
    return pl.pallas_call(
        kernel,
        out_shape=[kind(s, F32) for s in outs],
        scratch_shapes=scratch,
        compiler_params=pltpu.CompilerParams(vmem_limit_bytes=40 * 1024 * 1024),
        cost_estimate=pl.CostEstimate(flops=int(products * 6 * full * size), bytes_accessed=16 * size, transcendentals=0),
        name=name,
        **specs,
    )


def anywhere(count):
    return [pl.BlockSpec(memory_space=pl.ANY)] * count


def after(x, *others):
    return lax.optimization_barrier((x, *others))[0]


def local(grads, moment_one, moment_two, left_stat, right_stat, left_basis, right_basis):
    tiles_here, rows_here, full = grads.shape
    size = lax.axis_size("shard")
    flat_rows = full * (full // 2) // LANES
    flat = (flat_rows, LANES)
    square = (full, full)
    block = (rows_here, full)
    parity = lax.axis_index("shard") % 2
    pairs = [(i, i ^ 1) for i in range(size)]
    sides = [list(range(k, size, 2)) for k in range(2)]
    near = size in (4, 8) and rows_here % 8 == 0
    hops = {4: (1,), 8: (2, 3, 1)}[size] if near else ()
    strips = (tiles_here, *block) if near else (1, full // 2, full)

    def exchange(x):
        return lax.all_to_all(x, "shard", split_axis=0, concat_axis=0, axis_index_groups=sides, tiled=True)

    def hop_by(x, hop):
        return lax.ppermute(x, "shard", [(i, i ^ (2 * hop)) for i in range(size)])

    def partner(x):
        return lax.ppermute(x, "shard", pairs)

    one, two, l_stat, r_stat, l_basis, r_basis = (
        x.reshape(flat) for x in (moment_one, moment_two, left_stat, right_stat, left_basis, right_basis)
    )
    count = corner_rows(flat_rows)
    outgoing_rows = flat_rows + (rows_here * (full // LANES) if near else 0)
    outgoing, corner, *pieces = call(
        functools.partial(pack_kernel, hops),
        [(outgoing_rows, LANES), (count, LANES)] + [block] * len(hops),
        [(flat_rows // 2, LANES)],
        0.1,
        full,
        "pack",
        copies=2 + len(hops) + full // LANES,
        kind=pltpu.VMEM,
        in_specs=anywhere(5),
        out_specs=anywhere(1) + [pl.BlockSpec(memory_space=pltpu.VMEM)] + anywhere(len(hops)),
    )(*(pltpu.with_memory_space_constraint(x, pltpu.HBM) for x in (l_stat, r_stat, l_basis, r_basis, grads)))
    got = partner(outgoing)
    if near:
        mine = [hop_by(piece, hop) for hop, piece in zip(hops, pieces)]
        theirs = [partner(x) for x in mine]
        rows = (grads, *mine, *theirs)
    else:
        mine = exchange(grads)
        theirs = partner(mine)
        even, odd = jnp.where(parity == 0, mine, theirs), jnp.where(parity == 0, theirs, mine)
        rows = (jnp.stack([even, odd], axis=1).reshape(square),)
        mine = [mine]
    got_corner = partner(after(corner, theirs[0] if near else mine[0]))
    grad, product, basis, right, inner, own, other, left = call(
        functools.partial(products_kernel, hops),
        [square, square, square, (full, 2 * LANES), (full, 2 * LANES), flat, flat, flat],
        [(3, full, LANES)],
        2,
        full,
        "products",
    )(l_stat, r_stat, l_basis, r_basis, got, *rows)
    first_left = partner(after(l_basis, product))
    new_stat, x = call(functools.partial(begin_kernel, 2), [square] * 2, [(3, full, LANES)], 7, full, "begin")(
        own, got_corner, product, basis
    )
    new_one, new_two, own_rows, other_rows = call(
        functools.partial(update_kernel, hops), [flat, flat, strips, strips], [(3, full, LANES), square], 2, full, "update"
    )(after(inner, x), basis, left, right, first_left, one, two)
    if not near:
        top = jnp.where(parity == 0, own_rows, other_rows)
        bottom = jnp.where(parity == 0, other_rows, own_rows)
        merged = jnp.concatenate([top, bottom], axis=1).reshape(tiles_here, 2, rows_here, full)
        own_rows = lax.dynamic_index_in_dim(merged, parity, 1, keepdims=False)
        other_rows = lax.dynamic_index_in_dim(merged, 1 - parity, 1, keepdims=False)
    got_rows = partner(other_rows)
    x, poly, send = call(
        functools.partial(end_kernel, NS_ITERS - 2), [square, square, flat], [(3, full, LANES)], 9, full, "end"
    )(after(x, other_rows))
    back = partner(send)
    keep, new_left, new_right = call(rest_kernel, [flat, flat, flat], [(3, full, LANES)], 1.5, full, "rest")(
        x, poly, grad, new_stat, other
    )
    if near:
        kept, *sums = call(add_kernel, [block] * (1 + len(hops)), [], 0.1, full, "add")(
            after(own_rows, send), after(got_rows, send)
        )
        returned = [hop_by(x, hop) for hop, x in zip(hops, sums)]
        update = call(
            functools.partial(rows_kernel, hops),
            [grads.shape],
            [],
            0.1,
            full,
            "rows",
            copies=1 + len(hops),
            in_specs=anywhere(1 + len(hops)),
            out_specs=anywhere(1),
        )(kept, *returned)[0]
    else:
        update = exchange(after(own_rows, send) + after(got_rows, send))
    new_l_basis, new_r_basis = call(
        bases_kernel, [flat, flat], [], 0.1, full, "bases", copies=2, in_specs=anywhere(2), out_specs=anywhere(2)
    )(keep, back)
    halves = (new_one, new_two, new_left, new_right, new_l_basis, new_r_basis)
    return (update, *(x.reshape(1, flat_rows * LANES) for x in halves))


def solution(mesh):
    halves = P(("tensor", "shard"), None)
    rows = P("tensor", "shard", None)
    return jax.shard_map(
        local, mesh=mesh, in_specs=(rows,) + (halves,) * 6, out_specs=(rows,) + (halves,) * 6, check_vma=False
    )
```

```python
import functools

import jax
import jax.numpy as jnp
from jax import lax
from jax.experimental import pallas as pl
from jax.experimental.pallas import tpu as pltpu
from jax.sharding import PartitionSpec as P

NS_ITERS = 5
EARLY_ITERS = 1
BETA_ONE = 0.9
BETA_TWO = 0.95
ADAM_EPS = 1e-08
NORM_EPS = 1e-06
LINEAR_COEFF = 3.4445
CUBIC_COEFF = -4.775
QUINTIC_COEFF = 2.0315
LANES = 128
F32 = jnp.float32


def split(x):
    high = x.astype(jnp.bfloat16)
    return high, (x - high.astype(F32)).astype(jnp.bfloat16)


def dot(a, b, dims=((1,), (0,))):
    return dot_parts(split(a), split(b), dims)


def dot_parts(a, b, dims=((1,), (0,))):
    (ka,), (kb,) = dims
    left = jnp.concatenate([a[0], a[0], a[1]], axis=ka)
    right = jnp.concatenate([b[0], b[1], b[0]], axis=kb)
    return lax.dot_general(left, right, (dims, ((), ())), preferred_element_type=F32)


def symmetric_dot(a, b, dims=((1,), (0,))):
    (ka,), (kb,) = dims
    cut = a[0].shape[0] - LANES
    head = lambda x, axis: lax.slice_in_dim(x, 0, cut, axis=axis)
    tail = lambda x, axis: lax.slice_in_dim(x, cut, cut + LANES, axis=axis)
    left = dot_parts(a, [head(x, 1 - kb) for x in b], dims)
    corner = dot_parts([tail(x, 1 - ka) for x in a], [tail(x, 1 - kb) for x in b], dims)
    right = jnp.concatenate([left[cut:].T, corner], axis=0)
    return jnp.concatenate([left, right], axis=1)


def swap(x):
    return pltpu.roll(x, LANES // 2, 1)


def low_lanes(shape):
    return lax.broadcasted_iota(jnp.int32, shape, 1) < LANES // 2


def pick(flag, x, y):
    return [jnp.where(flag, u, v) for u, v in zip(x, y)]


def thirds(ref, start=0, rows=None):
    rows = ref.shape[0] if rows is None else rows
    return [ref[pl.ds(start + k, rows // 3, stride=3), :] for k in range(3)]


def put_thirds(ref, parts):
    for k in range(3):
        ref[pl.ds(k, parts[k].shape[0], stride=3), :] = parts[k]


def interleave(scratch, index, even, odd):
    scratch[index, pl.ds(0, even.shape[0], stride=2), :] = even
    scratch[index, pl.ds(1, odd.shape[0], stride=2), :] = odd


def whole_of(scratch, first, second):
    a, b, c = first
    d, e, f = second
    low = low_lanes(a.shape)
    sb, sc, sd, se = swap(b), swap(c), swap(d), swap(e)
    interleave(scratch, 0, a, jnp.where(low, sb, sc))
    interleave(scratch, 1, jnp.where(low, b, sd), jnp.where(low, sc, e))
    interleave(scratch, 2, jnp.where(low, sd, se), f)
    return jnp.concatenate([scratch[0], scratch[1], scratch[2]], axis=1)


def half_of(scratch, flat):
    a, b, c = flat
    low = low_lanes(a.shape)
    sb, sc = swap(b), swap(c)
    interleave(scratch, 0, a, jnp.where(low, sb, sc))
    interleave(scratch, 1, jnp.where(low, b, 0.0), jnp.where(low, sc, 0.0))
    return jnp.concatenate([scratch[0], scratch[1]], axis=1)


def flat_of(scratch, half):
    scratch[0] = half[:, :LANES]
    scratch[1] = half[:, LANES:]
    pairs = half.shape[0] // 2
    even0 = scratch[0, pl.ds(0, pairs, stride=2), :]
    odd0 = swap(scratch[0, pl.ds(1, pairs, stride=2), :])
    even1 = scratch[1, pl.ds(0, pairs, stride=2), :]
    odd1 = swap(scratch[1, pl.ds(1, pairs, stride=2), :])
    low = low_lanes(even0.shape)
    return [even0, jnp.where(low, even1, odd0), jnp.where(low, odd0, odd1)]


def take_half(whole, first):
    one, two, three = whole[:, :LANES], whole[:, LANES : 2 * LANES], whole[:, 2 * LANES :]
    low = low_lanes(one.shape)
    s2, s3 = swap(two), swap(three)
    head = jnp.where(first, one, jnp.where(low, s2, s3))
    tail = jnp.where(low, jnp.where(first, two, s3), 0.0)
    return jnp.concatenate([head, tail], axis=1)


def is_first():
    return lax.rem(lax.axis_index("shard"), 2) == 0


def is_left():
    return lax.rem(lax.axis_index("shard") + lax.axis_index("tensor"), 2) == 0


def pack_kernel(hops, l_stat_ref, r_stat_ref, l_basis_ref, r_basis_ref, grads_ref, *refs):
    out_ref, small_ref, *refs = refs
    piece_refs, (corner, sems) = refs[: len(hops)], refs[len(hops) :]
    left = is_left()
    flat_rows = l_basis_ref.shape[0]
    half_rows = flat_rows // 2
    rows = grads_ref.shape[1]
    here = lax.axis_index("shard") // 2

    start = pl.multiple_of(jnp.where(is_first(), 0, half_rows), 8)

    def copies(basis_ref, stat_ref):
        return [
            pltpu.make_async_copy(stat_ref.at[pl.ds(start, half_rows)], corner, sems.at[0]),
            pltpu.make_async_copy(basis_ref, out_ref.at[pl.ds(0, flat_rows)], sems.at[1]),
        ]

    @pl.when(left)
    def _():
        for copy in copies(r_basis_ref, r_stat_ref):
            copy.start()

    @pl.when(jnp.logical_not(left))
    def _():
        for copy in copies(l_basis_ref, l_stat_ref):
            copy.start()

    more = []
    for number, (hop, piece_ref) in enumerate(zip(hops, piece_refs)):
        more.append(pltpu.make_async_copy(grads_ref.at[here ^ hop], piece_ref, sems.at[2 + number]))
    if hops:
        for k in range(grads_ref.shape[2] // LANES):
            source = grads_ref.at[here, :, pl.ds(k * LANES, LANES)]
            target = out_ref.at[pl.ds(flat_rows + k * rows, rows)]
            more.append(pltpu.make_async_copy(source, target, sems.at[2 + len(hops) + k]))
    for copy in more:
        copy.start()
    first, second = copies(l_basis_ref, l_stat_ref)
    first.wait()
    third = half_rows // 9
    a, b, c = thirds(corner)
    low = low_lanes((third, LANES))
    middle = slice(third, 2 * third)
    small_ref[pl.ds(0, third)] = jnp.where(low, a[:third], b[:third])
    small_ref[pl.ds(third, third)] = a[middle]
    small_ref[pl.ds(2 * third, third)] = jnp.where(low, swap(b[middle]), swap(c[middle]))
    small_ref[pl.ds(3 * third, 3 * third)] = corner[pl.ds(6 * third, 3 * third)]
    for copy in [second, *more]:
        copy.wait()


def corner_rows(flat_rows):
    return flat_rows // 3


def unpack_corner(got_ref):
    third = got_ref.shape[0] // 6
    small = got_ref[pl.ds(0, third), :]
    even = got_ref[pl.ds(third, third), :]
    odd = swap(got_ref[pl.ds(2 * third, third), :])
    a, b, c = thirds(got_ref, 3 * third, 3 * third)
    low = low_lanes(small.shape)
    zero = jnp.zeros_like(small)
    return [
        jnp.concatenate([jnp.where(low, small, zero), even, a], axis=0),
        jnp.concatenate([jnp.where(low, zero, small), jnp.where(low, zero, odd), b], axis=0),
        jnp.concatenate([zero, jnp.where(low, odd, zero), c], axis=0),
    ]


def statistic(first, own, got_ref, scratch):
    corner = unpack_corner(got_ref)
    placed = [jnp.concatenate([jnp.where(first, 0.0, c), jnp.where(first, c, 0.0)], axis=0) for c in corner]
    known = whole_of(scratch, pick(first, own, placed), pick(first, placed, own))
    half = known.shape[0] // 2
    part = half // 3
    row = lax.broadcasted_iota(jnp.int32, known.shape, 0)
    column = lax.broadcasted_iota(jnp.int32, known.shape, 1)
    missing = (jnp.where(first, row, column) < half) & (jnp.where(first, column, row) >= half)
    offset = jnp.where(first, half, 0)
    row, column = row - offset, column - offset
    limit = jnp.where(row < part, part, 2 * part)
    missing |= (row >= 0) & (row < 2 * part) & (column < half) & (column >= limit)
    return jnp.where(missing, known.T, known)


def place_rows(grad_ref, block, rows, value):
    grad_ref[pl.ds(pl.multiple_of(block * rows, 8), rows), :] = value


def polynomial(parts):
    gram = dot_parts(parts, parts, ((1,), (1,)))
    gram_parts = split(gram)
    return CUBIC_COEFF * gram + QUINTIC_COEFF * dot_parts(gram_parts, gram_parts)


def iterate(x, steps):
    for _ in range(steps):
        parts = split(x)
        x = LINEAR_COEFF * x + dot_parts(split(polynomial(parts)), parts)
    return x


def products_kernel(hops, l_stat_ref, r_stat_ref, l_basis_ref, r_basis_ref, got_ref, *refs):
    left = is_left()
    outs = refs[-9:]
    grad_ref, product_ref, basis_ref, right_ref, inner_ref, own_ref, other_ref, copy_ref, scratch = outs
    if hops:
        grads_ref, mine_refs, theirs_refs = refs[0], refs[1 : 1 + len(hops)], refs[1 + len(hops) : 1 + 2 * len(hops)]
        rows = grads_ref.shape[1]
        here = lax.axis_index("shard") // 2
        parity = lax.axis_index("shard") % 2
        start = l_basis_ref.shape[0]
        received = [got_ref[pl.ds(start + k * rows, rows), :] for k in range(grad_ref.shape[1] // LANES)]
        place_rows(grad_ref, 2 * here + parity, rows, grads_ref[here])
        place_rows(grad_ref, 2 * here + 1 - parity, rows, jnp.concatenate(received, axis=1))
        for hop, mine, theirs in zip(hops, mine_refs, theirs_refs):
            place_rows(grad_ref, 2 * (here ^ hop) + parity, rows, mine[...])
            place_rows(grad_ref, 2 * (here ^ hop) + 1 - parity, rows, theirs[...])
    else:
        grad_ref[...] = refs[0][...]
    own = pick(left, thirds(l_basis_ref), thirds(r_basis_ref))
    got = thirds(got_ref, 0, l_basis_ref.shape[0])
    first = is_first()
    basis_ref[...] = whole_of(scratch, pick(first, own, got), pick(first, got, own))
    own_ref[...] = jnp.where(left, l_stat_ref[...], r_stat_ref[...])
    other_ref[...] = jnp.where(left, r_stat_ref[...], l_stat_ref[...])
    copy_ref[...] = l_basis_ref[...]
    right = half_of(scratch, thirds(r_basis_ref))
    right_ref[...] = right
    grad = grad_ref[...]
    parts = split(jnp.where(left, grad, grad.T))
    product_ref[...] = symmetric_dot(parts, parts, ((1,), (1,)))
    inner_ref[...] = dot(grad, right)


def begin_kernel(steps, own_ref, corner_ref, product_ref, basis_ref, new_stat_ref, x_ref, scratch):
    new_stat = 0.5 * statistic(is_first(), thirds(own_ref), corner_ref, scratch) + 0.5 * product_ref[...]
    new_stat_ref[...] = new_stat
    power = dot(new_stat, basis_ref[...])
    x_ref[...] = iterate(power * (1.0 / jnp.sqrt(jnp.sum(power * power) + NORM_EPS)), steps)


def end_kernel(steps, start_ref, x_ref, poly_ref, send_ref, scratch):
    x = iterate(start_ref[...], steps - 1)
    x_ref[...] = x
    poly = polynomial(split(x))
    poly_ref[...] = poly
    half = take_half(x, jnp.logical_not(is_first()))
    put_thirds(send_ref, flat_of(scratch, LINEAR_COEFF * half + dot(poly, half)))


def update_kernel(
    hops,
    inner_ref,
    basis_ref,
    left_ref,
    right_ref,
    other_left_ref,
    one_ref,
    two_ref,
    new_one_ref,
    new_two_ref,
    mine_ref,
    theirs_ref,
    scratch,
    partial_ref,
):
    left = is_left()
    first = is_first()
    own, got = thirds(left_ref), thirds(other_left_ref)
    basis_left = jnp.where(left, basis_ref[...], whole_of(scratch, pick(first, own, got), pick(first, got, own)))
    left_parts = split(basis_left)
    basis_right = split(right_ref[...])
    rotated = flat_of(scratch, dot(basis_left.T, inner_ref[...]))
    ones = thirds(one_ref)
    twos = thirds(two_ref)
    new_one = [BETA_ONE * m + (1.0 - BETA_ONE) * r for m, r in zip(ones, rotated)]
    new_two = [BETA_TWO * v + (1.0 - BETA_TWO) * r * r for v, r in zip(twos, rotated)]
    put_thirds(new_one_ref, new_one)
    put_thirds(new_two_ref, new_two)
    direction = [m / (jnp.sqrt(v) + ADAM_EPS) for m, v in zip(new_one, new_two)]
    outer = dot_parts(left_parts, split(half_of(scratch, direction)))
    partial_ref[...] = dot_parts(split(outer), basis_right, ((1,), (1,)))
    rows = mine_ref.shape[1]
    here = lax.axis_index("shard") // 2
    parity = lax.axis_index("shard") % 2
    for k, hop in enumerate((0, *hops)):
        block = 2 * (here ^ hop) if hops else 0
        mine_ref[k] = partial_ref[pl.ds(pl.multiple_of((block + parity) * rows, 8), rows), :]
        theirs_ref[k] = partial_ref[pl.ds(pl.multiple_of((block + 1 - parity) * rows, 8), rows), :]


def add_kernel(mine_ref, theirs_ref, *out_refs):
    for k, out_ref in enumerate(out_refs):
        out_ref[...] = mine_ref[k] + theirs_ref[k]


def bases_kernel(keep_ref, back_ref, new_left_ref, new_right_ref, sems):
    left = is_left()

    def copies(own_ref, other_ref):
        return [
            pltpu.make_async_copy(keep_ref, own_ref, sems.at[0]),
            pltpu.make_async_copy(back_ref, other_ref, sems.at[1]),
        ]

    @pl.when(left)
    def _():
        for copy in copies(new_left_ref, new_right_ref):
            copy.start()

    @pl.when(jnp.logical_not(left))
    def _():
        for copy in copies(new_right_ref, new_left_ref):
            copy.start()

    for copy in copies(new_left_ref, new_right_ref):
        copy.wait()


def rows_kernel(hops, *refs):
    rows_refs, (update_ref, sems) = refs[:-2], refs[-2:]
    here = lax.axis_index("shard") // 2
    copies = [
        pltpu.make_async_copy(rows_refs[k], update_ref.at[here ^ hop], sems.at[k]) for k, hop in enumerate((0, *hops))
    ]
    for copy in copies:
        copy.start()
    for copy in copies:
        copy.wait()


def rest_kernel(x_ref, poly_ref, grad_ref, new_stat_ref, other_ref, keep_ref, new_left_ref, new_right_ref, scratch):
    left = is_left()
    first = is_first()
    half = take_half(x_ref[...], first)
    put_thirds(keep_ref, flat_of(scratch, LINEAR_COEFF * half + dot(poly_ref[...], half)))
    grad = grad_ref[...]
    turned = grad.T
    a = jnp.where(left, grad, turned)
    b = jnp.where(left, turned, grad)
    new_own = flat_of(scratch, take_half(new_stat_ref[...], first))
    product = flat_of(scratch, dot(b, take_half(a, first)))
    new_other = [0.5 * u + 0.5 * v for u, v in zip(thirds(other_ref), product)]
    put_thirds(new_left_ref, pick(left, new_own, new_other))
    put_thirds(new_right_ref, pick(left, new_other, new_own))


def call(kernel, outs, scratch, products, full, name, copies=0, kind=jax.ShapeDtypeStruct, **specs):
    size = full * full
    scratch = [pltpu.VMEM(s, F32) for s in scratch]
    if copies:
        scratch.append(pltpu.SemaphoreType.DMA((copies,)))
    return pl.pallas_call(
        kernel,
        out_shape=[kind(s, F32) for s in outs],
        scratch_shapes=scratch,
        compiler_params=pltpu.CompilerParams(vmem_limit_bytes=40 * 1024 * 1024),
        cost_estimate=pl.CostEstimate(flops=int(products * 6 * full * size), bytes_accessed=16 * size, transcendentals=0),
        name=name,
        **specs,
    )


def anywhere(count):
    return [pl.BlockSpec(memory_space=pl.ANY)] * count


def after(x, *others):
    return lax.optimization_barrier((x, *others))[0]


def local(grads, moment_one, moment_two, left_stat, right_stat, left_basis, right_basis):
    tiles_here, rows_here, full = grads.shape
    size = lax.axis_size("shard")
    flat_rows = full * (full // 2) // LANES
    flat = (flat_rows, LANES)
    square = (full, full)
    block = (rows_here, full)
    parity = lax.axis_index("shard") % 2
    pairs = [(i, i ^ 1) for i in range(size)]
    sides = [list(range(k, size, 2)) for k in range(2)]
    near = size in (4, 8) and rows_here % 8 == 0
    hops = {4: (1,), 8: (2, 3, 1)}[size] if near else ()
    strips = (tiles_here, *block) if near else (1, full // 2, full)

    def exchange(x):
        return lax.all_to_all(x, "shard", split_axis=0, concat_axis=0, axis_index_groups=sides, tiled=True)

    def hop_by(x, hop):
        return lax.ppermute(x, "shard", [(i, i ^ (2 * hop)) for i in range(size)])

    def partner(x):
        return lax.ppermute(x, "shard", pairs)

    one, two, l_stat, r_stat, l_basis, r_basis = (
        x.reshape(flat) for x in (moment_one, moment_two, left_stat, right_stat, left_basis, right_basis)
    )
    count = corner_rows(flat_rows)
    outgoing_rows = flat_rows + (rows_here * (full // LANES) if near else 0)
    outgoing, corner, *pieces = call(
        functools.partial(pack_kernel, hops),
        [(outgoing_rows, LANES), (count, LANES)] + [block] * len(hops),
        [(flat_rows // 2, LANES)],
        0.1,
        full,
        "pack",
        copies=2 + len(hops) + full // LANES,
        kind=pltpu.VMEM,
        in_specs=anywhere(5),
        out_specs=anywhere(1) + [pl.BlockSpec(memory_space=pltpu.VMEM)] + anywhere(len(hops)),
    )(*(pltpu.with_memory_space_constraint(x, pltpu.HBM) for x in (l_stat, r_stat, l_basis, r_basis, grads)))
    got = partner(outgoing)
    if near:
        mine = [hop_by(piece, hop) for hop, piece in zip(hops, pieces)]
        theirs = [partner(x) for x in mine]
        rows = (grads, *mine, *theirs)
    else:
        mine = exchange(grads)
        theirs = partner(mine)
        even, odd = jnp.where(parity == 0, mine, theirs), jnp.where(parity == 0, theirs, mine)
        rows = (jnp.stack([even, odd], axis=1).reshape(square),)
        mine = [mine]
    got_corner = partner(after(corner, theirs[0] if near else mine[0]))
    grad, product, basis, right, inner, own, other, left = call(
        functools.partial(products_kernel, hops),
        [square, square, square, (full, 2 * LANES), (full, 2 * LANES), flat, flat, flat],
        [(3, full, LANES)],
        2,
        full,
        "products",
    )(l_stat, r_stat, l_basis, r_basis, got, *rows)
    tensors = lax.axis_size("tensor")
    place = lambda t, i: i * tensors + t
    cycle = []
    for t in range(0, tensors - tensors % 2, 2):
        for i in range(0, size, 2):
            cycle += [(place(t, i), place(t, i + 1)), (place(t, i + 1), place(t + 1, i + 1))]
            cycle += [(place(t + 1, i + 1), place(t + 1, i)), (place(t + 1, i), place(t, i))]
    cycle += [(place(t, i), place(t, i ^ 1)) for t in range(tensors - tensors % 2, tensors) for i in range(size)]
    other_left = lax.ppermute(after(l_basis, *(theirs[:2] if near else mine)), ("shard", "tensor"), cycle)
    new_stat, x = call(functools.partial(begin_kernel, EARLY_ITERS), [square] * 2, [(3, full, LANES)], 7, full, "begin")(
        own, got_corner, product, basis
    )
    new_one, new_two, own_rows, other_rows = call(
        functools.partial(update_kernel, hops), [flat, flat, strips, strips], [(3, full, LANES), square], 2, full, "update"
    )(after(inner, x), basis, left, right, other_left, one, two)
    if not near:
        top = jnp.where(parity == 0, own_rows, other_rows)
        bottom = jnp.where(parity == 0, other_rows, own_rows)
        merged = jnp.concatenate([top, bottom], axis=1).reshape(tiles_here, 2, rows_here, full)
        own_rows = lax.dynamic_index_in_dim(merged, parity, 1, keepdims=False)
        other_rows = lax.dynamic_index_in_dim(merged, 1 - parity, 1, keepdims=False)
    got_rows = partner(other_rows)
    x, poly, send = call(
        functools.partial(end_kernel, NS_ITERS - EARLY_ITERS), [square, square, flat], [(3, full, LANES)], 9, full, "end"
    )(after(x, other_rows))
    back = partner(send)
    keep, new_left, new_right = call(rest_kernel, [flat, flat, flat], [(3, full, LANES)], 1.5, full, "rest")(
        x, poly, grad, new_stat, other
    )
    if near:
        kept, *sums = call(add_kernel, [block] * (1 + len(hops)), [], 0.1, full, "add")(
            after(own_rows, send), after(got_rows, send)
        )
        returned = [hop_by(x, hop) for hop, x in zip(hops, sums)]
        update = call(
            functools.partial(rows_kernel, hops),
            [grads.shape],
            [],
            0.1,
            full,
            "rows",
            copies=1 + len(hops),
            in_specs=anywhere(1 + len(hops)),
            out_specs=anywhere(1),
        )(kept, *returned)[0]
    else:
        update = exchange(after(own_rows, send) + after(got_rows, send))
    new_l_basis, new_r_basis = call(
        bases_kernel, [flat, flat], [], 0.1, full, "bases", copies=2, in_specs=anywhere(2), out_specs=anywhere(2)
    )(keep, back)
    halves = (new_one, new_two, new_left, new_right, new_l_basis, new_r_basis)
    return (update, *(x.reshape(1, flat_rows * LANES) for x in halves))


def solution(mesh):
    halves = P(("tensor", "shard"), None)
    rows = P("tensor", "shard", None)
    return jax.shard_map(
        local, mesh=mesh, in_specs=(rows,) + (halves,) * 6, out_specs=(rows,) + (halves,) * 6, check_vma=False
    )
```

```python
import functools

import jax
import jax.numpy as jnp
from jax import lax
from jax.experimental import pallas as pl
from jax.experimental.pallas import tpu as pltpu
from jax.sharding import PartitionSpec as P

NS_ITERS = 5
EARLY_ITERS = 1
BETA_ONE = 0.9
BETA_TWO = 0.95
ADAM_EPS = 1e-08
NORM_EPS = 1e-06
LINEAR_COEFF = 3.4445
CUBIC_COEFF = -4.775
QUINTIC_COEFF = 2.0315
LANES = 128
F32 = jnp.float32


def split(x):
    high = x.astype(jnp.bfloat16)
    return high, (x - high.astype(F32)).astype(jnp.bfloat16)


def dot(a, b, dims=((1,), (0,))):
    return dot_parts(split(a), split(b), dims)


def dot_parts(a, b, dims=((1,), (0,))):
    (ka,), (kb,) = dims
    left = jnp.concatenate([a[0], a[0], a[1]], axis=ka)
    right = jnp.concatenate([b[0], b[1], b[0]], axis=kb)
    return lax.dot_general(left, right, (dims, ((), ())), preferred_element_type=F32)


def symmetric_dot(a, b, dims=((1,), (0,))):
    (ka,), (kb,) = dims
    cut = a[0].shape[0] - LANES
    head = lambda x, axis: lax.slice_in_dim(x, 0, cut, axis=axis)
    tail = lambda x, axis: lax.slice_in_dim(x, cut, cut + LANES, axis=axis)
    left = dot_parts(a, [head(x, 1 - kb) for x in b], dims)
    corner = dot_parts([tail(x, 1 - ka) for x in a], [tail(x, 1 - kb) for x in b], dims)
    right = jnp.concatenate([left[cut:].T, corner], axis=0)
    return jnp.concatenate([left, right], axis=1)


def swap(x):
    return pltpu.roll(x, LANES // 2, 1)


def low_lanes(shape):
    return lax.broadcasted_iota(jnp.int32, shape, 1) < LANES // 2


def pick(flag, x, y):
    return [jnp.where(flag, u, v) for u, v in zip(x, y)]


def thirds(ref, start=0, rows=None):
    rows = ref.shape[0] if rows is None else rows
    return [ref[pl.ds(start + k, rows // 3, stride=3), :] for k in range(3)]


def put_thirds(ref, parts):
    for k in range(3):
        ref[pl.ds(k, parts[k].shape[0], stride=3), :] = parts[k]


def interleave(scratch, index, even, odd):
    scratch[index, pl.ds(0, even.shape[0], stride=2), :] = even
    scratch[index, pl.ds(1, odd.shape[0], stride=2), :] = odd


def whole_of(scratch, first, second):
    a, b, c = first
    d, e, f = second
    low = low_lanes(a.shape)
    sb, sc, sd, se = swap(b), swap(c), swap(d), swap(e)
    interleave(scratch, 0, a, jnp.where(low, sb, sc))
    interleave(scratch, 1, jnp.where(low, b, sd), jnp.where(low, sc, e))
    interleave(scratch, 2, jnp.where(low, sd, se), f)
    return jnp.concatenate([scratch[0], scratch[1], scratch[2]], axis=1)


def half_of(scratch, flat):
    a, b, c = flat
    low = low_lanes(a.shape)
    sb, sc = swap(b), swap(c)
    interleave(scratch, 0, a, jnp.where(low, sb, sc))
    interleave(scratch, 1, jnp.where(low, b, 0.0), jnp.where(low, sc, 0.0))
    return jnp.concatenate([scratch[0], scratch[1]], axis=1)


def flat_of(scratch, half):
    scratch[0] = half[:, :LANES]
    scratch[1] = half[:, LANES:]
    pairs = half.shape[0] // 2
    even0 = scratch[0, pl.ds(0, pairs, stride=2), :]
    odd0 = swap(scratch[0, pl.ds(1, pairs, stride=2), :])
    even1 = scratch[1, pl.ds(0, pairs, stride=2), :]
    odd1 = swap(scratch[1, pl.ds(1, pairs, stride=2), :])
    low = low_lanes(even0.shape)
    return [even0, jnp.where(low, even1, odd0), jnp.where(low, odd0, odd1)]


def take_half(whole, first):
    one, two, three = whole[:, :LANES], whole[:, LANES : 2 * LANES], whole[:, 2 * LANES :]
    low = low_lanes(one.shape)
    s2, s3 = swap(two), swap(three)
    head = jnp.where(first, one, jnp.where(low, s2, s3))
    tail = jnp.where(low, jnp.where(first, two, s3), 0.0)
    return jnp.concatenate([head, tail], axis=1)


def is_first():
    return lax.rem(lax.axis_index("shard"), 2) == 0


def is_left():
    return lax.rem(lax.axis_index("shard") + lax.axis_index("tensor"), 2) == 0


def first_pack_kernel(blocks, l_basis_ref, r_basis_ref, grads_ref, out_ref, sems):
    left = is_left()
    flat_rows = l_basis_ref.shape[0]
    rows = grads_ref.shape[1]
    here = lax.axis_index("shard") // 2
    basis_copy = lambda ref: pltpu.make_async_copy(ref, out_ref.at[pl.ds(0, flat_rows)], sems.at[0])

    @pl.when(left)
    def _():
        basis_copy(r_basis_ref).start()

    @pl.when(jnp.logical_not(left))
    def _():
        basis_copy(l_basis_ref).start()

    copies = []
    for k in range(blocks):
        source = grads_ref.at[here, :, pl.ds(k * LANES, LANES)]
        target = out_ref.at[pl.ds(flat_rows + k * rows, rows)]
        copies.append(pltpu.make_async_copy(source, target, sems.at[1 + k]))
    for copy in copies:
        copy.start()
    basis_copy(l_basis_ref).wait()
    for copy in copies:
        copy.wait()


def pack_kernel(hops, l_stat_ref, r_stat_ref, grads_ref, small_ref, *refs):
    piece_refs, (corner, sems) = refs[: len(hops)], refs[len(hops) :]
    left = is_left()
    half_rows = l_stat_ref.shape[0] // 2
    here = lax.axis_index("shard") // 2
    start = pl.multiple_of(jnp.where(is_first(), 0, half_rows), 8)
    stat_copy = lambda ref: pltpu.make_async_copy(ref.at[pl.ds(start, half_rows)], corner, sems.at[0])

    @pl.when(left)
    def _():
        stat_copy(r_stat_ref).start()

    @pl.when(jnp.logical_not(left))
    def _():
        stat_copy(l_stat_ref).start()

    copies = [
        pltpu.make_async_copy(grads_ref.at[here ^ hop], piece_ref, sems.at[1 + number])
        for number, (hop, piece_ref) in enumerate(zip(hops, piece_refs))
    ]
    for copy in copies:
        copy.start()
    stat_copy(l_stat_ref).wait()
    third = half_rows // 9
    a, b, c = thirds(corner)
    low = low_lanes((third, LANES))
    middle = slice(third, 2 * third)
    small_ref[pl.ds(0, third)] = jnp.where(low, a[:third], b[:third])
    small_ref[pl.ds(third, third)] = a[middle]
    small_ref[pl.ds(2 * third, third)] = jnp.where(low, swap(b[middle]), swap(c[middle]))
    small_ref[pl.ds(3 * third, 3 * third)] = corner[pl.ds(6 * third, 3 * third)]
    for copy in copies:
        copy.wait()


def corner_rows(flat_rows):
    return flat_rows // 3


def unpack_corner(got_ref):
    third = got_ref.shape[0] // 6
    small = got_ref[pl.ds(0, third), :]
    even = got_ref[pl.ds(third, third), :]
    odd = swap(got_ref[pl.ds(2 * third, third), :])
    a, b, c = thirds(got_ref, 3 * third, 3 * third)
    low = low_lanes(small.shape)
    zero = jnp.zeros_like(small)
    return [
        jnp.concatenate([jnp.where(low, small, zero), even, a], axis=0),
        jnp.concatenate([jnp.where(low, zero, small), jnp.where(low, zero, odd), b], axis=0),
        jnp.concatenate([zero, jnp.where(low, odd, zero), c], axis=0),
    ]


def statistic(first, own, got_ref, scratch):
    corner = unpack_corner(got_ref)
    placed = [jnp.concatenate([jnp.where(first, 0.0, c), jnp.where(first, c, 0.0)], axis=0) for c in corner]
    known = whole_of(scratch, pick(first, own, placed), pick(first, placed, own))
    half = known.shape[0] // 2
    part = half // 3
    row = lax.broadcasted_iota(jnp.int32, known.shape, 0)
    column = lax.broadcasted_iota(jnp.int32, known.shape, 1)
    missing = (jnp.where(first, row, column) < half) & (jnp.where(first, column, row) >= half)
    offset = jnp.where(first, half, 0)
    row, column = row - offset, column - offset
    limit = jnp.where(row < part, part, 2 * part)
    missing |= (row >= 0) & (row < 2 * part) & (column < half) & (column >= limit)
    return jnp.where(missing, known.T, known)


def place_rows(grad_ref, block, rows, value):
    grad_ref[pl.ds(pl.multiple_of(block * rows, 8), rows), :] = value


def polynomial(parts):
    gram = dot_parts(parts, parts, ((1,), (1,)))
    gram_parts = split(gram)
    return CUBIC_COEFF * gram + QUINTIC_COEFF * dot_parts(gram_parts, gram_parts)


def iterate(x, steps):
    for _ in range(steps):
        parts = split(x)
        x = LINEAR_COEFF * x + dot_parts(split(polynomial(parts)), parts)
    return x


def products_kernel(hops, l_stat_ref, r_stat_ref, l_basis_ref, r_basis_ref, got_ref, *refs):
    left = is_left()
    outs = refs[-9:]
    grad_ref, product_ref, basis_ref, right_ref, inner_ref, own_ref, other_ref, copy_ref, scratch = outs
    if hops:
        grads_ref, mine_refs, theirs_refs = refs[0], refs[1 : 1 + len(hops)], refs[1 + len(hops) : 1 + 2 * len(hops)]
        rows = grads_ref.shape[1]
        here = lax.axis_index("shard") // 2
        parity = lax.axis_index("shard") % 2
        start = l_basis_ref.shape[0]
        received = [got_ref[pl.ds(start + k * rows, rows), :] for k in range(grad_ref.shape[1] // LANES)]
        place_rows(grad_ref, 2 * here + parity, rows, grads_ref[here])
        place_rows(grad_ref, 2 * here + 1 - parity, rows, jnp.concatenate(received, axis=1))
        for hop, mine, theirs in zip(hops, mine_refs, theirs_refs):
            place_rows(grad_ref, 2 * (here ^ hop) + parity, rows, mine[...])
            place_rows(grad_ref, 2 * (here ^ hop) + 1 - parity, rows, theirs[...])
    else:
        grad_ref[...] = refs[0][...]
    own = pick(left, thirds(l_basis_ref), thirds(r_basis_ref))
    got = thirds(got_ref, 0, l_basis_ref.shape[0])
    first = is_first()
    basis_ref[...] = whole_of(scratch, pick(first, own, got), pick(first, got, own))
    own_ref[...] = jnp.where(left, l_stat_ref[...], r_stat_ref[...])
    other_ref[...] = jnp.where(left, r_stat_ref[...], l_stat_ref[...])
    copy_ref[...] = l_basis_ref[...]
    right = half_of(scratch, thirds(r_basis_ref))
    right_ref[...] = right
    grad = grad_ref[...]
    parts = split(jnp.where(left, grad, grad.T))
    product_ref[...] = symmetric_dot(parts, parts, ((1,), (1,)))
    inner_ref[...] = dot(grad, right)


def begin_kernel(steps, own_ref, corner_ref, product_ref, basis_ref, new_stat_ref, x_ref, scratch):
    new_stat = 0.5 * statistic(is_first(), thirds(own_ref), corner_ref, scratch) + 0.5 * product_ref[...]
    new_stat_ref[...] = new_stat
    power = dot(new_stat, basis_ref[...])
    x_ref[...] = iterate(power * (1.0 / jnp.sqrt(jnp.sum(power * power) + NORM_EPS)), steps)


def rows_for(hops, outer_ref, right_parts, out_ref, offset):
    rows = out_ref.shape[1]
    here = lax.axis_index("shard") // 2
    starts = [pl.multiple_of((2 * (here ^ hop) + offset) * rows, 8) if hops else 0 for hop in (0, *hops)]
    outer = [outer_ref[pl.ds(start, rows), :] for start in starts]
    partial = dot_parts(split(jnp.concatenate(outer, axis=0)), right_parts, ((1,), (1,)))
    for k in range(len(starts)):
        out_ref[k] = partial[k * rows : (k + 1) * rows]


def update_kernel(
    hops,
    inner_ref,
    basis_ref,
    left_ref,
    right_ref,
    other_left_ref,
    one_ref,
    two_ref,
    start_ref,
    new_one_ref,
    new_two_ref,
    theirs_ref,
    outer_ref,
    x_ref,
    scratch,
):
    left, first = is_left(), is_first()
    own, got = thirds(left_ref), thirds(other_left_ref)
    basis_left = jnp.where(left, basis_ref[...], whole_of(scratch, pick(first, own, got), pick(first, got, own)))
    left_parts = split(basis_left)
    right_parts = split(right_ref[...])
    rotated = flat_of(scratch, dot(basis_left.T, inner_ref[...]))
    x_ref[...] = iterate(start_ref[...], 1)
    ones = thirds(one_ref)
    twos = thirds(two_ref)
    new_one = [BETA_ONE * m + (1.0 - BETA_ONE) * r for m, r in zip(ones, rotated)]
    new_two = [BETA_TWO * v + (1.0 - BETA_TWO) * r * r for v, r in zip(twos, rotated)]
    put_thirds(new_one_ref, new_one)
    put_thirds(new_two_ref, new_two)
    direction = [m / (jnp.sqrt(v) + ADAM_EPS) for m, v in zip(new_one, new_two)]
    outer_ref[...] = dot_parts(left_parts, split(half_of(scratch, direction)))
    rows_for(hops, outer_ref, right_parts, theirs_ref, 1 - lax.axis_index("shard") % 2)


def end_kernel(hops, steps, start_ref, outer_ref, right_ref, x_ref, poly_ref, send_ref, mine_ref, scratch):
    x = iterate(start_ref[...], steps - 1)
    x_ref[...] = x
    rows_for(hops, outer_ref, split(right_ref[...]), mine_ref, lax.axis_index("shard") % 2)
    poly = polynomial(split(x))
    poly_ref[...] = poly
    half = take_half(x, jnp.logical_not(is_first()))
    put_thirds(send_ref, flat_of(scratch, LINEAR_COEFF * half + dot(poly, half)))


def add_kernel(mine_ref, theirs_ref, *out_refs):
    for k, out_ref in enumerate(out_refs):
        out_ref[...] = mine_ref[k] + theirs_ref[k]


def bases_kernel(keep_ref, back_ref, new_left_ref, new_right_ref, sems):
    left = is_left()

    def copies(own_ref, other_ref):
        return [
            pltpu.make_async_copy(keep_ref, own_ref, sems.at[0]),
            pltpu.make_async_copy(back_ref, other_ref, sems.at[1]),
        ]

    @pl.when(left)
    def _():
        for copy in copies(new_left_ref, new_right_ref):
            copy.start()

    @pl.when(jnp.logical_not(left))
    def _():
        for copy in copies(new_right_ref, new_left_ref):
            copy.start()

    for copy in copies(new_left_ref, new_right_ref):
        copy.wait()


def rows_kernel(hops, *refs):
    rows_refs, (update_ref, sems) = refs[:-2], refs[-2:]
    here = lax.axis_index("shard") // 2
    copies = [
        pltpu.make_async_copy(rows_refs[k], update_ref.at[here ^ hop], sems.at[k]) for k, hop in enumerate((0, *hops))
    ]
    for copy in copies:
        copy.start()
    for copy in copies:
        copy.wait()


def rest_kernel(x_ref, poly_ref, grad_ref, new_stat_ref, other_ref, keep_ref, new_left_ref, new_right_ref, scratch):
    left = is_left()
    first = is_first()
    half = take_half(x_ref[...], first)
    put_thirds(keep_ref, flat_of(scratch, LINEAR_COEFF * half + dot(poly_ref[...], half)))
    grad = grad_ref[...]
    turned = grad.T
    a = jnp.where(left, grad, turned)
    b = jnp.where(left, turned, grad)
    new_own = flat_of(scratch, take_half(new_stat_ref[...], first))
    product = flat_of(scratch, dot(b, take_half(a, first)))
    new_other = [0.5 * u + 0.5 * v for u, v in zip(thirds(other_ref), product)]
    put_thirds(new_left_ref, pick(left, new_own, new_other))
    put_thirds(new_right_ref, pick(left, new_other, new_own))


def call(kernel, outs, scratch, products, full, name, copies=0, kind=jax.ShapeDtypeStruct, **specs):
    size = full * full
    scratch = [pltpu.VMEM(s, F32) for s in scratch]
    if copies:
        scratch.append(pltpu.SemaphoreType.DMA((copies,)))
    return pl.pallas_call(
        kernel,
        out_shape=[kind(s, F32) for s in outs],
        scratch_shapes=scratch,
        compiler_params=pltpu.CompilerParams(vmem_limit_bytes=40 * 1024 * 1024),
        cost_estimate=pl.CostEstimate(flops=int(products * 6 * full * size), bytes_accessed=16 * size, transcendentals=0),
        name=name,
        **specs,
    )


def anywhere(count):
    return [pl.BlockSpec(memory_space=pl.ANY)] * count


def after(x, *others):
    return lax.optimization_barrier((x, *others))[0]


def local(grads, moment_one, moment_two, left_stat, right_stat, left_basis, right_basis):
    tiles_here, rows_here, full = grads.shape
    size = lax.axis_size("shard")
    flat_rows = full * (full // 2) // LANES
    flat = (flat_rows, LANES)
    square = (full, full)
    block = (rows_here, full)
    parity = lax.axis_index("shard") % 2
    pairs = [(i, i ^ 1) for i in range(size)]
    sides = [list(range(k, size, 2)) for k in range(2)]
    near = size in (4, 8) and rows_here % 8 == 0
    hops = {4: (1,), 8: (2, 3, 1)}[size] if near else ()
    strips = (tiles_here, *block) if near else (1, full, full)

    def exchange(x):
        return lax.all_to_all(x, "shard", split_axis=0, concat_axis=0, axis_index_groups=sides, tiled=True)

    def hop_by(x, hop):
        return lax.ppermute(x, "shard", [(i, i ^ (2 * hop)) for i in range(size)])

    def partner(x):
        return lax.ppermute(x, "shard", pairs)

    one, two, l_stat, r_stat, l_basis, r_basis = (
        x.reshape(flat) for x in (moment_one, moment_two, left_stat, right_stat, left_basis, right_basis)
    )
    count = corner_rows(flat_rows)
    outgoing_rows = flat_rows + (rows_here * (full // LANES) if near else 0)
    in_hbm = lambda *xs: [pltpu.with_memory_space_constraint(x, pltpu.HBM) for x in xs]
    blocks = full // LANES if near else 0
    (outgoing,) = call(
        functools.partial(first_pack_kernel, blocks),
        [(outgoing_rows, LANES)],
        [],
        0.1,
        full,
        "first_pack",
        copies=1 + blocks,
        kind=pltpu.VMEM,
        in_specs=anywhere(3),
        out_specs=anywhere(1),
    )(*in_hbm(l_basis, r_basis, grads))
    corner, *pieces = call(
        functools.partial(pack_kernel, hops),
        [(count, LANES)] + [block] * len(hops),
        [(flat_rows // 2, LANES)],
        0.1,
        full,
        "pack",
        copies=1 + len(hops),
        kind=pltpu.VMEM,
        in_specs=anywhere(3),
        out_specs=[pl.BlockSpec(memory_space=pltpu.VMEM)] + anywhere(len(hops)),
    )(*in_hbm(l_stat, r_stat, grads))
    got = partner(outgoing)
    if near:
        mine = [hop_by(piece, hop) for hop, piece in zip(hops, pieces)]
        theirs = [partner(x) for x in mine]
        rows = (grads, *mine, *theirs)
    else:
        mine = exchange(grads)
        theirs = partner(mine)
        even, odd = jnp.where(parity == 0, mine, theirs), jnp.where(parity == 0, theirs, mine)
        rows = (jnp.stack([even, odd], axis=1).reshape(square),)
        mine = [mine]
    got_corner = partner(after(corner, theirs[0] if near else mine[0]))
    grad, product, basis, right, inner, own, other, left = call(
        functools.partial(products_kernel, hops),
        [square, square, square, (full, 2 * LANES), (full, 2 * LANES), flat, flat, flat],
        [(3, full, LANES)],
        2,
        full,
        "products",
    )(l_stat, r_stat, l_basis, r_basis, got, *rows)
    tensors = lax.axis_size("tensor")
    place = lambda t, i: i * tensors + t
    cycle = []
    for t in range(0, tensors - tensors % 2, 2):
        for i in range(0, size, 2):
            cycle += [(place(t, i), place(t, i + 1)), (place(t, i + 1), place(t + 1, i + 1))]
            cycle += [(place(t + 1, i + 1), place(t + 1, i)), (place(t + 1, i), place(t, i))]
    cycle += [(place(t, i), place(t, i ^ 1)) for t in range(tensors - tensors % 2, tensors) for i in range(size)]
    other_left = lax.ppermute(after(l_basis, *(theirs[:2] if near else mine)), ("shard", "tensor"), cycle)
    new_stat, x = call(functools.partial(begin_kernel, EARLY_ITERS), [square] * 2, [(3, full, LANES)], 7, full, "begin")(
        own, got_corner, product, basis
    )
    wide = (full, 2 * LANES)
    new_one, new_two, other_rows, outer, x = call(
        functools.partial(update_kernel, hops), [flat, flat, strips, wide, square], [(3, full, LANES)], 5, full, "update"
    )(inner, basis, left, right, other_left, one, two, x)
    if not near:
        partial = other_rows.reshape(tiles_here, 2, rows_here, full)
        other_rows = lax.dynamic_index_in_dim(partial, 1 - parity, 1, keepdims=False)
    got_rows = partner(other_rows)
    x, poly, send, own_rows = call(
        functools.partial(end_kernel, hops, NS_ITERS - EARLY_ITERS - 1),
        [square, square, flat, strips],
        [(3, full, LANES)],
        9,
        full,
        "end",
    )(after(x, other_rows), outer, right)
    back = partner(send)
    keep, new_left, new_right = call(rest_kernel, [flat, flat, flat], [(3, full, LANES)], 1.5, full, "rest")(
        x, poly, grad, new_stat, other
    )
    if near:
        kept, *sums = call(add_kernel, [block] * (1 + len(hops)), [], 0.1, full, "add")(
            after(own_rows, send), after(got_rows, send)
        )
        returned = [hop_by(x, hop) for hop, x in zip(hops, sums)]
        update = call(
            functools.partial(rows_kernel, hops),
            [grads.shape],
            [],
            0.1,
            full,
            "rows",
            copies=1 + len(hops),
            in_specs=anywhere(1 + len(hops)),
            out_specs=anywhere(1),
        )(kept, *returned)[0]
    else:
        own_rows = lax.dynamic_index_in_dim(partial, parity, 1, keepdims=False)
        update = exchange(after(own_rows, send) + after(got_rows, send))
    new_l_basis, new_r_basis = call(
        bases_kernel, [flat, flat], [], 0.1, full, "bases", copies=2, in_specs=anywhere(2), out_specs=anywhere(2)
    )(keep, back)
    halves = (new_one, new_two, new_left, new_right, new_l_basis, new_r_basis)
    return (update, *(x.reshape(1, flat_rows * LANES) for x in halves))


def solution(mesh):
    halves = P(("tensor", "shard"), None)
    rows = P("tensor", "shard", None)
    return jax.shard_map(
        local, mesh=mesh, in_specs=(rows,) + (halves,) * 6, out_specs=(rows,) + (halves,) * 6, check_vma=False
    )
```

```python
import functools

import jax
import jax.numpy as jnp
from jax import lax
from jax.experimental import pallas as pl
from jax.experimental.pallas import tpu as pltpu
from jax.sharding import PartitionSpec as P

NS_ITERS = 5
EARLY_ITERS = 1
BETA_ONE = 0.9
BETA_TWO = 0.95
ADAM_EPS = 1e-08
NORM_EPS = 1e-06
LINEAR_COEFF = 3.4445
CUBIC_COEFF = -4.775
QUINTIC_COEFF = 2.0315
LANES = 128
F32 = jnp.float32


def split(x):
    high = x.astype(jnp.bfloat16)
    return high, (x - high.astype(F32)).astype(jnp.bfloat16)


def dot(a, b, dims=((1,), (0,))):
    return dot_parts(split(a), split(b), dims)


def dot_parts(a, b, dims=((1,), (0,))):
    (ka,), (kb,) = dims
    left = jnp.concatenate([a[0], a[0], a[1]], axis=ka)
    right = jnp.concatenate([b[0], b[1], b[0]], axis=kb)
    return lax.dot_general(left, right, (dims, ((), ())), preferred_element_type=F32)


def symmetric_dot(a, b, dims=((1,), (0,))):
    (ka,), (kb,) = dims
    cut = a[0].shape[0] - LANES
    head = lambda x, axis: lax.slice_in_dim(x, 0, cut, axis=axis)
    tail = lambda x, axis: lax.slice_in_dim(x, cut, cut + LANES, axis=axis)
    left = dot_parts(a, [head(x, 1 - kb) for x in b], dims)
    corner = dot_parts([tail(x, 1 - ka) for x in a], [tail(x, 1 - kb) for x in b], dims)
    right = jnp.concatenate([left[cut:].T, corner], axis=0)
    return jnp.concatenate([left, right], axis=1)


def swap(x):
    return pltpu.roll(x, LANES // 2, 1)


def low_lanes(shape):
    return lax.broadcasted_iota(jnp.int32, shape, 1) < LANES // 2


def pick(flag, x, y):
    return [jnp.where(flag, u, v) for u, v in zip(x, y)]


def thirds(ref, start=0, rows=None):
    rows = ref.shape[0] if rows is None else rows
    return [ref[pl.ds(start + k, rows // 3, stride=3), :] for k in range(3)]


def put_thirds(ref, parts):
    for k in range(3):
        ref[pl.ds(k, parts[k].shape[0], stride=3), :] = parts[k]


def interleave(scratch, index, even, odd):
    scratch[index, pl.ds(0, even.shape[0], stride=2), :] = even
    scratch[index, pl.ds(1, odd.shape[0], stride=2), :] = odd


def whole_of(scratch, first, second):
    a, b, c = first
    d, e, f = second
    low = low_lanes(a.shape)
    sb, sc, sd, se = swap(b), swap(c), swap(d), swap(e)
    interleave(scratch, 0, a, jnp.where(low, sb, sc))
    interleave(scratch, 1, jnp.where(low, b, sd), jnp.where(low, sc, e))
    interleave(scratch, 2, jnp.where(low, sd, se), f)
    return jnp.concatenate([scratch[0], scratch[1], scratch[2]], axis=1)


def half_of(scratch, flat):
    a, b, c = flat
    low = low_lanes(a.shape)
    sb, sc = swap(b), swap(c)
    interleave(scratch, 0, a, jnp.where(low, sb, sc))
    interleave(scratch, 1, jnp.where(low, b, 0.0), jnp.where(low, sc, 0.0))
    return jnp.concatenate([scratch[0], scratch[1]], axis=1)


def flat_of(scratch, half):
    scratch[0] = half[:, :LANES]
    scratch[1] = half[:, LANES:]
    pairs = half.shape[0] // 2
    even0 = scratch[0, pl.ds(0, pairs, stride=2), :]
    odd0 = swap(scratch[0, pl.ds(1, pairs, stride=2), :])
    even1 = scratch[1, pl.ds(0, pairs, stride=2), :]
    odd1 = swap(scratch[1, pl.ds(1, pairs, stride=2), :])
    low = low_lanes(even0.shape)
    return [even0, jnp.where(low, even1, odd0), jnp.where(low, odd0, odd1)]


def take_half(whole, first):
    one, two, three = whole[:, :LANES], whole[:, LANES : 2 * LANES], whole[:, 2 * LANES :]
    low = low_lanes(one.shape)
    s2, s3 = swap(two), swap(three)
    head = jnp.where(first, one, jnp.where(low, s2, s3))
    tail = jnp.where(low, jnp.where(first, two, s3), 0.0)
    return jnp.concatenate([head, tail], axis=1)


def is_first():
    return lax.rem(lax.axis_index("shard"), 2) == 0


def is_left():
    return lax.rem(lax.axis_index("shard") + lax.axis_index("tensor"), 2) == 0


def pack_kernel(hops, l_stat_ref, r_stat_ref, l_basis_ref, r_basis_ref, grads_ref, *refs):
    out_ref, small_ref, *refs = refs
    piece_refs, (corner, sems) = refs[: len(hops)], refs[len(hops) :]
    left = is_left()
    flat_rows = l_basis_ref.shape[0]
    half_rows = flat_rows // 2
    rows = grads_ref.shape[1]
    here = lax.axis_index("shard") // 2

    start = pl.multiple_of(jnp.where(is_first(), 0, half_rows), 8)

    def copies(basis_ref, stat_ref):
        return [
            pltpu.make_async_copy(stat_ref.at[pl.ds(start, half_rows)], corner, sems.at[0]),
            pltpu.make_async_copy(basis_ref, out_ref.at[pl.ds(0, flat_rows)], sems.at[1]),
        ]

    @pl.when(left)
    def _():
        for copy in copies(r_basis_ref, r_stat_ref):
            copy.start()

    @pl.when(jnp.logical_not(left))
    def _():
        for copy in copies(l_basis_ref, l_stat_ref):
            copy.start()

    more = []
    for number, (hop, piece_ref) in enumerate(zip(hops, piece_refs)):
        more.append(pltpu.make_async_copy(grads_ref.at[here ^ hop], piece_ref, sems.at[2 + number]))
    if hops:
        for k in range(grads_ref.shape[2] // LANES):
            source = grads_ref.at[here, :, pl.ds(k * LANES, LANES)]
            target = out_ref.at[pl.ds(flat_rows + k * rows, rows)]
            more.append(pltpu.make_async_copy(source, target, sems.at[2 + len(hops) + k]))
    for copy in more:
        copy.start()
    first, second = copies(l_basis_ref, l_stat_ref)
    first.wait()
    third = half_rows // 9
    a, b, c = thirds(corner)
    low = low_lanes((third, LANES))
    middle = slice(third, 2 * third)
    small_ref[pl.ds(0, third)] = jnp.where(low, a[:third], b[:third])
    small_ref[pl.ds(third, third)] = a[middle]
    small_ref[pl.ds(2 * third, third)] = jnp.where(low, swap(b[middle]), swap(c[middle]))
    small_ref[pl.ds(3 * third, 3 * third)] = corner[pl.ds(6 * third, 3 * third)]
    for copy in [second, *more]:
        copy.wait()


def corner_rows(flat_rows):
    return flat_rows // 3


def unpack_corner(got_ref):
    third = got_ref.shape[0] // 6
    small = got_ref[pl.ds(0, third), :]
    even = got_ref[pl.ds(third, third), :]
    odd = swap(got_ref[pl.ds(2 * third, third), :])
    a, b, c = thirds(got_ref, 3 * third, 3 * third)
    low = low_lanes(small.shape)
    zero = jnp.zeros_like(small)
    return [
        jnp.concatenate([jnp.where(low, small, zero), even, a], axis=0),
        jnp.concatenate([jnp.where(low, zero, small), jnp.where(low, zero, odd), b], axis=0),
        jnp.concatenate([zero, jnp.where(low, odd, zero), c], axis=0),
    ]


def statistic(first, own, got_ref, scratch):
    corner = unpack_corner(got_ref)
    placed = [jnp.concatenate([jnp.where(first, 0.0, c), jnp.where(first, c, 0.0)], axis=0) for c in corner]
    known = whole_of(scratch, pick(first, own, placed), pick(first, placed, own))
    half = known.shape[0] // 2
    part = half // 3
    row = lax.broadcasted_iota(jnp.int32, known.shape, 0)
    column = lax.broadcasted_iota(jnp.int32, known.shape, 1)
    missing = (jnp.where(first, row, column) < half) & (jnp.where(first, column, row) >= half)
    offset = jnp.where(first, half, 0)
    row, column = row - offset, column - offset
    limit = jnp.where(row < part, part, 2 * part)
    missing |= (row >= 0) & (row < 2 * part) & (column < half) & (column >= limit)
    return jnp.where(missing, known.T, known)


def place_rows(grad_ref, block, rows, value):
    grad_ref[pl.ds(pl.multiple_of(block * rows, 8), rows), :] = value


def polynomial(parts):
    gram = dot_parts(parts, parts, ((1,), (1,)))
    gram_parts = split(gram)
    return CUBIC_COEFF * gram + QUINTIC_COEFF * dot_parts(gram_parts, gram_parts)


def blocked_step(x):
    parts = split(x)
    gram = dot_parts(parts, parts, ((1,), (1,)))
    gram_parts = split(gram)
    rows = x.shape[0] // 2
    blocks = []
    for k in range(2):
        block = slice(k * rows, (k + 1) * rows)
        poly = CUBIC_COEFF * gram[block] + QUINTIC_COEFF * dot_parts([part[block] for part in gram_parts], gram_parts)
        blocks.append(LINEAR_COEFF * x[block] + dot_parts(split(poly), parts))
    return jnp.concatenate(blocks, axis=0)


def iterate(x, steps):
    for _ in range(steps):
        parts = split(x)
        x = LINEAR_COEFF * x + dot_parts(split(polynomial(parts)), parts)
    return x


def products_kernel(hops, l_stat_ref, r_stat_ref, l_basis_ref, r_basis_ref, got_ref, *refs):
    left = is_left()
    outs = refs[-9:]
    grad_ref, product_ref, basis_ref, right_ref, inner_ref, own_ref, other_ref, copy_ref, scratch = outs
    if hops:
        grads_ref, mine_refs, theirs_refs = refs[0], refs[1 : 1 + len(hops)], refs[1 + len(hops) : 1 + 2 * len(hops)]
        rows = grads_ref.shape[1]
        here = lax.axis_index("shard") // 2
        parity = lax.axis_index("shard") % 2
        start = l_basis_ref.shape[0]
        received = [got_ref[pl.ds(start + k * rows, rows), :] for k in range(grad_ref.shape[1] // LANES)]
        place_rows(grad_ref, 2 * here + parity, rows, grads_ref[here])
        place_rows(grad_ref, 2 * here + 1 - parity, rows, jnp.concatenate(received, axis=1))
        for hop, mine, theirs in zip(hops, mine_refs, theirs_refs):
            place_rows(grad_ref, 2 * (here ^ hop) + parity, rows, mine[...])
            place_rows(grad_ref, 2 * (here ^ hop) + 1 - parity, rows, theirs[...])
    else:
        grad_ref[...] = refs[0][...]
    own = pick(left, thirds(l_basis_ref), thirds(r_basis_ref))
    got = thirds(got_ref, 0, l_basis_ref.shape[0])
    first = is_first()
    basis_ref[...] = whole_of(scratch, pick(first, own, got), pick(first, got, own))
    own_ref[...] = jnp.where(left, l_stat_ref[...], r_stat_ref[...])
    other_ref[...] = jnp.where(left, r_stat_ref[...], l_stat_ref[...])
    copy_ref[...] = l_basis_ref[...]
    right = half_of(scratch, thirds(r_basis_ref))
    right_ref[...] = right
    grad = grad_ref[...]
    parts = split(jnp.where(left, grad, grad.T))
    product_ref[...] = symmetric_dot(parts, parts, ((1,), (1,)))
    inner_ref[...] = dot(grad, right)


def begin_kernel(steps, own_ref, corner_ref, product_ref, basis_ref, new_stat_ref, x_ref, scratch):
    new_stat = 0.5 * statistic(is_first(), thirds(own_ref), corner_ref, scratch) + 0.5 * product_ref[...]
    new_stat_ref[...] = new_stat
    power = dot(new_stat, basis_ref[...])
    x_ref[...] = iterate(power * (1.0 / jnp.sqrt(jnp.sum(power * power) + NORM_EPS)), steps)


def rows_for(hops, outer_ref, right_parts, out_ref, offset):
    rows = out_ref.shape[1]
    here = lax.axis_index("shard") // 2
    starts = [pl.multiple_of((2 * (here ^ hop) + offset) * rows, 8) if hops else 0 for hop in (0, *hops)]
    outer = [outer_ref[pl.ds(start, rows), :] for start in starts]
    partial = dot_parts(split(jnp.concatenate(outer, axis=0)), right_parts, ((1,), (1,)))
    for k in range(len(starts)):
        out_ref[k] = partial[k * rows : (k + 1) * rows]


def update_kernel(
    hops,
    inner_ref,
    basis_ref,
    left_ref,
    right_ref,
    other_left_ref,
    one_ref,
    two_ref,
    start_ref,
    new_one_ref,
    new_two_ref,
    theirs_ref,
    outer_ref,
    x_ref,
    scratch,
):
    left, first = is_left(), is_first()
    x = start_ref[...]
    parts = split(x)
    gram = dot_parts(parts, parts, ((1,), (1,)))
    own, got = thirds(left_ref), thirds(other_left_ref)
    basis_left = jnp.where(left, basis_ref[...], whole_of(scratch, pick(first, own, got), pick(first, got, own)))
    rotated = dot(basis_left.T, inner_ref[...])
    gram_parts = split(gram)
    square = dot_parts(gram_parts, gram_parts)
    rotated = flat_of(scratch, rotated)
    ones = thirds(one_ref)
    twos = thirds(two_ref)
    new_one = [BETA_ONE * m + (1.0 - BETA_ONE) * r for m, r in zip(ones, rotated)]
    new_two = [BETA_TWO * v + (1.0 - BETA_TWO) * r * r for v, r in zip(twos, rotated)]
    put_thirds(new_one_ref, new_one)
    put_thirds(new_two_ref, new_two)
    direction = [m / (jnp.sqrt(v) + ADAM_EPS) for m, v in zip(new_one, new_two)]
    outer_ref[...] = dot_parts(split(basis_left), split(half_of(scratch, direction)))
    poly_parts = split(CUBIC_COEFF * gram + QUINTIC_COEFF * square)
    moved = dot_parts(poly_parts, parts)
    rows_for(hops, outer_ref, split(right_ref[...]), theirs_ref, 1 - lax.axis_index("shard") % 2)
    x_ref[...] = LINEAR_COEFF * x + moved


def end_kernel(hops, steps, start_ref, outer_ref, right_ref, x_ref, poly_ref, send_ref, mine_ref, scratch):
    x = start_ref[...]
    for _ in range(steps - 1):
        x = blocked_step(x)
    x_ref[...] = x
    rows_for(hops, outer_ref, split(right_ref[...]), mine_ref, lax.axis_index("shard") % 2)
    poly = polynomial(split(x))
    poly_ref[...] = poly
    half = take_half(x, jnp.logical_not(is_first()))
    put_thirds(send_ref, flat_of(scratch, LINEAR_COEFF * half + dot(poly, half)))


def add_kernel(mine_ref, theirs_ref, *out_refs):
    for k, out_ref in enumerate(out_refs):
        out_ref[...] = mine_ref[k] + theirs_ref[k]


def bases_kernel(keep_ref, back_ref, new_left_ref, new_right_ref, sems):
    left = is_left()

    def copies(own_ref, other_ref):
        return [
            pltpu.make_async_copy(keep_ref, own_ref, sems.at[0]),
            pltpu.make_async_copy(back_ref, other_ref, sems.at[1]),
        ]

    @pl.when(left)
    def _():
        for copy in copies(new_left_ref, new_right_ref):
            copy.start()

    @pl.when(jnp.logical_not(left))
    def _():
        for copy in copies(new_right_ref, new_left_ref):
            copy.start()

    for copy in copies(new_left_ref, new_right_ref):
        copy.wait()


def rows_kernel(hops, *refs):
    rows_refs, (update_ref, sems) = refs[:-2], refs[-2:]
    here = lax.axis_index("shard") // 2
    copies = [
        pltpu.make_async_copy(rows_refs[k], update_ref.at[here ^ hop], sems.at[k]) for k, hop in enumerate((0, *hops))
    ]
    for copy in copies:
        copy.start()
    for copy in copies:
        copy.wait()


def rest_kernel(x_ref, poly_ref, grad_ref, new_stat_ref, other_ref, keep_ref, new_left_ref, new_right_ref, scratch):
    left = is_left()
    first = is_first()
    half = take_half(x_ref[...], first)
    put_thirds(keep_ref, flat_of(scratch, LINEAR_COEFF * half + dot(poly_ref[...], half)))
    grad = grad_ref[...]
    turned = grad.T
    a = jnp.where(left, grad, turned)
    b = jnp.where(left, turned, grad)
    new_own = flat_of(scratch, take_half(new_stat_ref[...], first))
    product = flat_of(scratch, dot(b, take_half(a, first)))
    new_other = [0.5 * u + 0.5 * v for u, v in zip(thirds(other_ref), product)]
    put_thirds(new_left_ref, pick(left, new_own, new_other))
    put_thirds(new_right_ref, pick(left, new_other, new_own))


def call(kernel, outs, scratch, products, full, name, copies=0, kind=jax.ShapeDtypeStruct, **specs):
    size = full * full
    scratch = [pltpu.VMEM(s, F32) for s in scratch]
    if copies:
        scratch.append(pltpu.SemaphoreType.DMA((copies,)))
    return pl.pallas_call(
        kernel,
        out_shape=[kind(s, F32) for s in outs],
        scratch_shapes=scratch,
        compiler_params=pltpu.CompilerParams(vmem_limit_bytes=40 * 1024 * 1024),
        cost_estimate=pl.CostEstimate(flops=int(products * 6 * full * size), bytes_accessed=16 * size, transcendentals=0),
        name=name,
        **specs,
    )


def anywhere(count):
    return [pl.BlockSpec(memory_space=pl.ANY)] * count


def after(x, *others):
    return lax.optimization_barrier((x, *others))[0]


def local(grads, moment_one, moment_two, left_stat, right_stat, left_basis, right_basis):
    tiles_here, rows_here, full = grads.shape
    size = lax.axis_size("shard")
    flat_rows = full * (full // 2) // LANES
    flat = (flat_rows, LANES)
    square = (full, full)
    block = (rows_here, full)
    parity = lax.axis_index("shard") % 2
    pairs = [(i, i ^ 1) for i in range(size)]
    sides = [list(range(k, size, 2)) for k in range(2)]
    near = size in (4, 8) and rows_here % 8 == 0
    hops = {4: (1,), 8: (2, 3, 1)}[size] if near else ()
    strips = (tiles_here, *block) if near else (1, full, full)

    def exchange(x):
        return lax.all_to_all(x, "shard", split_axis=0, concat_axis=0, axis_index_groups=sides, tiled=True)

    def hop_by(x, hop):
        return lax.ppermute(x, "shard", [(i, i ^ (2 * hop)) for i in range(size)])

    def partner(x):
        return lax.ppermute(x, "shard", pairs)

    one, two, l_stat, r_stat, l_basis, r_basis = (
        x.reshape(flat) for x in (moment_one, moment_two, left_stat, right_stat, left_basis, right_basis)
    )
    count = corner_rows(flat_rows)
    outgoing_rows = flat_rows + (rows_here * (full // LANES) if near else 0)
    outgoing, corner, *pieces = call(
        functools.partial(pack_kernel, hops),
        [(outgoing_rows, LANES), (count, LANES)] + [block] * len(hops),
        [(flat_rows // 2, LANES)],
        0.1,
        full,
        "pack",
        copies=2 + len(hops) + full // LANES,
        kind=pltpu.VMEM,
        in_specs=anywhere(5),
        out_specs=anywhere(1) + [pl.BlockSpec(memory_space=pltpu.VMEM)] + anywhere(len(hops)),
    )(*(pltpu.with_memory_space_constraint(x, pltpu.HBM) for x in (l_stat, r_stat, l_basis, r_basis, grads)))
    got = partner(outgoing)
    if near:
        mine = [hop_by(piece, hop) for hop, piece in zip(hops, pieces)]
        theirs = [partner(x) for x in mine]
        rows = (grads, *mine, *theirs)
    else:
        mine = exchange(grads)
        theirs = partner(mine)
        even, odd = jnp.where(parity == 0, mine, theirs), jnp.where(parity == 0, theirs, mine)
        rows = (jnp.stack([even, odd], axis=1).reshape(square),)
        mine = [mine]
    got_corner = partner(after(corner, theirs[0] if near else mine[0]))
    grad, product, basis, right, inner, own, other, left = call(
        functools.partial(products_kernel, hops),
        [square, square, square, (full, 2 * LANES), (full, 2 * LANES), flat, flat, flat],
        [(3, full, LANES)],
        2,
        full,
        "products",
    )(l_stat, r_stat, l_basis, r_basis, got, *rows)
    tensors = lax.axis_size("tensor")
    place = lambda t, i: i * tensors + t
    cycle = []
    for t in range(0, tensors - tensors % 2, 2):
        for i in range(0, size, 2):
            cycle += [(place(t, i), place(t, i + 1)), (place(t, i + 1), place(t + 1, i + 1))]
            cycle += [(place(t + 1, i + 1), place(t + 1, i)), (place(t + 1, i), place(t, i))]
    cycle += [(place(t, i), place(t, i ^ 1)) for t in range(tensors - tensors % 2, tensors) for i in range(size)]
    other_left = lax.ppermute(after(l_basis, *(theirs[:2] if near else mine)), ("shard", "tensor"), cycle)
    new_stat, x = call(functools.partial(begin_kernel, EARLY_ITERS), [square] * 2, [(3, full, LANES)], 7, full, "begin")(
        own, got_corner, product, basis
    )
    wide = (full, 2 * LANES)
    new_one, new_two, other_rows, outer, x = call(
        functools.partial(update_kernel, hops), [flat, flat, strips, wide, square], [(3, full, LANES)], 5, full, "update"
    )(inner, basis, left, right, other_left, one, two, x)
    if not near:
        partial = other_rows.reshape(tiles_here, 2, rows_here, full)
        other_rows = lax.dynamic_index_in_dim(partial, 1 - parity, 1, keepdims=False)
    got_rows = partner(other_rows)
    x, poly, send, own_rows = call(
        functools.partial(end_kernel, hops, NS_ITERS - EARLY_ITERS - 1),
        [square, square, flat, strips],
        [(3, full, LANES)],
        9,
        full,
        "end",
    )(after(x, other_rows), outer, right)
    back = partner(send)
    keep, new_left, new_right = call(rest_kernel, [flat, flat, flat], [(3, full, LANES)], 1.5, full, "rest")(
        x, poly, grad, new_stat, other
    )
    if near:
        kept, *sums = call(add_kernel, [block] * (1 + len(hops)), [], 0.1, full, "add")(
            after(own_rows, send), after(got_rows, send)
        )
        returned = [hop_by(x, hop) for hop, x in zip(hops, sums)]
        update = call(
            functools.partial(rows_kernel, hops),
            [grads.shape],
            [],
            0.1,
            full,
            "rows",
            copies=1 + len(hops),
            in_specs=anywhere(1 + len(hops)),
            out_specs=anywhere(1),
        )(kept, *returned)[0]
    else:
        own_rows = lax.dynamic_index_in_dim(partial, parity, 1, keepdims=False)
        update = exchange(after(own_rows, send) + after(got_rows, send))
    new_l_basis, new_r_basis = call(
        bases_kernel, [flat, flat], [], 0.1, full, "bases", copies=2, in_specs=anywhere(2), out_specs=anywhere(2)
    )(keep, back)
    halves = (new_one, new_two, new_left, new_right, new_l_basis, new_r_basis)
    return (update, *(x.reshape(1, flat_rows * LANES) for x in halves))


def solution(mesh):
    halves = P(("tensor", "shard"), None)
    rows = P("tensor", "shard", None)
    return jax.shard_map(
        local, mesh=mesh, in_specs=(rows,) + (halves,) * 6, out_specs=(rows,) + (halves,) * 6, check_vma=False
    )
```

```python
import functools

import jax
import jax.numpy as jnp
from jax import lax
from jax.experimental import pallas as pl
from jax.experimental.pallas import tpu as pltpu
from jax.sharding import PartitionSpec as P

NS_ITERS = 5
EARLY_ITERS = 1
BETA_ONE = 0.9
BETA_TWO = 0.95
ADAM_EPS = 1e-08
NORM_EPS = 1e-06
LINEAR_COEFF = 3.4445
CUBIC_COEFF = -4.775
QUINTIC_COEFF = 2.0315
LANES = 128
F32 = jnp.float32


def split(x):
    high = x.astype(jnp.bfloat16)
    return high, (x - high.astype(F32)).astype(jnp.bfloat16)


def dot(a, b, dims=((1,), (0,))):
    return dot_parts(split(a), split(b), dims)


def dot_parts(a, b, dims=((1,), (0,))):
    (ka,), (kb,) = dims
    left = jnp.concatenate([a[0], a[0], a[1]], axis=ka)
    right = jnp.concatenate([b[0], b[1], b[0]], axis=kb)
    return lax.dot_general(left, right, (dims, ((), ())), preferred_element_type=F32)


def symmetric_dot(a, b, dims=((1,), (0,))):
    (ka,), (kb,) = dims
    cut = a[0].shape[0] - LANES
    head = lambda x, axis: lax.slice_in_dim(x, 0, cut, axis=axis)
    tail = lambda x, axis: lax.slice_in_dim(x, cut, cut + LANES, axis=axis)
    left = dot_parts(a, [head(x, 1 - kb) for x in b], dims)
    corner = dot_parts([tail(x, 1 - ka) for x in a], [tail(x, 1 - kb) for x in b], dims)
    right = jnp.concatenate([left[cut:].T, corner], axis=0)
    return jnp.concatenate([left, right], axis=1)


def swap(x):
    return pltpu.roll(x, LANES // 2, 1)


def low_lanes(shape):
    return lax.broadcasted_iota(jnp.int32, shape, 1) < LANES // 2


def pick(flag, x, y):
    return [jnp.where(flag, u, v) for u, v in zip(x, y)]


def thirds(ref, start=0, rows=None):
    rows = ref.shape[0] if rows is None else rows
    return [ref[pl.ds(start + k, rows // 3, stride=3), :] for k in range(3)]


def put_thirds(ref, parts):
    for k in range(3):
        ref[pl.ds(k, parts[k].shape[0], stride=3), :] = parts[k]


def interleave(scratch, index, even, odd):
    scratch[index, pl.ds(0, even.shape[0], stride=2), :] = even
    scratch[index, pl.ds(1, odd.shape[0], stride=2), :] = odd


def whole_of(scratch, first, second):
    a, b, c = first
    d, e, f = second
    low = low_lanes(a.shape)
    sb, sc, sd, se = swap(b), swap(c), swap(d), swap(e)
    interleave(scratch, 0, a, jnp.where(low, sb, sc))
    interleave(scratch, 1, jnp.where(low, b, sd), jnp.where(low, sc, e))
    interleave(scratch, 2, jnp.where(low, sd, se), f)
    return jnp.concatenate([scratch[0], scratch[1], scratch[2]], axis=1)


def half_of(scratch, flat):
    a, b, c = flat
    low = low_lanes(a.shape)
    sb, sc = swap(b), swap(c)
    interleave(scratch, 0, a, jnp.where(low, sb, sc))
    interleave(scratch, 1, jnp.where(low, b, 0.0), jnp.where(low, sc, 0.0))
    return jnp.concatenate([scratch[0], scratch[1]], axis=1)


def flat_of(scratch, half):
    scratch[0] = half[:, :LANES]
    scratch[1] = half[:, LANES:]
    pairs = half.shape[0] // 2
    even0 = scratch[0, pl.ds(0, pairs, stride=2), :]
    odd0 = swap(scratch[0, pl.ds(1, pairs, stride=2), :])
    even1 = scratch[1, pl.ds(0, pairs, stride=2), :]
    odd1 = swap(scratch[1, pl.ds(1, pairs, stride=2), :])
    low = low_lanes(even0.shape)
    return [even0, jnp.where(low, even1, odd0), jnp.where(low, odd0, odd1)]


def take_half(whole, first):
    one, two, three = whole[:, :LANES], whole[:, LANES : 2 * LANES], whole[:, 2 * LANES :]
    low = low_lanes(one.shape)
    s2, s3 = swap(two), swap(three)
    head = jnp.where(first, one, jnp.where(low, s2, s3))
    tail = jnp.where(low, jnp.where(first, two, s3), 0.0)
    return jnp.concatenate([head, tail], axis=1)


def is_first():
    return lax.rem(lax.axis_index("shard"), 2) == 0


def is_left():
    return lax.rem(lax.axis_index("shard") + lax.axis_index("tensor"), 2) == 0


def pack_kernel(hops, l_stat_ref, r_stat_ref, l_basis_ref, r_basis_ref, grads_ref, out_ref, *refs):
    piece_refs, (corner, sems) = refs[: len(hops)], refs[len(hops) :]
    left = is_left()
    flat_rows = l_basis_ref.shape[0]
    half_rows = flat_rows // 2
    here = lax.axis_index("shard") // 2
    start = pl.multiple_of(jnp.where(is_first(), 0, half_rows), 8)

    def copies(basis_ref, stat_ref):
        return [
            pltpu.make_async_copy(stat_ref.at[pl.ds(start, half_rows)], corner, sems.at[0]),
            pltpu.make_async_copy(basis_ref, out_ref.at[pl.ds(0, flat_rows)], sems.at[1]),
        ]

    @pl.when(left)
    def _():
        for copy in copies(r_basis_ref, r_stat_ref):
            copy.start()

    @pl.when(jnp.logical_not(left))
    def _():
        for copy in copies(l_basis_ref, l_stat_ref):
            copy.start()

    more = [
        pltpu.make_async_copy(grads_ref.at[here ^ hop], piece_ref, sems.at[2 + number])
        for number, (hop, piece_ref) in enumerate(zip(hops, piece_refs))
    ]
    for copy in more:
        copy.start()
    first, second = copies(l_basis_ref, l_stat_ref)
    first.wait()
    third = half_rows // 9
    a, b, c = thirds(corner)
    low = low_lanes((third, LANES))
    middle = slice(third, 2 * third)
    out_ref[pl.ds(flat_rows, third)] = jnp.where(low, a[:third], b[:third])
    out_ref[pl.ds(flat_rows + third, third)] = a[middle]
    out_ref[pl.ds(flat_rows + 2 * third, third)] = jnp.where(low, swap(b[middle]), swap(c[middle]))
    out_ref[pl.ds(flat_rows + 3 * third, 3 * third)] = corner[pl.ds(6 * third, 3 * third)]
    for copy in [second, *more]:
        copy.wait()


def slices_kernel(hops, grads_ref, *piece_refs):
    here = lax.axis_index("shard") // 2
    for hop, piece_ref in zip(hops, piece_refs):
        piece_ref[...] = grads_ref[here ^ hop]


def corner_rows(flat_rows):
    return flat_rows // 3


def unpack_corner(got_ref, start, count):
    third = count // 6
    small = got_ref[pl.ds(start, third), :]
    even = got_ref[pl.ds(start + third, third), :]
    odd = swap(got_ref[pl.ds(start + 2 * third, third), :])
    a, b, c = thirds(got_ref, start + 3 * third, 3 * third)
    low = low_lanes(small.shape)
    zero = jnp.zeros_like(small)
    return [
        jnp.concatenate([jnp.where(low, small, zero), even, a], axis=0),
        jnp.concatenate([jnp.where(low, zero, small), jnp.where(low, zero, odd), b], axis=0),
        jnp.concatenate([zero, jnp.where(low, odd, zero), c], axis=0),
    ]


def statistic(first, own, got_ref, scratch):
    flat_rows = got_ref.shape[0] * 3 // 4
    corner = unpack_corner(got_ref, flat_rows, corner_rows(flat_rows))
    placed = [jnp.concatenate([jnp.where(first, 0.0, c), jnp.where(first, c, 0.0)], axis=0) for c in corner]
    known = whole_of(scratch, pick(first, own, placed), pick(first, placed, own))
    half = known.shape[0] // 2
    part = half // 3
    row = lax.broadcasted_iota(jnp.int32, known.shape, 0)
    column = lax.broadcasted_iota(jnp.int32, known.shape, 1)
    missing = (jnp.where(first, row, column) < half) & (jnp.where(first, column, row) >= half)
    offset = jnp.where(first, half, 0)
    row, column = row - offset, column - offset
    limit = jnp.where(row < part, part, 2 * part)
    missing |= (row >= 0) & (row < 2 * part) & (column < half) & (column >= limit)
    return jnp.where(missing, known.T, known)


def place_rows(grad_ref, block, rows, value):
    grad_ref[pl.ds(pl.multiple_of(block * rows, 8), rows), :] = value


def polynomial(parts):
    gram = dot_parts(parts, parts, ((1,), (1,)))
    gram_parts = split(gram)
    return CUBIC_COEFF * gram + QUINTIC_COEFF * dot_parts(gram_parts, gram_parts)


def iterate(x, steps):
    for _ in range(steps):
        parts = split(x)
        x = LINEAR_COEFF * x + dot_parts(split(polynomial(parts)), parts)
    return x


def products_kernel(hops, r_basis_ref, *refs):
    left = is_left()
    grad_ref, product_ref, right_ref, inner_ref, scratch = refs[-5:]
    if hops:
        grads_ref, swapped_ref = refs[:2]
        mine_refs, theirs_refs = refs[2 : 2 + len(hops)], refs[2 + len(hops) : 2 + 2 * len(hops)]
        rows = grads_ref.shape[1]
        here = lax.axis_index("shard") // 2
        parity = lax.axis_index("shard") % 2
        place_rows(grad_ref, 2 * here + parity, rows, grads_ref[here])
        place_rows(grad_ref, 2 * here + 1 - parity, rows, swapped_ref[here])
        for hop, mine, theirs in zip(hops, mine_refs, theirs_refs):
            place_rows(grad_ref, 2 * (here ^ hop) + parity, rows, mine[...])
            place_rows(grad_ref, 2 * (here ^ hop) + 1 - parity, rows, theirs[...])
    else:
        grad_ref[...] = refs[0][...]
    right = half_of(scratch, thirds(r_basis_ref))
    right_ref[...] = right
    grad = grad_ref[...]
    parts = split(jnp.where(left, grad, grad.T))
    product_ref[...] = symmetric_dot(parts, parts, ((1,), (1,)))
    inner_ref[...] = dot(grad, right)


def prepare_kernel(l_stat_ref, r_stat_ref, l_basis_ref, r_basis_ref, got_ref, stat_ref, basis_ref, other_ref, copy_ref, scratch):
    left, first = is_left(), is_first()
    own = pick(left, thirds(l_basis_ref), thirds(r_basis_ref))
    got = thirds(got_ref, 0, l_basis_ref.shape[0])
    basis_ref[...] = whole_of(scratch, pick(first, own, got), pick(first, got, own))
    other_ref[...] = jnp.where(left, r_stat_ref[...], l_stat_ref[...])
    copy_ref[...] = l_basis_ref[...]
    own = pick(left, thirds(l_stat_ref), thirds(r_stat_ref))
    stat_ref[...] = 0.5 * statistic(first, own, got_ref, scratch)


def begin_kernel(steps, stat_ref, product_ref, basis_ref, new_stat_ref, x_ref):
    new_stat = stat_ref[...] + 0.5 * product_ref[...]
    new_stat_ref[...] = new_stat
    power = dot(new_stat, basis_ref[...])
    x_ref[...] = iterate(power * (1.0 / jnp.sqrt(jnp.sum(power * power) + NORM_EPS)), steps)


def rows_for(hops, outer_ref, right_parts, out_ref, offset):
    rows = out_ref.shape[1]
    here = lax.axis_index("shard") // 2
    starts = [pl.multiple_of((2 * (here ^ hop) + offset) * rows, 8) if hops else 0 for hop in (0, *hops)]
    outer = [outer_ref[pl.ds(start, rows), :] for start in starts]
    partial = dot_parts(split(jnp.concatenate(outer, axis=0)), right_parts, ((1,), (1,)))
    for k in range(len(starts)):
        out_ref[k] = partial[k * rows : (k + 1) * rows]


def update_kernel(
    hops,
    inner_ref,
    basis_ref,
    left_ref,
    right_ref,
    other_left_ref,
    one_ref,
    two_ref,
    start_ref,
    new_one_ref,
    new_two_ref,
    theirs_ref,
    outer_ref,
    x_ref,
    scratch,
):
    left, first = is_left(), is_first()
    x = start_ref[...]
    parts = split(x)
    gram = dot_parts(parts, parts, ((1,), (1,)))
    own, got = thirds(left_ref), thirds(other_left_ref)
    basis_left = jnp.where(left, basis_ref[...], whole_of(scratch, pick(first, own, got), pick(first, got, own)))
    rotated = dot(basis_left.T, inner_ref[...])
    gram_parts = split(gram)
    square = dot_parts(gram_parts, gram_parts)
    rotated = flat_of(scratch, rotated)
    ones = thirds(one_ref)
    twos = thirds(two_ref)
    new_one = [BETA_ONE * m + (1.0 - BETA_ONE) * r for m, r in zip(ones, rotated)]
    new_two = [BETA_TWO * v + (1.0 - BETA_TWO) * r * r for v, r in zip(twos, rotated)]
    put_thirds(new_one_ref, new_one)
    put_thirds(new_two_ref, new_two)
    direction = [m / (jnp.sqrt(v) + ADAM_EPS) for m, v in zip(new_one, new_two)]
    outer_ref[...] = dot_parts(split(basis_left), split(half_of(scratch, direction)))
    poly_parts = split(CUBIC_COEFF * gram + QUINTIC_COEFF * square)
    moved = dot_parts(poly_parts, parts)
    rows_for(hops, outer_ref, split(right_ref[...]), theirs_ref, 1 - lax.axis_index("shard") % 2)
    x_ref[...] = LINEAR_COEFF * x + moved


def end_kernel(hops, steps, start_ref, outer_ref, right_ref, x_ref, poly_ref, send_ref, mine_ref, scratch):
    x = iterate(start_ref[...], steps - 1)
    x_ref[...] = x
    rows_for(hops, outer_ref, split(right_ref[...]), mine_ref, lax.axis_index("shard") % 2)
    poly = polynomial(split(x))
    poly_ref[...] = poly
    half = take_half(x, jnp.logical_not(is_first()))
    put_thirds(send_ref, flat_of(scratch, LINEAR_COEFF * half + dot(poly, half)))


def add_kernel(mine_ref, theirs_ref, *out_refs):
    for k, out_ref in enumerate(out_refs):
        out_ref[...] = mine_ref[k] + theirs_ref[k]


def bases_kernel(keep_ref, back_ref, new_left_ref, new_right_ref, sems):
    left = is_left()

    def copies(own_ref, other_ref):
        return [
            pltpu.make_async_copy(keep_ref, own_ref, sems.at[0]),
            pltpu.make_async_copy(back_ref, other_ref, sems.at[1]),
        ]

    @pl.when(left)
    def _():
        for copy in copies(new_left_ref, new_right_ref):
            copy.start()

    @pl.when(jnp.logical_not(left))
    def _():
        for copy in copies(new_right_ref, new_left_ref):
            copy.start()

    for copy in copies(new_left_ref, new_right_ref):
        copy.wait()


def rows_kernel(hops, *refs):
    rows_refs, (update_ref, sems) = refs[:-2], refs[-2:]
    here = lax.axis_index("shard") // 2
    copies = [
        pltpu.make_async_copy(rows_refs[k], update_ref.at[here ^ hop], sems.at[k]) for k, hop in enumerate((0, *hops))
    ]
    for copy in copies:
        copy.start()
    for copy in copies:
        copy.wait()


def rest_kernel(x_ref, poly_ref, grad_ref, new_stat_ref, other_ref, keep_ref, new_left_ref, new_right_ref, scratch):
    left = is_left()
    first = is_first()
    half = take_half(x_ref[...], first)
    put_thirds(keep_ref, flat_of(scratch, LINEAR_COEFF * half + dot(poly_ref[...], half)))
    grad = grad_ref[...]
    turned = grad.T
    a = jnp.where(left, grad, turned)
    b = jnp.where(left, turned, grad)
    new_own = flat_of(scratch, take_half(new_stat_ref[...], first))
    product = flat_of(scratch, dot(b, take_half(a, first)))
    new_other = [0.5 * u + 0.5 * v for u, v in zip(thirds(other_ref), product)]
    put_thirds(new_left_ref, pick(left, new_own, new_other))
    put_thirds(new_right_ref, pick(left, new_other, new_own))


def call(kernel, outs, scratch, products, full, name, copies=0, kind=jax.ShapeDtypeStruct, **specs):
    size = full * full
    scratch = [pltpu.VMEM(s, F32) for s in scratch]
    if copies:
        scratch.append(pltpu.SemaphoreType.DMA((copies,)))
    return pl.pallas_call(
        kernel,
        out_shape=[kind(s, F32) for s in outs],
        scratch_shapes=scratch,
        compiler_params=pltpu.CompilerParams(vmem_limit_bytes=40 * 1024 * 1024),
        cost_estimate=pl.CostEstimate(flops=int(products * 6 * full * size), bytes_accessed=16 * size, transcendentals=0),
        name=name,
        **specs,
    )


def anywhere(count):
    return [pl.BlockSpec(memory_space=pl.ANY)] * count


def after(x, *others):
    return lax.optimization_barrier((x, *others))[0]


def local(grads, moment_one, moment_two, left_stat, right_stat, left_basis, right_basis):
    tiles_here, rows_here, full = grads.shape
    size = lax.axis_size("shard")
    flat_rows = full * (full // 2) // LANES
    flat = (flat_rows, LANES)
    square = (full, full)
    block = (rows_here, full)
    parity = lax.axis_index("shard") % 2
    pairs = [(i, i ^ 1) for i in range(size)]
    sides = [list(range(k, size, 2)) for k in range(2)]
    near = size in (4, 8) and rows_here % 8 == 0
    hops = {4: (1,), 8: (2, 3, 1)}[size] if near else ()
    strips = (tiles_here, *block) if near else (1, full, full)

    def exchange(x):
        return lax.all_to_all(x, "shard", split_axis=0, concat_axis=0, axis_index_groups=sides, tiled=True)

    def hop_by(x, hop):
        return lax.ppermute(x, "shard", [(i, i ^ (2 * hop)) for i in range(size)])

    def partner(x):
        return lax.ppermute(x, "shard", pairs)

    one, two, l_stat, r_stat, l_basis, r_basis = (
        x.reshape(flat) for x in (moment_one, moment_two, left_stat, right_stat, left_basis, right_basis)
    )
    outgoing, *pieces = call(
        functools.partial(pack_kernel, hops),
        [(flat_rows + corner_rows(flat_rows), LANES)] + [block] * len(hops),
        [(flat_rows // 2, LANES)],
        0.1,
        full,
        "pack",
        copies=2 + len(hops),
        kind=pltpu.VMEM,
        in_specs=anywhere(5),
        out_specs=[pl.BlockSpec(memory_space=pltpu.VMEM)] + anywhere(len(hops)),
    )(*(pltpu.with_memory_space_constraint(x, pltpu.HBM) for x in (l_stat, r_stat, l_basis, r_basis, grads)))
    if near:
        swapped = partner(grads)
        mine = [hop_by(piece, hop) for hop, piece in zip(hops, pieces)]
        got = partner(outgoing)
        pieces = call(functools.partial(slices_kernel, hops), [block] * len(hops), [], 0.1, full, "slices")(swapped)
        theirs = [hop_by(after(piece, x), hop) for hop, piece, x in zip(hops, pieces, mine)]
        rows = (grads, swapped, *mine, *theirs)
    else:
        got = partner(outgoing)
        mine = exchange(grads)
        theirs = partner(mine)
        even, odd = jnp.where(parity == 0, mine, theirs), jnp.where(parity == 0, theirs, mine)
        rows = (jnp.stack([even, odd], axis=1).reshape(square),)
        theirs = [theirs]
    wide = (full, 2 * LANES)
    grad, product, right, inner = call(
        functools.partial(products_kernel, hops), [square, square, wide, wide], [(3, full, LANES)], 2, full, "products"
    )(r_basis, *rows)
    stat, basis, other, left = call(
        prepare_kernel, [square, square, flat, flat], [(3, full, LANES)], 0.1, full, "prepare"
    )(l_stat, r_stat, l_basis, r_basis, got)
    tensors = lax.axis_size("tensor")
    place = lambda t, i: i * tensors + t
    cycle = []
    for t in range(0, tensors - tensors % 2, 2):
        for i in range(0, size, 2):
            cycle += [(place(t, i), place(t, i + 1)), (place(t, i + 1), place(t + 1, i + 1))]
            cycle += [(place(t + 1, i + 1), place(t + 1, i)), (place(t + 1, i), place(t, i))]
    cycle += [(place(t, i), place(t, i ^ 1)) for t in range(tensors - tensors % 2, tensors) for i in range(size)]
    other_left = lax.ppermute(after(l_basis, theirs[0]), ("shard", "tensor"), cycle)
    new_stat, x = call(functools.partial(begin_kernel, EARLY_ITERS), [square] * 2, [], 7, full, "begin")(
        stat, product, basis
    )
    new_one, new_two, other_rows, outer, x = call(
        functools.partial(update_kernel, hops), [flat, flat, strips, wide, square], [(3, full, LANES)], 5, full, "update"
    )(inner, basis, left, right, other_left, one, two, x)
    if not near:
        partial = other_rows.reshape(tiles_here, 2, rows_here, full)
        other_rows = lax.dynamic_index_in_dim(partial, 1 - parity, 1, keepdims=False)
    got_rows = partner(other_rows)
    x, poly, send, own_rows = call(
        functools.partial(end_kernel, hops, NS_ITERS - EARLY_ITERS - 1),
        [square, square, flat, strips],
        [(3, full, LANES)],
        9,
        full,
        "end",
    )(after(x, other_rows), outer, right)
    back = partner(send)
    keep, new_left, new_right = call(rest_kernel, [flat, flat, flat], [(3, full, LANES)], 1.5, full, "rest")(
        x, poly, grad, new_stat, other
    )
    if near:
        kept, *sums = call(add_kernel, [block] * (1 + len(hops)), [], 0.1, full, "add")(
            after(own_rows, send), after(got_rows, send)
        )
        returned = [hop_by(x, hop) for hop, x in zip(hops, sums)]
        update = call(
            functools.partial(rows_kernel, hops),
            [grads.shape],
            [],
            0.1,
            full,
            "rows",
            copies=1 + len(hops),
            in_specs=anywhere(1 + len(hops)),
            out_specs=anywhere(1),
        )(kept, *returned)[0]
    else:
        own_rows = lax.dynamic_index_in_dim(partial, parity, 1, keepdims=False)
        update = exchange(after(own_rows, send) + after(got_rows, send))
    new_l_basis, new_r_basis = call(
        bases_kernel, [flat, flat], [], 0.1, full, "bases", copies=2, in_specs=anywhere(2), out_specs=anywhere(2)
    )(keep, back)
    halves = (new_one, new_two, new_left, new_right, new_l_basis, new_r_basis)
    return (update, *(x.reshape(1, flat_rows * LANES) for x in halves))


def solution(mesh):
    halves = P(("tensor", "shard"), None)
    rows = P("tensor", "shard", None)
    return jax.shard_map(
        local, mesh=mesh, in_specs=(rows,) + (halves,) * 6, out_specs=(rows,) + (halves,) * 6, check_vma=False
    )
```

```python
import functools

import jax
import jax.numpy as jnp
from jax import lax
from jax.experimental import pallas as pl
from jax.experimental.pallas import tpu as pltpu
from jax.sharding import PartitionSpec as P

NS_ITERS = 5
BETA_ONE = 0.9
BETA_TWO = 0.95
ADAM_EPS = 1e-08
NORM_EPS = 1e-06
LINEAR_COEFF = 3.4445
CUBIC_COEFF = -4.775
QUINTIC_COEFF = 2.0315
LANES = 128
F32 = jnp.float32


def split(x):
    high = x.astype(jnp.bfloat16)
    return high, (x - high.astype(F32)).astype(jnp.bfloat16)


def dot(a, b, dims=((1,), (0,))):
    return dot_parts(split(a), split(b), dims)


def dot_parts(a, b, dims=((1,), (0,))):
    (ka,), (kb,) = dims
    left = jnp.concatenate([a[0], a[0], a[1]], axis=ka)
    right = jnp.concatenate([b[0], b[1], b[0]], axis=kb)
    return lax.dot_general(left, right, (dims, ((), ())), preferred_element_type=F32)


def symmetric_dot(a, b, dims=((1,), (0,))):
    (ka,), (kb,) = dims
    cut = a[0].shape[0] - LANES
    head = lambda x, axis: lax.slice_in_dim(x, 0, cut, axis=axis)
    tail = lambda x, axis: lax.slice_in_dim(x, cut, cut + LANES, axis=axis)
    left = dot_parts(a, [head(x, 1 - kb) for x in b], dims)
    corner = dot_parts([tail(x, 1 - ka) for x in a], [tail(x, 1 - kb) for x in b], dims)
    right = jnp.concatenate([left[cut:].T, corner], axis=0)
    return jnp.concatenate([left, right], axis=1)


def swap(x):
    return pltpu.roll(x, LANES // 2, 1)


def low_lanes(shape):
    return lax.broadcasted_iota(jnp.int32, shape, 1) < LANES // 2


def pick(flag, x, y):
    return [jnp.where(flag, u, v) for u, v in zip(x, y)]


def thirds(ref, start=0, rows=None):
    rows = ref.shape[0] if rows is None else rows
    return [ref[pl.ds(start + k, rows // 3, stride=3), :] for k in range(3)]


def put_thirds(ref, parts):
    for k in range(3):
        ref[pl.ds(k, parts[k].shape[0], stride=3), :] = parts[k]


def interleave(scratch, index, even, odd):
    scratch[index, pl.ds(0, even.shape[0], stride=2), :] = even
    scratch[index, pl.ds(1, odd.shape[0], stride=2), :] = odd


def whole_of(scratch, first, second):
    a, b, c = first
    d, e, f = second
    low = low_lanes(a.shape)
    sb, sc, sd, se = swap(b), swap(c), swap(d), swap(e)
    interleave(scratch, 0, a, jnp.where(low, sb, sc))
    interleave(scratch, 1, jnp.where(low, b, sd), jnp.where(low, sc, e))
    interleave(scratch, 2, jnp.where(low, sd, se), f)
    return jnp.concatenate([scratch[0], scratch[1], scratch[2]], axis=1)


def half_of(scratch, flat):
    a, b, c = flat
    low = low_lanes(a.shape)
    sb, sc = swap(b), swap(c)
    interleave(scratch, 0, a, jnp.where(low, sb, sc))
    interleave(scratch, 1, jnp.where(low, b, 0.0), jnp.where(low, sc, 0.0))
    return jnp.concatenate([scratch[0], scratch[1]], axis=1)


def flat_of(scratch, half):
    scratch[0] = half[:, :LANES]
    scratch[1] = half[:, LANES:]
    pairs = half.shape[0] // 2
    even0 = scratch[0, pl.ds(0, pairs, stride=2), :]
    odd0 = swap(scratch[0, pl.ds(1, pairs, stride=2), :])
    even1 = scratch[1, pl.ds(0, pairs, stride=2), :]
    odd1 = swap(scratch[1, pl.ds(1, pairs, stride=2), :])
    low = low_lanes(even0.shape)
    return [even0, jnp.where(low, even1, odd0), jnp.where(low, odd0, odd1)]


def take_half(whole, first):
    one, two, three = whole[:, :LANES], whole[:, LANES : 2 * LANES], whole[:, 2 * LANES :]
    low = low_lanes(one.shape)
    s2, s3 = swap(two), swap(three)
    head = jnp.where(first, one, jnp.where(low, s2, s3))
    tail = jnp.where(low, jnp.where(first, two, s3), 0.0)
    return jnp.concatenate([head, tail], axis=1)


def is_first():
    return lax.rem(lax.axis_index("shard"), 2) == 0


def is_left():
    return lax.rem(lax.axis_index("shard") + lax.axis_index("tensor"), 2) == 0


def pack_kernel(hops, l_stat_ref, r_stat_ref, grads_ref, small_ref, *refs):
    piece_refs, (corner, sems) = refs[:-2], refs[-2:]
    left = is_left()
    half_rows = l_stat_ref.shape[0] // 2
    here = lax.axis_index("shard") // 2
    start = pl.multiple_of(jnp.where(is_first(), 0, half_rows), 8)
    stat_copy = lambda ref: pltpu.make_async_copy(ref.at[pl.ds(start, half_rows)], corner, sems.at[0])
    copies = [
        pltpu.make_async_copy(grads_ref.at[here ^ hop], piece_ref, sems.at[1 + number])
        for number, (hop, piece_ref) in enumerate(zip((*hops, 0), piece_refs))
    ]
    for copy in copies:
        copy.start()

    @pl.when(left)
    def _():
        stat_copy(r_stat_ref).start()

    @pl.when(jnp.logical_not(left))
    def _():
        stat_copy(l_stat_ref).start()

    stat_copy(l_stat_ref).wait()
    third = half_rows // 9
    a, b, c = thirds(corner)
    low = low_lanes((third, LANES))
    middle = slice(third, 2 * third)
    small_ref[pl.ds(0, third)] = jnp.where(low, a[:third], b[:third])
    small_ref[pl.ds(third, third)] = a[middle]
    small_ref[pl.ds(2 * third, third)] = jnp.where(low, swap(b[middle]), swap(c[middle]))
    small_ref[pl.ds(3 * third, 3 * third)] = corner[pl.ds(6 * third, 3 * third)]
    for copy in copies:
        copy.wait()


def corner_rows(flat_rows):
    return flat_rows // 3


def unpack_corner(got_ref):
    third = got_ref.shape[0] // 6
    small = got_ref[pl.ds(0, third), :]
    even = got_ref[pl.ds(third, third), :]
    odd = swap(got_ref[pl.ds(2 * third, third), :])
    a, b, c = thirds(got_ref, 3 * third, 3 * third)
    low = low_lanes(small.shape)
    zero = jnp.zeros_like(small)
    return [
        jnp.concatenate([jnp.where(low, small, zero), even, a], axis=0),
        jnp.concatenate([jnp.where(low, zero, small), jnp.where(low, zero, odd), b], axis=0),
        jnp.concatenate([zero, jnp.where(low, odd, zero), c], axis=0),
    ]


def statistic(first, own, got_ref, scratch):
    corner = unpack_corner(got_ref)
    placed = [jnp.concatenate([jnp.where(first, 0.0, c), jnp.where(first, c, 0.0)], axis=0) for c in corner]
    known = whole_of(scratch, pick(first, own, placed), pick(first, placed, own))
    half = known.shape[0] // 2
    part = half // 3
    row = lax.broadcasted_iota(jnp.int32, known.shape, 0)
    column = lax.broadcasted_iota(jnp.int32, known.shape, 1)
    missing = (jnp.where(first, row, column) < half) & (jnp.where(first, column, row) >= half)
    offset = jnp.where(first, half, 0)
    row, column = row - offset, column - offset
    limit = jnp.where(row < part, part, 2 * part)
    missing |= (row >= 0) & (row < 2 * part) & (column < half) & (column >= limit)
    return jnp.where(missing, known.T, known)


def place_rows(grad_ref, block, rows, value):
    grad_ref[pl.ds(pl.multiple_of(block * rows, 8), rows), :] = value


def polynomial(parts):
    gram = dot_parts(parts, parts, ((1,), (1,)))
    gram_parts = split(gram)
    return CUBIC_COEFF * gram + QUINTIC_COEFF * dot_parts(gram_parts, gram_parts)


def iterate(x, steps):
    for _ in range(steps):
        parts = split(x)
        x = LINEAR_COEFF * x + dot_parts(split(polynomial(parts)), parts)
    return x


def products_kernel(hops, l_stat_ref, r_stat_ref, l_basis_ref, r_basis_ref, *refs):
    left = is_left()
    outs = refs[-9:]
    grad_ref, product_ref, right_ref, inner_ref, own_ref, other_ref, left_copy_ref, right_copy_ref, scratch = outs
    if hops:
        grads_ref, swapped_ref = refs[:2]
        mine_refs, theirs_refs = refs[2 : 2 + len(hops)], refs[2 + len(hops) : 2 + 2 * len(hops)]
        rows = grads_ref.shape[1]
        here = lax.axis_index("shard") // 2
        parity = lax.axis_index("shard") % 2
        place_rows(grad_ref, 2 * here + parity, rows, grads_ref[here])
        place_rows(grad_ref, 2 * here + 1 - parity, rows, swapped_ref[...])
        for hop, mine, theirs in zip(hops, mine_refs, theirs_refs):
            place_rows(grad_ref, 2 * (here ^ hop) + parity, rows, mine[...])
            place_rows(grad_ref, 2 * (here ^ hop) + 1 - parity, rows, theirs[...])
    else:
        grad_ref[...] = refs[0][...]
    own_ref[...] = jnp.where(left, l_stat_ref[...], r_stat_ref[...])
    other_ref[...] = jnp.where(left, r_stat_ref[...], l_stat_ref[...])
    left_copy_ref[...] = l_basis_ref[...]
    right_copy_ref[...] = r_basis_ref[...]
    right = half_of(scratch, thirds(r_basis_ref))
    right_ref[...] = right
    grad = grad_ref[...]
    parts = split(jnp.where(left, grad, grad.T))
    product_ref[...] = symmetric_dot(parts, parts, ((1,), (1,)))
    inner_ref[...] = dot(grad, right)


def rows_for(hops, outer_ref, right_parts, out_ref, offset):
    rows = out_ref.shape[1]
    here = lax.axis_index("shard") // 2
    starts = [pl.multiple_of((2 * (here ^ hop) + offset) * rows, 8) if hops else 0 for hop in (0, *hops)]
    outer = [outer_ref[pl.ds(start, rows), :] for start in starts]
    partial = dot_parts(split(jnp.concatenate(outer, axis=0)), right_parts, ((1,), (1,)))
    for k in range(len(starts)):
        out_ref[k] = partial[k * rows : (k + 1) * rows]


def whole_basis(scratch, own_ref, got_ref):
    first = is_first()
    own, got = thirds(own_ref), thirds(got_ref)
    return whole_of(scratch, pick(first, own, got), pick(first, got, own))


def update_kernel(
    hops,
    inner_ref,
    left_ref,
    got_left_ref,
    right_ref,
    one_ref,
    two_ref,
    new_one_ref,
    new_two_ref,
    theirs_ref,
    outer_ref,
    basis_left_ref,
    scratch,
):
    basis_left = whole_basis(scratch, left_ref, got_left_ref)
    basis_left_ref[...] = basis_left
    rotated = flat_of(scratch, dot(basis_left.T, inner_ref[...]))
    ones = thirds(one_ref)
    twos = thirds(two_ref)
    new_one = [BETA_ONE * m + (1.0 - BETA_ONE) * r for m, r in zip(ones, rotated)]
    new_two = [BETA_TWO * v + (1.0 - BETA_TWO) * r * r for v, r in zip(twos, rotated)]
    put_thirds(new_one_ref, new_one)
    put_thirds(new_two_ref, new_two)
    direction = [m / (jnp.sqrt(v) + ADAM_EPS) for m, v in zip(new_one, new_two)]
    outer_ref[...] = dot_parts(split(basis_left), split(half_of(scratch, direction)))
    rows_for(hops, outer_ref, split(right_ref[...]), theirs_ref, 1 - lax.axis_index("shard") % 2)


def refresh_kernel(
    hops,
    own_ref,
    corner_ref,
    product_ref,
    basis_left_ref,
    right_flat_ref,
    got_right_ref,
    outer_ref,
    right_ref,
    new_stat_ref,
    x_ref,
    poly_ref,
    send_ref,
    mine_ref,
    scratch,
):
    left, first = is_left(), is_first()
    new_stat = 0.5 * statistic(first, thirds(own_ref), corner_ref, scratch) + 0.5 * product_ref[...]
    new_stat_ref[...] = new_stat
    basis = jnp.where(left, basis_left_ref[...], whole_basis(scratch, right_flat_ref, got_right_ref))
    power = dot(new_stat, basis)
    x = iterate(power * (1.0 / jnp.sqrt(jnp.sum(power * power) + NORM_EPS)), NS_ITERS - 1)
    x_ref[...] = x
    rows_for(hops, outer_ref, split(right_ref[...]), mine_ref, lax.axis_index("shard") % 2)
    poly = polynomial(split(x))
    poly_ref[...] = poly
    half = take_half(x, jnp.logical_not(first))
    put_thirds(send_ref, flat_of(scratch, LINEAR_COEFF * half + dot(poly, half)))


def add_kernel(mine_ref, theirs_ref, *out_refs):
    for k, out_ref in enumerate(out_refs):
        out_ref[...] = mine_ref[k] + theirs_ref[k]


def bases_kernel(keep_ref, back_ref, new_left_ref, new_right_ref, sems):
    left = is_left()

    def copies(own_ref, other_ref):
        return [
            pltpu.make_async_copy(keep_ref, own_ref, sems.at[0]),
            pltpu.make_async_copy(back_ref, other_ref, sems.at[1]),
        ]

    @pl.when(left)
    def _():
        for copy in copies(new_left_ref, new_right_ref):
            copy.start()

    @pl.when(jnp.logical_not(left))
    def _():
        for copy in copies(new_right_ref, new_left_ref):
            copy.start()

    for copy in copies(new_left_ref, new_right_ref):
        copy.wait()


def rows_kernel(hops, *refs):
    rows_refs, (update_ref, sems) = refs[:-2], refs[-2:]
    here = lax.axis_index("shard") // 2
    copies = [
        pltpu.make_async_copy(rows_refs[k], update_ref.at[here ^ hop], sems.at[k]) for k, hop in enumerate((0, *hops))
    ]
    for copy in copies:
        copy.start()
    for copy in copies:
        copy.wait()


def rest_kernel(x_ref, poly_ref, grad_ref, new_stat_ref, other_ref, keep_ref, new_left_ref, new_right_ref, scratch):
    left = is_left()
    first = is_first()
    half = take_half(x_ref[...], first)
    put_thirds(keep_ref, flat_of(scratch, LINEAR_COEFF * half + dot(poly_ref[...], half)))
    grad = grad_ref[...]
    turned = grad.T
    a = jnp.where(left, grad, turned)
    b = jnp.where(left, turned, grad)
    new_own = flat_of(scratch, take_half(new_stat_ref[...], first))
    product = flat_of(scratch, dot(b, take_half(a, first)))
    new_other = [0.5 * u + 0.5 * v for u, v in zip(thirds(other_ref), product)]
    put_thirds(new_left_ref, pick(left, new_own, new_other))
    put_thirds(new_right_ref, pick(left, new_other, new_own))


def call(kernel, outs, scratch, products, full, name, copies=0, kind=jax.ShapeDtypeStruct, **specs):
    size = full * full
    scratch = [pltpu.VMEM(s, F32) for s in scratch]
    if copies:
        scratch.append(pltpu.SemaphoreType.DMA((copies,)))
    return pl.pallas_call(
        kernel,
        out_shape=[kind(s, F32) for s in outs],
        scratch_shapes=scratch,
        compiler_params=pltpu.CompilerParams(vmem_limit_bytes=40 * 1024 * 1024),
        cost_estimate=pl.CostEstimate(flops=int(products * 6 * full * size), bytes_accessed=16 * size, transcendentals=0),
        name=name,
        **specs,
    )


def anywhere(count):
    return [pl.BlockSpec(memory_space=pl.ANY)] * count


def after(x, *others):
    return lax.optimization_barrier((x, *others))[0]


def local(grads, moment_one, moment_two, left_stat, right_stat, left_basis, right_basis):
    tiles_here, rows_here, full = grads.shape
    size = lax.axis_size("shard")
    flat_rows = full * (full // 2) // LANES
    flat = (flat_rows, LANES)
    square = (full, full)
    block = (rows_here, full)
    parity = lax.axis_index("shard") % 2
    pairs = [(i, i ^ 1) for i in range(size)]
    sides = [list(range(k, size, 2)) for k in range(2)]
    near = size in (4, 8) and rows_here % 8 == 0
    hops = {4: (1,), 8: (2, 3, 1)}[size] if near else ()
    strips = (tiles_here, *block) if near else (1, full, full)

    def exchange(x):
        return lax.all_to_all(x, "shard", split_axis=0, concat_axis=0, axis_index_groups=sides, tiled=True)

    def hop_by(x, hop):
        return lax.ppermute(x, "shard", [(i, i ^ (2 * hop)) for i in range(size)])

    def partner(x):
        return lax.ppermute(x, "shard", pairs)

    one, two, l_stat, r_stat, l_basis, r_basis = (
        x.reshape(flat) for x in (moment_one, moment_two, left_stat, right_stat, left_basis, right_basis)
    )
    tensors = lax.axis_size("tensor")
    place = lambda t, i: i * tensors + t
    cycle = []
    for t in range(0, tensors - tensors % 2, 2):
        for i in range(0, size, 2):
            cycle += [(place(t, i), place(t, i + 1)), (place(t, i + 1), place(t + 1, i + 1))]
            cycle += [(place(t + 1, i + 1), place(t + 1, i)), (place(t + 1, i), place(t, i))]
    cycle += [(place(t, i), place(t, i ^ 1)) for t in range(tensors - tensors % 2, tensors) for i in range(size)]

    got_left = partner(l_basis)
    count = len(hops) + 1 if near else 0
    corner, *pieces = call(
        functools.partial(pack_kernel, hops),
        [(corner_rows(flat_rows), LANES)] + [block] * count,
        [(flat_rows // 2, LANES)],
        0.1,
        full,
        "pack",
        copies=1 + count,
        kind=pltpu.VMEM,
        in_specs=anywhere(3),
        out_specs=[pl.BlockSpec(memory_space=pltpu.VMEM)] + anywhere(count),
    )(*(pltpu.with_memory_space_constraint(x, pltpu.HBM) for x in (l_stat, r_stat, grads)))
    if near:
        mine = [hop_by(piece, hop) for hop, piece in zip(hops, pieces)]
        swapped = partner(pieces[-1])
        theirs = [partner(x) for x in mine]
        rows = (grads, swapped, *mine, *theirs)
    else:
        mine = exchange(grads)
        theirs = partner(mine)
        even, odd = jnp.where(parity == 0, mine, theirs), jnp.where(parity == 0, theirs, mine)
        rows = (jnp.stack([even, odd], axis=1).reshape(square),)
        mine, theirs = [mine], [theirs]
    got_right = lax.ppermute(after(r_basis, got_left, *([swapped] if near else []), *theirs), ("shard", "tensor"), cycle)
    got_corner = partner(after(corner, got_left, theirs[0]))
    wide = (full, 2 * LANES)
    grad, product, right, inner, own, other, left, right_flat = call(
        functools.partial(products_kernel, hops),
        [square, square, wide, wide, flat, flat, flat, flat],
        [(3, full, LANES)],
        2,
        full,
        "products",
    )(l_stat, r_stat, l_basis, r_basis, *rows)
    new_one, new_two, other_rows, outer, basis_left = call(
        functools.partial(update_kernel, hops), [flat, flat, strips, wide, square], [(3, full, LANES)], 3, full, "update"
    )(inner, left, got_left, right, one, two)
    if not near:
        partial = other_rows.reshape(tiles_here, 2, rows_here, full)
        other_rows = lax.dynamic_index_in_dim(partial, 1 - parity, 1, keepdims=False)
    got_rows = partner(other_rows)
    new_stat, x, poly, send, own_rows = call(
        functools.partial(refresh_kernel, hops),
        [square, square, square, flat, strips],
        [(3, full, LANES)],
        16,
        full,
        "refresh",
    )(after(own, other_rows), got_corner, product, basis_left, right_flat, got_right, outer, right)
    back = partner(send)
    keep, new_left, new_right = call(rest_kernel, [flat, flat, flat], [(3, full, LANES)], 1.5, full, "rest")(
        x, poly, grad, new_stat, other
    )
    if near:
        kept, *sums = call(add_kernel, [block] * (1 + len(hops)), [], 0.1, full, "add")(
            after(own_rows, send), after(got_rows, send)
        )
        returned = [hop_by(x, hop) for hop, x in zip(hops, sums)]
        update = call(
            functools.partial(rows_kernel, hops),
            [grads.shape],
            [],
            0.1,
            full,
            "rows",
            copies=1 + len(hops),
            in_specs=anywhere(1 + len(hops)),
            out_specs=anywhere(1),
        )(kept, *returned)[0]
    else:
        own_rows = lax.dynamic_index_in_dim(partial, parity, 1, keepdims=False)
        update = exchange(after(own_rows, send) + after(got_rows, send))
    new_l_basis, new_r_basis = call(
        bases_kernel, [flat, flat], [], 0.1, full, "bases", copies=2, in_specs=anywhere(2), out_specs=anywhere(2)
    )(keep, back)
    halves = (new_one, new_two, new_left, new_right, new_l_basis, new_r_basis)
    return (update, *(x.reshape(1, flat_rows * LANES) for x in halves))


def solution(mesh):
    halves = P(("tensor", "shard"), None)
    rows = P("tensor", "shard", None)
    return jax.shard_map(
        local, mesh=mesh, in_specs=(rows,) + (halves,) * 6, out_specs=(rows,) + (halves,) * 6, check_vma=False
    )
```

```python
import functools

import jax
import jax.numpy as jnp
from jax import lax
from jax.experimental import pallas as pl
from jax.experimental.pallas import tpu as pltpu
from jax.sharding import PartitionSpec as P

NS_ITERS = 5
EARLY_ITERS = 1
BETA_ONE = 0.9
BETA_TWO = 0.95
ADAM_EPS = 1e-08
NORM_EPS = 1e-06
LINEAR_COEFF = 3.4445
CUBIC_COEFF = -4.775
QUINTIC_COEFF = 2.0315
LANES = 128
F32 = jnp.float32


def split(x):
    high = x.astype(jnp.bfloat16)
    return high, (x - high.astype(F32)).astype(jnp.bfloat16)


def dot(a, b, dims=((1,), (0,))):
    return dot_parts(split(a), split(b), dims)


def dot_parts(a, b, dims=((1,), (0,))):
    (ka,), (kb,) = dims
    left = jnp.concatenate([a[0], a[0], a[1]], axis=ka)
    right = jnp.concatenate([b[0], b[1], b[0]], axis=kb)
    return lax.dot_general(left, right, (dims, ((), ())), preferred_element_type=F32)


def symmetric_dot(a, b, dims=((1,), (0,))):
    (ka,), (kb,) = dims
    cut = a[0].shape[0] - LANES
    head = lambda x, axis: lax.slice_in_dim(x, 0, cut, axis=axis)
    tail = lambda x, axis: lax.slice_in_dim(x, cut, cut + LANES, axis=axis)
    left = dot_parts(a, [head(x, 1 - kb) for x in b], dims)
    corner = dot_parts([tail(x, 1 - ka) for x in a], [tail(x, 1 - kb) for x in b], dims)
    right = jnp.concatenate([left[cut:].T, corner], axis=0)
    return jnp.concatenate([left, right], axis=1)


def swap(x):
    return pltpu.roll(x, LANES // 2, 1)


def low_lanes(shape):
    return lax.broadcasted_iota(jnp.int32, shape, 1) < LANES // 2


def pick(flag, x, y):
    return [jnp.where(flag, u, v) for u, v in zip(x, y)]


def thirds(ref, start=0, rows=None):
    rows = ref.shape[0] if rows is None else rows
    return [ref[pl.ds(start + k, rows // 3, stride=3), :] for k in range(3)]


def put_thirds(ref, parts):
    for k in range(3):
        ref[pl.ds(k, parts[k].shape[0], stride=3), :] = parts[k]


def interleave(scratch, index, even, odd):
    scratch[index, pl.ds(0, even.shape[0], stride=2), :] = even
    scratch[index, pl.ds(1, odd.shape[0], stride=2), :] = odd


def whole_of(scratch, first, second):
    a, b, c = first
    d, e, f = second
    low = low_lanes(a.shape)
    sb, sc, sd, se = swap(b), swap(c), swap(d), swap(e)
    interleave(scratch, 0, a, jnp.where(low, sb, sc))
    interleave(scratch, 1, jnp.where(low, b, sd), jnp.where(low, sc, e))
    interleave(scratch, 2, jnp.where(low, sd, se), f)
    return jnp.concatenate([scratch[0], scratch[1], scratch[2]], axis=1)


def half_of(scratch, flat):
    a, b, c = flat
    low = low_lanes(a.shape)
    sb, sc = swap(b), swap(c)
    interleave(scratch, 0, a, jnp.where(low, sb, sc))
    interleave(scratch, 1, jnp.where(low, b, 0.0), jnp.where(low, sc, 0.0))
    return jnp.concatenate([scratch[0], scratch[1]], axis=1)


def flat_of(scratch, half):
    scratch[0] = half[:, :LANES]
    scratch[1] = half[:, LANES:]
    pairs = half.shape[0] // 2
    even0 = scratch[0, pl.ds(0, pairs, stride=2), :]
    odd0 = swap(scratch[0, pl.ds(1, pairs, stride=2), :])
    even1 = scratch[1, pl.ds(0, pairs, stride=2), :]
    odd1 = swap(scratch[1, pl.ds(1, pairs, stride=2), :])
    low = low_lanes(even0.shape)
    return [even0, jnp.where(low, even1, odd0), jnp.where(low, odd0, odd1)]


def take_half(whole, first):
    one, two, three = whole[:, :LANES], whole[:, LANES : 2 * LANES], whole[:, 2 * LANES :]
    low = low_lanes(one.shape)
    s2, s3 = swap(two), swap(three)
    head = jnp.where(first, one, jnp.where(low, s2, s3))
    tail = jnp.where(low, jnp.where(first, two, s3), 0.0)
    return jnp.concatenate([head, tail], axis=1)


def is_first():
    return lax.rem(lax.axis_index("shard"), 2) == 0


def is_left():
    return lax.rem(lax.axis_index("shard") + lax.axis_index("tensor"), 2) == 0


def pack_kernel(hops, l_stat_ref, r_stat_ref, l_basis_ref, r_basis_ref, grads_ref, *refs):
    out_ref, small_ref, *refs = refs
    piece_refs, (corner, sems) = refs[: len(hops)], refs[len(hops) :]
    left = is_left()
    flat_rows = l_basis_ref.shape[0]
    half_rows = flat_rows // 2
    rows = grads_ref.shape[1]
    here = lax.axis_index("shard") // 2

    start = pl.multiple_of(jnp.where(is_first(), 0, half_rows), 8)

    def copies(basis_ref, stat_ref):
        return [
            pltpu.make_async_copy(stat_ref.at[pl.ds(start, half_rows)], corner, sems.at[0]),
            pltpu.make_async_copy(basis_ref, out_ref.at[pl.ds(0, flat_rows)], sems.at[1]),
        ]

    @pl.when(left)
    def _():
        for copy in copies(r_basis_ref, r_stat_ref):
            copy.start()

    @pl.when(jnp.logical_not(left))
    def _():
        for copy in copies(l_basis_ref, l_stat_ref):
            copy.start()

    more = []
    for number, (hop, piece_ref) in enumerate(zip(hops, piece_refs)):
        more.append(pltpu.make_async_copy(grads_ref.at[here ^ hop], piece_ref, sems.at[2 + number]))
    if hops:
        for k in range(grads_ref.shape[2] // LANES):
            source = grads_ref.at[here, :, pl.ds(k * LANES, LANES)]
            target = out_ref.at[pl.ds(flat_rows + k * rows, rows)]
            more.append(pltpu.make_async_copy(source, target, sems.at[2 + len(hops) + k]))
    for copy in more:
        copy.start()
    first, second = copies(l_basis_ref, l_stat_ref)
    first.wait()
    third = half_rows // 9
    a, b, c = thirds(corner)
    low = low_lanes((third, LANES))
    middle = slice(third, 2 * third)
    small_ref[pl.ds(0, third)] = jnp.where(low, a[:third], b[:third])
    small_ref[pl.ds(third, third)] = a[middle]
    small_ref[pl.ds(2 * third, third)] = jnp.where(low, swap(b[middle]), swap(c[middle]))
    small_ref[pl.ds(3 * third, 3 * third)] = corner[pl.ds(6 * third, 3 * third)]
    for copy in [second, *more]:
        copy.wait()


def corner_rows(flat_rows):
    return flat_rows // 3


def unpack_corner(got_ref):
    third = got_ref.shape[0] // 6
    small = got_ref[pl.ds(0, third), :]
    even = got_ref[pl.ds(third, third), :]
    odd = swap(got_ref[pl.ds(2 * third, third), :])
    a, b, c = thirds(got_ref, 3 * third, 3 * third)
    low = low_lanes(small.shape)
    zero = jnp.zeros_like(small)
    return [
        jnp.concatenate([jnp.where(low, small, zero), even, a], axis=0),
        jnp.concatenate([jnp.where(low, zero, small), jnp.where(low, zero, odd), b], axis=0),
        jnp.concatenate([zero, jnp.where(low, odd, zero), c], axis=0),
    ]


def statistic(first, own, got_ref, scratch):
    corner = unpack_corner(got_ref)
    placed = [jnp.concatenate([jnp.where(first, 0.0, c), jnp.where(first, c, 0.0)], axis=0) for c in corner]
    known = whole_of(scratch, pick(first, own, placed), pick(first, placed, own))
    half = known.shape[0] // 2
    part = half // 3
    row = lax.broadcasted_iota(jnp.int32, known.shape, 0)
    column = lax.broadcasted_iota(jnp.int32, known.shape, 1)
    missing = (jnp.where(first, row, column) < half) & (jnp.where(first, column, row) >= half)
    offset = jnp.where(first, half, 0)
    row, column = row - offset, column - offset
    limit = jnp.where(row < part, part, 2 * part)
    missing |= (row >= 0) & (row < 2 * part) & (column < half) & (column >= limit)
    return jnp.where(missing, known.T, known)


def place_rows(grad_ref, block, rows, value):
    grad_ref[pl.ds(pl.multiple_of(block * rows, 8), rows), :] = value


def polynomial(parts):
    gram = dot_parts(parts, parts, ((1,), (1,)))
    gram_parts = split(gram)
    return CUBIC_COEFF * gram + QUINTIC_COEFF * dot_parts(gram_parts, gram_parts)


def iterate(x, steps):
    for _ in range(steps):
        parts = split(x)
        x = LINEAR_COEFF * x + dot_parts(split(polynomial(parts)), parts)
    return x


def products_kernel(hops, l_stat_ref, r_stat_ref, l_basis_ref, r_basis_ref, got_ref, *refs):
    left = is_left()
    outs = refs[-9:]
    grad_ref, product_ref, basis_ref, right_ref, inner_ref, own_ref, other_ref, copy_ref, scratch = outs
    if hops:
        grads_ref, mine_refs, theirs_refs = refs[0], refs[1 : 1 + len(hops)], refs[1 + len(hops) : 1 + 2 * len(hops)]
        rows = grads_ref.shape[1]
        here = lax.axis_index("shard") // 2
        parity = lax.axis_index("shard") % 2
        start = l_basis_ref.shape[0]
        received = [got_ref[pl.ds(start + k * rows, rows), :] for k in range(grad_ref.shape[1] // LANES)]
        place_rows(grad_ref, 2 * here + parity, rows, grads_ref[here])
        place_rows(grad_ref, 2 * here + 1 - parity, rows, jnp.concatenate(received, axis=1))
        for hop, mine, theirs in zip(hops, mine_refs, theirs_refs):
            place_rows(grad_ref, 2 * (here ^ hop) + parity, rows, mine[...])
            place_rows(grad_ref, 2 * (here ^ hop) + 1 - parity, rows, theirs[...])
    else:
        grad_ref[...] = refs[0][...]
    own = pick(left, thirds(l_basis_ref), thirds(r_basis_ref))
    got = thirds(got_ref, 0, l_basis_ref.shape[0])
    first = is_first()
    basis_ref[...] = whole_of(scratch, pick(first, own, got), pick(first, got, own))
    own_ref[...] = jnp.where(left, l_stat_ref[...], r_stat_ref[...])
    other_ref[...] = jnp.where(left, r_stat_ref[...], l_stat_ref[...])
    copy_ref[...] = l_basis_ref[...]
    right = half_of(scratch, thirds(r_basis_ref))
    right_ref[...] = right
    grad = grad_ref[...]
    parts = split(jnp.where(left, grad, grad.T))
    product_ref[...] = symmetric_dot(parts, parts, ((1,), (1,)))
    inner_ref[...] = dot(grad, right)


def begin_kernel(steps, own_ref, corner_ref, product_ref, basis_ref, new_stat_ref, x_ref, scratch):
    new_stat = 0.5 * statistic(is_first(), thirds(own_ref), corner_ref, scratch) + 0.5 * product_ref[...]
    new_stat_ref[...] = new_stat
    power = dot(new_stat, basis_ref[...])
    x_ref[...] = iterate(power * (1.0 / jnp.sqrt(jnp.sum(power * power) + NORM_EPS)), steps)


def rows_for(hops, outer_ref, right_parts, out_ref, offset):
    rows = out_ref.shape[1]
    here = lax.axis_index("shard") // 2
    starts = [pl.multiple_of((2 * (here ^ hop) + offset) * rows, 8) if hops else 0 for hop in (0, *hops)]
    outer = [outer_ref[pl.ds(start, rows), :] for start in starts]
    partial = dot_parts(split(jnp.concatenate(outer, axis=0)), right_parts, ((1,), (1,)))
    for k in range(len(starts)):
        out_ref[k] = partial[k * rows : (k + 1) * rows]


def update_kernel(
    hops,
    inner_ref,
    basis_ref,
    left_ref,
    right_ref,
    other_left_ref,
    one_ref,
    two_ref,
    start_ref,
    new_one_ref,
    new_two_ref,
    theirs_ref,
    outer_ref,
    x_ref,
    scratch,
):
    left, first = is_left(), is_first()
    x = start_ref[...]
    parts = split(x)
    gram = dot_parts(parts, parts, ((1,), (1,)))
    own, got = thirds(left_ref), thirds(other_left_ref)
    basis_left = jnp.where(left, basis_ref[...], whole_of(scratch, pick(first, own, got), pick(first, got, own)))
    rotated = dot(basis_left.T, inner_ref[...])
    gram_parts = split(gram)
    square = dot_parts(gram_parts, gram_parts)
    rotated = flat_of(scratch, rotated)
    ones = thirds(one_ref)
    twos = thirds(two_ref)
    new_one = [BETA_ONE * m + (1.0 - BETA_ONE) * r for m, r in zip(ones, rotated)]
    new_two = [BETA_TWO * v + (1.0 - BETA_TWO) * r * r for v, r in zip(twos, rotated)]
    put_thirds(new_one_ref, new_one)
    put_thirds(new_two_ref, new_two)
    direction = [m / (jnp.sqrt(v) + ADAM_EPS) for m, v in zip(new_one, new_two)]
    outer_ref[...] = dot_parts(split(basis_left), split(half_of(scratch, direction)))
    poly_parts = split(CUBIC_COEFF * gram + QUINTIC_COEFF * square)
    moved = dot_parts(poly_parts, parts)
    rows_for(hops, outer_ref, split(right_ref[...]), theirs_ref, 1 - lax.axis_index("shard") % 2)
    x_ref[...] = LINEAR_COEFF * x + moved


def end_kernel(hops, steps, start_ref, outer_ref, right_ref, x_ref, poly_ref, send_ref, mine_ref, scratch):
    x = iterate(start_ref[...], steps - 1)
    x_ref[...] = x
    rows_for(hops, outer_ref, split(right_ref[...]), mine_ref, lax.axis_index("shard") % 2)
    poly = polynomial(split(x))
    poly_ref[...] = poly
    half = take_half(x, jnp.logical_not(is_first()))
    put_thirds(send_ref, flat_of(scratch, LINEAR_COEFF * half + dot(poly, half)))


def add_kernel(mine_ref, theirs_ref, *out_refs):
    for k, out_ref in enumerate(out_refs):
        out_ref[...] = mine_ref[k] + theirs_ref[k]


def bases_kernel(keep_ref, back_ref, new_left_ref, new_right_ref, sems):
    left = is_left()

    def copies(own_ref, other_ref):
        return [
            pltpu.make_async_copy(keep_ref, own_ref, sems.at[0]),
            pltpu.make_async_copy(back_ref, other_ref, sems.at[1]),
        ]

    @pl.when(left)
    def _():
        for copy in copies(new_left_ref, new_right_ref):
            copy.start()

    @pl.when(jnp.logical_not(left))
    def _():
        for copy in copies(new_right_ref, new_left_ref):
            copy.start()

    for copy in copies(new_left_ref, new_right_ref):
        copy.wait()


def rows_kernel(hops, *refs):
    rows_refs, (update_ref, sems) = refs[:-2], refs[-2:]
    here = lax.axis_index("shard") // 2
    copies = [
        pltpu.make_async_copy(rows_refs[k], update_ref.at[here ^ hop], sems.at[k]) for k, hop in enumerate((0, *hops))
    ]
    for copy in copies:
        copy.start()
    for copy in copies:
        copy.wait()


def rest_kernel(x_ref, poly_ref, grad_ref, new_stat_ref, other_ref, keep_ref, new_left_ref, new_right_ref, scratch):
    left = is_left()
    first = is_first()
    half = take_half(x_ref[...], first)
    put_thirds(keep_ref, flat_of(scratch, LINEAR_COEFF * half + dot(poly_ref[...], half)))
    grad = grad_ref[...]
    turned = grad.T
    a = jnp.where(left, grad, turned)
    b = jnp.where(left, turned, grad)
    new_own = flat_of(scratch, take_half(new_stat_ref[...], first))
    product = flat_of(scratch, dot(b, take_half(a, first)))
    new_other = [0.5 * u + 0.5 * v for u, v in zip(thirds(other_ref), product)]
    put_thirds(new_left_ref, pick(left, new_own, new_other))
    put_thirds(new_right_ref, pick(left, new_other, new_own))


def call(kernel, outs, scratch, products, full, name, copies=0, kind=jax.ShapeDtypeStruct, **specs):
    size = full * full
    scratch = [pltpu.VMEM(s, F32) for s in scratch]
    if copies:
        scratch.append(pltpu.SemaphoreType.DMA((copies,)))
    return pl.pallas_call(
        kernel,
        out_shape=[kind(s, F32) for s in outs],
        scratch_shapes=scratch,
        compiler_params=pltpu.CompilerParams(vmem_limit_bytes=40 * 1024 * 1024),
        cost_estimate=pl.CostEstimate(flops=int(products * 6 * full * size), bytes_accessed=16 * size, transcendentals=0),
        name=name,
        **specs,
    )


def anywhere(count):
    return [pl.BlockSpec(memory_space=pl.ANY)] * count


def after(x, *others):
    return lax.optimization_barrier((x, *others))[0]


def local(grads, moment_one, moment_two, left_stat, right_stat, left_basis, right_basis):
    tiles_here, rows_here, full = grads.shape
    size = lax.axis_size("shard")
    flat_rows = full * (full // 2) // LANES
    flat = (flat_rows, LANES)
    square = (full, full)
    block = (rows_here, full)
    parity = lax.axis_index("shard") % 2
    pairs = [(i, i ^ 1) for i in range(size)]
    sides = [list(range(k, size, 2)) for k in range(2)]
    near = size in (4, 8) and rows_here % 8 == 0
    hops = {4: (1,), 8: (2, 3, 1)}[size] if near else ()
    strips = (tiles_here, *block) if near else (1, full, full)

    def exchange(x):
        return lax.all_to_all(x, "shard", split_axis=0, concat_axis=0, axis_index_groups=sides, tiled=True)

    def hop_by(x, hop):
        return lax.ppermute(x, "shard", [(i, i ^ (2 * hop)) for i in range(size)])

    def partner(x):
        return lax.ppermute(x, "shard", pairs)

    one, two, l_stat, r_stat, l_basis, r_basis = (
        x.reshape(flat) for x in (moment_one, moment_two, left_stat, right_stat, left_basis, right_basis)
    )
    count = corner_rows(flat_rows)
    outgoing_rows = flat_rows + (rows_here * (full // LANES) if near else 0)
    outgoing, corner, *pieces = call(
        functools.partial(pack_kernel, hops),
        [(outgoing_rows, LANES), (count, LANES)] + [block] * len(hops),
        [(flat_rows // 2, LANES)],
        0.1,
        full,
        "pack",
        copies=2 + len(hops) + full // LANES,
        kind=pltpu.VMEM,
        in_specs=anywhere(5),
        out_specs=anywhere(1) + [pl.BlockSpec(memory_space=pltpu.VMEM)] + anywhere(len(hops)),
    )(*(pltpu.with_memory_space_constraint(x, pltpu.HBM) for x in (l_stat, r_stat, l_basis, r_basis, grads)))
    got = partner(outgoing)
    if near:
        mine = [hop_by(piece, hop) for hop, piece in zip(hops, pieces)]
        theirs = [partner(x) for x in mine]
        rows = (grads, *mine, *theirs)
    else:
        mine = exchange(grads)
        theirs = partner(mine)
        even, odd = jnp.where(parity == 0, mine, theirs), jnp.where(parity == 0, theirs, mine)
        rows = (jnp.stack([even, odd], axis=1).reshape(square),)
        mine = [mine]
    got_corner = partner(after(corner, theirs[0] if near else mine[0]))
    grad, product, basis, right, inner, own, other, left = call(
        functools.partial(products_kernel, hops),
        [square, square, square, (full, 2 * LANES), (full, 2 * LANES), flat, flat, flat],
        [(3, full, LANES)],
        2,
        full,
        "products",
    )(l_stat, r_stat, l_basis, r_basis, got, *rows)
    tensors = lax.axis_size("tensor")
    place = lambda t, i: i * tensors + t
    cycle = []
    for t in range(0, tensors - tensors % 2, 2):
        for i in range(0, size, 2):
            cycle += [(place(t, i), place(t, i + 1)), (place(t, i + 1), place(t + 1, i + 1))]
            cycle += [(place(t + 1, i + 1), place(t + 1, i)), (place(t + 1, i), place(t, i))]
    cycle += [(place(t, i), place(t, i ^ 1)) for t in range(tensors - tensors % 2, tensors) for i in range(size)]
    other_left = lax.ppermute(after(l_basis, product), ("shard", "tensor"), cycle)
    new_stat, x = call(functools.partial(begin_kernel, EARLY_ITERS), [square] * 2, [(3, full, LANES)], 7, full, "begin")(
        own, got_corner, product, basis
    )
    wide = (full, 2 * LANES)
    new_one, new_two, other_rows, outer, x = call(
        functools.partial(update_kernel, hops), [flat, flat, strips, wide, square], [(3, full, LANES)], 5, full, "update"
    )(inner, basis, left, right, other_left, one, two, x)
    if not near:
        partial = other_rows.reshape(tiles_here, 2, rows_here, full)
        other_rows = lax.dynamic_index_in_dim(partial, 1 - parity, 1, keepdims=False)
    got_rows = partner(other_rows)
    x, poly, send, own_rows = call(
        functools.partial(end_kernel, hops, NS_ITERS - EARLY_ITERS - 1),
        [square, square, flat, strips],
        [(3, full, LANES)],
        9,
        full,
        "end",
    )(after(x, other_rows), outer, right)
    back = partner(send)
    keep, new_left, new_right = call(rest_kernel, [flat, flat, flat], [(3, full, LANES)], 1.5, full, "rest")(
        x, poly, grad, new_stat, other
    )
    if near:
        kept, *sums = call(add_kernel, [block] * (1 + len(hops)), [], 0.1, full, "add")(
            after(own_rows, send), after(got_rows, send)
        )
        returned = [hop_by(x, hop) for hop, x in zip(hops, sums)]
        update = call(
            functools.partial(rows_kernel, hops),
            [grads.shape],
            [],
            0.1,
            full,
            "rows",
            copies=1 + len(hops),
            in_specs=anywhere(1 + len(hops)),
            out_specs=anywhere(1),
        )(kept, *returned)[0]
    else:
        own_rows = lax.dynamic_index_in_dim(partial, parity, 1, keepdims=False)
        update = exchange(after(own_rows, send) + after(got_rows, send))
    new_l_basis, new_r_basis = call(
        bases_kernel, [flat, flat], [], 0.1, full, "bases", copies=2, in_specs=anywhere(2), out_specs=anywhere(2)
    )(keep, back)
    halves = (new_one, new_two, new_left, new_right, new_l_basis, new_r_basis)
    return (update, *(x.reshape(1, flat_rows * LANES) for x in halves))


def solution(mesh):
    halves = P(("tensor", "shard"), None)
    rows = P("tensor", "shard", None)
    return jax.shard_map(
        local, mesh=mesh, in_specs=(rows,) + (halves,) * 6, out_specs=(rows,) + (halves,) * 6, check_vma=False
    )
```

```python
import functools

import jax
import jax.numpy as jnp
from jax import lax
from jax.experimental import pallas as pl
from jax.experimental.pallas import tpu as pltpu
from jax.sharding import PartitionSpec as P

NS_ITERS = 5
EARLY_ITERS = 1
BETA_ONE = 0.9
BETA_TWO = 0.95
ADAM_EPS = 1e-08
NORM_EPS = 1e-06
LINEAR_COEFF = 3.4445
CUBIC_COEFF = -4.775
QUINTIC_COEFF = 2.0315
LANES = 128
F32 = jnp.float32


def split(x):
    high = x.astype(jnp.bfloat16)
    return high, (x - high.astype(F32)).astype(jnp.bfloat16)


def dot(a, b, dims=((1,), (0,))):
    return dot_parts(split(a), split(b), dims)


def dot_parts(a, b, dims=((1,), (0,))):
    (ka,), (kb,) = dims
    left = jnp.concatenate([a[0], a[0], a[1]], axis=ka)
    right = jnp.concatenate([b[0], b[1], b[0]], axis=kb)
    return lax.dot_general(left, right, (dims, ((), ())), preferred_element_type=F32)


def symmetric_dot(a, b, dims=((1,), (0,))):
    (ka,), (kb,) = dims
    cut = a[0].shape[0] - LANES
    head = lambda x, axis: lax.slice_in_dim(x, 0, cut, axis=axis)
    tail = lambda x, axis: lax.slice_in_dim(x, cut, cut + LANES, axis=axis)
    left = dot_parts(a, [head(x, 1 - kb) for x in b], dims)
    corner = dot_parts([tail(x, 1 - ka) for x in a], [tail(x, 1 - kb) for x in b], dims)
    right = jnp.concatenate([left[cut:].T, corner], axis=0)
    return jnp.concatenate([left, right], axis=1)


def swap(x):
    return pltpu.roll(x, LANES // 2, 1)


def low_lanes(shape):
    return lax.broadcasted_iota(jnp.int32, shape, 1) < LANES // 2


def pick(flag, x, y):
    return [jnp.where(flag, u, v) for u, v in zip(x, y)]


def thirds(ref, start=0, rows=None):
    rows = ref.shape[0] if rows is None else rows
    return [ref[pl.ds(start + k, rows // 3, stride=3), :] for k in range(3)]


def put_thirds(ref, parts):
    for k in range(3):
        ref[pl.ds(k, parts[k].shape[0], stride=3), :] = parts[k]


def interleave(scratch, index, even, odd):
    scratch[index, pl.ds(0, even.shape[0], stride=2), :] = even
    scratch[index, pl.ds(1, odd.shape[0], stride=2), :] = odd


def whole_of(scratch, first, second):
    a, b, c = first
    d, e, f = second
    low = low_lanes(a.shape)
    sb, sc, sd, se = swap(b), swap(c), swap(d), swap(e)
    interleave(scratch, 0, a, jnp.where(low, sb, sc))
    interleave(scratch, 1, jnp.where(low, b, sd), jnp.where(low, sc, e))
    interleave(scratch, 2, jnp.where(low, sd, se), f)
    return jnp.concatenate([scratch[0], scratch[1], scratch[2]], axis=1)


def half_of(scratch, flat):
    a, b, c = flat
    low = low_lanes(a.shape)
    sb, sc = swap(b), swap(c)
    interleave(scratch, 0, a, jnp.where(low, sb, sc))
    interleave(scratch, 1, jnp.where(low, b, 0.0), jnp.where(low, sc, 0.0))
    return jnp.concatenate([scratch[0], scratch[1]], axis=1)


def flat_of(scratch, half):
    scratch[0] = half[:, :LANES]
    scratch[1] = half[:, LANES:]
    pairs = half.shape[0] // 2
    even0 = scratch[0, pl.ds(0, pairs, stride=2), :]
    odd0 = swap(scratch[0, pl.ds(1, pairs, stride=2), :])
    even1 = scratch[1, pl.ds(0, pairs, stride=2), :]
    odd1 = swap(scratch[1, pl.ds(1, pairs, stride=2), :])
    low = low_lanes(even0.shape)
    return [even0, jnp.where(low, even1, odd0), jnp.where(low, odd0, odd1)]


def take_half(whole, first):
    one, two, three = whole[:, :LANES], whole[:, LANES : 2 * LANES], whole[:, 2 * LANES :]
    low = low_lanes(one.shape)
    s2, s3 = swap(two), swap(three)
    head = jnp.where(first, one, jnp.where(low, s2, s3))
    tail = jnp.where(low, jnp.where(first, two, s3), 0.0)
    return jnp.concatenate([head, tail], axis=1)


def is_first():
    return lax.rem(lax.axis_index("shard"), 2) == 0


def is_left():
    return lax.rem(lax.axis_index("shard") + lax.axis_index("tensor"), 2) == 0


def pack_kernel(hops, l_stat_ref, r_stat_ref, l_basis_ref, r_basis_ref, grads_ref, *refs):
    out_ref, small_ref, *refs = refs
    piece_refs, (corner, sems) = refs[: len(hops)], refs[len(hops) :]
    left = is_left()
    flat_rows = l_basis_ref.shape[0]
    half_rows = flat_rows // 2
    rows = grads_ref.shape[1]
    here = lax.axis_index("shard") // 2

    start = pl.multiple_of(jnp.where(is_first(), 0, half_rows), 8)

    def copies(basis_ref, stat_ref):
        return [
            pltpu.make_async_copy(stat_ref.at[pl.ds(start, half_rows)], corner, sems.at[0]),
            pltpu.make_async_copy(basis_ref, out_ref.at[pl.ds(0, flat_rows)], sems.at[1]),
        ]

    @pl.when(left)
    def _():
        for copy in copies(r_basis_ref, r_stat_ref):
            copy.start()

    @pl.when(jnp.logical_not(left))
    def _():
        for copy in copies(l_basis_ref, l_stat_ref):
            copy.start()

    more = []
    for number, (hop, piece_ref) in enumerate(zip(hops, piece_refs)):
        more.append(pltpu.make_async_copy(grads_ref.at[here ^ hop], piece_ref, sems.at[2 + number]))
    if hops:
        for k in range(grads_ref.shape[2] // LANES):
            source = grads_ref.at[here, :, pl.ds(k * LANES, LANES)]
            target = out_ref.at[pl.ds(flat_rows + k * rows, rows)]
            more.append(pltpu.make_async_copy(source, target, sems.at[2 + len(hops) + k]))
    for copy in more:
        copy.start()
    first, second = copies(l_basis_ref, l_stat_ref)
    first.wait()
    third = half_rows // 9
    a, b, c = thirds(corner)
    low = low_lanes((third, LANES))
    middle = slice(third, 2 * third)
    small_ref[pl.ds(0, third)] = jnp.where(low, a[:third], b[:third])
    small_ref[pl.ds(third, third)] = a[middle]
    small_ref[pl.ds(2 * third, third)] = jnp.where(low, swap(b[middle]), swap(c[middle]))
    small_ref[pl.ds(3 * third, 3 * third)] = corner[pl.ds(6 * third, 3 * third)]
    for copy in [second, *more]:
        copy.wait()


def corner_rows(flat_rows):
    return flat_rows // 3


def unpack_corner(got_ref):
    third = got_ref.shape[0] // 6
    small = got_ref[pl.ds(0, third), :]
    even = got_ref[pl.ds(third, third), :]
    odd = swap(got_ref[pl.ds(2 * third, third), :])
    a, b, c = thirds(got_ref, 3 * third, 3 * third)
    low = low_lanes(small.shape)
    zero = jnp.zeros_like(small)
    return [
        jnp.concatenate([jnp.where(low, small, zero), even, a], axis=0),
        jnp.concatenate([jnp.where(low, zero, small), jnp.where(low, zero, odd), b], axis=0),
        jnp.concatenate([zero, jnp.where(low, odd, zero), c], axis=0),
    ]


def known_part(first, own, scratch):
    zeros = [jnp.zeros_like(x) for x in own]
    known = whole_of(scratch, pick(first, own, zeros), pick(first, zeros, own))
    half = known.shape[0] // 2
    row = lax.broadcasted_iota(jnp.int32, known.shape, 0)
    column = lax.broadcasted_iota(jnp.int32, known.shape, 1)
    missing = (jnp.where(first, row, column) < half) & (jnp.where(first, column, row) >= half)
    return jnp.where(missing, known.T, known)


def corner_part(corner_ref, scratch):
    corner = half_of(scratch, unpack_corner(corner_ref))
    rows, wide = corner.shape
    turned = jnp.concatenate([corner, jnp.zeros((wide - rows, wide), F32)], axis=0).T[:rows]
    part = rows // 3
    row = lax.broadcasted_iota(jnp.int32, corner.shape, 0)
    column = lax.broadcasted_iota(jnp.int32, corner.shape, 1)
    missing = (row < 2 * part) & (column >= jnp.where(row < part, part, 2 * part))
    return jnp.where(missing, turned, corner)


def place_rows(grad_ref, block, rows, value):
    grad_ref[pl.ds(pl.multiple_of(block * rows, 8), rows), :] = value


def polynomial(parts):
    gram = dot_parts(parts, parts, ((1,), (1,)))
    gram_parts = split(gram)
    return CUBIC_COEFF * gram + QUINTIC_COEFF * dot_parts(gram_parts, gram_parts)


def iterate(x, steps):
    for _ in range(steps):
        parts = split(x)
        x = LINEAR_COEFF * x + dot_parts(split(polynomial(parts)), parts)
    return x


def products_kernel(hops, l_stat_ref, r_stat_ref, l_basis_ref, r_basis_ref, got_ref, *refs):
    left = is_left()
    outs = refs[-9:]
    grad_ref, stat_ref, power_ref, basis_ref, right_ref, inner_ref, other_ref, copy_ref, scratch = outs
    if hops:
        grads_ref, mine_refs, theirs_refs = refs[0], refs[1 : 1 + len(hops)], refs[1 + len(hops) : 1 + 2 * len(hops)]
        rows = grads_ref.shape[1]
        here = lax.axis_index("shard") // 2
        parity = lax.axis_index("shard") % 2
        start = l_basis_ref.shape[0]
        received = [got_ref[pl.ds(start + k * rows, rows), :] for k in range(grad_ref.shape[1] // LANES)]
        place_rows(grad_ref, 2 * here + parity, rows, grads_ref[here])
        place_rows(grad_ref, 2 * here + 1 - parity, rows, jnp.concatenate(received, axis=1))
        for hop, mine, theirs in zip(hops, mine_refs, theirs_refs):
            place_rows(grad_ref, 2 * (here ^ hop) + parity, rows, mine[...])
            place_rows(grad_ref, 2 * (here ^ hop) + 1 - parity, rows, theirs[...])
    else:
        grad_ref[...] = refs[0][...]
    own = pick(left, thirds(l_basis_ref), thirds(r_basis_ref))
    got = thirds(got_ref, 0, l_basis_ref.shape[0])
    first = is_first()
    basis = whole_of(scratch, pick(first, own, got), pick(first, got, own))
    basis_ref[...] = basis
    known = known_part(first, pick(left, thirds(l_stat_ref), thirds(r_stat_ref)), scratch)
    other_ref[...] = jnp.where(left, r_stat_ref[...], l_stat_ref[...])
    copy_ref[...] = l_basis_ref[...]
    right = half_of(scratch, thirds(r_basis_ref))
    right_ref[...] = right
    grad = grad_ref[...]
    parts = split(jnp.where(left, grad, grad.T))
    stat = 0.5 * known + 0.5 * symmetric_dot(parts, parts, ((1,), (1,)))
    stat_ref[...] = stat
    power_ref[...] = dot(stat, basis)
    inner_ref[...] = dot(grad, right)


def begin_kernel(steps, corner_ref, power_ref, basis_ref, x_ref, scratch):
    first = is_first()
    corner = corner_part(corner_ref, scratch)
    rows, wide = corner.shape
    basis = jnp.where(first, basis_ref[pl.ds(rows, rows), :], basis_ref[pl.ds(0, rows), :])
    basis = jnp.concatenate([basis, jnp.zeros((wide - rows, 2 * rows), F32)], axis=0)
    term = 0.5 * dot(corner, basis)
    power = power_ref[...] + jnp.concatenate([jnp.where(first, 0.0, term), jnp.where(first, term, 0.0)], axis=0)
    x_ref[...] = iterate(power * (1.0 / jnp.sqrt(jnp.sum(power * power) + NORM_EPS)), steps)


def rows_for(hops, outer_ref, right_parts, out_ref, offset):
    rows = out_ref.shape[1]
    here = lax.axis_index("shard") // 2
    starts = [pl.multiple_of((2 * (here ^ hop) + offset) * rows, 8) if hops else 0 for hop in (0, *hops)]
    outer = [outer_ref[pl.ds(start, rows), :] for start in starts]
    partial = dot_parts(split(jnp.concatenate(outer, axis=0)), right_parts, ((1,), (1,)))
    for k in range(len(starts)):
        out_ref[k] = partial[k * rows : (k + 1) * rows]


def update_kernel(
    hops,
    inner_ref,
    basis_ref,
    left_ref,
    right_ref,
    other_left_ref,
    one_ref,
    two_ref,
    start_ref,
    new_one_ref,
    new_two_ref,
    theirs_ref,
    outer_ref,
    x_ref,
    scratch,
):
    left, first = is_left(), is_first()
    x = start_ref[...]
    parts = split(x)
    gram = dot_parts(parts, parts, ((1,), (1,)))
    own, got = thirds(left_ref), thirds(other_left_ref)
    basis_left = jnp.where(left, basis_ref[...], whole_of(scratch, pick(first, own, got), pick(first, got, own)))
    rotated = dot(basis_left.T, inner_ref[...])
    gram_parts = split(gram)
    square = dot_parts(gram_parts, gram_parts)
    rotated = flat_of(scratch, rotated)
    ones = thirds(one_ref)
    twos = thirds(two_ref)
    new_one = [BETA_ONE * m + (1.0 - BETA_ONE) * r for m, r in zip(ones, rotated)]
    new_two = [BETA_TWO * v + (1.0 - BETA_TWO) * r * r for v, r in zip(twos, rotated)]
    put_thirds(new_one_ref, new_one)
    put_thirds(new_two_ref, new_two)
    direction = [m / (jnp.sqrt(v) + ADAM_EPS) for m, v in zip(new_one, new_two)]
    outer_ref[...] = dot_parts(split(basis_left), split(half_of(scratch, direction)))
    poly_parts = split(CUBIC_COEFF * gram + QUINTIC_COEFF * square)
    moved = dot_parts(poly_parts, parts)
    rows_for(hops, outer_ref, split(right_ref[...]), theirs_ref, 1 - lax.axis_index("shard") % 2)
    x_ref[...] = LINEAR_COEFF * x + moved


def end_kernel(hops, steps, start_ref, outer_ref, right_ref, x_ref, poly_ref, send_ref, mine_ref, scratch):
    x = iterate(start_ref[...], steps - 1)
    x_ref[...] = x
    rows_for(hops, outer_ref, split(right_ref[...]), mine_ref, lax.axis_index("shard") % 2)
    poly = polynomial(split(x))
    poly_ref[...] = poly
    half = take_half(x, jnp.logical_not(is_first()))
    put_thirds(send_ref, flat_of(scratch, LINEAR_COEFF * half + dot(poly, half)))


def add_kernel(mine_ref, theirs_ref, *out_refs):
    for k, out_ref in enumerate(out_refs):
        out_ref[...] = mine_ref[k] + theirs_ref[k]


def bases_kernel(keep_ref, back_ref, new_left_ref, new_right_ref, sems):
    left = is_left()

    def copies(own_ref, other_ref):
        return [
            pltpu.make_async_copy(keep_ref, own_ref, sems.at[0]),
            pltpu.make_async_copy(back_ref, other_ref, sems.at[1]),
        ]

    @pl.when(left)
    def _():
        for copy in copies(new_left_ref, new_right_ref):
            copy.start()

    @pl.when(jnp.logical_not(left))
    def _():
        for copy in copies(new_right_ref, new_left_ref):
            copy.start()

    for copy in copies(new_left_ref, new_right_ref):
        copy.wait()


def rows_kernel(hops, *refs):
    rows_refs, (update_ref, sems) = refs[:-2], refs[-2:]
    here = lax.axis_index("shard") // 2
    copies = [
        pltpu.make_async_copy(rows_refs[k], update_ref.at[here ^ hop], sems.at[k]) for k, hop in enumerate((0, *hops))
    ]
    for copy in copies:
        copy.start()
    for copy in copies:
        copy.wait()


def rest_kernel(x_ref, poly_ref, grad_ref, new_stat_ref, other_ref, keep_ref, new_left_ref, new_right_ref, scratch):
    left = is_left()
    first = is_first()
    half = take_half(x_ref[...], first)
    put_thirds(keep_ref, flat_of(scratch, LINEAR_COEFF * half + dot(poly_ref[...], half)))
    grad = grad_ref[...]
    turned = grad.T
    a = jnp.where(left, grad, turned)
    b = jnp.where(left, turned, grad)
    new_own = flat_of(scratch, take_half(new_stat_ref[...], first))
    product = flat_of(scratch, dot(b, take_half(a, first)))
    new_other = [0.5 * u + 0.5 * v for u, v in zip(thirds(other_ref), product)]
    put_thirds(new_left_ref, pick(left, new_own, new_other))
    put_thirds(new_right_ref, pick(left, new_other, new_own))


def call(kernel, outs, scratch, products, full, name, copies=0, kind=jax.ShapeDtypeStruct, **specs):
    size = full * full
    scratch = [pltpu.VMEM(s, F32) for s in scratch]
    if copies:
        scratch.append(pltpu.SemaphoreType.DMA((copies,)))
    return pl.pallas_call(
        kernel,
        out_shape=[kind(s, F32) for s in outs],
        scratch_shapes=scratch,
        compiler_params=pltpu.CompilerParams(vmem_limit_bytes=40 * 1024 * 1024),
        cost_estimate=pl.CostEstimate(flops=int(products * 6 * full * size), bytes_accessed=16 * size, transcendentals=0),
        name=name,
        **specs,
    )


def anywhere(count):
    return [pl.BlockSpec(memory_space=pl.ANY)] * count


def after(x, *others):
    return lax.optimization_barrier((x, *others))[0]


def local(grads, moment_one, moment_two, left_stat, right_stat, left_basis, right_basis):
    tiles_here, rows_here, full = grads.shape
    size = lax.axis_size("shard")
    flat_rows = full * (full // 2) // LANES
    flat = (flat_rows, LANES)
    square = (full, full)
    block = (rows_here, full)
    parity = lax.axis_index("shard") % 2
    pairs = [(i, i ^ 1) for i in range(size)]
    sides = [list(range(k, size, 2)) for k in range(2)]
    near = size in (4, 8) and rows_here % 8 == 0
    hops = {4: (1,), 8: (2, 3, 1)}[size] if near else ()
    strips = (tiles_here, *block) if near else (1, full, full)

    def exchange(x):
        return lax.all_to_all(x, "shard", split_axis=0, concat_axis=0, axis_index_groups=sides, tiled=True)

    def hop_by(x, hop):
        return lax.ppermute(x, "shard", [(i, i ^ (2 * hop)) for i in range(size)])

    def partner(x):
        return lax.ppermute(x, "shard", pairs)

    one, two, l_stat, r_stat, l_basis, r_basis = (
        x.reshape(flat) for x in (moment_one, moment_two, left_stat, right_stat, left_basis, right_basis)
    )
    count = corner_rows(flat_rows)
    outgoing_rows = flat_rows + (rows_here * (full // LANES) if near else 0)
    outgoing, corner, *pieces = call(
        functools.partial(pack_kernel, hops),
        [(outgoing_rows, LANES), (count, LANES)] + [block] * len(hops),
        [(flat_rows // 2, LANES)],
        0.1,
        full,
        "pack",
        copies=2 + len(hops) + full // LANES,
        kind=pltpu.VMEM,
        in_specs=anywhere(5),
        out_specs=anywhere(1) + [pl.BlockSpec(memory_space=pltpu.VMEM)] + anywhere(len(hops)),
    )(*(pltpu.with_memory_space_constraint(x, pltpu.HBM) for x in (l_stat, r_stat, l_basis, r_basis, grads)))
    got = partner(outgoing)
    if near:
        mine = [hop_by(piece, hop) for hop, piece in zip(hops, pieces)]
        theirs = [partner(x) for x in mine]
        rows = (grads, *mine, *theirs)
    else:
        mine = exchange(grads)
        theirs = partner(mine)
        even, odd = jnp.where(parity == 0, mine, theirs), jnp.where(parity == 0, theirs, mine)
        rows = (jnp.stack([even, odd], axis=1).reshape(square),)
        mine = [mine]
    got_corner = partner(after(corner, theirs[0] if near else mine[0]))
    grad, new_stat, power, basis, right, inner, other, left = call(
        functools.partial(products_kernel, hops),
        [square, square, square, square, (full, 2 * LANES), (full, 2 * LANES), flat, flat],
        [(3, full, LANES)],
        2,
        full,
        "products",
    )(l_stat, r_stat, l_basis, r_basis, got, *rows)
    tensors = lax.axis_size("tensor")
    place = lambda t, i: i * tensors + t
    cycle = []
    for t in range(0, tensors - tensors % 2, 2):
        for i in range(0, size, 2):
            cycle += [(place(t, i), place(t, i + 1)), (place(t, i + 1), place(t + 1, i + 1))]
            cycle += [(place(t + 1, i + 1), place(t + 1, i)), (place(t + 1, i), place(t, i))]
    cycle += [(place(t, i), place(t, i ^ 1)) for t in range(tensors - tensors % 2, tensors) for i in range(size)]
    other_left = lax.ppermute(after(l_basis, *(theirs[:2] if near else mine)), ("shard", "tensor"), cycle)
    (x,) = call(
        functools.partial(begin_kernel, EARLY_ITERS), [square], [(2, full // 2, LANES)], 7, full, "begin"
    )(got_corner, power, basis)
    wide = (full, 2 * LANES)
    new_one, new_two, other_rows, outer, x = call(
        functools.partial(update_kernel, hops), [flat, flat, strips, wide, square], [(3, full, LANES)], 5, full, "update"
    )(inner, basis, left, right, other_left, one, two, x)
    if not near:
        partial = other_rows.reshape(tiles_here, 2, rows_here, full)
        other_rows = lax.dynamic_index_in_dim(partial, 1 - parity, 1, keepdims=False)
    got_rows = partner(other_rows)
    x, poly, send, own_rows = call(
        functools.partial(end_kernel, hops, NS_ITERS - EARLY_ITERS - 1),
        [square, square, flat, strips],
        [(3, full, LANES)],
        9,
        full,
        "end",
    )(after(x, other_rows), outer, right)
    back = partner(send)
    keep, new_left, new_right = call(rest_kernel, [flat, flat, flat], [(3, full, LANES)], 1.5, full, "rest")(
        x, poly, grad, new_stat, other
    )
    if near:
        kept, *sums = call(add_kernel, [block] * (1 + len(hops)), [], 0.1, full, "add")(
            after(own_rows, send), after(got_rows, send)
        )
        returned = [hop_by(x, hop) for hop, x in zip(hops, sums)]
        update = call(
            functools.partial(rows_kernel, hops),
            [grads.shape],
            [],
            0.1,
            full,
            "rows",
            copies=1 + len(hops),
            in_specs=anywhere(1 + len(hops)),
            out_specs=anywhere(1),
        )(kept, *returned)[0]
    else:
        own_rows = lax.dynamic_index_in_dim(partial, parity, 1, keepdims=False)
        update = exchange(after(own_rows, send) + after(got_rows, send))
    new_l_basis, new_r_basis = call(
        bases_kernel, [flat, flat], [], 0.1, full, "bases", copies=2, in_specs=anywhere(2), out_specs=anywhere(2)
    )(keep, back)
    halves = (new_one, new_two, new_left, new_right, new_l_basis, new_r_basis)
    return (update, *(x.reshape(1, flat_rows * LANES) for x in halves))


def solution(mesh):
    halves = P(("tensor", "shard"), None)
    rows = P("tensor", "shard", None)
    return jax.shard_map(
        local, mesh=mesh, in_specs=(rows,) + (halves,) * 6, out_specs=(rows,) + (halves,) * 6, check_vma=False
    )
```

```python
import functools

import jax
import jax.numpy as jnp
from jax import lax
from jax.experimental import pallas as pl
from jax.experimental.pallas import tpu as pltpu
from jax.sharding import PartitionSpec as P

NS_ITERS = 5
EARLY_ITERS = 1
BETA_ONE = 0.9
BETA_TWO = 0.95
ADAM_EPS = 1e-08
NORM_EPS = 1e-06
LINEAR_COEFF = 3.4445
CUBIC_COEFF = -4.775
QUINTIC_COEFF = 2.0315
LANES = 128
F32 = jnp.float32


def split(x):
    high = x.astype(jnp.bfloat16)
    return high, (x - high.astype(F32)).astype(jnp.bfloat16)


def dot(a, b, dims=((1,), (0,))):
    return dot_parts(split(a), split(b), dims)


def dot_parts(a, b, dims=((1,), (0,))):
    (ka,), (kb,) = dims
    left = jnp.concatenate([a[0], a[0], a[1]], axis=ka)
    right = jnp.concatenate([b[0], b[1], b[0]], axis=kb)
    return lax.dot_general(left, right, (dims, ((), ())), preferred_element_type=F32)


def symmetric_dot(a, b, dims=((1,), (0,))):
    (ka,), (kb,) = dims
    cut = a[0].shape[0] - LANES
    head = lambda x, axis: lax.slice_in_dim(x, 0, cut, axis=axis)
    tail = lambda x, axis: lax.slice_in_dim(x, cut, cut + LANES, axis=axis)
    left = dot_parts(a, [head(x, 1 - kb) for x in b], dims)
    corner = dot_parts([tail(x, 1 - ka) for x in a], [tail(x, 1 - kb) for x in b], dims)
    right = jnp.concatenate([left[cut:].T, corner], axis=0)
    return jnp.concatenate([left, right], axis=1)


def swap(x):
    return pltpu.roll(x, LANES // 2, 1)


def low_lanes(shape):
    return lax.broadcasted_iota(jnp.int32, shape, 1) < LANES // 2


def pick(flag, x, y):
    return [jnp.where(flag, u, v) for u, v in zip(x, y)]


def thirds(ref, start=0, rows=None):
    rows = ref.shape[0] if rows is None else rows
    return [ref[pl.ds(start + k, rows // 3, stride=3), :] for k in range(3)]


def put_thirds(ref, parts):
    for k in range(3):
        ref[pl.ds(k, parts[k].shape[0], stride=3), :] = parts[k]


def interleave(scratch, index, even, odd):
    scratch[index, pl.ds(0, even.shape[0], stride=2), :] = even
    scratch[index, pl.ds(1, odd.shape[0], stride=2), :] = odd


def whole_of(scratch, first, second):
    a, b, c = first
    d, e, f = second
    low = low_lanes(a.shape)
    sb, sc, sd, se = swap(b), swap(c), swap(d), swap(e)
    interleave(scratch, 0, a, jnp.where(low, sb, sc))
    interleave(scratch, 1, jnp.where(low, b, sd), jnp.where(low, sc, e))
    interleave(scratch, 2, jnp.where(low, sd, se), f)
    return jnp.concatenate([scratch[0], scratch[1], scratch[2]], axis=1)


def half_of(scratch, flat):
    a, b, c = flat
    low = low_lanes(a.shape)
    sb, sc = swap(b), swap(c)
    interleave(scratch, 0, a, jnp.where(low, sb, sc))
    interleave(scratch, 1, jnp.where(low, b, 0.0), jnp.where(low, sc, 0.0))
    return jnp.concatenate([scratch[0], scratch[1]], axis=1)


def flat_of(scratch, half):
    scratch[0] = half[:, :LANES]
    scratch[1] = half[:, LANES:]
    pairs = half.shape[0] // 2
    even0 = scratch[0, pl.ds(0, pairs, stride=2), :]
    odd0 = swap(scratch[0, pl.ds(1, pairs, stride=2), :])
    even1 = scratch[1, pl.ds(0, pairs, stride=2), :]
    odd1 = swap(scratch[1, pl.ds(1, pairs, stride=2), :])
    low = low_lanes(even0.shape)
    return [even0, jnp.where(low, even1, odd0), jnp.where(low, odd0, odd1)]


def take_half(whole, first):
    one, two, three = whole[:, :LANES], whole[:, LANES : 2 * LANES], whole[:, 2 * LANES :]
    low = low_lanes(one.shape)
    s2, s3 = swap(two), swap(three)
    head = jnp.where(first, one, jnp.where(low, s2, s3))
    tail = jnp.where(low, jnp.where(first, two, s3), 0.0)
    return jnp.concatenate([head, tail], axis=1)


def is_first():
    return lax.rem(lax.axis_index("shard"), 2) == 0


def is_left():
    return lax.rem(lax.axis_index("shard") + lax.axis_index("tensor"), 2) == 0


def pack_kernel(hops, l_stat_ref, r_stat_ref, l_basis_ref, r_basis_ref, grads_ref, *refs):
    out_ref, small_ref, *refs = refs
    piece_refs, (corner, sems) = refs[: len(hops)], refs[len(hops) :]
    left = is_left()
    flat_rows = l_basis_ref.shape[0]
    half_rows = flat_rows // 2
    rows = grads_ref.shape[1]
    here = lax.axis_index("shard") // 2

    start = pl.multiple_of(jnp.where(is_first(), 0, half_rows), 8)

    def copies(basis_ref, stat_ref):
        return [
            pltpu.make_async_copy(stat_ref.at[pl.ds(start, half_rows)], corner, sems.at[0]),
            pltpu.make_async_copy(basis_ref, out_ref.at[pl.ds(0, flat_rows)], sems.at[1]),
        ]

    @pl.when(left)
    def _():
        for copy in copies(r_basis_ref, r_stat_ref):
            copy.start()

    @pl.when(jnp.logical_not(left))
    def _():
        for copy in copies(l_basis_ref, l_stat_ref):
            copy.start()

    more = []
    for number, (hop, piece_ref) in enumerate(zip(hops, piece_refs)):
        more.append(pltpu.make_async_copy(grads_ref.at[here ^ hop], piece_ref, sems.at[2 + number]))
    if hops:
        for k in range(grads_ref.shape[2] // LANES):
            source = grads_ref.at[here, :, pl.ds(k * LANES, LANES)]
            target = out_ref.at[pl.ds(flat_rows + k * rows, rows)]
            more.append(pltpu.make_async_copy(source, target, sems.at[2 + len(hops) + k]))
    for copy in more:
        copy.start()
    first, second = copies(l_basis_ref, l_stat_ref)
    first.wait()
    third = half_rows // 9
    a, b, c = thirds(corner)
    low = low_lanes((third, LANES))
    middle = slice(third, 2 * third)
    small_ref[pl.ds(0, third)] = jnp.where(low, a[:third], b[:third])
    small_ref[pl.ds(third, third)] = a[middle]
    small_ref[pl.ds(2 * third, third)] = jnp.where(low, swap(b[middle]), swap(c[middle]))
    small_ref[pl.ds(3 * third, 3 * third)] = corner[pl.ds(6 * third, 3 * third)]
    for copy in [second, *more]:
        copy.wait()


def corner_rows(flat_rows):
    return flat_rows // 3


def unpack_corner(got_ref):
    third = got_ref.shape[0] // 6
    small = got_ref[pl.ds(0, third), :]
    even = got_ref[pl.ds(third, third), :]
    odd = swap(got_ref[pl.ds(2 * third, third), :])
    a, b, c = thirds(got_ref, 3 * third, 3 * third)
    low = low_lanes(small.shape)
    zero = jnp.zeros_like(small)
    return [
        jnp.concatenate([jnp.where(low, small, zero), even, a], axis=0),
        jnp.concatenate([jnp.where(low, zero, small), jnp.where(low, zero, odd), b], axis=0),
        jnp.concatenate([zero, jnp.where(low, odd, zero), c], axis=0),
    ]


def known_part(first, own, scratch):
    zeros = [jnp.zeros_like(x) for x in own]
    known = whole_of(scratch, pick(first, own, zeros), pick(first, zeros, own))
    half = known.shape[0] // 2
    row = lax.broadcasted_iota(jnp.int32, known.shape, 0)
    column = lax.broadcasted_iota(jnp.int32, known.shape, 1)
    missing = (jnp.where(first, row, column) < half) & (jnp.where(first, column, row) >= half)
    return jnp.where(missing, known.T, known)


def corner_part(corner_ref, scratch):
    corner = half_of(scratch, unpack_corner(corner_ref))
    rows, wide = corner.shape
    turned = jnp.concatenate([corner, jnp.zeros((wide - rows, wide), F32)], axis=0).T[:rows]
    part = rows // 3
    row = lax.broadcasted_iota(jnp.int32, corner.shape, 0)
    column = lax.broadcasted_iota(jnp.int32, corner.shape, 1)
    missing = (row < 2 * part) & (column >= jnp.where(row < part, part, 2 * part))
    return jnp.where(missing, turned, corner)


def place_rows(grad_ref, block, rows, value):
    grad_ref[pl.ds(pl.multiple_of(block * rows, 8), rows), :] = value


def polynomial(parts):
    gram = dot_parts(parts, parts, ((1,), (1,)))
    gram_parts = split(gram)
    return CUBIC_COEFF * gram + QUINTIC_COEFF * dot_parts(gram_parts, gram_parts)


def iterate(x, steps):
    for _ in range(steps):
        parts = split(x)
        x = LINEAR_COEFF * x + dot_parts(split(polynomial(parts)), parts)
    return x


def products_kernel(hops, l_stat_ref, r_stat_ref, l_basis_ref, r_basis_ref, got_ref, *refs):
    left = is_left()
    outs = refs[-9:]
    grad_ref, stat_ref, power_ref, basis_ref, right_ref, inner_ref, other_ref, copy_ref, scratch = outs
    if hops:
        grads_ref, mine_refs, theirs_refs = refs[0], refs[1 : 1 + len(hops)], refs[1 + len(hops) : 1 + 2 * len(hops)]
        rows = grads_ref.shape[1]
        here = lax.axis_index("shard") // 2
        parity = lax.axis_index("shard") % 2
        start = l_basis_ref.shape[0]
        received = [got_ref[pl.ds(start + k * rows, rows), :] for k in range(grad_ref.shape[1] // LANES)]
        place_rows(grad_ref, 2 * here + parity, rows, grads_ref[here])
        place_rows(grad_ref, 2 * here + 1 - parity, rows, jnp.concatenate(received, axis=1))
        for hop, mine, theirs in zip(hops, mine_refs, theirs_refs):
            place_rows(grad_ref, 2 * (here ^ hop) + parity, rows, mine[...])
            place_rows(grad_ref, 2 * (here ^ hop) + 1 - parity, rows, theirs[...])
    else:
        grad_ref[...] = refs[0][...]
    own = pick(left, thirds(l_basis_ref), thirds(r_basis_ref))
    got = thirds(got_ref, 0, l_basis_ref.shape[0])
    first = is_first()
    basis = whole_of(scratch, pick(first, own, got), pick(first, got, own))
    basis_ref[...] = basis
    known = known_part(first, pick(left, thirds(l_stat_ref), thirds(r_stat_ref)), scratch)
    other_ref[...] = jnp.where(left, r_stat_ref[...], l_stat_ref[...])
    copy_ref[...] = l_basis_ref[...]
    right = half_of(scratch, thirds(r_basis_ref))
    right_ref[...] = right
    grad = grad_ref[...]
    parts = split(jnp.where(left, grad, grad.T))
    stat = 0.5 * known + 0.5 * symmetric_dot(parts, parts, ((1,), (1,)))
    stat_ref[...] = stat
    power_ref[...] = dot(stat, basis)
    inner_ref[...] = dot(grad, right)


def begin_kernel(steps, corner_ref, power_ref, basis_ref, x_ref, scratch):
    first = is_first()
    corner = corner_part(corner_ref, scratch)
    rows, wide = corner.shape
    basis = jnp.where(first, basis_ref[pl.ds(rows, rows), :], basis_ref[pl.ds(0, rows), :])
    basis = jnp.concatenate([basis, jnp.zeros((wide - rows, 2 * rows), F32)], axis=0)
    term = 0.5 * dot(corner, basis)
    power = power_ref[...] + jnp.concatenate([jnp.where(first, 0.0, term), jnp.where(first, term, 0.0)], axis=0)
    x_ref[...] = iterate(power * (1.0 / jnp.sqrt(jnp.sum(power * power) + NORM_EPS)), steps)


def rows_for(hops, outer_ref, right_parts, out_ref, offset):
    rows = out_ref.shape[1]
    here = lax.axis_index("shard") // 2
    starts = [pl.multiple_of((2 * (here ^ hop) + offset) * rows, 8) if hops else 0 for hop in (0, *hops)]
    outer = [outer_ref[pl.ds(start, rows), :] for start in starts]
    partial = dot_parts(split(jnp.concatenate(outer, axis=0)), right_parts, ((1,), (1,)))
    for k in range(len(starts)):
        out_ref[k] = partial[k * rows : (k + 1) * rows]


def update_kernel(
    hops,
    inner_ref,
    basis_ref,
    left_ref,
    right_ref,
    other_left_ref,
    one_ref,
    two_ref,
    start_ref,
    new_one_ref,
    new_two_ref,
    theirs_ref,
    outer_ref,
    x_ref,
    scratch,
):
    left, first = is_left(), is_first()
    x = start_ref[...]
    parts = split(x)
    gram = dot_parts(parts, parts, ((1,), (1,)))
    own, got = thirds(left_ref), thirds(other_left_ref)
    basis_left = jnp.where(left, basis_ref[...], whole_of(scratch, pick(first, own, got), pick(first, got, own)))
    rotated = dot(basis_left.T, inner_ref[...])
    gram_parts = split(gram)
    square = dot_parts(gram_parts, gram_parts)
    rotated = flat_of(scratch, rotated)
    ones = thirds(one_ref)
    twos = thirds(two_ref)
    new_one = [BETA_ONE * m + (1.0 - BETA_ONE) * r for m, r in zip(ones, rotated)]
    new_two = [BETA_TWO * v + (1.0 - BETA_TWO) * r * r for v, r in zip(twos, rotated)]
    put_thirds(new_one_ref, new_one)
    put_thirds(new_two_ref, new_two)
    direction = [m / (jnp.sqrt(v) + ADAM_EPS) for m, v in zip(new_one, new_two)]
    outer_ref[...] = dot_parts(split(basis_left), split(half_of(scratch, direction)))
    poly_parts = split(CUBIC_COEFF * gram + QUINTIC_COEFF * square)
    moved = dot_parts(poly_parts, parts)
    rows_for(hops, outer_ref, split(right_ref[...]), theirs_ref, 1 - lax.axis_index("shard") % 2)
    x_ref[...] = LINEAR_COEFF * x + moved


def end_kernel(hops, steps, start_ref, outer_ref, right_ref, x_ref, poly_ref, send_ref, mine_ref, scratch):
    x = iterate(start_ref[...], steps - 1)
    x_ref[...] = x
    rows_for(hops, outer_ref, split(right_ref[...]), mine_ref, lax.axis_index("shard") % 2)
    poly = polynomial(split(x))
    poly_ref[...] = poly
    half = take_half(x, jnp.logical_not(is_first()))
    put_thirds(send_ref, flat_of(scratch, LINEAR_COEFF * half + dot(poly, half)))


def add_kernel(mine_ref, theirs_ref, *out_refs):
    for k, out_ref in enumerate(out_refs):
        out_ref[...] = mine_ref[k] + theirs_ref[k]


def bases_kernel(keep_ref, back_ref, new_left_ref, new_right_ref, sems):
    left = is_left()

    def copies(own_ref, other_ref):
        return [
            pltpu.make_async_copy(keep_ref, own_ref, sems.at[0]),
            pltpu.make_async_copy(back_ref, other_ref, sems.at[1]),
        ]

    @pl.when(left)
    def _():
        for copy in copies(new_left_ref, new_right_ref):
            copy.start()

    @pl.when(jnp.logical_not(left))
    def _():
        for copy in copies(new_right_ref, new_left_ref):
            copy.start()

    for copy in copies(new_left_ref, new_right_ref):
        copy.wait()


def rows_kernel(hops, *refs):
    rows_refs, (update_ref, sems) = refs[:-2], refs[-2:]
    here = lax.axis_index("shard") // 2
    copies = [
        pltpu.make_async_copy(rows_refs[k], update_ref.at[here ^ hop], sems.at[k]) for k, hop in enumerate((0, *hops))
    ]
    for copy in copies:
        copy.start()
    for copy in copies:
        copy.wait()


def rest_kernel(x_ref, poly_ref, grad_ref, new_stat_ref, other_ref, keep_ref, new_left_ref, new_right_ref, scratch):
    left = is_left()
    first = is_first()
    half = take_half(x_ref[...], first)
    put_thirds(keep_ref, flat_of(scratch, LINEAR_COEFF * half + dot(poly_ref[...], half)))
    grad = grad_ref[...]
    turned = grad.T
    a = jnp.where(left, grad, turned)
    b = jnp.where(left, turned, grad)
    new_own = flat_of(scratch, take_half(new_stat_ref[...], first))
    product = flat_of(scratch, dot(b, take_half(a, first)))
    new_other = [0.5 * u + 0.5 * v for u, v in zip(thirds(other_ref), product)]
    put_thirds(new_left_ref, pick(left, new_own, new_other))
    put_thirds(new_right_ref, pick(left, new_other, new_own))


def call(kernel, outs, scratch, products, full, name, copies=0, kind=jax.ShapeDtypeStruct, **specs):
    size = full * full
    scratch = [pltpu.VMEM(s, F32) for s in scratch]
    if copies:
        scratch.append(pltpu.SemaphoreType.DMA((copies,)))
    return pl.pallas_call(
        kernel,
        out_shape=[kind(s, F32) for s in outs],
        scratch_shapes=scratch,
        compiler_params=pltpu.CompilerParams(vmem_limit_bytes=40 * 1024 * 1024),
        cost_estimate=pl.CostEstimate(flops=int(products * 6 * full * size), bytes_accessed=16 * size, transcendentals=0),
        name=name,
        **specs,
    )


def anywhere(count):
    return [pl.BlockSpec(memory_space=pl.ANY)] * count


def after(x, *others):
    return lax.optimization_barrier((x, *others))[0]


def local(grads, moment_one, moment_two, left_stat, right_stat, left_basis, right_basis):
    tiles_here, rows_here, full = grads.shape
    size = lax.axis_size("shard")
    flat_rows = full * (full // 2) // LANES
    flat = (flat_rows, LANES)
    square = (full, full)
    block = (rows_here, full)
    parity = lax.axis_index("shard") % 2
    pairs = [(i, i ^ 1) for i in range(size)]
    sides = [list(range(k, size, 2)) for k in range(2)]
    near = size in (4, 8) and rows_here % 8 == 0
    hops = {4: (1,), 8: (2, 3, 1)}[size] if near else ()
    strips = (tiles_here, *block) if near else (1, full, full)

    def exchange(x):
        return lax.all_to_all(x, "shard", split_axis=0, concat_axis=0, axis_index_groups=sides, tiled=True)

    def hop_by(x, hop):
        return lax.ppermute(x, "shard", [(i, i ^ (2 * hop)) for i in range(size)])

    def partner(x):
        return lax.ppermute(x, "shard", pairs)

    one, two, l_stat, r_stat, l_basis, r_basis = (
        x.reshape(flat) for x in (moment_one, moment_two, left_stat, right_stat, left_basis, right_basis)
    )
    count = corner_rows(flat_rows)
    outgoing_rows = flat_rows + (rows_here * (full // LANES) if near else 0)
    outgoing, corner, *pieces = call(
        functools.partial(pack_kernel, hops),
        [(outgoing_rows, LANES), (count, LANES)] + [block] * len(hops),
        [(flat_rows // 2, LANES)],
        0.1,
        full,
        "pack",
        copies=2 + len(hops) + full // LANES,
        kind=pltpu.VMEM,
        in_specs=anywhere(5),
        out_specs=anywhere(1) + [pl.BlockSpec(memory_space=pltpu.VMEM)] + anywhere(len(hops)),
    )(*(pltpu.with_memory_space_constraint(x, pltpu.HBM) for x in (l_stat, r_stat, l_basis, r_basis, grads)))
    got = partner(outgoing)
    if near:
        mine = [hop_by(piece, hop) for hop, piece in zip(hops, pieces)]
        theirs = [partner(x) for x in mine]
        rows = (grads, *mine, *theirs)
    else:
        mine = exchange(grads)
        theirs = partner(mine)
        even, odd = jnp.where(parity == 0, mine, theirs), jnp.where(parity == 0, theirs, mine)
        rows = (jnp.stack([even, odd], axis=1).reshape(square),)
        mine = [mine]
    got_corner = partner(after(corner, theirs[0] if near else mine[0]))
    grad, new_stat, power, basis, right, inner, other, left = call(
        functools.partial(products_kernel, hops),
        [square, square, square, square, (full, 2 * LANES), (full, 2 * LANES), flat, flat],
        [(3, full, LANES)],
        2,
        full,
        "products",
    )(l_stat, r_stat, l_basis, r_basis, got, *rows)
    tensors = lax.axis_size("tensor")
    one_way = [(i * tensors + t, (i ^ 1) * tensors + t) for i in range(size) for t in range(tensors) if (i + t) % 2 == 0]
    other_left = lax.ppermute(after(l_basis, *(theirs[:2] if near else mine)), ("shard", "tensor"), one_way)
    (x,) = call(
        functools.partial(begin_kernel, EARLY_ITERS), [square], [(2, full // 2, LANES)], 7, full, "begin"
    )(got_corner, power, basis)
    wide = (full, 2 * LANES)
    new_one, new_two, other_rows, outer, x = call(
        functools.partial(update_kernel, hops), [flat, flat, strips, wide, square], [(3, full, LANES)], 5, full, "update"
    )(inner, basis, left, right, other_left, one, two, x)
    if not near:
        partial = other_rows.reshape(tiles_here, 2, rows_here, full)
        other_rows = lax.dynamic_index_in_dim(partial, 1 - parity, 1, keepdims=False)
    got_rows = partner(other_rows)
    x, poly, send, own_rows = call(
        functools.partial(end_kernel, hops, NS_ITERS - EARLY_ITERS - 1),
        [square, square, flat, strips],
        [(3, full, LANES)],
        9,
        full,
        "end",
    )(after(x, other_rows), outer, right)
    back = partner(send)
    keep, new_left, new_right = call(rest_kernel, [flat, flat, flat], [(3, full, LANES)], 1.5, full, "rest")(
        x, poly, grad, new_stat, other
    )
    if near:
        kept, *sums = call(add_kernel, [block] * (1 + len(hops)), [], 0.1, full, "add")(
            after(own_rows, send), after(got_rows, send)
        )
        returned = [hop_by(x, hop) for hop, x in zip(hops, sums)]
        update = call(
            functools.partial(rows_kernel, hops),
            [grads.shape],
            [],
            0.1,
            full,
            "rows",
            copies=1 + len(hops),
            in_specs=anywhere(1 + len(hops)),
            out_specs=anywhere(1),
        )(kept, *returned)[0]
    else:
        own_rows = lax.dynamic_index_in_dim(partial, parity, 1, keepdims=False)
        update = exchange(after(own_rows, send) + after(got_rows, send))
    new_l_basis, new_r_basis = call(
        bases_kernel, [flat, flat], [], 0.1, full, "bases", copies=2, in_specs=anywhere(2), out_specs=anywhere(2)
    )(keep, back)
    halves = (new_one, new_two, new_left, new_right, new_l_basis, new_r_basis)
    return (update, *(x.reshape(1, flat_rows * LANES) for x in halves))


def solution(mesh):
    halves = P(("tensor", "shard"), None)
    rows = P("tensor", "shard", None)
    return jax.shard_map(
        local, mesh=mesh, in_specs=(rows,) + (halves,) * 6, out_specs=(rows,) + (halves,) * 6, check_vma=False
    )
```

```python
import functools

import jax
import jax.numpy as jnp
from jax import lax
from jax.experimental import pallas as pl
from jax.experimental.pallas import tpu as pltpu
from jax.sharding import PartitionSpec as P

NS_ITERS = 5
EARLY_ITERS = 1
BETA_ONE = 0.9
BETA_TWO = 0.95
ADAM_EPS = 1e-08
NORM_EPS = 1e-06
LINEAR_COEFF = 3.4445
CUBIC_COEFF = -4.775
QUINTIC_COEFF = 2.0315
LANES = 128
F32 = jnp.float32


def split(x):
    high = x.astype(jnp.bfloat16)
    return high, (x - high.astype(F32)).astype(jnp.bfloat16)


def dot(a, b, dims=((1,), (0,))):
    return dot_parts(split(a), split(b), dims)


def dot_parts(a, b, dims=((1,), (0,))):
    (ka,), (kb,) = dims
    left = jnp.concatenate([a[0], a[0], a[1]], axis=ka)
    right = jnp.concatenate([b[0], b[1], b[0]], axis=kb)
    return lax.dot_general(left, right, (dims, ((), ())), preferred_element_type=F32)


def symmetric_dot(a, b, dims=((1,), (0,))):
    (ka,), (kb,) = dims
    cut = a[0].shape[0] - LANES
    head = lambda x, axis: lax.slice_in_dim(x, 0, cut, axis=axis)
    tail = lambda x, axis: lax.slice_in_dim(x, cut, cut + LANES, axis=axis)
    left = dot_parts(a, [head(x, 1 - kb) for x in b], dims)
    corner = dot_parts([tail(x, 1 - ka) for x in a], [tail(x, 1 - kb) for x in b], dims)
    right = jnp.concatenate([left[cut:].T, corner], axis=0)
    return jnp.concatenate([left, right], axis=1)


def swap(x):
    return pltpu.roll(x, LANES // 2, 1)


def low_lanes(shape):
    return lax.broadcasted_iota(jnp.int32, shape, 1) < LANES // 2


def pick(flag, x, y):
    return [jnp.where(flag, u, v) for u, v in zip(x, y)]


def thirds(ref, start=0, rows=None):
    rows = ref.shape[0] if rows is None else rows
    return [ref[pl.ds(start + k, rows // 3, stride=3), :] for k in range(3)]


def put_thirds(ref, parts):
    for k in range(3):
        ref[pl.ds(k, parts[k].shape[0], stride=3), :] = parts[k]


def interleave(scratch, index, even, odd):
    scratch[index, pl.ds(0, even.shape[0], stride=2), :] = even
    scratch[index, pl.ds(1, odd.shape[0], stride=2), :] = odd


def whole_of(scratch, first, second):
    a, b, c = first
    d, e, f = second
    low = low_lanes(a.shape)
    sb, sc, sd, se = swap(b), swap(c), swap(d), swap(e)
    interleave(scratch, 0, a, jnp.where(low, sb, sc))
    interleave(scratch, 1, jnp.where(low, b, sd), jnp.where(low, sc, e))
    interleave(scratch, 2, jnp.where(low, sd, se), f)
    return jnp.concatenate([scratch[0], scratch[1], scratch[2]], axis=1)


def half_of(scratch, flat):
    a, b, c = flat
    low = low_lanes(a.shape)
    sb, sc = swap(b), swap(c)
    interleave(scratch, 0, a, jnp.where(low, sb, sc))
    interleave(scratch, 1, jnp.where(low, b, 0.0), jnp.where(low, sc, 0.0))
    return jnp.concatenate([scratch[0], scratch[1]], axis=1)


def flat_of(scratch, half):
    scratch[0] = half[:, :LANES]
    scratch[1] = half[:, LANES:]
    pairs = half.shape[0] // 2
    even0 = scratch[0, pl.ds(0, pairs, stride=2), :]
    odd0 = swap(scratch[0, pl.ds(1, pairs, stride=2), :])
    even1 = scratch[1, pl.ds(0, pairs, stride=2), :]
    odd1 = swap(scratch[1, pl.ds(1, pairs, stride=2), :])
    low = low_lanes(even0.shape)
    return [even0, jnp.where(low, even1, odd0), jnp.where(low, odd0, odd1)]


def take_half(whole, first):
    one, two, three = whole[:, :LANES], whole[:, LANES : 2 * LANES], whole[:, 2 * LANES :]
    low = low_lanes(one.shape)
    s2, s3 = swap(two), swap(three)
    head = jnp.where(first, one, jnp.where(low, s2, s3))
    tail = jnp.where(low, jnp.where(first, two, s3), 0.0)
    return jnp.concatenate([head, tail], axis=1)


def is_first():
    return lax.rem(lax.axis_index("shard"), 2) == 0


def is_left():
    return lax.rem(lax.axis_index("shard") + lax.axis_index("tensor"), 2) == 0


def pack_kernel(hops, l_stat_ref, r_stat_ref, l_basis_ref, r_basis_ref, grads_ref, *refs):
    out_ref, small_ref, *refs = refs
    piece_refs, (corner, sems) = refs[: len(hops)], refs[len(hops) :]
    left = is_left()
    flat_rows = l_basis_ref.shape[0]
    half_rows = flat_rows // 2
    rows = grads_ref.shape[1]
    here = lax.axis_index("shard") // 2

    start = pl.multiple_of(jnp.where(is_first(), 0, half_rows), 8)

    def copies(basis_ref, stat_ref):
        return [
            pltpu.make_async_copy(stat_ref.at[pl.ds(start, half_rows)], corner, sems.at[0]),
            pltpu.make_async_copy(basis_ref, out_ref.at[pl.ds(0, flat_rows)], sems.at[1]),
        ]

    @pl.when(left)
    def _():
        for copy in copies(r_basis_ref, r_stat_ref):
            copy.start()

    @pl.when(jnp.logical_not(left))
    def _():
        for copy in copies(l_basis_ref, l_stat_ref):
            copy.start()

    more = []
    for number, (hop, piece_ref) in enumerate(zip(hops, piece_refs)):
        more.append(pltpu.make_async_copy(grads_ref.at[here ^ hop], piece_ref, sems.at[2 + number]))
    if hops:
        for k in range(grads_ref.shape[2] // LANES):
            source = grads_ref.at[here, :, pl.ds(k * LANES, LANES)]
            target = out_ref.at[pl.ds(flat_rows + k * rows, rows)]
            more.append(pltpu.make_async_copy(source, target, sems.at[2 + len(hops) + k]))
    for copy in more:
        copy.start()
    first, second = copies(l_basis_ref, l_stat_ref)
    first.wait()
    third = half_rows // 9
    a, b, c = thirds(corner)
    low = low_lanes((third, LANES))
    middle = slice(third, 2 * third)
    small_ref[pl.ds(0, third)] = jnp.where(low, a[:third], b[:third])
    small_ref[pl.ds(third, third)] = a[middle]
    small_ref[pl.ds(2 * third, third)] = jnp.where(low, swap(b[middle]), swap(c[middle]))
    small_ref[pl.ds(3 * third, 3 * third)] = corner[pl.ds(6 * third, 3 * third)]
    for copy in [second, *more]:
        copy.wait()


def corner_rows(flat_rows):
    return flat_rows // 3


def unpack_corner(got_ref):
    third = got_ref.shape[0] // 6
    small = got_ref[pl.ds(0, third), :]
    even = got_ref[pl.ds(third, third), :]
    odd = swap(got_ref[pl.ds(2 * third, third), :])
    a, b, c = thirds(got_ref, 3 * third, 3 * third)
    low = low_lanes(small.shape)
    zero = jnp.zeros_like(small)
    return [
        jnp.concatenate([jnp.where(low, small, zero), even, a], axis=0),
        jnp.concatenate([jnp.where(low, zero, small), jnp.where(low, zero, odd), b], axis=0),
        jnp.concatenate([zero, jnp.where(low, odd, zero), c], axis=0),
    ]


def known_part(first, own, scratch):
    zeros = [jnp.zeros_like(x) for x in own]
    known = whole_of(scratch, pick(first, own, zeros), pick(first, zeros, own))
    half = known.shape[0] // 2
    row = lax.broadcasted_iota(jnp.int32, known.shape, 0)
    column = lax.broadcasted_iota(jnp.int32, known.shape, 1)
    missing = (jnp.where(first, row, column) < half) & (jnp.where(first, column, row) >= half)
    return jnp.where(missing, known.T, known)


def corner_part(corner_ref, scratch):
    corner = half_of(scratch, unpack_corner(corner_ref))
    rows, wide = corner.shape
    turned = jnp.concatenate([corner, jnp.zeros((wide - rows, wide), F32)], axis=0).T[:rows]
    part = rows // 3
    row = lax.broadcasted_iota(jnp.int32, corner.shape, 0)
    column = lax.broadcasted_iota(jnp.int32, corner.shape, 1)
    missing = (row < 2 * part) & (column >= jnp.where(row < part, part, 2 * part))
    return jnp.where(missing, turned, corner)


def place_rows(grad_ref, block, rows, value):
    grad_ref[pl.ds(pl.multiple_of(block * rows, 8), rows), :] = value


def polynomial(parts):
    gram = dot_parts(parts, parts, ((1,), (1,)))
    gram_parts = split(gram)
    return CUBIC_COEFF * gram + QUINTIC_COEFF * dot_parts(gram_parts, gram_parts)


def iterate(x, steps):
    for _ in range(steps):
        parts = split(x)
        x = LINEAR_COEFF * x + dot_parts(split(polynomial(parts)), parts)
    return x


def prepare_kernel(
    l_stat_ref, r_stat_ref, l_basis_ref, r_basis_ref, got_ref, basis_ref, known_ref, right_ref, other_ref, copy_ref, scratch
):
    left, first = is_left(), is_first()
    own = pick(left, thirds(l_basis_ref), thirds(r_basis_ref))
    got = thirds(got_ref, 0, l_basis_ref.shape[0])
    basis_ref[...] = whole_of(scratch, pick(first, own, got), pick(first, got, own))
    known_ref[...] = 0.5 * known_part(first, pick(left, thirds(l_stat_ref), thirds(r_stat_ref)), scratch)
    right_ref[...] = half_of(scratch, thirds(r_basis_ref))
    other_ref[...] = jnp.where(left, r_stat_ref[...], l_stat_ref[...])
    copy_ref[...] = l_basis_ref[...]


def products_kernel(hops, basis_ref, known_ref, right_ref, got_ref, *refs):
    left = is_left()
    grad_ref, stat_ref, power_ref, inner_ref = refs[-4:]
    if hops:
        grads_ref, mine_refs, theirs_refs = refs[0], refs[1 : 1 + len(hops)], refs[1 + len(hops) : 1 + 2 * len(hops)]
        rows = grads_ref.shape[1]
        here = lax.axis_index("shard") // 2
        parity = lax.axis_index("shard") % 2
        blocks = grad_ref.shape[1] // LANES
        start = got_ref.shape[0] - blocks * rows
        received = [got_ref[pl.ds(start + k * rows, rows), :] for k in range(blocks)]
        place_rows(grad_ref, 2 * here + parity, rows, grads_ref[here])
        place_rows(grad_ref, 2 * here + 1 - parity, rows, jnp.concatenate(received, axis=1))
        for hop, mine, theirs in zip(hops, mine_refs, theirs_refs):
            place_rows(grad_ref, 2 * (here ^ hop) + parity, rows, mine[...])
            place_rows(grad_ref, 2 * (here ^ hop) + 1 - parity, rows, theirs[...])
    else:
        grad_ref[...] = refs[0][...]
    grad = grad_ref[...]
    parts = split(jnp.where(left, grad, grad.T))
    stat = known_ref[...] + 0.5 * symmetric_dot(parts, parts, ((1,), (1,)))
    stat_ref[...] = stat
    power_ref[...] = dot(stat, basis_ref[...])
    inner_ref[...] = dot(grad, right_ref[...])


def begin_kernel(steps, corner_ref, power_ref, basis_ref, x_ref, scratch):
    first = is_first()
    corner = corner_part(corner_ref, scratch)
    rows, wide = corner.shape
    basis = jnp.where(first, basis_ref[pl.ds(rows, rows), :], basis_ref[pl.ds(0, rows), :])
    basis = jnp.concatenate([basis, jnp.zeros((wide - rows, 2 * rows), F32)], axis=0)
    term = 0.5 * dot(corner, basis)
    power = power_ref[...] + jnp.concatenate([jnp.where(first, 0.0, term), jnp.where(first, term, 0.0)], axis=0)
    x_ref[...] = iterate(power * (1.0 / jnp.sqrt(jnp.sum(power * power) + NORM_EPS)), steps)


def rows_for(hops, outer_ref, right_parts, out_ref, offset):
    rows = out_ref.shape[1]
    here = lax.axis_index("shard") // 2
    starts = [pl.multiple_of((2 * (here ^ hop) + offset) * rows, 8) if hops else 0 for hop in (0, *hops)]
    outer = [outer_ref[pl.ds(start, rows), :] for start in starts]
    partial = dot_parts(split(jnp.concatenate(outer, axis=0)), right_parts, ((1,), (1,)))
    for k in range(len(starts)):
        out_ref[k] = partial[k * rows : (k + 1) * rows]


def update_kernel(
    hops,
    inner_ref,
    basis_ref,
    left_ref,
    right_ref,
    other_left_ref,
    one_ref,
    two_ref,
    start_ref,
    new_one_ref,
    new_two_ref,
    theirs_ref,
    outer_ref,
    x_ref,
    scratch,
):
    left, first = is_left(), is_first()
    x = start_ref[...]
    parts = split(x)
    gram = dot_parts(parts, parts, ((1,), (1,)))
    own, got = thirds(left_ref), thirds(other_left_ref)
    basis_left = jnp.where(left, basis_ref[...], whole_of(scratch, pick(first, own, got), pick(first, got, own)))
    rotated = dot(basis_left.T, inner_ref[...])
    gram_parts = split(gram)
    square = dot_parts(gram_parts, gram_parts)
    rotated = flat_of(scratch, rotated)
    ones = thirds(one_ref)
    twos = thirds(two_ref)
    new_one = [BETA_ONE * m + (1.0 - BETA_ONE) * r for m, r in zip(ones, rotated)]
    new_two = [BETA_TWO * v + (1.0 - BETA_TWO) * r * r for v, r in zip(twos, rotated)]
    put_thirds(new_one_ref, new_one)
    put_thirds(new_two_ref, new_two)
    direction = [m / (jnp.sqrt(v) + ADAM_EPS) for m, v in zip(new_one, new_two)]
    outer_ref[...] = dot_parts(split(basis_left), split(half_of(scratch, direction)))
    poly_parts = split(CUBIC_COEFF * gram + QUINTIC_COEFF * square)
    moved = dot_parts(poly_parts, parts)
    rows_for(hops, outer_ref, split(right_ref[...]), theirs_ref, 1 - lax.axis_index("shard") % 2)
    x_ref[...] = LINEAR_COEFF * x + moved


def end_kernel(hops, steps, start_ref, outer_ref, right_ref, x_ref, poly_ref, send_ref, mine_ref, scratch):
    x = iterate(start_ref[...], steps - 1)
    x_ref[...] = x
    rows_for(hops, outer_ref, split(right_ref[...]), mine_ref, lax.axis_index("shard") % 2)
    poly = polynomial(split(x))
    poly_ref[...] = poly
    half = take_half(x, jnp.logical_not(is_first()))
    put_thirds(send_ref, flat_of(scratch, LINEAR_COEFF * half + dot(poly, half)))


def add_kernel(mine_ref, theirs_ref, *out_refs):
    for k, out_ref in enumerate(out_refs):
        out_ref[...] = mine_ref[k] + theirs_ref[k]


def bases_kernel(keep_ref, back_ref, new_left_ref, new_right_ref, sems):
    left = is_left()

    def copies(own_ref, other_ref):
        return [
            pltpu.make_async_copy(keep_ref, own_ref, sems.at[0]),
            pltpu.make_async_copy(back_ref, other_ref, sems.at[1]),
        ]

    @pl.when(left)
    def _():
        for copy in copies(new_left_ref, new_right_ref):
            copy.start()

    @pl.when(jnp.logical_not(left))
    def _():
        for copy in copies(new_right_ref, new_left_ref):
            copy.start()

    for copy in copies(new_left_ref, new_right_ref):
        copy.wait()


def rows_kernel(hops, *refs):
    rows_refs, (update_ref, sems) = refs[:-2], refs[-2:]
    here = lax.axis_index("shard") // 2
    copies = [
        pltpu.make_async_copy(rows_refs[k], update_ref.at[here ^ hop], sems.at[k]) for k, hop in enumerate((0, *hops))
    ]
    for copy in copies:
        copy.start()
    for copy in copies:
        copy.wait()


def rest_kernel(x_ref, poly_ref, grad_ref, new_stat_ref, other_ref, keep_ref, new_left_ref, new_right_ref, scratch):
    left = is_left()
    first = is_first()
    half = take_half(x_ref[...], first)
    put_thirds(keep_ref, flat_of(scratch, LINEAR_COEFF * half + dot(poly_ref[...], half)))
    grad = grad_ref[...]
    turned = grad.T
    a = jnp.where(left, grad, turned)
    b = jnp.where(left, turned, grad)
    new_own = flat_of(scratch, take_half(new_stat_ref[...], first))
    product = flat_of(scratch, dot(b, take_half(a, first)))
    new_other = [0.5 * u + 0.5 * v for u, v in zip(thirds(other_ref), product)]
    put_thirds(new_left_ref, pick(left, new_own, new_other))
    put_thirds(new_right_ref, pick(left, new_other, new_own))


def call(kernel, outs, scratch, products, full, name, copies=0, kind=jax.ShapeDtypeStruct, **specs):
    size = full * full
    scratch = [pltpu.VMEM(s, F32) for s in scratch]
    if copies:
        scratch.append(pltpu.SemaphoreType.DMA((copies,)))
    return pl.pallas_call(
        kernel,
        out_shape=[kind(s, F32) for s in outs],
        scratch_shapes=scratch,
        compiler_params=pltpu.CompilerParams(vmem_limit_bytes=40 * 1024 * 1024),
        cost_estimate=pl.CostEstimate(flops=int(products * 6 * full * size), bytes_accessed=16 * size, transcendentals=0),
        name=name,
        **specs,
    )


def anywhere(count):
    return [pl.BlockSpec(memory_space=pl.ANY)] * count


def after(x, *others):
    return lax.optimization_barrier((x, *others))[0]


def local(grads, moment_one, moment_two, left_stat, right_stat, left_basis, right_basis):
    tiles_here, rows_here, full = grads.shape
    size = lax.axis_size("shard")
    flat_rows = full * (full // 2) // LANES
    flat = (flat_rows, LANES)
    square = (full, full)
    block = (rows_here, full)
    parity = lax.axis_index("shard") % 2
    pairs = [(i, i ^ 1) for i in range(size)]
    sides = [list(range(k, size, 2)) for k in range(2)]
    near = size in (4, 8) and rows_here % 8 == 0
    hops = {4: (1,), 8: (2, 3, 1)}[size] if near else ()
    strips = (tiles_here, *block) if near else (1, full, full)

    def exchange(x):
        return lax.all_to_all(x, "shard", split_axis=0, concat_axis=0, axis_index_groups=sides, tiled=True)

    def hop_by(x, hop):
        return lax.ppermute(x, "shard", [(i, i ^ (2 * hop)) for i in range(size)])

    def partner(x):
        return lax.ppermute(x, "shard", pairs)

    one, two, l_stat, r_stat, l_basis, r_basis = (
        x.reshape(flat) for x in (moment_one, moment_two, left_stat, right_stat, left_basis, right_basis)
    )
    count = corner_rows(flat_rows)
    outgoing_rows = flat_rows + (rows_here * (full // LANES) if near else 0)
    outgoing, corner, *pieces = call(
        functools.partial(pack_kernel, hops),
        [(outgoing_rows, LANES), (count, LANES)] + [block] * len(hops),
        [(flat_rows // 2, LANES)],
        0.1,
        full,
        "pack",
        copies=2 + len(hops) + full // LANES,
        kind=pltpu.VMEM,
        in_specs=anywhere(5),
        out_specs=anywhere(1) + [pl.BlockSpec(memory_space=pltpu.VMEM)] + anywhere(len(hops)),
    )(*(pltpu.with_memory_space_constraint(x, pltpu.HBM) for x in (l_stat, r_stat, l_basis, r_basis, grads)))
    got = partner(outgoing)
    if near:
        mine = [hop_by(piece, hop) for hop, piece in zip(hops, pieces)]
        theirs = [partner(x) for x in mine]
        rows = (grads, *mine, *theirs)
    else:
        mine = exchange(grads)
        theirs = partner(mine)
        even, odd = jnp.where(parity == 0, mine, theirs), jnp.where(parity == 0, theirs, mine)
        rows = (jnp.stack([even, odd], axis=1).reshape(square),)
        mine = [mine]
    got_corner = partner(after(corner, theirs[0] if near else mine[0]))
    wide = (full, 2 * LANES)
    basis, known, right, other, left = call(
        prepare_kernel, [square, square, wide, flat, flat], [(3, full, LANES)], 0.1, full, "prepare"
    )(l_stat, r_stat, l_basis, r_basis, got)
    grad, new_stat, power, inner = call(
        functools.partial(products_kernel, hops), [square, square, square, wide], [], 3, full, "products"
    )(basis, known, right, got, *rows)
    tensors = lax.axis_size("tensor")
    place = lambda t, i: i * tensors + t
    cycle = []
    for t in range(0, tensors - tensors % 2, 2):
        for i in range(0, size, 2):
            cycle += [(place(t, i), place(t, i + 1)), (place(t, i + 1), place(t + 1, i + 1))]
            cycle += [(place(t + 1, i + 1), place(t + 1, i)), (place(t + 1, i), place(t, i))]
    cycle += [(place(t, i), place(t, i ^ 1)) for t in range(tensors - tensors % 2, tensors) for i in range(size)]
    other_left = lax.ppermute(after(l_basis, basis, *(theirs[:2] if near else mine)), ("shard", "tensor"), cycle)
    (x,) = call(
        functools.partial(begin_kernel, EARLY_ITERS), [square], [(2, full // 2, LANES)], 7, full, "begin"
    )(got_corner, power, basis)
    new_one, new_two, other_rows, outer, x = call(
        functools.partial(update_kernel, hops), [flat, flat, strips, wide, square], [(3, full, LANES)], 5, full, "update"
    )(inner, basis, left, right, other_left, one, two, x)
    if not near:
        partial = other_rows.reshape(tiles_here, 2, rows_here, full)
        other_rows = lax.dynamic_index_in_dim(partial, 1 - parity, 1, keepdims=False)
    got_rows = partner(other_rows)
    x, poly, send, own_rows = call(
        functools.partial(end_kernel, hops, NS_ITERS - EARLY_ITERS - 1),
        [square, square, flat, strips],
        [(3, full, LANES)],
        9,
        full,
        "end",
    )(after(x, other_rows), outer, right)
    back = partner(send)
    keep, new_left, new_right = call(rest_kernel, [flat, flat, flat], [(3, full, LANES)], 1.5, full, "rest")(
        x, poly, grad, new_stat, other
    )
    if near:
        kept, *sums = call(add_kernel, [block] * (1 + len(hops)), [], 0.1, full, "add")(
            after(own_rows, send), after(got_rows, send)
        )
        returned = [hop_by(x, hop) for hop, x in zip(hops, sums)]
        update = call(
            functools.partial(rows_kernel, hops),
            [grads.shape],
            [],
            0.1,
            full,
            "rows",
            copies=1 + len(hops),
            in_specs=anywhere(1 + len(hops)),
            out_specs=anywhere(1),
        )(kept, *returned)[0]
    else:
        own_rows = lax.dynamic_index_in_dim(partial, parity, 1, keepdims=False)
        update = exchange(after(own_rows, send) + after(got_rows, send))
    new_l_basis, new_r_basis = call(
        bases_kernel, [flat, flat], [], 0.1, full, "bases", copies=2, in_specs=anywhere(2), out_specs=anywhere(2)
    )(keep, back)
    halves = (new_one, new_two, new_left, new_right, new_l_basis, new_r_basis)
    return (update, *(x.reshape(1, flat_rows * LANES) for x in halves))


def solution(mesh):
    halves = P(("tensor", "shard"), None)
    rows = P("tensor", "shard", None)
    return jax.shard_map(
        local, mesh=mesh, in_specs=(rows,) + (halves,) * 6, out_specs=(rows,) + (halves,) * 6, check_vma=False
    )
```

```python
import functools

import jax
import jax.numpy as jnp
from jax import lax
from jax.experimental import pallas as pl
from jax.experimental.pallas import tpu as pltpu
from jax.sharding import PartitionSpec as P

NS_ITERS = 5
BETA_ONE = 0.9
BETA_TWO = 0.95
ADAM_EPS = 1e-08
NORM_EPS = 1e-06
LINEAR_COEFF = 3.4445
CUBIC_COEFF = -4.775
QUINTIC_COEFF = 2.0315
LANES = 128
F32 = jnp.float32


def split(x):
    high = x.astype(jnp.bfloat16)
    return high, (x - high.astype(F32)).astype(jnp.bfloat16)


def dot(a, b, dims=((1,), (0,))):
    return dot_parts(split(a), split(b), dims)


def dot_parts(a, b, dims=((1,), (0,))):
    (ka,), (kb,) = dims
    left = jnp.concatenate([a[0], a[0], a[1]], axis=ka)
    right = jnp.concatenate([b[0], b[1], b[0]], axis=kb)
    return lax.dot_general(left, right, (dims, ((), ())), preferred_element_type=F32)


def symmetric_dot(a, b, dims=((1,), (0,))):
    (ka,), (kb,) = dims
    cut = a[0].shape[0] - LANES
    head = lambda x, axis: lax.slice_in_dim(x, 0, cut, axis=axis)
    tail = lambda x, axis: lax.slice_in_dim(x, cut, cut + LANES, axis=axis)
    left = dot_parts(a, [head(x, 1 - kb) for x in b], dims)
    corner = dot_parts([tail(x, 1 - ka) for x in a], [tail(x, 1 - kb) for x in b], dims)
    right = jnp.concatenate([left[cut:].T, corner], axis=0)
    return jnp.concatenate([left, right], axis=1)


def swap(x):
    return pltpu.roll(x, LANES // 2, 1)


def low_lanes(shape):
    return lax.broadcasted_iota(jnp.int32, shape, 1) < LANES // 2


def pick(flag, x, y):
    return [jnp.where(flag, u, v) for u, v in zip(x, y)]


def thirds(ref, start=0, rows=None):
    rows = ref.shape[0] if rows is None else rows
    return [ref[pl.ds(start + k, rows // 3, stride=3), :] for k in range(3)]


def put_thirds(ref, parts):
    for k in range(3):
        ref[pl.ds(k, parts[k].shape[0], stride=3), :] = parts[k]


def interleave(scratch, index, even, odd):
    scratch[index, pl.ds(0, even.shape[0], stride=2), :] = even
    scratch[index, pl.ds(1, odd.shape[0], stride=2), :] = odd


def whole_of(scratch, first, second):
    a, b, c = first
    d, e, f = second
    low = low_lanes(a.shape)
    sb, sc, sd, se = swap(b), swap(c), swap(d), swap(e)
    interleave(scratch, 0, a, jnp.where(low, sb, sc))
    interleave(scratch, 1, jnp.where(low, b, sd), jnp.where(low, sc, e))
    interleave(scratch, 2, jnp.where(low, sd, se), f)
    return jnp.concatenate([scratch[0], scratch[1], scratch[2]], axis=1)


def half_of(scratch, flat):
    a, b, c = flat
    low = low_lanes(a.shape)
    sb, sc = swap(b), swap(c)
    interleave(scratch, 0, a, jnp.where(low, sb, sc))
    interleave(scratch, 1, jnp.where(low, b, 0.0), jnp.where(low, sc, 0.0))
    return jnp.concatenate([scratch[0], scratch[1]], axis=1)


def flat_of(scratch, half):
    scratch[0] = half[:, :LANES]
    scratch[1] = half[:, LANES:]
    pairs = half.shape[0] // 2
    even0 = scratch[0, pl.ds(0, pairs, stride=2), :]
    odd0 = swap(scratch[0, pl.ds(1, pairs, stride=2), :])
    even1 = scratch[1, pl.ds(0, pairs, stride=2), :]
    odd1 = swap(scratch[1, pl.ds(1, pairs, stride=2), :])
    low = low_lanes(even0.shape)
    return [even0, jnp.where(low, even1, odd0), jnp.where(low, odd0, odd1)]


def take_half(whole, first):
    one, two, three = whole[:, :LANES], whole[:, LANES : 2 * LANES], whole[:, 2 * LANES :]
    low = low_lanes(one.shape)
    s2, s3 = swap(two), swap(three)
    head = jnp.where(first, one, jnp.where(low, s2, s3))
    tail = jnp.where(low, jnp.where(first, two, s3), 0.0)
    return jnp.concatenate([head, tail], axis=1)


def is_first():
    return lax.rem(lax.axis_index("shard"), 2) == 0


def is_left():
    return lax.rem(lax.axis_index("shard") + lax.axis_index("tensor"), 2) == 0


def pack_kernel(hops, l_stat_ref, r_stat_ref, l_basis_ref, r_basis_ref, grads_ref, *refs):
    out_ref, small_ref, *refs = refs
    piece_refs, (corner, sems) = refs[: len(hops)], refs[len(hops) :]
    left = is_left()
    flat_rows = l_basis_ref.shape[0]
    half_rows = flat_rows // 2
    rows = grads_ref.shape[1]
    here = lax.axis_index("shard") // 2

    start = pl.multiple_of(jnp.where(is_first(), 0, half_rows), 8)

    def copies(basis_ref, stat_ref):
        return [
            pltpu.make_async_copy(stat_ref.at[pl.ds(start, half_rows)], corner, sems.at[0]),
            pltpu.make_async_copy(basis_ref, out_ref.at[pl.ds(0, flat_rows)], sems.at[1]),
        ]

    @pl.when(left)
    def _():
        for copy in copies(r_basis_ref, r_stat_ref):
            copy.start()

    @pl.when(jnp.logical_not(left))
    def _():
        for copy in copies(l_basis_ref, l_stat_ref):
            copy.start()

    more = []
    for number, (hop, piece_ref) in enumerate(zip(hops, piece_refs)):
        more.append(pltpu.make_async_copy(grads_ref.at[here ^ hop], piece_ref, sems.at[2 + number]))
    if hops:
        for k in range(grads_ref.shape[2] // LANES):
            source = grads_ref.at[here, :, pl.ds(k * LANES, LANES)]
            target = out_ref.at[pl.ds(flat_rows + k * rows, rows)]
            more.append(pltpu.make_async_copy(source, target, sems.at[2 + len(hops) + k]))
    for copy in more:
        copy.start()
    first, second = copies(l_basis_ref, l_stat_ref)
    first.wait()
    third = half_rows // 9
    a, b, c = thirds(corner)
    low = low_lanes((third, LANES))
    middle = slice(third, 2 * third)
    small_ref[pl.ds(0, third)] = jnp.where(low, a[:third], b[:third])
    small_ref[pl.ds(third, third)] = a[middle]
    small_ref[pl.ds(2 * third, third)] = jnp.where(low, swap(b[middle]), swap(c[middle]))
    small_ref[pl.ds(3 * third, 3 * third)] = corner[pl.ds(6 * third, 3 * third)]
    for copy in [second, *more]:
        copy.wait()


def corner_rows(flat_rows):
    return flat_rows // 3


def unpack_corner(got_ref):
    third = got_ref.shape[0] // 6
    small = got_ref[pl.ds(0, third), :]
    even = got_ref[pl.ds(third, third), :]
    odd = swap(got_ref[pl.ds(2 * third, third), :])
    a, b, c = thirds(got_ref, 3 * third, 3 * third)
    low = low_lanes(small.shape)
    zero = jnp.zeros_like(small)
    return [
        jnp.concatenate([jnp.where(low, small, zero), even, a], axis=0),
        jnp.concatenate([jnp.where(low, zero, small), jnp.where(low, zero, odd), b], axis=0),
        jnp.concatenate([zero, jnp.where(low, odd, zero), c], axis=0),
    ]


def known_part(first, own, scratch):
    zeros = [jnp.zeros_like(x) for x in own]
    known = whole_of(scratch, pick(first, own, zeros), pick(first, zeros, own))
    half = known.shape[0] // 2
    row = lax.broadcasted_iota(jnp.int32, known.shape, 0)
    column = lax.broadcasted_iota(jnp.int32, known.shape, 1)
    missing = (jnp.where(first, row, column) < half) & (jnp.where(first, column, row) >= half)
    return jnp.where(missing, known.T, known)


def corner_part(corner_ref, scratch):
    corner = half_of(scratch, unpack_corner(corner_ref))
    rows, wide = corner.shape
    turned = jnp.concatenate([corner, jnp.zeros((wide - rows, wide), F32)], axis=0).T[:rows]
    part = rows // 3
    row = lax.broadcasted_iota(jnp.int32, corner.shape, 0)
    column = lax.broadcasted_iota(jnp.int32, corner.shape, 1)
    missing = (row < 2 * part) & (column >= jnp.where(row < part, part, 2 * part))
    return jnp.where(missing, turned, corner)


def place_rows(grad_ref, block, rows, value):
    grad_ref[pl.ds(pl.multiple_of(block * rows, 8), rows), :] = value


def polynomial(parts):
    gram = dot_parts(parts, parts, ((1,), (1,)))
    gram_parts = split(gram)
    return CUBIC_COEFF * gram + QUINTIC_COEFF * dot_parts(gram_parts, gram_parts)


def iterate(x, steps):
    for _ in range(steps):
        parts = split(x)
        x = LINEAR_COEFF * x + dot_parts(split(polynomial(parts)), parts)
    return x


def prepare_kernel(
    l_stat_ref, r_stat_ref, l_basis_ref, r_basis_ref, got_ref, basis_ref, known_ref, right_ref, other_ref, copy_ref, scratch
):
    left, first = is_left(), is_first()
    own = pick(left, thirds(l_basis_ref), thirds(r_basis_ref))
    got = thirds(got_ref, 0, l_basis_ref.shape[0])
    basis_ref[...] = whole_of(scratch, pick(first, own, got), pick(first, got, own))
    known_ref[...] = 0.5 * known_part(first, pick(left, thirds(l_stat_ref), thirds(r_stat_ref)), scratch)
    right_ref[...] = half_of(scratch, thirds(r_basis_ref))
    other_ref[...] = jnp.where(left, r_stat_ref[...], l_stat_ref[...])
    copy_ref[...] = l_basis_ref[...]


def products_kernel(hops, basis_ref, known_ref, got_ref, *refs):
    left = is_left()
    grad_ref, stat_ref, power_ref = refs[-3:]
    if hops:
        grads_ref, mine_refs, theirs_refs = refs[0], refs[1 : 1 + len(hops)], refs[1 + len(hops) : 1 + 2 * len(hops)]
        rows = grads_ref.shape[1]
        here = lax.axis_index("shard") // 2
        parity = lax.axis_index("shard") % 2
        blocks = grad_ref.shape[1] // LANES
        start = got_ref.shape[0] - blocks * rows
        received = [got_ref[pl.ds(start + k * rows, rows), :] for k in range(blocks)]
        place_rows(grad_ref, 2 * here + parity, rows, grads_ref[here])
        place_rows(grad_ref, 2 * here + 1 - parity, rows, jnp.concatenate(received, axis=1))
        for hop, mine, theirs in zip(hops, mine_refs, theirs_refs):
            place_rows(grad_ref, 2 * (here ^ hop) + parity, rows, mine[...])
            place_rows(grad_ref, 2 * (here ^ hop) + 1 - parity, rows, theirs[...])
    else:
        grad_ref[...] = refs[0][...]
    grad = grad_ref[...]
    parts = split(jnp.where(left, grad, grad.T))
    stat = known_ref[...] + 0.5 * symmetric_dot(parts, parts, ((1,), (1,)))
    stat_ref[...] = stat
    power_ref[...] = dot(stat, basis_ref[...])


def begin_kernel(corner_ref, power_ref, basis_ref, grad_ref, right_ref, x_ref, inner_ref, scratch):
    first = is_first()
    corner = corner_part(corner_ref, scratch)
    rows, wide = corner.shape
    basis = jnp.where(first, basis_ref[pl.ds(rows, rows), :], basis_ref[pl.ds(0, rows), :])
    basis = jnp.concatenate([basis, jnp.zeros((wide - rows, 2 * rows), F32)], axis=0)
    term = 0.5 * dot(corner, basis)
    power = power_ref[...] + jnp.concatenate([jnp.where(first, 0.0, term), jnp.where(first, term, 0.0)], axis=0)
    grad_parts, right_parts = split(grad_ref[...]), split(right_ref[...])
    x = power * (1.0 / jnp.sqrt(jnp.sum(power * power) + NORM_EPS))
    parts = split(x)
    gram = dot_parts(parts, parts, ((1,), (1,)))
    inner_ref[...] = dot_parts(grad_parts, right_parts)
    gram_parts = split(gram)
    poly = CUBIC_COEFF * gram + QUINTIC_COEFF * dot_parts(gram_parts, gram_parts)
    x_ref[...] = LINEAR_COEFF * x + dot_parts(split(poly), parts)


def rows_for(hops, outer_ref, right_parts, out_ref, offset):
    rows = out_ref.shape[1]
    here = lax.axis_index("shard") // 2
    starts = [pl.multiple_of((2 * (here ^ hop) + offset) * rows, 8) if hops else 0 for hop in (0, *hops)]
    outer = [outer_ref[pl.ds(start, rows), :] for start in starts]
    partial = dot_parts(split(jnp.concatenate(outer, axis=0)), right_parts, ((1,), (1,)))
    for k in range(len(starts)):
        out_ref[k] = partial[k * rows : (k + 1) * rows]


def update_kernel(
    hops,
    inner_ref,
    basis_ref,
    left_ref,
    right_ref,
    other_left_ref,
    one_ref,
    two_ref,
    start_ref,
    new_one_ref,
    new_two_ref,
    theirs_ref,
    outer_ref,
    x_ref,
    scratch,
):
    left, first = is_left(), is_first()
    x = start_ref[...]
    parts = split(x)
    gram = dot_parts(parts, parts, ((1,), (1,)))
    own, got = thirds(left_ref), thirds(other_left_ref)
    basis_left = jnp.where(left, basis_ref[...], whole_of(scratch, pick(first, own, got), pick(first, got, own)))
    rotated = dot(basis_left.T, inner_ref[...])
    gram_parts = split(gram)
    square = dot_parts(gram_parts, gram_parts)
    rotated = flat_of(scratch, rotated)
    ones = thirds(one_ref)
    twos = thirds(two_ref)
    new_one = [BETA_ONE * m + (1.0 - BETA_ONE) * r for m, r in zip(ones, rotated)]
    new_two = [BETA_TWO * v + (1.0 - BETA_TWO) * r * r for v, r in zip(twos, rotated)]
    put_thirds(new_one_ref, new_one)
    put_thirds(new_two_ref, new_two)
    direction = [m / (jnp.sqrt(v) + ADAM_EPS) for m, v in zip(new_one, new_two)]
    outer_ref[...] = dot_parts(split(basis_left), split(half_of(scratch, direction)))
    poly_parts = split(CUBIC_COEFF * gram + QUINTIC_COEFF * square)
    moved = dot_parts(poly_parts, parts)
    rows_for(hops, outer_ref, split(right_ref[...]), theirs_ref, 1 - lax.axis_index("shard") % 2)
    x_ref[...] = LINEAR_COEFF * x + moved


def end_kernel(steps, start_ref, x_ref, poly_ref, send_ref, scratch):
    x = iterate(start_ref[...], steps - 1)
    x_ref[...] = x
    poly = polynomial(split(x))
    poly_ref[...] = poly
    half = take_half(x, jnp.logical_not(is_first()))
    put_thirds(send_ref, flat_of(scratch, LINEAR_COEFF * half + dot(poly, half)))


def own_rows_kernel(hops, outer_ref, right_ref, mine_ref):
    rows_for(hops, outer_ref, split(right_ref[...]), mine_ref, lax.axis_index("shard") % 2)


def add_kernel(mine_ref, theirs_ref, *out_refs):
    for k, out_ref in enumerate(out_refs):
        out_ref[...] = mine_ref[k] + theirs_ref[k]


def bases_kernel(keep_ref, back_ref, new_left_ref, new_right_ref, sems):
    left = is_left()

    def copies(own_ref, other_ref):
        return [
            pltpu.make_async_copy(keep_ref, own_ref, sems.at[0]),
            pltpu.make_async_copy(back_ref, other_ref, sems.at[1]),
        ]

    @pl.when(left)
    def _():
        for copy in copies(new_left_ref, new_right_ref):
            copy.start()

    @pl.when(jnp.logical_not(left))
    def _():
        for copy in copies(new_right_ref, new_left_ref):
            copy.start()

    for copy in copies(new_left_ref, new_right_ref):
        copy.wait()


def rows_kernel(hops, *refs):
    rows_refs, (update_ref, sems) = refs[:-2], refs[-2:]
    here = lax.axis_index("shard") // 2
    copies = [
        pltpu.make_async_copy(rows_refs[k], update_ref.at[here ^ hop], sems.at[k]) for k, hop in enumerate((0, *hops))
    ]
    for copy in copies:
        copy.start()
    for copy in copies:
        copy.wait()


def rest_kernel(x_ref, poly_ref, grad_ref, new_stat_ref, other_ref, keep_ref, new_left_ref, new_right_ref, scratch):
    left = is_left()
    first = is_first()
    half = take_half(x_ref[...], first)
    put_thirds(keep_ref, flat_of(scratch, LINEAR_COEFF * half + dot(poly_ref[...], half)))
    grad = grad_ref[...]
    turned = grad.T
    a = jnp.where(left, grad, turned)
    b = jnp.where(left, turned, grad)
    new_own = flat_of(scratch, take_half(new_stat_ref[...], first))
    product = flat_of(scratch, dot(b, take_half(a, first)))
    new_other = [0.5 * u + 0.5 * v for u, v in zip(thirds(other_ref), product)]
    put_thirds(new_left_ref, pick(left, new_own, new_other))
    put_thirds(new_right_ref, pick(left, new_other, new_own))


def call(kernel, outs, scratch, products, full, name, copies=0, kind=jax.ShapeDtypeStruct, **specs):
    size = full * full
    scratch = [pltpu.VMEM(s, F32) for s in scratch]
    if copies:
        scratch.append(pltpu.SemaphoreType.DMA((copies,)))
    return pl.pallas_call(
        kernel,
        out_shape=[kind(s, F32) for s in outs],
        scratch_shapes=scratch,
        compiler_params=pltpu.CompilerParams(vmem_limit_bytes=40 * 1024 * 1024),
        cost_estimate=pl.CostEstimate(flops=int(products * 6 * full * size), bytes_accessed=16 * size, transcendentals=0),
        name=name,
        **specs,
    )


def anywhere(count):
    return [pl.BlockSpec(memory_space=pl.ANY)] * count


def after(x, *others):
    return lax.optimization_barrier((x, *others))[0]


def local(grads, moment_one, moment_two, left_stat, right_stat, left_basis, right_basis):
    tiles_here, rows_here, full = grads.shape
    size = lax.axis_size("shard")
    flat_rows = full * (full // 2) // LANES
    flat = (flat_rows, LANES)
    square = (full, full)
    block = (rows_here, full)
    parity = lax.axis_index("shard") % 2
    pairs = [(i, i ^ 1) for i in range(size)]
    sides = [list(range(k, size, 2)) for k in range(2)]
    near = size in (4, 8) and rows_here % 8 == 0
    hops = {4: (1,), 8: (2, 3, 1)}[size] if near else ()
    strips = (tiles_here, *block) if near else (1, full, full)

    def exchange(x):
        return lax.all_to_all(x, "shard", split_axis=0, concat_axis=0, axis_index_groups=sides, tiled=True)

    def hop_by(x, hop):
        return lax.ppermute(x, "shard", [(i, i ^ (2 * hop)) for i in range(size)])

    def partner(x):
        return lax.ppermute(x, "shard", pairs)

    one, two, l_stat, r_stat, l_basis, r_basis = (
        x.reshape(flat) for x in (moment_one, moment_two, left_stat, right_stat, left_basis, right_basis)
    )
    count = corner_rows(flat_rows)
    outgoing_rows = flat_rows + (rows_here * (full // LANES) if near else 0)
    outgoing, corner, *pieces = call(
        functools.partial(pack_kernel, hops),
        [(outgoing_rows, LANES), (count, LANES)] + [block] * len(hops),
        [(flat_rows // 2, LANES)],
        0.1,
        full,
        "pack",
        copies=2 + len(hops) + full // LANES,
        kind=pltpu.VMEM,
        in_specs=anywhere(5),
        out_specs=anywhere(1) + [pl.BlockSpec(memory_space=pltpu.VMEM)] + anywhere(len(hops)),
    )(*(pltpu.with_memory_space_constraint(x, pltpu.HBM) for x in (l_stat, r_stat, l_basis, r_basis, grads)))
    got = partner(outgoing)
    if near:
        mine = [hop_by(piece, hop) for hop, piece in zip(hops, pieces)]
        theirs = [partner(x) for x in mine]
        rows = (grads, *mine, *theirs)
    else:
        mine = exchange(grads)
        theirs = partner(mine)
        even, odd = jnp.where(parity == 0, mine, theirs), jnp.where(parity == 0, theirs, mine)
        rows = (jnp.stack([even, odd], axis=1).reshape(square),)
        mine = [mine]
    got_corner = partner(after(corner, theirs[0] if near else mine[0]))
    wide = (full, 2 * LANES)
    basis, known, right, other, left = call(
        prepare_kernel, [square, square, wide, flat, flat], [(3, full, LANES)], 0.1, full, "prepare"
    )(l_stat, r_stat, l_basis, r_basis, got)
    grad, new_stat, power = call(
        functools.partial(products_kernel, hops), [square, square, square], [], 3, full, "products"
    )(basis, known, got, *rows)
    tensors = lax.axis_size("tensor")
    place = lambda t, i: i * tensors + t
    cycle = []
    for t in range(0, tensors - tensors % 2, 2):
        for i in range(0, size, 2):
            cycle += [(place(t, i), place(t, i + 1)), (place(t, i + 1), place(t + 1, i + 1))]
            cycle += [(place(t + 1, i + 1), place(t + 1, i)), (place(t + 1, i), place(t, i))]
    cycle += [(place(t, i), place(t, i ^ 1)) for t in range(tensors - tensors % 2, tensors) for i in range(size)]
    other_left = lax.ppermute(after(l_basis, basis, *(theirs[:2] if near else mine)), ("shard", "tensor"), cycle)
    x, inner = call(begin_kernel, [square, wide], [(2, full // 2, LANES)], 7, full, "begin")(
        got_corner, power, basis, grad, right
    )
    new_one, new_two, other_rows, outer, x = call(
        functools.partial(update_kernel, hops), [flat, flat, strips, wide, square], [(3, full, LANES)], 5, full, "update"
    )(inner, basis, left, right, other_left, one, two, x)
    if not near:
        partial = other_rows.reshape(tiles_here, 2, rows_here, full)
        other_rows = lax.dynamic_index_in_dim(partial, 1 - parity, 1, keepdims=False)
    got_rows = partner(other_rows)
    x, poly, send = call(
        functools.partial(end_kernel, NS_ITERS - 2), [square, square, flat], [(3, full, LANES)], 9, full, "end"
    )(after(x, other_rows))
    back = partner(send)
    keep, new_left, new_right = call(rest_kernel, [flat, flat, flat], [(3, full, LANES)], 1.5, full, "rest")(
        x, poly, grad, new_stat, other
    )
    if near:
        (own_rows,) = call(functools.partial(own_rows_kernel, hops), [strips], [], 0.5, full, "own_rows")(
            after(outer, send), right
        )
        kept, *sums = call(add_kernel, [block] * (1 + len(hops)), [], 0.1, full, "add")(own_rows, after(got_rows, send))
        returned = [hop_by(x, hop) for hop, x in zip(hops, sums)]
        update = call(
            functools.partial(rows_kernel, hops),
            [grads.shape],
            [],
            0.1,
            full,
            "rows",
            copies=1 + len(hops),
            in_specs=anywhere(1 + len(hops)),
            out_specs=anywhere(1),
        )(kept, *returned)[0]
    else:
        own_rows = lax.dynamic_index_in_dim(partial, parity, 1, keepdims=False)
        update = exchange(after(own_rows, send) + after(got_rows, send))
    new_l_basis, new_r_basis = call(
        bases_kernel, [flat, flat], [], 0.1, full, "bases", copies=2, in_specs=anywhere(2), out_specs=anywhere(2)
    )(keep, back)
    halves = (new_one, new_two, new_left, new_right, new_l_basis, new_r_basis)
    return (update, *(x.reshape(1, flat_rows * LANES) for x in halves))


def solution(mesh):
    halves = P(("tensor", "shard"), None)
    rows = P("tensor", "shard", None)
    return jax.shard_map(
        local, mesh=mesh, in_specs=(rows,) + (halves,) * 6, out_specs=(rows,) + (halves,) * 6, check_vma=False
    )
```

```python
import functools

import jax
import jax.numpy as jnp
from jax import lax
from jax.experimental import pallas as pl
from jax.experimental.pallas import tpu as pltpu
from jax.sharding import PartitionSpec as P

NS_ITERS = 5
BETA_ONE = 0.9
BETA_TWO = 0.95
ADAM_EPS = 1e-08
NORM_EPS = 1e-06
LINEAR_COEFF = 3.4445
CUBIC_COEFF = -4.775
QUINTIC_COEFF = 2.0315
LANES = 128
F32 = jnp.float32


def split(x):
    high = x.astype(jnp.bfloat16)
    return high, (x - high.astype(F32)).astype(jnp.bfloat16)


def dot(a, b, dims=((1,), (0,))):
    return dot_parts(split(a), split(b), dims)


def dot_parts(a, b, dims=((1,), (0,))):
    (ka,), (kb,) = dims
    left = jnp.concatenate([a[0], a[0], a[1]], axis=ka)
    right = jnp.concatenate([b[0], b[1], b[0]], axis=kb)
    return lax.dot_general(left, right, (dims, ((), ())), preferred_element_type=F32)


def symmetric_dot(a, b, dims=((1,), (0,))):
    (ka,), (kb,) = dims
    cut = a[0].shape[0] - LANES
    head = lambda x, axis: lax.slice_in_dim(x, 0, cut, axis=axis)
    tail = lambda x, axis: lax.slice_in_dim(x, cut, cut + LANES, axis=axis)
    left = dot_parts(a, [head(x, 1 - kb) for x in b], dims)
    corner = dot_parts([tail(x, 1 - ka) for x in a], [tail(x, 1 - kb) for x in b], dims)
    right = jnp.concatenate([left[cut:].T, corner], axis=0)
    return jnp.concatenate([left, right], axis=1)


def swap(x):
    return pltpu.roll(x, LANES // 2, 1)


def low_lanes(shape):
    return lax.broadcasted_iota(jnp.int32, shape, 1) < LANES // 2


def pick(flag, x, y):
    return [jnp.where(flag, u, v) for u, v in zip(x, y)]


def thirds(ref, start=0, rows=None):
    rows = ref.shape[0] if rows is None else rows
    return [ref[pl.ds(start + k, rows // 3, stride=3), :] for k in range(3)]


def put_thirds(ref, parts):
    for k in range(3):
        ref[pl.ds(k, parts[k].shape[0], stride=3), :] = parts[k]


def interleave(scratch, index, even, odd):
    scratch[index, pl.ds(0, even.shape[0], stride=2), :] = even
    scratch[index, pl.ds(1, odd.shape[0], stride=2), :] = odd


def whole_of(scratch, first, second):
    a, b, c = first
    d, e, f = second
    low = low_lanes(a.shape)
    sb, sc, sd, se = swap(b), swap(c), swap(d), swap(e)
    interleave(scratch, 0, a, jnp.where(low, sb, sc))
    interleave(scratch, 1, jnp.where(low, b, sd), jnp.where(low, sc, e))
    interleave(scratch, 2, jnp.where(low, sd, se), f)
    return jnp.concatenate([scratch[0], scratch[1], scratch[2]], axis=1)


def half_of(scratch, flat):
    a, b, c = flat
    low = low_lanes(a.shape)
    sb, sc = swap(b), swap(c)
    interleave(scratch, 0, a, jnp.where(low, sb, sc))
    interleave(scratch, 1, jnp.where(low, b, 0.0), jnp.where(low, sc, 0.0))
    return jnp.concatenate([scratch[0], scratch[1]], axis=1)


def flat_of(scratch, half):
    scratch[0] = half[:, :LANES]
    scratch[1] = half[:, LANES:]
    pairs = half.shape[0] // 2
    even0 = scratch[0, pl.ds(0, pairs, stride=2), :]
    odd0 = swap(scratch[0, pl.ds(1, pairs, stride=2), :])
    even1 = scratch[1, pl.ds(0, pairs, stride=2), :]
    odd1 = swap(scratch[1, pl.ds(1, pairs, stride=2), :])
    low = low_lanes(even0.shape)
    return [even0, jnp.where(low, even1, odd0), jnp.where(low, odd0, odd1)]


def take_half(whole, first):
    one, two, three = whole[:, :LANES], whole[:, LANES : 2 * LANES], whole[:, 2 * LANES :]
    low = low_lanes(one.shape)
    s2, s3 = swap(two), swap(three)
    head = jnp.where(first, one, jnp.where(low, s2, s3))
    tail = jnp.where(low, jnp.where(first, two, s3), 0.0)
    return jnp.concatenate([head, tail], axis=1)


def is_first():
    return lax.rem(lax.axis_index("shard"), 2) == 0


def is_left():
    return lax.rem(lax.axis_index("shard") + lax.axis_index("tensor"), 2) == 0


def pack_kernel(hops, l_stat_ref, r_stat_ref, l_basis_ref, r_basis_ref, grads_ref, *refs):
    out_ref, small_ref, *refs = refs
    piece_refs, (corner, sems) = refs[: len(hops)], refs[len(hops) :]
    left = is_left()
    flat_rows = l_basis_ref.shape[0]
    half_rows = flat_rows // 2
    rows = grads_ref.shape[1]
    here = lax.axis_index("shard") // 2

    start = pl.multiple_of(jnp.where(is_first(), 0, half_rows), 8)

    def copies(basis_ref, stat_ref):
        return [
            pltpu.make_async_copy(stat_ref.at[pl.ds(start, half_rows)], corner, sems.at[0]),
            pltpu.make_async_copy(basis_ref, out_ref.at[pl.ds(0, flat_rows)], sems.at[1]),
        ]

    @pl.when(left)
    def _():
        for copy in copies(r_basis_ref, r_stat_ref):
            copy.start()

    @pl.when(jnp.logical_not(left))
    def _():
        for copy in copies(l_basis_ref, l_stat_ref):
            copy.start()

    more = []
    for number, (hop, piece_ref) in enumerate(zip(hops, piece_refs)):
        more.append(pltpu.make_async_copy(grads_ref.at[here ^ hop], piece_ref, sems.at[2 + number]))
    if hops:
        for k in range(grads_ref.shape[2] // LANES):
            source = grads_ref.at[here, :, pl.ds(k * LANES, LANES)]
            target = out_ref.at[pl.ds(flat_rows + k * rows, rows)]
            more.append(pltpu.make_async_copy(source, target, sems.at[2 + len(hops) + k]))
    for copy in more:
        copy.start()
    first, second = copies(l_basis_ref, l_stat_ref)
    first.wait()
    third = half_rows // 9
    a, b, c = thirds(corner)
    low = low_lanes((third, LANES))
    middle = slice(third, 2 * third)
    small_ref[pl.ds(0, third)] = jnp.where(low, a[:third], b[:third])
    small_ref[pl.ds(third, third)] = a[middle]
    small_ref[pl.ds(2 * third, third)] = jnp.where(low, swap(b[middle]), swap(c[middle]))
    small_ref[pl.ds(3 * third, 3 * third)] = corner[pl.ds(6 * third, 3 * third)]
    for copy in [second, *more]:
        copy.wait()


def corner_rows(flat_rows):
    return flat_rows // 3


def unpack_corner(got_ref):
    third = got_ref.shape[0] // 6
    small = got_ref[pl.ds(0, third), :]
    even = got_ref[pl.ds(third, third), :]
    odd = swap(got_ref[pl.ds(2 * third, third), :])
    a, b, c = thirds(got_ref, 3 * third, 3 * third)
    low = low_lanes(small.shape)
    zero = jnp.zeros_like(small)
    return [
        jnp.concatenate([jnp.where(low, small, zero), even, a], axis=0),
        jnp.concatenate([jnp.where(low, zero, small), jnp.where(low, zero, odd), b], axis=0),
        jnp.concatenate([zero, jnp.where(low, odd, zero), c], axis=0),
    ]


def known_part(first, own, scratch):
    zeros = [jnp.zeros_like(x) for x in own]
    known = whole_of(scratch, pick(first, own, zeros), pick(first, zeros, own))
    half = known.shape[0] // 2
    row = lax.broadcasted_iota(jnp.int32, known.shape, 0)
    column = lax.broadcasted_iota(jnp.int32, known.shape, 1)
    missing = (jnp.where(first, row, column) < half) & (jnp.where(first, column, row) >= half)
    return jnp.where(missing, known.T, known)


def corner_part(corner_ref, scratch):
    corner = half_of(scratch, unpack_corner(corner_ref))
    rows, wide = corner.shape
    turned = jnp.concatenate([corner, jnp.zeros((wide - rows, wide), F32)], axis=0).T[:rows]
    part = rows // 3
    row = lax.broadcasted_iota(jnp.int32, corner.shape, 0)
    column = lax.broadcasted_iota(jnp.int32, corner.shape, 1)
    missing = (row < 2 * part) & (column >= jnp.where(row < part, part, 2 * part))
    return jnp.where(missing, turned, corner)


def place_rows(grad_ref, block, rows, value):
    grad_ref[pl.ds(pl.multiple_of(block * rows, 8), rows), :] = value


def polynomial(parts):
    gram = dot_parts(parts, parts, ((1,), (1,)))
    gram_parts = split(gram)
    return CUBIC_COEFF * gram + QUINTIC_COEFF * dot_parts(gram_parts, gram_parts)


def iterate(x, steps):
    for _ in range(steps):
        parts = split(x)
        x = LINEAR_COEFF * x + dot_parts(split(polynomial(parts)), parts)
    return x


def prepare_kernel(
    l_stat_ref, r_stat_ref, l_basis_ref, r_basis_ref, got_ref, basis_ref, known_ref, right_ref, other_ref, copy_ref, scratch
):
    left, first = is_left(), is_first()
    own = pick(left, thirds(l_basis_ref), thirds(r_basis_ref))
    got = thirds(got_ref, 0, l_basis_ref.shape[0])
    basis_ref[...] = whole_of(scratch, pick(first, own, got), pick(first, got, own))
    known_ref[...] = 0.5 * known_part(first, pick(left, thirds(l_stat_ref), thirds(r_stat_ref)), scratch)
    right_ref[...] = half_of(scratch, thirds(r_basis_ref))
    other_ref[...] = jnp.where(left, r_stat_ref[...], l_stat_ref[...])
    copy_ref[...] = l_basis_ref[...]


def products_kernel(hops, basis_ref, known_ref, got_ref, *refs):
    left = is_left()
    grad_ref, stat_ref, power_ref = refs[-3:]
    if hops:
        grads_ref, mine_refs, theirs_refs = refs[0], refs[1 : 1 + len(hops)], refs[1 + len(hops) : 1 + 2 * len(hops)]
        rows = grads_ref.shape[1]
        here = lax.axis_index("shard") // 2
        parity = lax.axis_index("shard") % 2
        blocks = grad_ref.shape[1] // LANES
        start = got_ref.shape[0] - blocks * rows
        received = [got_ref[pl.ds(start + k * rows, rows), :] for k in range(blocks)]
        place_rows(grad_ref, 2 * here + parity, rows, grads_ref[here])
        place_rows(grad_ref, 2 * here + 1 - parity, rows, jnp.concatenate(received, axis=1))
        for hop, mine, theirs in zip(hops, mine_refs, theirs_refs):
            place_rows(grad_ref, 2 * (here ^ hop) + parity, rows, mine[...])
            place_rows(grad_ref, 2 * (here ^ hop) + 1 - parity, rows, theirs[...])
    else:
        grad_ref[...] = refs[0][...]
    grad = grad_ref[...]
    parts = split(jnp.where(left, grad, grad.T))
    stat = known_ref[...] + 0.5 * symmetric_dot(parts, parts, ((1,), (1,)))
    stat_ref[...] = stat
    power_ref[...] = dot(stat, basis_ref[...])


def begin_kernel(corner_ref, power_ref, basis_ref, grad_ref, right_ref, x_ref, inner_ref, scratch):
    first = is_first()
    corner = corner_part(corner_ref, scratch)
    rows, wide = corner.shape
    basis = jnp.where(first, basis_ref[pl.ds(rows, rows), :], basis_ref[pl.ds(0, rows), :])
    basis = jnp.concatenate([basis, jnp.zeros((wide - rows, 2 * rows), F32)], axis=0)
    term = 0.5 * dot(corner, basis)
    power = power_ref[...] + jnp.concatenate([jnp.where(first, 0.0, term), jnp.where(first, term, 0.0)], axis=0)
    grad_parts, right_parts = split(grad_ref[...]), split(right_ref[...])
    x = power * (1.0 / jnp.sqrt(jnp.sum(power * power) + NORM_EPS))
    parts = split(x)
    gram = dot_parts(parts, parts, ((1,), (1,)))
    inner_ref[...] = dot_parts(grad_parts, right_parts)
    gram_parts = split(gram)
    poly = CUBIC_COEFF * gram + QUINTIC_COEFF * dot_parts(gram_parts, gram_parts)
    x_ref[...] = LINEAR_COEFF * x + dot_parts(split(poly), parts)


def rows_for(hops, outer_ref, right_parts, out_ref, offset):
    rows = out_ref.shape[1]
    here = lax.axis_index("shard") // 2
    starts = [pl.multiple_of((2 * (here ^ hop) + offset) * rows, 8) if hops else 0 for hop in (0, *hops)]
    outer = [outer_ref[pl.ds(start, rows), :] for start in starts]
    partial = dot_parts(split(jnp.concatenate(outer, axis=0)), right_parts, ((1,), (1,)))
    for k in range(len(starts)):
        out_ref[k] = partial[k * rows : (k + 1) * rows]


def update_kernel(
    hops,
    inner_ref,
    basis_ref,
    left_ref,
    right_ref,
    other_left_ref,
    one_ref,
    two_ref,
    start_ref,
    new_one_ref,
    new_two_ref,
    theirs_ref,
    outer_ref,
    x_ref,
    scratch,
):
    left, first = is_left(), is_first()
    x = start_ref[...]
    parts = split(x)
    gram = dot_parts(parts, parts, ((1,), (1,)))
    own, got = thirds(left_ref), thirds(other_left_ref)
    basis_left = jnp.where(left, basis_ref[...], whole_of(scratch, pick(first, own, got), pick(first, got, own)))
    rotated = dot(basis_left.T, inner_ref[...])
    gram_parts = split(gram)
    square = dot_parts(gram_parts, gram_parts)
    rotated = flat_of(scratch, rotated)
    ones = thirds(one_ref)
    twos = thirds(two_ref)
    new_one = [BETA_ONE * m + (1.0 - BETA_ONE) * r for m, r in zip(ones, rotated)]
    new_two = [BETA_TWO * v + (1.0 - BETA_TWO) * r * r for v, r in zip(twos, rotated)]
    put_thirds(new_one_ref, new_one)
    put_thirds(new_two_ref, new_two)
    direction = [m / (jnp.sqrt(v) + ADAM_EPS) for m, v in zip(new_one, new_two)]
    outer_ref[...] = dot_parts(split(basis_left), split(half_of(scratch, direction)))
    poly_parts = split(CUBIC_COEFF * gram + QUINTIC_COEFF * square)
    moved = dot_parts(poly_parts, parts)
    rows_for(hops, outer_ref, split(right_ref[...]), theirs_ref, 1 - lax.axis_index("shard") % 2)
    x_ref[...] = LINEAR_COEFF * x + moved


def end_kernel(hops, steps, start_ref, outer_ref, right_ref, x_ref, poly_ref, send_ref, mine_ref, scratch):
    x = iterate(start_ref[...], steps - 1)
    x_ref[...] = x
    rows_for(hops, outer_ref, split(right_ref[...]), mine_ref, lax.axis_index("shard") % 2)
    poly = polynomial(split(x))
    poly_ref[...] = poly
    half = take_half(x, jnp.logical_not(is_first()))
    put_thirds(send_ref, flat_of(scratch, LINEAR_COEFF * half + dot(poly, half)))


def add_kernel(mine_ref, theirs_ref, *out_refs):
    for k, out_ref in enumerate(out_refs):
        out_ref[...] = mine_ref[k] + theirs_ref[k]


def bases_kernel(keep_ref, back_ref, new_left_ref, new_right_ref, sems):
    left = is_left()

    def copies(own_ref, other_ref):
        return [
            pltpu.make_async_copy(keep_ref, own_ref, sems.at[0]),
            pltpu.make_async_copy(back_ref, other_ref, sems.at[1]),
        ]

    @pl.when(left)
    def _():
        for copy in copies(new_left_ref, new_right_ref):
            copy.start()

    @pl.when(jnp.logical_not(left))
    def _():
        for copy in copies(new_right_ref, new_left_ref):
            copy.start()

    for copy in copies(new_left_ref, new_right_ref):
        copy.wait()


def rows_kernel(hops, *refs):
    rows_refs, (update_ref, sems) = refs[:-2], refs[-2:]
    here = lax.axis_index("shard") // 2
    copies = [
        pltpu.make_async_copy(rows_refs[k], update_ref.at[here ^ hop], sems.at[k]) for k, hop in enumerate((0, *hops))
    ]
    for copy in copies:
        copy.start()
    for copy in copies:
        copy.wait()


def rest_kernel(x_ref, poly_ref, grad_ref, new_stat_ref, other_ref, keep_ref, new_left_ref, new_right_ref, scratch):
    left = is_left()
    first = is_first()
    half = take_half(x_ref[...], first)
    put_thirds(keep_ref, flat_of(scratch, LINEAR_COEFF * half + dot(poly_ref[...], half)))
    grad = grad_ref[...]
    turned = grad.T
    a = jnp.where(left, grad, turned)
    b = jnp.where(left, turned, grad)
    new_own = flat_of(scratch, take_half(new_stat_ref[...], first))
    product = flat_of(scratch, dot(b, take_half(a, first)))
    new_other = [0.5 * u + 0.5 * v for u, v in zip(thirds(other_ref), product)]
    put_thirds(new_left_ref, pick(left, new_own, new_other))
    put_thirds(new_right_ref, pick(left, new_other, new_own))


def call(kernel, outs, scratch, products, full, name, copies=0, kind=jax.ShapeDtypeStruct, **specs):
    size = full * full
    scratch = [pltpu.VMEM(s, F32) for s in scratch]
    if copies:
        scratch.append(pltpu.SemaphoreType.DMA((copies,)))
    return pl.pallas_call(
        kernel,
        out_shape=[kind(s, F32) for s in outs],
        scratch_shapes=scratch,
        compiler_params=pltpu.CompilerParams(vmem_limit_bytes=40 * 1024 * 1024),
        cost_estimate=pl.CostEstimate(flops=int(products * 6 * full * size), bytes_accessed=16 * size, transcendentals=0),
        name=name,
        **specs,
    )


def anywhere(count):
    return [pl.BlockSpec(memory_space=pl.ANY)] * count


def after(x, *others):
    return lax.optimization_barrier((x, *others))[0]


def local(grads, moment_one, moment_two, left_stat, right_stat, left_basis, right_basis):
    tiles_here, rows_here, full = grads.shape
    size = lax.axis_size("shard")
    flat_rows = full * (full // 2) // LANES
    flat = (flat_rows, LANES)
    square = (full, full)
    block = (rows_here, full)
    parity = lax.axis_index("shard") % 2
    pairs = [(i, i ^ 1) for i in range(size)]
    sides = [list(range(k, size, 2)) for k in range(2)]
    near = size in (4, 8) and rows_here % 8 == 0
    hops = {4: (1,), 8: (2, 3, 1)}[size] if near else ()
    strips = (tiles_here, *block) if near else (1, full, full)

    def exchange(x):
        return lax.all_to_all(x, "shard", split_axis=0, concat_axis=0, axis_index_groups=sides, tiled=True)

    def hop_by(x, hop):
        return lax.ppermute(x, "shard", [(i, i ^ (2 * hop)) for i in range(size)])

    def partner(x):
        return lax.ppermute(x, "shard", pairs)

    one, two, l_stat, r_stat, l_basis, r_basis = (
        x.reshape(flat) for x in (moment_one, moment_two, left_stat, right_stat, left_basis, right_basis)
    )
    count = corner_rows(flat_rows)
    outgoing_rows = flat_rows + (rows_here * (full // LANES) if near else 0)
    outgoing, corner, *pieces = call(
        functools.partial(pack_kernel, hops),
        [(outgoing_rows, LANES), (count, LANES)] + [block] * len(hops),
        [(flat_rows // 2, LANES)],
        0.1,
        full,
        "pack",
        copies=2 + len(hops) + full // LANES,
        kind=pltpu.VMEM,
        in_specs=anywhere(5),
        out_specs=anywhere(1) + [pl.BlockSpec(memory_space=pltpu.VMEM)] + anywhere(len(hops)),
    )(*(pltpu.with_memory_space_constraint(x, pltpu.HBM) for x in (l_stat, r_stat, l_basis, r_basis, grads)))
    got = partner(outgoing)
    if near:
        mine = [hop_by(piece, hop) for hop, piece in zip(hops, pieces)]
        theirs = [partner(x) for x in mine]
        rows = (grads, *mine, *theirs)
    else:
        mine = exchange(grads)
        theirs = partner(mine)
        even, odd = jnp.where(parity == 0, mine, theirs), jnp.where(parity == 0, theirs, mine)
        rows = (jnp.stack([even, odd], axis=1).reshape(square),)
        mine = [mine]
    got_corner = partner(after(corner, theirs[0] if near else mine[0]))
    wide = (full, 2 * LANES)
    basis, known, right, other, left = call(
        prepare_kernel, [square, square, wide, flat, flat], [(3, full, LANES)], 0.1, full, "prepare"
    )(l_stat, r_stat, l_basis, r_basis, got)
    grad, new_stat, power = call(
        functools.partial(products_kernel, hops), [square, square, square], [], 3, full, "products"
    )(basis, known, got, *rows)
    tensors = lax.axis_size("tensor")
    place = lambda t, i: i * tensors + t
    cycle = []
    for t in range(0, tensors - tensors % 2, 2):
        for i in range(0, size, 2):
            cycle += [(place(t, i), place(t, i + 1)), (place(t, i + 1), place(t + 1, i + 1))]
            cycle += [(place(t + 1, i + 1), place(t + 1, i)), (place(t + 1, i), place(t, i))]
    cycle += [(place(t, i), place(t, i ^ 1)) for t in range(tensors - tensors % 2, tensors) for i in range(size)]
    other_left = lax.ppermute(after(l_basis, basis, *(theirs[:2] if near else mine)), ("shard", "tensor"), cycle)
    x, inner = call(begin_kernel, [square, wide], [(2, full // 2, LANES)], 7, full, "begin")(
        got_corner, power, basis, grad, right
    )
    new_one, new_two, other_rows, outer, x = call(
        functools.partial(update_kernel, hops), [flat, flat, strips, wide, square], [(3, full, LANES)], 5, full, "update"
    )(inner, basis, left, right, other_left, one, two, x)
    if not near:
        partial = other_rows.reshape(tiles_here, 2, rows_here, full)
        other_rows = lax.dynamic_index_in_dim(partial, 1 - parity, 1, keepdims=False)
    got_rows = partner(other_rows)
    x, poly, send, own_rows = call(
        functools.partial(end_kernel, hops, NS_ITERS - 2),
        [square, square, flat, strips],
        [(3, full, LANES)],
        9,
        full,
        "end",
    )(after(x, other_rows), outer, right)
    back = partner(send)
    keep, new_left, new_right = call(rest_kernel, [flat, flat, flat], [(3, full, LANES)], 1.5, full, "rest")(
        x, poly, grad, new_stat, other
    )
    if near:
        kept, *sums = call(add_kernel, [block] * (1 + len(hops)), [], 0.1, full, "add")(
            after(own_rows, send), after(got_rows, send)
        )
        returned = [hop_by(x, hop) for hop, x in zip(hops, sums)]
        update = call(
            functools.partial(rows_kernel, hops),
            [grads.shape],
            [],
            0.1,
            full,
            "rows",
            copies=1 + len(hops),
            in_specs=anywhere(1 + len(hops)),
            out_specs=anywhere(1),
        )(kept, *returned)[0]
    else:
        own_rows = lax.dynamic_index_in_dim(partial, parity, 1, keepdims=False)
        update = exchange(after(own_rows, send) + after(got_rows, send))
    new_l_basis, new_r_basis = call(
        bases_kernel, [flat, flat], [], 0.1, full, "bases", copies=2, in_specs=anywhere(2), out_specs=anywhere(2)
    )(keep, back)
    halves = (new_one, new_two, new_left, new_right, new_l_basis, new_r_basis)
    return (update, *(x.reshape(1, flat_rows * LANES) for x in halves))


def solution(mesh):
    halves = P(("tensor", "shard"), None)
    rows = P("tensor", "shard", None)
    return jax.shard_map(
        local, mesh=mesh, in_specs=(rows,) + (halves,) * 6, out_specs=(rows,) + (halves,) * 6, check_vma=False
    )
```

```python
import functools

import jax
import jax.numpy as jnp
from jax import lax
from jax.experimental import pallas as pl
from jax.experimental.pallas import tpu as pltpu
from jax.sharding import PartitionSpec as P

NS_ITERS = 5
BETA_ONE = 0.9
BETA_TWO = 0.95
ADAM_EPS = 1e-08
NORM_EPS = 1e-06
LINEAR_COEFF = 3.4445
CUBIC_COEFF = -4.775
QUINTIC_COEFF = 2.0315
LANES = 128
F32 = jnp.float32


def split(x):
    high = x.astype(jnp.bfloat16)
    return high, (x - high.astype(F32)).astype(jnp.bfloat16)


def dot(a, b, dims=((1,), (0,))):
    return dot_parts(split(a), split(b), dims)


def dot_parts(a, b, dims=((1,), (0,))):
    (ka,), (kb,) = dims
    left = jnp.concatenate([a[0], a[0], a[1]], axis=ka)
    right = jnp.concatenate([b[0], b[1], b[0]], axis=kb)
    return lax.dot_general(left, right, (dims, ((), ())), preferred_element_type=F32)


def symmetric_dot(a, b, dims=((1,), (0,))):
    (ka,), (kb,) = dims
    cut = a[0].shape[0] - LANES
    head = lambda x, axis: lax.slice_in_dim(x, 0, cut, axis=axis)
    tail = lambda x, axis: lax.slice_in_dim(x, cut, cut + LANES, axis=axis)
    left = dot_parts(a, [head(x, 1 - kb) for x in b], dims)
    corner = dot_parts([tail(x, 1 - ka) for x in a], [tail(x, 1 - kb) for x in b], dims)
    right = jnp.concatenate([left[cut:].T, corner], axis=0)
    return jnp.concatenate([left, right], axis=1)


def swap(x):
    return pltpu.roll(x, LANES // 2, 1)


def low_lanes(shape):
    return lax.broadcasted_iota(jnp.int32, shape, 1) < LANES // 2


def pick(flag, x, y):
    return [jnp.where(flag, u, v) for u, v in zip(x, y)]


def thirds(ref, start=0, rows=None):
    rows = ref.shape[0] if rows is None else rows
    return [ref[pl.ds(start + k, rows // 3, stride=3), :] for k in range(3)]


def put_thirds(ref, parts):
    for k in range(3):
        ref[pl.ds(k, parts[k].shape[0], stride=3), :] = parts[k]


def interleave(scratch, index, even, odd):
    scratch[index, pl.ds(0, even.shape[0], stride=2), :] = even
    scratch[index, pl.ds(1, odd.shape[0], stride=2), :] = odd


def whole_of(scratch, first, second):
    a, b, c = first
    d, e, f = second
    low = low_lanes(a.shape)
    sb, sc, sd, se = swap(b), swap(c), swap(d), swap(e)
    interleave(scratch, 0, a, jnp.where(low, sb, sc))
    interleave(scratch, 1, jnp.where(low, b, sd), jnp.where(low, sc, e))
    interleave(scratch, 2, jnp.where(low, sd, se), f)
    return jnp.concatenate([scratch[0], scratch[1], scratch[2]], axis=1)


def half_of(scratch, flat):
    a, b, c = flat
    low = low_lanes(a.shape)
    sb, sc = swap(b), swap(c)
    interleave(scratch, 0, a, jnp.where(low, sb, sc))
    interleave(scratch, 1, jnp.where(low, b, 0.0), jnp.where(low, sc, 0.0))
    return jnp.concatenate([scratch[0], scratch[1]], axis=1)


def flat_of(scratch, half):
    scratch[0] = half[:, :LANES]
    scratch[1] = half[:, LANES:]
    pairs = half.shape[0] // 2
    even0 = scratch[0, pl.ds(0, pairs, stride=2), :]
    odd0 = swap(scratch[0, pl.ds(1, pairs, stride=2), :])
    even1 = scratch[1, pl.ds(0, pairs, stride=2), :]
    odd1 = swap(scratch[1, pl.ds(1, pairs, stride=2), :])
    low = low_lanes(even0.shape)
    return [even0, jnp.where(low, even1, odd0), jnp.where(low, odd0, odd1)]


def take_half(whole, first):
    one, two, three = whole[:, :LANES], whole[:, LANES : 2 * LANES], whole[:, 2 * LANES :]
    low = low_lanes(one.shape)
    s2, s3 = swap(two), swap(three)
    head = jnp.where(first, one, jnp.where(low, s2, s3))
    tail = jnp.where(low, jnp.where(first, two, s3), 0.0)
    return jnp.concatenate([head, tail], axis=1)


def is_first():
    return lax.rem(lax.axis_index("shard"), 2) == 0


def is_left():
    return lax.rem(lax.axis_index("shard") + lax.axis_index("tensor"), 2) == 0


def pack_kernel(hops, l_stat_ref, r_stat_ref, l_basis_ref, r_basis_ref, grads_ref, *refs):
    out_ref, small_ref, *refs = refs
    piece_refs, (corner, sems) = refs[: len(hops)], refs[len(hops) :]
    left = is_left()
    flat_rows = l_basis_ref.shape[0]
    half_rows = flat_rows // 2
    rows = grads_ref.shape[1]
    here = lax.axis_index("shard") // 2

    start = pl.multiple_of(jnp.where(is_first(), 0, half_rows), 8)

    def copies(basis_ref, stat_ref):
        return [
            pltpu.make_async_copy(stat_ref.at[pl.ds(start, half_rows)], corner, sems.at[0]),
            pltpu.make_async_copy(basis_ref, out_ref.at[pl.ds(0, flat_rows)], sems.at[1]),
        ]

    @pl.when(left)
    def _():
        for copy in copies(r_basis_ref, r_stat_ref):
            copy.start()

    @pl.when(jnp.logical_not(left))
    def _():
        for copy in copies(l_basis_ref, l_stat_ref):
            copy.start()

    more = []
    for number, (hop, piece_ref) in enumerate(zip(hops, piece_refs)):
        more.append(pltpu.make_async_copy(grads_ref.at[here ^ hop], piece_ref, sems.at[2 + number]))
    if hops:
        for k in range(grads_ref.shape[2] // LANES):
            source = grads_ref.at[here, :, pl.ds(k * LANES, LANES)]
            target = out_ref.at[pl.ds(flat_rows + k * rows, rows)]
            more.append(pltpu.make_async_copy(source, target, sems.at[2 + len(hops) + k]))
    for copy in more:
        copy.start()
    first, second = copies(l_basis_ref, l_stat_ref)
    first.wait()
    third = half_rows // 9
    a, b, c = thirds(corner)
    low = low_lanes((third, LANES))
    middle = slice(third, 2 * third)
    small_ref[pl.ds(0, third)] = jnp.where(low, a[:third], b[:third])
    small_ref[pl.ds(third, third)] = a[middle]
    small_ref[pl.ds(2 * third, third)] = jnp.where(low, swap(b[middle]), swap(c[middle]))
    small_ref[pl.ds(3 * third, 3 * third)] = corner[pl.ds(6 * third, 3 * third)]
    for copy in [second, *more]:
        copy.wait()


def corner_rows(flat_rows):
    return flat_rows // 3


def unpack_corner(got_ref):
    third = got_ref.shape[0] // 6
    small = got_ref[pl.ds(0, third), :]
    even = got_ref[pl.ds(third, third), :]
    odd = swap(got_ref[pl.ds(2 * third, third), :])
    a, b, c = thirds(got_ref, 3 * third, 3 * third)
    low = low_lanes(small.shape)
    zero = jnp.zeros_like(small)
    return [
        jnp.concatenate([jnp.where(low, small, zero), even, a], axis=0),
        jnp.concatenate([jnp.where(low, zero, small), jnp.where(low, zero, odd), b], axis=0),
        jnp.concatenate([zero, jnp.where(low, odd, zero), c], axis=0),
    ]


def known_part(first, own, scratch):
    zeros = [jnp.zeros_like(x) for x in own]
    known = whole_of(scratch, pick(first, own, zeros), pick(first, zeros, own))
    half = known.shape[0] // 2
    row = lax.broadcasted_iota(jnp.int32, known.shape, 0)
    column = lax.broadcasted_iota(jnp.int32, known.shape, 1)
    missing = (jnp.where(first, row, column) < half) & (jnp.where(first, column, row) >= half)
    return jnp.where(missing, known.T, known)


def corner_part(corner_ref, scratch):
    corner = half_of(scratch, unpack_corner(corner_ref))
    rows, wide = corner.shape
    turned = jnp.concatenate([corner, jnp.zeros((wide - rows, wide), F32)], axis=0).T[:rows]
    part = rows // 3
    row = lax.broadcasted_iota(jnp.int32, corner.shape, 0)
    column = lax.broadcasted_iota(jnp.int32, corner.shape, 1)
    missing = (row < 2 * part) & (column >= jnp.where(row < part, part, 2 * part))
    return jnp.where(missing, turned, corner)


def place_rows(grad_ref, block, rows, value):
    grad_ref[pl.ds(pl.multiple_of(block * rows, 8), rows), :] = value


def polynomial(parts):
    gram = dot_parts(parts, parts, ((1,), (1,)))
    gram_parts = split(gram)
    return CUBIC_COEFF * gram + QUINTIC_COEFF * dot_parts(gram_parts, gram_parts)


def iterate(x, steps):
    for _ in range(steps):
        parts = split(x)
        x = LINEAR_COEFF * x + dot_parts(split(polynomial(parts)), parts)
    return x


def prepare_kernel(
    l_stat_ref,
    r_stat_ref,
    l_basis_ref,
    r_basis_ref,
    got_ref,
    basis_ref,
    known_ref,
    right_ref,
    turned_ref,
    other_ref,
    copy_ref,
    scratch,
):
    left, first = is_left(), is_first()
    own = pick(left, thirds(l_basis_ref), thirds(r_basis_ref))
    got = thirds(got_ref, 0, l_basis_ref.shape[0])
    basis_ref[...] = whole_of(scratch, pick(first, own, got), pick(first, got, own))
    known_ref[...] = 0.5 * known_part(first, pick(left, thirds(l_stat_ref), thirds(r_stat_ref)), scratch)
    right = half_of(scratch, thirds(r_basis_ref))
    right_ref[...] = right
    turned_ref[...] = right.T
    other_ref[...] = jnp.where(left, r_stat_ref[...], l_stat_ref[...])
    copy_ref[...] = l_basis_ref[...]


def products_kernel(hops, basis_ref, known_ref, got_ref, *refs):
    left = is_left()
    grad_ref, stat_ref, power_ref = refs[-3:]
    if hops:
        grads_ref, mine_refs, theirs_refs = refs[0], refs[1 : 1 + len(hops)], refs[1 + len(hops) : 1 + 2 * len(hops)]
        rows = grads_ref.shape[1]
        here = lax.axis_index("shard") // 2
        parity = lax.axis_index("shard") % 2
        blocks = grad_ref.shape[1] // LANES
        start = got_ref.shape[0] - blocks * rows
        received = [got_ref[pl.ds(start + k * rows, rows), :] for k in range(blocks)]
        place_rows(grad_ref, 2 * here + parity, rows, grads_ref[here])
        place_rows(grad_ref, 2 * here + 1 - parity, rows, jnp.concatenate(received, axis=1))
        for hop, mine, theirs in zip(hops, mine_refs, theirs_refs):
            place_rows(grad_ref, 2 * (here ^ hop) + parity, rows, mine[...])
            place_rows(grad_ref, 2 * (here ^ hop) + 1 - parity, rows, theirs[...])
    else:
        grad_ref[...] = refs[0][...]
    grad = grad_ref[...]
    parts = split(jnp.where(left, grad, grad.T))
    stat = known_ref[...] + 0.5 * symmetric_dot(parts, parts, ((1,), (1,)))
    stat_ref[...] = stat
    power_ref[...] = dot(stat, basis_ref[...])


def begin_kernel(corner_ref, power_ref, basis_ref, grad_ref, turned_ref, x_ref, inner_ref, scratch):
    first = is_first()
    corner = corner_part(corner_ref, scratch)
    rows, wide = corner.shape
    basis = jnp.where(first, basis_ref[pl.ds(rows, rows), :], basis_ref[pl.ds(0, rows), :])
    basis = jnp.concatenate([basis, jnp.zeros((wide - rows, 2 * rows), F32)], axis=0)
    term = 0.5 * dot(corner, basis)
    power = power_ref[...] + jnp.concatenate([jnp.where(first, 0.0, term), jnp.where(first, term, 0.0)], axis=0)
    grad_parts, turned_parts = split(grad_ref[...]), split(turned_ref[...])
    x = power * (1.0 / jnp.sqrt(jnp.sum(power * power) + NORM_EPS))
    parts = split(x)
    gram = dot_parts(parts, parts, ((1,), (1,)))
    inner_ref[...] = dot_parts(turned_parts, grad_parts, ((1,), (1,)))
    gram_parts = split(gram)
    poly = CUBIC_COEFF * gram + QUINTIC_COEFF * dot_parts(gram_parts, gram_parts)
    x_ref[...] = LINEAR_COEFF * x + dot_parts(split(poly), parts)


def rows_for(hops, outer_ref, right_parts, out_ref, offset):
    rows = out_ref.shape[1]
    here = lax.axis_index("shard") // 2
    starts = [pl.multiple_of((2 * (here ^ hop) + offset) * rows, 8) if hops else 0 for hop in (0, *hops)]
    outer = [outer_ref[pl.ds(start, rows), :] for start in starts]
    partial = dot_parts(split(jnp.concatenate(outer, axis=0)), right_parts, ((1,), (1,)))
    for k in range(len(starts)):
        out_ref[k] = partial[k * rows : (k + 1) * rows]


def update_kernel(
    hops,
    inner_ref,
    basis_ref,
    left_ref,
    right_ref,
    other_left_ref,
    one_ref,
    two_ref,
    start_ref,
    new_one_ref,
    new_two_ref,
    theirs_ref,
    outer_ref,
    x_ref,
    scratch,
):
    left, first = is_left(), is_first()
    x = start_ref[...]
    parts = split(x)
    gram = dot_parts(parts, parts, ((1,), (1,)))
    own, got = thirds(left_ref), thirds(other_left_ref)
    basis_left = jnp.where(left, basis_ref[...], whole_of(scratch, pick(first, own, got), pick(first, got, own)))
    left_parts = split(basis_left)
    rotated = dot_parts(split(inner_ref[...]), left_parts).T
    gram_parts = split(gram)
    square = dot_parts(gram_parts, gram_parts)
    rotated = flat_of(scratch, rotated)
    ones = thirds(one_ref)
    twos = thirds(two_ref)
    new_one = [BETA_ONE * m + (1.0 - BETA_ONE) * r for m, r in zip(ones, rotated)]
    new_two = [BETA_TWO * v + (1.0 - BETA_TWO) * r * r for v, r in zip(twos, rotated)]
    put_thirds(new_one_ref, new_one)
    put_thirds(new_two_ref, new_two)
    direction = [m / (jnp.sqrt(v) + ADAM_EPS) for m, v in zip(new_one, new_two)]
    outer_ref[...] = dot_parts(left_parts, split(half_of(scratch, direction)))
    poly_parts = split(CUBIC_COEFF * gram + QUINTIC_COEFF * square)
    moved = dot_parts(poly_parts, parts)
    rows_for(hops, outer_ref, split(right_ref[...]), theirs_ref, 1 - lax.axis_index("shard") % 2)
    x_ref[...] = LINEAR_COEFF * x + moved


def end_kernel(hops, steps, start_ref, outer_ref, right_ref, x_ref, poly_ref, send_ref, mine_ref, scratch):
    x = iterate(start_ref[...], steps - 1)
    x_ref[...] = x
    rows_for(hops, outer_ref, split(right_ref[...]), mine_ref, lax.axis_index("shard") % 2)
    poly = polynomial(split(x))
    poly_ref[...] = poly
    half = take_half(x, jnp.logical_not(is_first()))
    put_thirds(send_ref, flat_of(scratch, LINEAR_COEFF * half + dot(poly, half)))


def add_kernel(mine_ref, theirs_ref, *out_refs):
    for k, out_ref in enumerate(out_refs):
        out_ref[...] = mine_ref[k] + theirs_ref[k]


def bases_kernel(keep_ref, back_ref, new_left_ref, new_right_ref, sems):
    left = is_left()

    def copies(own_ref, other_ref):
        return [
            pltpu.make_async_copy(keep_ref, own_ref, sems.at[0]),
            pltpu.make_async_copy(back_ref, other_ref, sems.at[1]),
        ]

    @pl.when(left)
    def _():
        for copy in copies(new_left_ref, new_right_ref):
            copy.start()

    @pl.when(jnp.logical_not(left))
    def _():
        for copy in copies(new_right_ref, new_left_ref):
            copy.start()

    for copy in copies(new_left_ref, new_right_ref):
        copy.wait()


def rows_kernel(hops, *refs):
    rows_refs, (update_ref, sems) = refs[:-2], refs[-2:]
    here = lax.axis_index("shard") // 2
    copies = [
        pltpu.make_async_copy(rows_refs[k], update_ref.at[here ^ hop], sems.at[k]) for k, hop in enumerate((0, *hops))
    ]
    for copy in copies:
        copy.start()
    for copy in copies:
        copy.wait()


def rest_kernel(x_ref, poly_ref, grad_ref, new_stat_ref, other_ref, keep_ref, new_left_ref, new_right_ref, scratch):
    left = is_left()
    first = is_first()
    half = take_half(x_ref[...], first)
    put_thirds(keep_ref, flat_of(scratch, LINEAR_COEFF * half + dot(poly_ref[...], half)))
    grad = grad_ref[...]
    turned = grad.T
    a = jnp.where(left, grad, turned)
    b = jnp.where(left, turned, grad)
    new_own = flat_of(scratch, take_half(new_stat_ref[...], first))
    product = flat_of(scratch, dot(b, take_half(a, first)))
    new_other = [0.5 * u + 0.5 * v for u, v in zip(thirds(other_ref), product)]
    put_thirds(new_left_ref, pick(left, new_own, new_other))
    put_thirds(new_right_ref, pick(left, new_other, new_own))


def call(kernel, outs, scratch, products, full, name, copies=0, kind=jax.ShapeDtypeStruct, **specs):
    size = full * full
    scratch = [pltpu.VMEM(s, F32) for s in scratch]
    if copies:
        scratch.append(pltpu.SemaphoreType.DMA((copies,)))
    return pl.pallas_call(
        kernel,
        out_shape=[kind(s, F32) for s in outs],
        scratch_shapes=scratch,
        compiler_params=pltpu.CompilerParams(vmem_limit_bytes=40 * 1024 * 1024),
        cost_estimate=pl.CostEstimate(flops=int(products * 6 * full * size), bytes_accessed=16 * size, transcendentals=0),
        name=name,
        **specs,
    )


def anywhere(count):
    return [pl.BlockSpec(memory_space=pl.ANY)] * count


def after(x, *others):
    return lax.optimization_barrier((x, *others))[0]


def local(grads, moment_one, moment_two, left_stat, right_stat, left_basis, right_basis):
    tiles_here, rows_here, full = grads.shape
    size = lax.axis_size("shard")
    flat_rows = full * (full // 2) // LANES
    flat = (flat_rows, LANES)
    square = (full, full)
    block = (rows_here, full)
    parity = lax.axis_index("shard") % 2
    pairs = [(i, i ^ 1) for i in range(size)]
    sides = [list(range(k, size, 2)) for k in range(2)]
    near = size in (4, 8) and rows_here % 8 == 0
    hops = {4: (1,), 8: (2, 3, 1)}[size] if near else ()
    strips = (tiles_here, *block) if near else (1, full, full)

    def exchange(x):
        return lax.all_to_all(x, "shard", split_axis=0, concat_axis=0, axis_index_groups=sides, tiled=True)

    def hop_by(x, hop):
        return lax.ppermute(x, "shard", [(i, i ^ (2 * hop)) for i in range(size)])

    def partner(x):
        return lax.ppermute(x, "shard", pairs)

    one, two, l_stat, r_stat, l_basis, r_basis = (
        x.reshape(flat) for x in (moment_one, moment_two, left_stat, right_stat, left_basis, right_basis)
    )
    count = corner_rows(flat_rows)
    outgoing_rows = flat_rows + (rows_here * (full // LANES) if near else 0)
    outgoing, corner, *pieces = call(
        functools.partial(pack_kernel, hops),
        [(outgoing_rows, LANES), (count, LANES)] + [block] * len(hops),
        [(flat_rows // 2, LANES)],
        0.1,
        full,
        "pack",
        copies=2 + len(hops) + full // LANES,
        kind=pltpu.VMEM,
        in_specs=anywhere(5),
        out_specs=anywhere(1) + [pl.BlockSpec(memory_space=pltpu.VMEM)] + anywhere(len(hops)),
    )(*(pltpu.with_memory_space_constraint(x, pltpu.HBM) for x in (l_stat, r_stat, l_basis, r_basis, grads)))
    got = partner(outgoing)
    if near:
        mine = [hop_by(piece, hop) for hop, piece in zip(hops, pieces)]
        theirs = [partner(x) for x in mine]
        rows = (grads, *mine, *theirs)
    else:
        mine = exchange(grads)
        theirs = partner(mine)
        even, odd = jnp.where(parity == 0, mine, theirs), jnp.where(parity == 0, theirs, mine)
        rows = (jnp.stack([even, odd], axis=1).reshape(square),)
        mine = [mine]
    got_corner = partner(after(corner, theirs[0] if near else mine[0]))
    wide = (full, 2 * LANES)
    tall = (2 * LANES, full)
    basis, known, right, turned, other, left = call(
        prepare_kernel, [square, square, wide, tall, flat, flat], [(3, full, LANES)], 0.1, full, "prepare"
    )(l_stat, r_stat, l_basis, r_basis, got)
    grad, new_stat, power = call(
        functools.partial(products_kernel, hops), [square, square, square], [], 3, full, "products"
    )(basis, known, got, *rows)
    tensors = lax.axis_size("tensor")
    place = lambda t, i: i * tensors + t
    cycle = []
    for t in range(0, tensors - tensors % 2, 2):
        for i in range(0, size, 2):
            cycle += [(place(t, i), place(t, i + 1)), (place(t, i + 1), place(t + 1, i + 1))]
            cycle += [(place(t + 1, i + 1), place(t + 1, i)), (place(t + 1, i), place(t, i))]
    cycle += [(place(t, i), place(t, i ^ 1)) for t in range(tensors - tensors % 2, tensors) for i in range(size)]
    other_left = lax.ppermute(after(l_basis, basis, *(theirs[:2] if near else mine)), ("shard", "tensor"), cycle)
    x, inner = call(begin_kernel, [square, tall], [(2, full // 2, LANES)], 7, full, "begin")(
        got_corner, power, basis, grad, turned
    )
    new_one, new_two, other_rows, outer, x = call(
        functools.partial(update_kernel, hops), [flat, flat, strips, wide, square], [(3, full, LANES)], 5, full, "update"
    )(inner, basis, left, right, other_left, one, two, x)
    if not near:
        partial = other_rows.reshape(tiles_here, 2, rows_here, full)
        other_rows = lax.dynamic_index_in_dim(partial, 1 - parity, 1, keepdims=False)
    got_rows = partner(other_rows)
    x, poly, send, own_rows = call(
        functools.partial(end_kernel, hops, NS_ITERS - 2),
        [square, square, flat, strips],
        [(3, full, LANES)],
        9,
        full,
        "end",
    )(after(x, other_rows), outer, right)
    back = partner(send)
    keep, new_left, new_right = call(rest_kernel, [flat, flat, flat], [(3, full, LANES)], 1.5, full, "rest")(
        x, poly, grad, new_stat, other
    )
    if near:
        kept, *sums = call(add_kernel, [block] * (1 + len(hops)), [], 0.1, full, "add")(
            after(own_rows, send), after(got_rows, send)
        )
        returned = [hop_by(x, hop) for hop, x in zip(hops, sums)]
        update = call(
            functools.partial(rows_kernel, hops),
            [grads.shape],
            [],
            0.1,
            full,
            "rows",
            copies=1 + len(hops),
            in_specs=anywhere(1 + len(hops)),
            out_specs=anywhere(1),
        )(kept, *returned)[0]
    else:
        own_rows = lax.dynamic_index_in_dim(partial, parity, 1, keepdims=False)
        update = exchange(after(own_rows, send) + after(got_rows, send))
    new_l_basis, new_r_basis = call(
        bases_kernel, [flat, flat], [], 0.1, full, "bases", copies=2, in_specs=anywhere(2), out_specs=anywhere(2)
    )(keep, back)
    halves = (new_one, new_two, new_left, new_right, new_l_basis, new_r_basis)
    return (update, *(x.reshape(1, flat_rows * LANES) for x in halves))


def solution(mesh):
    halves = P(("tensor", "shard"), None)
    rows = P("tensor", "shard", None)
    return jax.shard_map(
        local, mesh=mesh, in_specs=(rows,) + (halves,) * 6, out_specs=(rows,) + (halves,) * 6, check_vma=False
    )
```

```python
import functools

import jax
import jax.numpy as jnp
from jax import lax
from jax.experimental import pallas as pl
from jax.experimental.pallas import tpu as pltpu
from jax.sharding import PartitionSpec as P

NS_ITERS = 5
BETA_ONE = 0.9
BETA_TWO = 0.95
ADAM_EPS = 1e-08
NORM_EPS = 1e-06
LINEAR_COEFF = 3.4445
CUBIC_COEFF = -4.775
QUINTIC_COEFF = 2.0315
LANES = 128
F32 = jnp.float32


def split(x):
    high = x.astype(jnp.bfloat16)
    return high, (x - high.astype(F32)).astype(jnp.bfloat16)


def dot(a, b, dims=((1,), (0,))):
    return dot_parts(split(a), split(b), dims)


def dot_parts(a, b, dims=((1,), (0,))):
    (ka,), (kb,) = dims
    left = jnp.concatenate([a[0], a[0], a[1]], axis=ka)
    right = jnp.concatenate([b[0], b[1], b[0]], axis=kb)
    return lax.dot_general(left, right, (dims, ((), ())), preferred_element_type=F32)


def symmetric_dot(a, b, dims=((1,), (0,))):
    (ka,), (kb,) = dims
    cut = a[0].shape[0] - LANES
    head = lambda x, axis: lax.slice_in_dim(x, 0, cut, axis=axis)
    tail = lambda x, axis: lax.slice_in_dim(x, cut, cut + LANES, axis=axis)
    left = dot_parts(a, [head(x, 1 - kb) for x in b], dims)
    corner = dot_parts([tail(x, 1 - ka) for x in a], [tail(x, 1 - kb) for x in b], dims)
    right = jnp.concatenate([left[cut:].T, corner], axis=0)
    return jnp.concatenate([left, right], axis=1)


def swap(x):
    return pltpu.roll(x, LANES // 2, 1)


def low_lanes(shape):
    return lax.broadcasted_iota(jnp.int32, shape, 1) < LANES // 2


def pick(flag, x, y):
    return [jnp.where(flag, u, v) for u, v in zip(x, y)]


def thirds(ref, start=0, rows=None):
    rows = ref.shape[0] if rows is None else rows
    return [ref[pl.ds(start + k, rows // 3, stride=3), :] for k in range(3)]


def put_thirds(ref, parts):
    for k in range(3):
        ref[pl.ds(k, parts[k].shape[0], stride=3), :] = parts[k]


def interleave(scratch, index, even, odd):
    scratch[index, pl.ds(0, even.shape[0], stride=2), :] = even
    scratch[index, pl.ds(1, odd.shape[0], stride=2), :] = odd


def whole_of(scratch, first, second):
    a, b, c = first
    d, e, f = second
    low = low_lanes(a.shape)
    sb, sc, sd, se = swap(b), swap(c), swap(d), swap(e)
    interleave(scratch, 0, a, jnp.where(low, sb, sc))
    interleave(scratch, 1, jnp.where(low, b, sd), jnp.where(low, sc, e))
    interleave(scratch, 2, jnp.where(low, sd, se), f)
    return jnp.concatenate([scratch[0], scratch[1], scratch[2]], axis=1)


def half_of(scratch, flat):
    a, b, c = flat
    low = low_lanes(a.shape)
    sb, sc = swap(b), swap(c)
    interleave(scratch, 0, a, jnp.where(low, sb, sc))
    interleave(scratch, 1, jnp.where(low, b, 0.0), jnp.where(low, sc, 0.0))
    return jnp.concatenate([scratch[0], scratch[1]], axis=1)


def flat_of(scratch, half):
    scratch[0] = half[:, :LANES]
    scratch[1] = half[:, LANES:]
    pairs = half.shape[0] // 2
    even0 = scratch[0, pl.ds(0, pairs, stride=2), :]
    odd0 = swap(scratch[0, pl.ds(1, pairs, stride=2), :])
    even1 = scratch[1, pl.ds(0, pairs, stride=2), :]
    odd1 = swap(scratch[1, pl.ds(1, pairs, stride=2), :])
    low = low_lanes(even0.shape)
    return [even0, jnp.where(low, even1, odd0), jnp.where(low, odd0, odd1)]


def take_half(whole, first):
    one, two, three = whole[:, :LANES], whole[:, LANES : 2 * LANES], whole[:, 2 * LANES :]
    low = low_lanes(one.shape)
    s2, s3 = swap(two), swap(three)
    head = jnp.where(first, one, jnp.where(low, s2, s3))
    tail = jnp.where(low, jnp.where(first, two, s3), 0.0)
    return jnp.concatenate([head, tail], axis=1)


def is_first():
    return lax.rem(lax.axis_index("shard"), 2) == 0


def is_left():
    return lax.rem(lax.axis_index("shard") + lax.axis_index("tensor"), 2) == 0


def pack_kernel(hops, l_stat_ref, r_stat_ref, l_basis_ref, r_basis_ref, grads_ref, *refs):
    out_ref, small_ref, *refs = refs
    piece_refs, (corner, sems) = refs[: len(hops)], refs[len(hops) :]
    left = is_left()
    flat_rows = l_basis_ref.shape[0]
    half_rows = flat_rows // 2
    rows = grads_ref.shape[1]
    here = lax.axis_index("shard") // 2

    start = pl.multiple_of(jnp.where(is_first(), 0, half_rows), 8)

    def copies(basis_ref, stat_ref):
        return [
            pltpu.make_async_copy(stat_ref.at[pl.ds(start, half_rows)], corner, sems.at[0]),
            pltpu.make_async_copy(basis_ref, out_ref.at[pl.ds(0, flat_rows)], sems.at[1]),
        ]

    @pl.when(left)
    def _():
        for copy in copies(r_basis_ref, r_stat_ref):
            copy.start()

    @pl.when(jnp.logical_not(left))
    def _():
        for copy in copies(l_basis_ref, l_stat_ref):
            copy.start()

    more = []
    for number, (hop, piece_ref) in enumerate(zip(hops, piece_refs)):
        more.append(pltpu.make_async_copy(grads_ref.at[here ^ hop], piece_ref, sems.at[2 + number]))
    if hops:
        for k in range(grads_ref.shape[2] // LANES):
            source = grads_ref.at[here, :, pl.ds(k * LANES, LANES)]
            target = out_ref.at[pl.ds(flat_rows + k * rows, rows)]
            more.append(pltpu.make_async_copy(source, target, sems.at[2 + len(hops) + k]))
    for copy in more:
        copy.start()
    first, second = copies(l_basis_ref, l_stat_ref)
    first.wait()
    third = half_rows // 9
    a, b, c = thirds(corner)
    low = low_lanes((third, LANES))
    middle = slice(third, 2 * third)
    small_ref[pl.ds(0, third)] = jnp.where(low, a[:third], b[:third])
    small_ref[pl.ds(third, third)] = a[middle]
    small_ref[pl.ds(2 * third, third)] = jnp.where(low, swap(b[middle]), swap(c[middle]))
    small_ref[pl.ds(3 * third, 3 * third)] = corner[pl.ds(6 * third, 3 * third)]
    for copy in [second, *more]:
        copy.wait()


def corner_rows(flat_rows):
    return flat_rows // 3


def unpack_corner(got_ref):
    third = got_ref.shape[0] // 6
    small = got_ref[pl.ds(0, third), :]
    even = got_ref[pl.ds(third, third), :]
    odd = swap(got_ref[pl.ds(2 * third, third), :])
    a, b, c = thirds(got_ref, 3 * third, 3 * third)
    low = low_lanes(small.shape)
    zero = jnp.zeros_like(small)
    return [
        jnp.concatenate([jnp.where(low, small, zero), even, a], axis=0),
        jnp.concatenate([jnp.where(low, zero, small), jnp.where(low, zero, odd), b], axis=0),
        jnp.concatenate([zero, jnp.where(low, odd, zero), c], axis=0),
    ]


def known_part(first, own, scratch):
    zeros = [jnp.zeros_like(x) for x in own]
    known = whole_of(scratch, pick(first, own, zeros), pick(first, zeros, own))
    half = known.shape[0] // 2
    row = lax.broadcasted_iota(jnp.int32, known.shape, 0)
    column = lax.broadcasted_iota(jnp.int32, known.shape, 1)
    missing = (jnp.where(first, row, column) < half) & (jnp.where(first, column, row) >= half)
    return jnp.where(missing, known.T, known)


def corner_part(corner_ref, scratch):
    corner = half_of(scratch, unpack_corner(corner_ref))
    rows, wide = corner.shape
    turned = jnp.concatenate([corner, jnp.zeros((wide - rows, wide), F32)], axis=0).T[:rows]
    part = rows // 3
    row = lax.broadcasted_iota(jnp.int32, corner.shape, 0)
    column = lax.broadcasted_iota(jnp.int32, corner.shape, 1)
    missing = (row < 2 * part) & (column >= jnp.where(row < part, part, 2 * part))
    return jnp.where(missing, turned, corner)


def place_rows(grad_ref, block, rows, value):
    grad_ref[pl.ds(pl.multiple_of(block * rows, 8), rows), :] = value


def polynomial(parts):
    gram = dot_parts(parts, parts, ((1,), (1,)))
    gram_parts = split(gram)
    return CUBIC_COEFF * gram + QUINTIC_COEFF * dot_parts(gram_parts, gram_parts)


def iterate(x, steps):
    for _ in range(steps):
        parts = split(x)
        x = LINEAR_COEFF * x + dot_parts(split(polynomial(parts)), parts)
    return x


def prepare_kernel(
    l_stat_ref,
    r_stat_ref,
    l_basis_ref,
    r_basis_ref,
    got_ref,
    basis_ref,
    known_ref,
    right_ref,
    turned_ref,
    other_ref,
    copy_ref,
    scratch,
):
    left, first = is_left(), is_first()
    own = pick(left, thirds(l_basis_ref), thirds(r_basis_ref))
    got = thirds(got_ref, 0, l_basis_ref.shape[0])
    basis_ref[...] = whole_of(scratch, pick(first, own, got), pick(first, got, own))
    known_ref[...] = 0.5 * known_part(first, pick(left, thirds(l_stat_ref), thirds(r_stat_ref)), scratch)
    right = half_of(scratch, thirds(r_basis_ref))
    right_ref[...] = right
    turned_ref[...] = right.T
    other_ref[...] = jnp.where(left, r_stat_ref[...], l_stat_ref[...])
    copy_ref[...] = l_basis_ref[...]


def products_kernel(hops, basis_ref, known_ref, turned_ref, got_ref, *refs):
    left = is_left()
    grad_ref, stat_ref, power_ref, inner_ref = refs[-4:]
    if hops:
        grads_ref, mine_refs, theirs_refs = refs[0], refs[1 : 1 + len(hops)], refs[1 + len(hops) : 1 + 2 * len(hops)]
        rows = grads_ref.shape[1]
        here = lax.axis_index("shard") // 2
        parity = lax.axis_index("shard") % 2
        blocks = grad_ref.shape[1] // LANES
        start = got_ref.shape[0] - blocks * rows
        received = [got_ref[pl.ds(start + k * rows, rows), :] for k in range(blocks)]
        place_rows(grad_ref, 2 * here + parity, rows, grads_ref[here])
        place_rows(grad_ref, 2 * here + 1 - parity, rows, jnp.concatenate(received, axis=1))
        for hop, mine, theirs in zip(hops, mine_refs, theirs_refs):
            place_rows(grad_ref, 2 * (here ^ hop) + parity, rows, mine[...])
            place_rows(grad_ref, 2 * (here ^ hop) + 1 - parity, rows, theirs[...])
    else:
        grad_ref[...] = refs[0][...]
    grad = grad_ref[...]
    parts = split(jnp.where(left, grad, grad.T))
    stat = known_ref[...] + 0.5 * symmetric_dot(parts, parts, ((1,), (1,)))
    stat_ref[...] = stat
    power_ref[...] = dot(stat, basis_ref[...])
    inner_ref[...] = dot(turned_ref[...], grad, ((1,), (1,)))


def begin_kernel(corner_ref, power_ref, basis_ref, x_ref, scratch):
    first = is_first()
    corner = corner_part(corner_ref, scratch)
    rows, wide = corner.shape
    basis = jnp.where(first, basis_ref[pl.ds(rows, rows), :], basis_ref[pl.ds(0, rows), :])
    basis = jnp.concatenate([basis, jnp.zeros((wide - rows, 2 * rows), F32)], axis=0)
    term = 0.5 * dot(corner, basis)
    power = power_ref[...] + jnp.concatenate([jnp.where(first, 0.0, term), jnp.where(first, term, 0.0)], axis=0)
    x_ref[...] = iterate(power * (1.0 / jnp.sqrt(jnp.sum(power * power) + NORM_EPS)), 1)


def rows_for(hops, outer_ref, right_parts, out_ref, offset):
    rows = out_ref.shape[1]
    here = lax.axis_index("shard") // 2
    starts = [pl.multiple_of((2 * (here ^ hop) + offset) * rows, 8) if hops else 0 for hop in (0, *hops)]
    outer = [outer_ref[pl.ds(start, rows), :] for start in starts]
    partial = dot_parts(split(jnp.concatenate(outer, axis=0)), right_parts, ((1,), (1,)))
    for k in range(len(starts)):
        out_ref[k] = partial[k * rows : (k + 1) * rows]


def update_kernel(
    hops,
    inner_ref,
    basis_ref,
    left_ref,
    right_ref,
    other_left_ref,
    one_ref,
    two_ref,
    start_ref,
    new_one_ref,
    new_two_ref,
    theirs_ref,
    outer_ref,
    x_ref,
    scratch,
):
    left, first = is_left(), is_first()
    x = start_ref[...]
    parts = split(x)
    gram = dot_parts(parts, parts, ((1,), (1,)))
    own, got = thirds(left_ref), thirds(other_left_ref)
    basis_left = jnp.where(left, basis_ref[...], whole_of(scratch, pick(first, own, got), pick(first, got, own)))
    left_parts = split(basis_left)
    rotated = dot_parts(split(inner_ref[...]), left_parts).T
    gram_parts = split(gram)
    square = dot_parts(gram_parts, gram_parts)
    rotated = flat_of(scratch, rotated)
    ones = thirds(one_ref)
    twos = thirds(two_ref)
    new_one = [BETA_ONE * m + (1.0 - BETA_ONE) * r for m, r in zip(ones, rotated)]
    new_two = [BETA_TWO * v + (1.0 - BETA_TWO) * r * r for v, r in zip(twos, rotated)]
    put_thirds(new_one_ref, new_one)
    put_thirds(new_two_ref, new_two)
    direction = [m / (jnp.sqrt(v) + ADAM_EPS) for m, v in zip(new_one, new_two)]
    outer_ref[...] = dot_parts(left_parts, split(half_of(scratch, direction)))
    poly_parts = split(CUBIC_COEFF * gram + QUINTIC_COEFF * square)
    moved = dot_parts(poly_parts, parts)
    rows_for(hops, outer_ref, split(right_ref[...]), theirs_ref, 1 - lax.axis_index("shard") % 2)
    x_ref[...] = LINEAR_COEFF * x + moved


def end_kernel(hops, steps, start_ref, outer_ref, right_ref, x_ref, poly_ref, send_ref, mine_ref, scratch):
    x = iterate(start_ref[...], steps - 1)
    x_ref[...] = x
    rows_for(hops, outer_ref, split(right_ref[...]), mine_ref, lax.axis_index("shard") % 2)
    poly = polynomial(split(x))
    poly_ref[...] = poly
    half = take_half(x, jnp.logical_not(is_first()))
    put_thirds(send_ref, flat_of(scratch, LINEAR_COEFF * half + dot(poly, half)))


def add_kernel(mine_ref, theirs_ref, *out_refs):
    for k, out_ref in enumerate(out_refs):
        out_ref[...] = mine_ref[k] + theirs_ref[k]


def bases_kernel(keep_ref, back_ref, new_left_ref, new_right_ref, sems):
    left = is_left()

    def copies(own_ref, other_ref):
        return [
            pltpu.make_async_copy(keep_ref, own_ref, sems.at[0]),
            pltpu.make_async_copy(back_ref, other_ref, sems.at[1]),
        ]

    @pl.when(left)
    def _():
        for copy in copies(new_left_ref, new_right_ref):
            copy.start()

    @pl.when(jnp.logical_not(left))
    def _():
        for copy in copies(new_right_ref, new_left_ref):
            copy.start()

    for copy in copies(new_left_ref, new_right_ref):
        copy.wait()


def rows_kernel(hops, *refs):
    rows_refs, (update_ref, sems) = refs[:-2], refs[-2:]
    here = lax.axis_index("shard") // 2
    copies = [
        pltpu.make_async_copy(rows_refs[k], update_ref.at[here ^ hop], sems.at[k]) for k, hop in enumerate((0, *hops))
    ]
    for copy in copies:
        copy.start()
    for copy in copies:
        copy.wait()


def rest_kernel(x_ref, poly_ref, grad_ref, new_stat_ref, other_ref, keep_ref, new_left_ref, new_right_ref, scratch):
    left = is_left()
    first = is_first()
    half = take_half(x_ref[...], first)
    put_thirds(keep_ref, flat_of(scratch, LINEAR_COEFF * half + dot(poly_ref[...], half)))
    grad = grad_ref[...]
    turned = grad.T
    a = jnp.where(left, grad, turned)
    b = jnp.where(left, turned, grad)
    new_own = flat_of(scratch, take_half(new_stat_ref[...], first))
    product = flat_of(scratch, dot(b, take_half(a, first)))
    new_other = [0.5 * u + 0.5 * v for u, v in zip(thirds(other_ref), product)]
    put_thirds(new_left_ref, pick(left, new_own, new_other))
    put_thirds(new_right_ref, pick(left, new_other, new_own))


def call(kernel, outs, scratch, products, full, name, copies=0, kind=jax.ShapeDtypeStruct, **specs):
    size = full * full
    scratch = [pltpu.VMEM(s, F32) for s in scratch]
    if copies:
        scratch.append(pltpu.SemaphoreType.DMA((copies,)))
    return pl.pallas_call(
        kernel,
        out_shape=[kind(s, F32) for s in outs],
        scratch_shapes=scratch,
        compiler_params=pltpu.CompilerParams(vmem_limit_bytes=40 * 1024 * 1024),
        cost_estimate=pl.CostEstimate(flops=int(products * 6 * full * size), bytes_accessed=16 * size, transcendentals=0),
        name=name,
        **specs,
    )


def anywhere(count):
    return [pl.BlockSpec(memory_space=pl.ANY)] * count


def after(x, *others):
    return lax.optimization_barrier((x, *others))[0]


def local(grads, moment_one, moment_two, left_stat, right_stat, left_basis, right_basis):
    tiles_here, rows_here, full = grads.shape
    size = lax.axis_size("shard")
    flat_rows = full * (full // 2) // LANES
    flat = (flat_rows, LANES)
    square = (full, full)
    block = (rows_here, full)
    parity = lax.axis_index("shard") % 2
    pairs = [(i, i ^ 1) for i in range(size)]
    sides = [list(range(k, size, 2)) for k in range(2)]
    near = size in (4, 8) and rows_here % 8 == 0
    hops = {4: (1,), 8: (2, 3, 1)}[size] if near else ()
    strips = (tiles_here, *block) if near else (1, full, full)

    def exchange(x):
        return lax.all_to_all(x, "shard", split_axis=0, concat_axis=0, axis_index_groups=sides, tiled=True)

    def hop_by(x, hop):
        return lax.ppermute(x, "shard", [(i, i ^ (2 * hop)) for i in range(size)])

    def partner(x):
        return lax.ppermute(x, "shard", pairs)

    one, two, l_stat, r_stat, l_basis, r_basis = (
        x.reshape(flat) for x in (moment_one, moment_two, left_stat, right_stat, left_basis, right_basis)
    )
    count = corner_rows(flat_rows)
    outgoing_rows = flat_rows + (rows_here * (full // LANES) if near else 0)
    outgoing, corner, *pieces = call(
        functools.partial(pack_kernel, hops),
        [(outgoing_rows, LANES), (count, LANES)] + [block] * len(hops),
        [(flat_rows // 2, LANES)],
        0.1,
        full,
        "pack",
        copies=2 + len(hops) + full // LANES,
        kind=pltpu.VMEM,
        in_specs=anywhere(5),
        out_specs=anywhere(1) + [pl.BlockSpec(memory_space=pltpu.VMEM)] + anywhere(len(hops)),
    )(*(pltpu.with_memory_space_constraint(x, pltpu.HBM) for x in (l_stat, r_stat, l_basis, r_basis, grads)))
    got = partner(outgoing)
    if near:
        mine = [hop_by(piece, hop) for hop, piece in zip(hops, pieces)]
        theirs = [partner(x) for x in mine]
        rows = (grads, *mine, *theirs)
    else:
        mine = exchange(grads)
        theirs = partner(mine)
        even, odd = jnp.where(parity == 0, mine, theirs), jnp.where(parity == 0, theirs, mine)
        rows = (jnp.stack([even, odd], axis=1).reshape(square),)
        mine = [mine]
    got_corner = partner(after(corner, theirs[0] if near else mine[0]))
    wide = (full, 2 * LANES)
    tall = (2 * LANES, full)
    basis, known, right, turned, other, left = call(
        prepare_kernel, [square, square, wide, tall, flat, flat], [(3, full, LANES)], 0.1, full, "prepare"
    )(l_stat, r_stat, l_basis, r_basis, got)
    grad, new_stat, power, inner = call(
        functools.partial(products_kernel, hops), [square, square, square, tall], [], 3, full, "products"
    )(basis, known, turned, got, *rows)
    tensors = lax.axis_size("tensor")
    place = lambda t, i: i * tensors + t
    cycle = []
    for t in range(0, tensors - tensors % 2, 2):
        for i in range(0, size, 2):
            cycle += [(place(t, i), place(t, i + 1)), (place(t, i + 1), place(t + 1, i + 1))]
            cycle += [(place(t + 1, i + 1), place(t + 1, i)), (place(t + 1, i), place(t, i))]
    cycle += [(place(t, i), place(t, i ^ 1)) for t in range(tensors - tensors % 2, tensors) for i in range(size)]
    other_left = lax.ppermute(after(l_basis, basis, *(theirs[:2] if near else mine)), ("shard", "tensor"), cycle)
    (x,) = call(begin_kernel, [square], [(2, full // 2, LANES)], 7, full, "begin")(got_corner, power, basis)
    new_one, new_two, other_rows, outer, x = call(
        functools.partial(update_kernel, hops), [flat, flat, strips, wide, square], [(3, full, LANES)], 5, full, "update"
    )(inner, basis, left, right, other_left, one, two, x)
    if not near:
        partial = other_rows.reshape(tiles_here, 2, rows_here, full)
        other_rows = lax.dynamic_index_in_dim(partial, 1 - parity, 1, keepdims=False)
    got_rows = partner(other_rows)
    x, poly, send, own_rows = call(
        functools.partial(end_kernel, hops, NS_ITERS - 2),
        [square, square, flat, strips],
        [(3, full, LANES)],
        9,
        full,
        "end",
    )(after(x, other_rows), outer, right)
    back = partner(send)
    keep, new_left, new_right = call(rest_kernel, [flat, flat, flat], [(3, full, LANES)], 1.5, full, "rest")(
        x, poly, grad, new_stat, other
    )
    if near:
        kept, *sums = call(add_kernel, [block] * (1 + len(hops)), [], 0.1, full, "add")(
            after(own_rows, send), after(got_rows, send)
        )
        returned = [hop_by(x, hop) for hop, x in zip(hops, sums)]
        update = call(
            functools.partial(rows_kernel, hops),
            [grads.shape],
            [],
            0.1,
            full,
            "rows",
            copies=1 + len(hops),
            in_specs=anywhere(1 + len(hops)),
            out_specs=anywhere(1),
        )(kept, *returned)[0]
    else:
        own_rows = lax.dynamic_index_in_dim(partial, parity, 1, keepdims=False)
        update = exchange(after(own_rows, send) + after(got_rows, send))
    new_l_basis, new_r_basis = call(
        bases_kernel, [flat, flat], [], 0.1, full, "bases", copies=2, in_specs=anywhere(2), out_specs=anywhere(2)
    )(keep, back)
    halves = (new_one, new_two, new_left, new_right, new_l_basis, new_r_basis)
    return (update, *(x.reshape(1, flat_rows * LANES) for x in halves))


def solution(mesh):
    halves = P(("tensor", "shard"), None)
    rows = P("tensor", "shard", None)
    return jax.shard_map(
        local, mesh=mesh, in_specs=(rows,) + (halves,) * 6, out_specs=(rows,) + (halves,) * 6, check_vma=False
    )
```

```python
import functools

import jax
import jax.numpy as jnp
from jax import lax
from jax.experimental import pallas as pl
from jax.experimental.pallas import tpu as pltpu
from jax.sharding import PartitionSpec as P

NS_ITERS = 5
BETA_ONE = 0.9
BETA_TWO = 0.95
ADAM_EPS = 1e-08
NORM_EPS = 1e-06
LINEAR_COEFF = 3.4445
CUBIC_COEFF = -4.775
QUINTIC_COEFF = 2.0315
LANES = 128
F32 = jnp.float32


def split(x):
    high = x.astype(jnp.bfloat16)
    return high, (x - high.astype(F32)).astype(jnp.bfloat16)


def dot(a, b, dims=((1,), (0,))):
    return dot_parts(split(a), split(b), dims)


def dot_parts(a, b, dims=((1,), (0,))):
    (ka,), (kb,) = dims
    left = jnp.concatenate([a[0], a[0], a[1]], axis=ka)
    right = jnp.concatenate([b[0], b[1], b[0]], axis=kb)
    return lax.dot_general(left, right, (dims, ((), ())), preferred_element_type=F32)


def symmetric_dot(a, b, dims=((1,), (0,))):
    (ka,), (kb,) = dims
    cut = a[0].shape[0] - LANES
    head = lambda x, axis: lax.slice_in_dim(x, 0, cut, axis=axis)
    tail = lambda x, axis: lax.slice_in_dim(x, cut, cut + LANES, axis=axis)
    left = dot_parts(a, [head(x, 1 - kb) for x in b], dims)
    corner = dot_parts([tail(x, 1 - ka) for x in a], [tail(x, 1 - kb) for x in b], dims)
    right = jnp.concatenate([left[cut:].T, corner], axis=0)
    return jnp.concatenate([left, right], axis=1)


def swap(x):
    return pltpu.roll(x, LANES // 2, 1)


def low_lanes(shape):
    return lax.broadcasted_iota(jnp.int32, shape, 1) < LANES // 2


def pick(flag, x, y):
    return [jnp.where(flag, u, v) for u, v in zip(x, y)]


def thirds(ref, start=0, rows=None):
    rows = ref.shape[0] if rows is None else rows
    return [ref[pl.ds(start + k, rows // 3, stride=3), :] for k in range(3)]


def put_thirds(ref, parts):
    for k in range(3):
        ref[pl.ds(k, parts[k].shape[0], stride=3), :] = parts[k]


def interleave(scratch, index, even, odd):
    scratch[index, pl.ds(0, even.shape[0], stride=2), :] = even
    scratch[index, pl.ds(1, odd.shape[0], stride=2), :] = odd


def whole_of(scratch, first, second):
    a, b, c = first
    d, e, f = second
    low = low_lanes(a.shape)
    sb, sc, sd, se = swap(b), swap(c), swap(d), swap(e)
    interleave(scratch, 0, a, jnp.where(low, sb, sc))
    interleave(scratch, 1, jnp.where(low, b, sd), jnp.where(low, sc, e))
    interleave(scratch, 2, jnp.where(low, sd, se), f)
    return jnp.concatenate([scratch[0], scratch[1], scratch[2]], axis=1)


def half_of(scratch, flat):
    a, b, c = flat
    low = low_lanes(a.shape)
    sb, sc = swap(b), swap(c)
    interleave(scratch, 0, a, jnp.where(low, sb, sc))
    interleave(scratch, 1, jnp.where(low, b, 0.0), jnp.where(low, sc, 0.0))
    return jnp.concatenate([scratch[0], scratch[1]], axis=1)


def flat_of(scratch, half):
    scratch[0] = half[:, :LANES]
    scratch[1] = half[:, LANES:]
    pairs = half.shape[0] // 2
    even0 = scratch[0, pl.ds(0, pairs, stride=2), :]
    odd0 = swap(scratch[0, pl.ds(1, pairs, stride=2), :])
    even1 = scratch[1, pl.ds(0, pairs, stride=2), :]
    odd1 = swap(scratch[1, pl.ds(1, pairs, stride=2), :])
    low = low_lanes(even0.shape)
    return [even0, jnp.where(low, even1, odd0), jnp.where(low, odd0, odd1)]


def take_half(whole, first):
    one, two, three = whole[:, :LANES], whole[:, LANES : 2 * LANES], whole[:, 2 * LANES :]
    low = low_lanes(one.shape)
    s2, s3 = swap(two), swap(three)
    head = jnp.where(first, one, jnp.where(low, s2, s3))
    tail = jnp.where(low, jnp.where(first, two, s3), 0.0)
    return jnp.concatenate([head, tail], axis=1)


def is_first():
    return lax.rem(lax.axis_index("shard"), 2) == 0


def is_left():
    return lax.rem(lax.axis_index("shard") + lax.axis_index("tensor"), 2) == 0


def pack_kernel(hops, l_stat_ref, r_stat_ref, l_basis_ref, r_basis_ref, grads_ref, *refs):
    out_ref, small_ref, *refs = refs
    piece_refs, (corner, sems) = refs[: len(hops)], refs[len(hops) :]
    left = is_left()
    flat_rows = l_basis_ref.shape[0]
    half_rows = flat_rows // 2
    rows = grads_ref.shape[1]
    here = lax.axis_index("shard") // 2

    start = pl.multiple_of(jnp.where(is_first(), 0, half_rows), 8)

    def copies(basis_ref, stat_ref):
        return [
            pltpu.make_async_copy(stat_ref.at[pl.ds(start, half_rows)], corner, sems.at[0]),
            pltpu.make_async_copy(basis_ref, out_ref.at[pl.ds(0, flat_rows)], sems.at[1]),
        ]

    @pl.when(left)
    def _():
        for copy in copies(r_basis_ref, r_stat_ref):
            copy.start()

    @pl.when(jnp.logical_not(left))
    def _():
        for copy in copies(l_basis_ref, l_stat_ref):
            copy.start()

    more = []
    for number, (hop, piece_ref) in enumerate(zip(hops, piece_refs)):
        more.append(pltpu.make_async_copy(grads_ref.at[here ^ hop], piece_ref, sems.at[2 + number]))
    if hops:
        for k in range(grads_ref.shape[2] // LANES):
            source = grads_ref.at[here, :, pl.ds(k * LANES, LANES)]
            target = out_ref.at[pl.ds(flat_rows + k * rows, rows)]
            more.append(pltpu.make_async_copy(source, target, sems.at[2 + len(hops) + k]))
    for copy in more:
        copy.start()
    first, second = copies(l_basis_ref, l_stat_ref)
    first.wait()
    third = half_rows // 9
    a, b, c = thirds(corner)
    low = low_lanes((third, LANES))
    middle = slice(third, 2 * third)
    small_ref[pl.ds(0, third)] = jnp.where(low, a[:third], b[:third])
    small_ref[pl.ds(third, third)] = a[middle]
    small_ref[pl.ds(2 * third, third)] = jnp.where(low, swap(b[middle]), swap(c[middle]))
    small_ref[pl.ds(3 * third, 3 * third)] = corner[pl.ds(6 * third, 3 * third)]
    for copy in [second, *more]:
        copy.wait()


def corner_rows(flat_rows):
    return flat_rows // 3


def unpack_corner(got_ref):
    third = got_ref.shape[0] // 6
    small = got_ref[pl.ds(0, third), :]
    even = got_ref[pl.ds(third, third), :]
    odd = swap(got_ref[pl.ds(2 * third, third), :])
    a, b, c = thirds(got_ref, 3 * third, 3 * third)
    low = low_lanes(small.shape)
    zero = jnp.zeros_like(small)
    return [
        jnp.concatenate([jnp.where(low, small, zero), even, a], axis=0),
        jnp.concatenate([jnp.where(low, zero, small), jnp.where(low, zero, odd), b], axis=0),
        jnp.concatenate([zero, jnp.where(low, odd, zero), c], axis=0),
    ]


def known_part(first, own, scratch):
    zeros = [jnp.zeros_like(x) for x in own]
    known = whole_of(scratch, pick(first, own, zeros), pick(first, zeros, own))
    half = known.shape[0] // 2
    row = lax.broadcasted_iota(jnp.int32, known.shape, 0)
    column = lax.broadcasted_iota(jnp.int32, known.shape, 1)
    missing = (jnp.where(first, row, column) < half) & (jnp.where(first, column, row) >= half)
    return jnp.where(missing, known.T, known)


def corner_part(corner_ref, scratch):
    corner = half_of(scratch, unpack_corner(corner_ref))
    rows, wide = corner.shape
    turned = jnp.concatenate([corner, jnp.zeros((wide - rows, wide), F32)], axis=0).T[:rows]
    part = rows // 3
    row = lax.broadcasted_iota(jnp.int32, corner.shape, 0)
    column = lax.broadcasted_iota(jnp.int32, corner.shape, 1)
    missing = (row < 2 * part) & (column >= jnp.where(row < part, part, 2 * part))
    return jnp.where(missing, turned, corner)


def place_rows(grad_ref, block, rows, value):
    grad_ref[pl.ds(pl.multiple_of(block * rows, 8), rows), :] = value


def polynomial(parts):
    gram = dot_parts(parts, parts, ((1,), (1,)))
    gram_parts = split(gram)
    return CUBIC_COEFF * gram + QUINTIC_COEFF * dot_parts(gram_parts, gram_parts)


def iterate(x, steps):
    for _ in range(steps):
        parts = split(x)
        x = LINEAR_COEFF * x + dot_parts(split(polynomial(parts)), parts)
    return x


def prepare_kernel(
    l_stat_ref,
    r_stat_ref,
    l_basis_ref,
    r_basis_ref,
    got_ref,
    basis_ref,
    known_ref,
    right_ref,
    turned_ref,
    other_ref,
    copy_ref,
    scratch,
):
    left, first = is_left(), is_first()
    own = pick(left, thirds(l_basis_ref), thirds(r_basis_ref))
    got = thirds(got_ref, 0, l_basis_ref.shape[0])
    basis_ref[...] = whole_of(scratch, pick(first, own, got), pick(first, got, own))
    known_ref[...] = 0.5 * known_part(first, pick(left, thirds(l_stat_ref), thirds(r_stat_ref)), scratch)
    right = half_of(scratch, thirds(r_basis_ref))
    right_ref[...] = right
    turned_ref[...] = right.T
    other_ref[...] = jnp.where(left, r_stat_ref[...], l_stat_ref[...])
    copy_ref[...] = l_basis_ref[...]


def products_kernel(hops, basis_ref, known_ref, turned_ref, got_ref, *refs):
    left = is_left()
    grad_ref, stat_ref, power_ref, inner_ref = refs[-4:]
    if hops:
        grads_ref, mine_refs, theirs_refs = refs[0], refs[1 : 1 + len(hops)], refs[1 + len(hops) : 1 + 2 * len(hops)]
        rows = grads_ref.shape[1]
        here = lax.axis_index("shard") // 2
        parity = lax.axis_index("shard") % 2
        blocks = grad_ref.shape[1] // LANES
        start = got_ref.shape[0] - blocks * rows
        received = [got_ref[pl.ds(start + k * rows, rows), :] for k in range(blocks)]
        place_rows(grad_ref, 2 * here + parity, rows, grads_ref[here])
        place_rows(grad_ref, 2 * here + 1 - parity, rows, jnp.concatenate(received, axis=1))
        for hop, mine, theirs in zip(hops, mine_refs, theirs_refs):
            place_rows(grad_ref, 2 * (here ^ hop) + parity, rows, mine[...])
            place_rows(grad_ref, 2 * (here ^ hop) + 1 - parity, rows, theirs[...])
    else:
        grad_ref[...] = refs[0][...]
    grad = grad_ref[...]
    parts = split(jnp.where(left, grad, grad.T))
    stat = known_ref[...] + 0.5 * symmetric_dot(parts, parts, ((1,), (1,)))
    stat_ref[...] = stat
    power_ref[...] = dot(stat, basis_ref[...])
    inner_ref[...] = dot(turned_ref[...], grad, ((1,), (1,)))


def begin_kernel(corner_ref, power_ref, basis_ref, x_ref, scratch):
    first = is_first()
    corner = corner_part(corner_ref, scratch)
    rows, wide = corner.shape
    basis = jnp.where(first, basis_ref[pl.ds(rows, rows), :], basis_ref[pl.ds(0, rows), :])
    basis = jnp.concatenate([basis, jnp.zeros((wide - rows, 2 * rows), F32)], axis=0)
    term = 0.5 * dot(corner, basis)
    power = power_ref[...] + jnp.concatenate([jnp.where(first, 0.0, term), jnp.where(first, term, 0.0)], axis=0)
    x_ref[...] = iterate(power * (1.0 / jnp.sqrt(jnp.sum(power * power) + NORM_EPS)), 1)


def rows_for(hops, outer_ref, right_parts, out_ref, offset):
    rows = out_ref.shape[1]
    here = lax.axis_index("shard") // 2
    starts = [pl.multiple_of((2 * (here ^ hop) + offset) * rows, 8) if hops else 0 for hop in (0, *hops)]
    outer = [outer_ref[pl.ds(start, rows), :] for start in starts]
    partial = dot_parts(split(jnp.concatenate(outer, axis=0)), right_parts, ((1,), (1,)))
    for k in range(len(starts)):
        out_ref[k] = partial[k * rows : (k + 1) * rows]


def update_kernel(
    hops,
    inner_ref,
    basis_ref,
    left_ref,
    right_ref,
    other_left_ref,
    one_ref,
    two_ref,
    start_ref,
    new_one_ref,
    new_two_ref,
    theirs_ref,
    outer_ref,
    x_ref,
    scratch,
):
    left, first = is_left(), is_first()
    x = start_ref[...]
    parts = split(x)
    gram = dot_parts(parts, parts, ((1,), (1,)))
    own, got = thirds(left_ref), thirds(other_left_ref)
    basis_left = jnp.where(left, basis_ref[...], whole_of(scratch, pick(first, own, got), pick(first, got, own)))
    left_parts = split(basis_left)
    rotated = dot_parts(split(inner_ref[...]), left_parts).T
    gram_parts = split(gram)
    square = dot_parts(gram_parts, gram_parts)
    rotated = flat_of(scratch, rotated)
    ones = thirds(one_ref)
    twos = thirds(two_ref)
    new_one = [BETA_ONE * m + (1.0 - BETA_ONE) * r for m, r in zip(ones, rotated)]
    new_two = [BETA_TWO * v + (1.0 - BETA_TWO) * r * r for v, r in zip(twos, rotated)]
    put_thirds(new_one_ref, new_one)
    put_thirds(new_two_ref, new_two)
    direction = [m / (jnp.sqrt(v) + ADAM_EPS) for m, v in zip(new_one, new_two)]
    outer_ref[...] = dot_parts(left_parts, split(half_of(scratch, direction)))
    poly_parts = split(CUBIC_COEFF * gram + QUINTIC_COEFF * square)
    moved = dot_parts(poly_parts, parts)
    rows_for(hops, outer_ref, split(right_ref[...]), theirs_ref, 1 - lax.axis_index("shard") % 2)
    x_ref[...] = LINEAR_COEFF * x + moved


def end_kernel(hops, steps, start_ref, outer_ref, right_ref, x_ref, poly_ref, send_ref, mine_ref, scratch):
    x = iterate(start_ref[...], steps - 1)
    x_ref[...] = x
    rows_for(hops, outer_ref, split(right_ref[...]), mine_ref, lax.axis_index("shard") % 2)
    poly = polynomial(split(x))
    poly_ref[...] = poly
    half = take_half(x, jnp.logical_not(is_first()))
    put_thirds(send_ref, flat_of(scratch, LINEAR_COEFF * half + dot(poly, half)))


def add_kernel(mine_ref, theirs_ref, *out_refs):
    for k, out_ref in enumerate(out_refs):
        out_ref[...] = mine_ref[k] + theirs_ref[k]


def bases_kernel(keep_ref, back_ref, new_left_ref, new_right_ref, sems):
    left = is_left()

    def copies(own_ref, other_ref):
        return [
            pltpu.make_async_copy(keep_ref, own_ref, sems.at[0]),
            pltpu.make_async_copy(back_ref, other_ref, sems.at[1]),
        ]

    @pl.when(left)
    def _():
        for copy in copies(new_left_ref, new_right_ref):
            copy.start()

    @pl.when(jnp.logical_not(left))
    def _():
        for copy in copies(new_right_ref, new_left_ref):
            copy.start()

    for copy in copies(new_left_ref, new_right_ref):
        copy.wait()


def rows_kernel(hops, *refs):
    rows_refs, (update_ref, sems) = refs[:-2], refs[-2:]
    here = lax.axis_index("shard") // 2
    copies = [
        pltpu.make_async_copy(rows_refs[k], update_ref.at[here ^ hop], sems.at[k]) for k, hop in enumerate((0, *hops))
    ]
    for copy in copies:
        copy.start()
    for copy in copies:
        copy.wait()


def rest_kernel(x_ref, poly_ref, grad_ref, new_stat_ref, other_ref, keep_ref, new_left_ref, new_right_ref, scratch):
    left = is_left()
    first = is_first()
    half = take_half(x_ref[...], first)
    put_thirds(keep_ref, flat_of(scratch, LINEAR_COEFF * half + dot(poly_ref[...], half)))
    grad = grad_ref[...]
    turned = grad.T
    a = jnp.where(left, grad, turned)
    b = jnp.where(left, turned, grad)
    new_own = flat_of(scratch, take_half(new_stat_ref[...], first))
    product = flat_of(scratch, dot(b, take_half(a, first)))
    new_other = [0.5 * u + 0.5 * v for u, v in zip(thirds(other_ref), product)]
    put_thirds(new_left_ref, pick(left, new_own, new_other))
    put_thirds(new_right_ref, pick(left, new_other, new_own))


def call(kernel, outs, scratch, products, full, name, copies=0, kind=jax.ShapeDtypeStruct, **specs):
    size = full * full
    scratch = [pltpu.VMEM(s, F32) for s in scratch]
    if copies:
        scratch.append(pltpu.SemaphoreType.DMA((copies,)))
    return pl.pallas_call(
        kernel,
        out_shape=[kind(s, F32) for s in outs],
        scratch_shapes=scratch,
        compiler_params=pltpu.CompilerParams(vmem_limit_bytes=40 * 1024 * 1024),
        cost_estimate=pl.CostEstimate(flops=int(products * 6 * full * size), bytes_accessed=16 * size, transcendentals=0),
        name=name,
        **specs,
    )


def anywhere(count):
    return [pl.BlockSpec(memory_space=pl.ANY)] * count


def after(x, *others):
    return lax.optimization_barrier((x, *others))[0]


def local(grads, moment_one, moment_two, left_stat, right_stat, left_basis, right_basis):
    tiles_here, rows_here, full = grads.shape
    size = lax.axis_size("shard")
    flat_rows = full * (full // 2) // LANES
    flat = (flat_rows, LANES)
    square = (full, full)
    block = (rows_here, full)
    parity = lax.axis_index("shard") % 2
    pairs = [(i, i ^ 1) for i in range(size)]
    sides = [list(range(k, size, 2)) for k in range(2)]
    near = size in (4, 8) and rows_here % 8 == 0
    hops = {4: (1,), 8: (2, 3, 1)}[size] if near else ()
    strips = (tiles_here, *block) if near else (1, full, full)

    def exchange(x):
        return lax.all_to_all(x, "shard", split_axis=0, concat_axis=0, axis_index_groups=sides, tiled=True)

    def hop_by(x, hop):
        return lax.ppermute(x, "shard", [(i, i ^ (2 * hop)) for i in range(size)])

    def partner(x):
        return lax.ppermute(x, "shard", pairs)

    one, two, l_stat, r_stat, l_basis, r_basis = (
        x.reshape(flat) for x in (moment_one, moment_two, left_stat, right_stat, left_basis, right_basis)
    )
    count = corner_rows(flat_rows)
    outgoing_rows = flat_rows + (rows_here * (full // LANES) if near else 0)
    outgoing, corner, *pieces = call(
        functools.partial(pack_kernel, hops),
        [(outgoing_rows, LANES), (count, LANES)] + [block] * len(hops),
        [(flat_rows // 2, LANES)],
        0.1,
        full,
        "pack",
        copies=2 + len(hops) + full // LANES,
        kind=pltpu.VMEM,
        in_specs=anywhere(5),
        out_specs=anywhere(1) + [pl.BlockSpec(memory_space=pltpu.VMEM)] + anywhere(len(hops)),
    )(*(pltpu.with_memory_space_constraint(x, pltpu.HBM) for x in (l_stat, r_stat, l_basis, r_basis, grads)))
    got = partner(outgoing)
    if near:
        mine = [hop_by(piece, hop) for hop, piece in zip(hops, pieces)]
        theirs = [partner(x) for x in mine]
        rows = (grads, *mine, *theirs)
    else:
        mine = exchange(grads)
        theirs = partner(mine)
        even, odd = jnp.where(parity == 0, mine, theirs), jnp.where(parity == 0, theirs, mine)
        rows = (jnp.stack([even, odd], axis=1).reshape(square),)
        mine = [mine]
    got_corner = partner(after(corner, theirs[0] if near else mine[0]))
    wide = (full, 2 * LANES)
    tall = (2 * LANES, full)
    basis, known, right, turned, other, left = call(
        prepare_kernel, [square, square, wide, tall, flat, flat], [(3, full, LANES)], 0.1, full, "prepare"
    )(l_stat, r_stat, l_basis, r_basis, got)
    grad, new_stat, power, inner = call(
        functools.partial(products_kernel, hops), [square, square, square, tall], [], 3, full, "products"
    )(basis, known, turned, got, *rows)
    tensors = lax.axis_size("tensor")
    place = lambda t, i: i * tensors + t
    cycle = []
    for t in range(0, tensors - tensors % 2, 2):
        for i in range(0, size, 2):
            cycle += [(place(t, i), place(t, i + 1)), (place(t, i + 1), place(t + 1, i + 1))]
            cycle += [(place(t + 1, i + 1), place(t + 1, i)), (place(t + 1, i), place(t, i))]
    cycle += [(place(t, i), place(t, i ^ 1)) for t in range(tensors - tensors % 2, tensors) for i in range(size)]
    other_left = lax.ppermute(after(l_basis, *(theirs[:2] if near else mine)), ("shard", "tensor"), cycle)
    (x,) = call(begin_kernel, [square], [(2, full // 2, LANES)], 7, full, "begin")(got_corner, power, basis)
    new_one, new_two, other_rows, outer, x = call(
        functools.partial(update_kernel, hops), [flat, flat, strips, wide, square], [(3, full, LANES)], 5, full, "update"
    )(inner, basis, left, right, other_left, one, two, x)
    if not near:
        partial = other_rows.reshape(tiles_here, 2, rows_here, full)
        other_rows = lax.dynamic_index_in_dim(partial, 1 - parity, 1, keepdims=False)
    got_rows = partner(other_rows)
    x, poly, send, own_rows = call(
        functools.partial(end_kernel, hops, NS_ITERS - 2),
        [square, square, flat, strips],
        [(3, full, LANES)],
        9,
        full,
        "end",
    )(after(x, other_rows), outer, right)
    back = partner(send)
    keep, new_left, new_right = call(rest_kernel, [flat, flat, flat], [(3, full, LANES)], 1.5, full, "rest")(
        x, poly, grad, new_stat, other
    )
    if near:
        kept, *sums = call(add_kernel, [block] * (1 + len(hops)), [], 0.1, full, "add")(
            after(own_rows, send), after(got_rows, send)
        )
        returned = [hop_by(x, hop) for hop, x in zip(hops, sums)]
        update = call(
            functools.partial(rows_kernel, hops),
            [grads.shape],
            [],
            0.1,
            full,
            "rows",
            copies=1 + len(hops),
            in_specs=anywhere(1 + len(hops)),
            out_specs=anywhere(1),
        )(kept, *returned)[0]
    else:
        own_rows = lax.dynamic_index_in_dim(partial, parity, 1, keepdims=False)
        update = exchange(after(own_rows, send) + after(got_rows, send))
    new_l_basis, new_r_basis = call(
        bases_kernel, [flat, flat], [], 0.1, full, "bases", copies=2, in_specs=anywhere(2), out_specs=anywhere(2)
    )(keep, back)
    halves = (new_one, new_two, new_left, new_right, new_l_basis, new_r_basis)
    return (update, *(x.reshape(1, flat_rows * LANES) for x in halves))


def solution(mesh):
    halves = P(("tensor", "shard"), None)
    rows = P("tensor", "shard", None)
    return jax.shard_map(
        local, mesh=mesh, in_specs=(rows,) + (halves,) * 6, out_specs=(rows,) + (halves,) * 6, check_vma=False
    )
```

```python
import functools

import jax
import jax.numpy as jnp
from jax import lax
from jax.experimental import pallas as pl
from jax.experimental.pallas import tpu as pltpu
from jax.sharding import PartitionSpec as P

NS_ITERS = 5
BETA_ONE = 0.9
BETA_TWO = 0.95
ADAM_EPS = 1e-08
NORM_EPS = 1e-06
LINEAR_COEFF = 3.4445
CUBIC_COEFF = -4.775
QUINTIC_COEFF = 2.0315
LANES = 128
F32 = jnp.float32


def split(x):
    high = x.astype(jnp.bfloat16)
    return high, (x - high.astype(F32)).astype(jnp.bfloat16)


def dot(a, b, dims=((1,), (0,))):
    return dot_parts(split(a), split(b), dims)


def dot_parts(a, b, dims=((1,), (0,))):
    (ka,), (kb,) = dims
    left = jnp.concatenate([a[0], a[0], a[1]], axis=ka)
    right = jnp.concatenate([b[0], b[1], b[0]], axis=kb)
    return lax.dot_general(left, right, (dims, ((), ())), preferred_element_type=F32)


def symmetric_dot(a, b, dims=((1,), (0,))):
    (ka,), (kb,) = dims
    cut = a[0].shape[0] - LANES
    head = lambda x, axis: lax.slice_in_dim(x, 0, cut, axis=axis)
    tail = lambda x, axis: lax.slice_in_dim(x, cut, cut + LANES, axis=axis)
    left = dot_parts(a, [head(x, 1 - kb) for x in b], dims)
    corner = dot_parts([tail(x, 1 - ka) for x in a], [tail(x, 1 - kb) for x in b], dims)
    right = jnp.concatenate([left[cut:].T, corner], axis=0)
    return jnp.concatenate([left, right], axis=1)


def swap(x):
    return pltpu.roll(x, LANES // 2, 1)


def low_lanes(shape):
    return lax.broadcasted_iota(jnp.int32, shape, 1) < LANES // 2


def pick(flag, x, y):
    return [jnp.where(flag, u, v) for u, v in zip(x, y)]


def thirds(ref, start=0, rows=None):
    rows = ref.shape[0] if rows is None else rows
    return [ref[pl.ds(start + k, rows // 3, stride=3), :] for k in range(3)]


def put_thirds(ref, parts):
    for k in range(3):
        ref[pl.ds(k, parts[k].shape[0], stride=3), :] = parts[k]


def interleave(scratch, index, even, odd):
    scratch[index, pl.ds(0, even.shape[0], stride=2), :] = even
    scratch[index, pl.ds(1, odd.shape[0], stride=2), :] = odd


def whole_of(scratch, first, second):
    a, b, c = first
    d, e, f = second
    low = low_lanes(a.shape)
    sb, sc, sd, se = swap(b), swap(c), swap(d), swap(e)
    interleave(scratch, 0, a, jnp.where(low, sb, sc))
    interleave(scratch, 1, jnp.where(low, b, sd), jnp.where(low, sc, e))
    interleave(scratch, 2, jnp.where(low, sd, se), f)
    return jnp.concatenate([scratch[0], scratch[1], scratch[2]], axis=1)


def half_of(scratch, flat):
    a, b, c = flat
    low = low_lanes(a.shape)
    sb, sc = swap(b), swap(c)
    interleave(scratch, 0, a, jnp.where(low, sb, sc))
    interleave(scratch, 1, jnp.where(low, b, 0.0), jnp.where(low, sc, 0.0))
    return jnp.concatenate([scratch[0], scratch[1]], axis=1)


def flat_of(scratch, half):
    scratch[0] = half[:, :LANES]
    scratch[1] = half[:, LANES:]
    pairs = half.shape[0] // 2
    even0 = scratch[0, pl.ds(0, pairs, stride=2), :]
    odd0 = swap(scratch[0, pl.ds(1, pairs, stride=2), :])
    even1 = scratch[1, pl.ds(0, pairs, stride=2), :]
    odd1 = swap(scratch[1, pl.ds(1, pairs, stride=2), :])
    low = low_lanes(even0.shape)
    return [even0, jnp.where(low, even1, odd0), jnp.where(low, odd0, odd1)]


def take_half(whole, first):
    one, two, three = whole[:, :LANES], whole[:, LANES : 2 * LANES], whole[:, 2 * LANES :]
    low = low_lanes(one.shape)
    s2, s3 = swap(two), swap(three)
    head = jnp.where(first, one, jnp.where(low, s2, s3))
    tail = jnp.where(low, jnp.where(first, two, s3), 0.0)
    return jnp.concatenate([head, tail], axis=1)


def is_first():
    return lax.rem(lax.axis_index("shard"), 2) == 0


def is_left():
    return lax.rem(lax.axis_index("shard") + lax.axis_index("tensor"), 2) == 0


def pack_kernel(hops, l_stat_ref, r_stat_ref, l_basis_ref, r_basis_ref, grads_ref, *refs):
    out_ref, small_ref, *refs = refs
    piece_refs, (corner, sems) = refs[: len(hops)], refs[len(hops) :]
    left = is_left()
    flat_rows = l_basis_ref.shape[0]
    half_rows = flat_rows // 2
    rows = grads_ref.shape[1]
    here = lax.axis_index("shard") // 2

    start = pl.multiple_of(jnp.where(is_first(), 0, half_rows), 8)

    def copies(basis_ref, stat_ref):
        return [
            pltpu.make_async_copy(stat_ref.at[pl.ds(start, half_rows)], corner, sems.at[0]),
            pltpu.make_async_copy(basis_ref, out_ref.at[pl.ds(0, flat_rows)], sems.at[1]),
        ]

    @pl.when(left)
    def _():
        for copy in copies(r_basis_ref, r_stat_ref):
            copy.start()

    @pl.when(jnp.logical_not(left))
    def _():
        for copy in copies(l_basis_ref, l_stat_ref):
            copy.start()

    more = []
    for number, (hop, piece_ref) in enumerate(zip(hops, piece_refs)):
        more.append(pltpu.make_async_copy(grads_ref.at[here ^ hop], piece_ref, sems.at[2 + number]))
    if hops:
        for k in range(grads_ref.shape[2] // LANES):
            source = grads_ref.at[here, :, pl.ds(k * LANES, LANES)]
            target = out_ref.at[pl.ds(flat_rows + k * rows, rows)]
            more.append(pltpu.make_async_copy(source, target, sems.at[2 + len(hops) + k]))
    for copy in more:
        copy.start()
    first, second = copies(l_basis_ref, l_stat_ref)
    first.wait()
    third = half_rows // 9
    a, b, c = thirds(corner)
    low = low_lanes((third, LANES))
    middle = slice(third, 2 * third)
    small_ref[pl.ds(0, third)] = jnp.where(low, a[:third], b[:third])
    small_ref[pl.ds(third, third)] = a[middle]
    small_ref[pl.ds(2 * third, third)] = jnp.where(low, swap(b[middle]), swap(c[middle]))
    small_ref[pl.ds(3 * third, 3 * third)] = corner[pl.ds(6 * third, 3 * third)]
    for copy in [second, *more]:
        copy.wait()


def corner_rows(flat_rows):
    return flat_rows // 3


def unpack_corner(got_ref):
    third = got_ref.shape[0] // 6
    small = got_ref[pl.ds(0, third), :]
    even = got_ref[pl.ds(third, third), :]
    odd = swap(got_ref[pl.ds(2 * third, third), :])
    a, b, c = thirds(got_ref, 3 * third, 3 * third)
    low = low_lanes(small.shape)
    zero = jnp.zeros_like(small)
    return [
        jnp.concatenate([jnp.where(low, small, zero), even, a], axis=0),
        jnp.concatenate([jnp.where(low, zero, small), jnp.where(low, zero, odd), b], axis=0),
        jnp.concatenate([zero, jnp.where(low, odd, zero), c], axis=0),
    ]


def known_part(first, own, scratch):
    zeros = [jnp.zeros_like(x) for x in own]
    known = whole_of(scratch, pick(first, own, zeros), pick(first, zeros, own))
    half = known.shape[0] // 2
    row = lax.broadcasted_iota(jnp.int32, known.shape, 0)
    column = lax.broadcasted_iota(jnp.int32, known.shape, 1)
    missing = (jnp.where(first, row, column) < half) & (jnp.where(first, column, row) >= half)
    return jnp.where(missing, known.T, known)


def corner_part(corner_ref, scratch):
    corner = half_of(scratch, unpack_corner(corner_ref))
    rows, wide = corner.shape
    turned = jnp.concatenate([corner, jnp.zeros((wide - rows, wide), F32)], axis=0).T[:rows]
    part = rows // 3
    row = lax.broadcasted_iota(jnp.int32, corner.shape, 0)
    column = lax.broadcasted_iota(jnp.int32, corner.shape, 1)
    missing = (row < 2 * part) & (column >= jnp.where(row < part, part, 2 * part))
    return jnp.where(missing, turned, corner)


def place_rows(grad_ref, block, rows, value):
    grad_ref[pl.ds(pl.multiple_of(block * rows, 8), rows), :] = value


def polynomial(parts):
    gram = dot_parts(parts, parts, ((1,), (1,)))
    gram_parts = split(gram)
    return CUBIC_COEFF * gram + QUINTIC_COEFF * dot_parts(gram_parts, gram_parts)


def iterate(x, steps):
    for _ in range(steps):
        parts = split(x)
        x = LINEAR_COEFF * x + dot_parts(split(polynomial(parts)), parts)
    return x


def prepare_kernel(
    l_stat_ref,
    r_stat_ref,
    l_basis_ref,
    r_basis_ref,
    got_ref,
    basis_ref,
    known_ref,
    right_ref,
    turned_ref,
    other_ref,
    copy_ref,
    scratch,
):
    left, first = is_left(), is_first()
    own = pick(left, thirds(l_basis_ref), thirds(r_basis_ref))
    got = thirds(got_ref, 0, l_basis_ref.shape[0])
    basis_ref[...] = whole_of(scratch, pick(first, own, got), pick(first, got, own))
    known_ref[...] = 0.5 * known_part(first, pick(left, thirds(l_stat_ref), thirds(r_stat_ref)), scratch)
    right = half_of(scratch, thirds(r_basis_ref))
    right_ref[...] = right
    turned_ref[...] = right.T
    other_ref[...] = jnp.where(left, r_stat_ref[...], l_stat_ref[...])
    copy_ref[...] = l_basis_ref[...]


def products_kernel(hops, basis_ref, known_ref, turned_ref, got_ref, *refs):
    left = is_left()
    grad_ref, stat_ref, power_ref, inner_ref = refs[-4:]
    if hops:
        grads_ref, mine_refs, theirs_refs = refs[0], refs[1 : 1 + len(hops)], refs[1 + len(hops) : 1 + 2 * len(hops)]
        rows = grads_ref.shape[1]
        here = lax.axis_index("shard") // 2
        parity = lax.axis_index("shard") % 2
        blocks = grad_ref.shape[1] // LANES
        start = got_ref.shape[0] - blocks * rows
        received = [got_ref[pl.ds(start + k * rows, rows), :] for k in range(blocks)]
        place_rows(grad_ref, 2 * here + parity, rows, grads_ref[here])
        place_rows(grad_ref, 2 * here + 1 - parity, rows, jnp.concatenate(received, axis=1))
        for hop, mine, theirs in zip(hops, mine_refs, theirs_refs):
            place_rows(grad_ref, 2 * (here ^ hop) + parity, rows, mine[...])
            place_rows(grad_ref, 2 * (here ^ hop) + 1 - parity, rows, theirs[...])
    else:
        grad_ref[...] = refs[0][...]
    grad = grad_ref[...]
    parts = split(jnp.where(left, grad, grad.T))
    stat = known_ref[...] + 0.5 * symmetric_dot(parts, parts, ((1,), (1,)))
    stat_ref[...] = stat
    power_ref[...] = dot(stat, basis_ref[...])
    inner_ref[...] = dot(turned_ref[...], grad, ((1,), (1,)))


def begin_kernel(corner_ref, power_ref, basis_ref, x_ref, scratch):
    first = is_first()
    corner = corner_part(corner_ref, scratch)
    rows, wide = corner.shape
    basis = jnp.where(first, basis_ref[pl.ds(rows, rows), :], basis_ref[pl.ds(0, rows), :])
    basis = jnp.concatenate([basis, jnp.zeros((wide - rows, 2 * rows), F32)], axis=0)
    term = 0.5 * dot(corner, basis)
    power = power_ref[...] + jnp.concatenate([jnp.where(first, 0.0, term), jnp.where(first, term, 0.0)], axis=0)
    x_ref[...] = iterate(power * (1.0 / jnp.sqrt(jnp.sum(power * power) + NORM_EPS)), 1)


def rows_for(hops, outer_ref, right_parts, out_ref, offset):
    rows = out_ref.shape[1]
    here = lax.axis_index("shard") // 2
    starts = [pl.multiple_of((2 * (here ^ hop) + offset) * rows, 8) if hops else 0 for hop in (0, *hops)]
    outer = [outer_ref[pl.ds(start, rows), :] for start in starts]
    partial = dot_parts(split(jnp.concatenate(outer, axis=0)), right_parts, ((1,), (1,)))
    for k in range(len(starts)):
        out_ref[k] = partial[k * rows : (k + 1) * rows]


def update_kernel(
    hops,
    inner_ref,
    basis_ref,
    left_ref,
    right_ref,
    other_left_ref,
    one_ref,
    two_ref,
    start_ref,
    new_one_ref,
    new_two_ref,
    theirs_ref,
    outer_ref,
    x_ref,
    scratch,
):
    left, first = is_left(), is_first()
    x = start_ref[...]
    parts = split(x)
    gram = dot_parts(parts, parts, ((1,), (1,)))
    own, got = thirds(left_ref), thirds(other_left_ref)
    basis_left = jnp.where(left, basis_ref[...], whole_of(scratch, pick(first, own, got), pick(first, got, own)))
    left_parts = split(basis_left)
    rotated = dot_parts(split(inner_ref[...]), left_parts).T
    gram_parts = split(gram)
    square = dot_parts(gram_parts, gram_parts)
    rotated = flat_of(scratch, rotated)
    ones = thirds(one_ref)
    twos = thirds(two_ref)
    new_one = [BETA_ONE * m + (1.0 - BETA_ONE) * r for m, r in zip(ones, rotated)]
    new_two = [BETA_TWO * v + (1.0 - BETA_TWO) * r * r for v, r in zip(twos, rotated)]
    put_thirds(new_one_ref, new_one)
    put_thirds(new_two_ref, new_two)
    direction = [m / (jnp.sqrt(v) + ADAM_EPS) for m, v in zip(new_one, new_two)]
    outer_ref[...] = dot_parts(left_parts, split(half_of(scratch, direction)))
    poly_parts = split(CUBIC_COEFF * gram + QUINTIC_COEFF * square)
    moved = dot_parts(poly_parts, parts)
    rows_for(hops, outer_ref, split(right_ref[...]), theirs_ref, 1 - lax.axis_index("shard") % 2)
    x_ref[...] = LINEAR_COEFF * x + moved


def end_kernel(hops, steps, start_ref, outer_ref, right_ref, x_ref, poly_ref, send_ref, mine_ref, scratch):
    x = iterate(start_ref[...], steps - 1)
    x_ref[...] = x
    rows_for(hops, outer_ref, split(right_ref[...]), mine_ref, lax.axis_index("shard") % 2)
    poly = polynomial(split(x))
    poly_ref[...] = poly
    half = take_half(x, jnp.logical_not(is_first()))
    put_thirds(send_ref, flat_of(scratch, LINEAR_COEFF * half + dot(poly, half)))


def add_kernel(mine_ref, theirs_ref, *out_refs):
    for k, out_ref in enumerate(out_refs):
        out_ref[...] = mine_ref[k] + theirs_ref[k]


def bases_kernel(keep_ref, back_ref, new_left_ref, new_right_ref, sems):
    left = is_left()

    def copies(own_ref, other_ref):
        return [
            pltpu.make_async_copy(keep_ref, own_ref, sems.at[0]),
            pltpu.make_async_copy(back_ref, other_ref, sems.at[1]),
        ]

    @pl.when(left)
    def _():
        for copy in copies(new_left_ref, new_right_ref):
            copy.start()

    @pl.when(jnp.logical_not(left))
    def _():
        for copy in copies(new_right_ref, new_left_ref):
            copy.start()

    for copy in copies(new_left_ref, new_right_ref):
        copy.wait()


def rows_kernel(hops, *refs):
    rows_refs, (update_ref, sems) = refs[:-2], refs[-2:]
    here = lax.axis_index("shard") // 2
    copies = [
        pltpu.make_async_copy(rows_refs[k], update_ref.at[here ^ hop], sems.at[k]) for k, hop in enumerate((0, *hops))
    ]
    for copy in copies:
        copy.start()
    for copy in copies:
        copy.wait()


def rest_kernel(x_ref, poly_ref, grad_ref, new_stat_ref, other_ref, keep_ref, new_left_ref, new_right_ref, scratch):
    left = is_left()
    first = is_first()
    half = take_half(x_ref[...], first)
    put_thirds(keep_ref, flat_of(scratch, LINEAR_COEFF * half + dot(poly_ref[...], half)))
    grad = grad_ref[...]
    turned = grad.T
    a = jnp.where(left, grad, turned)
    b = jnp.where(left, turned, grad)
    new_own = flat_of(scratch, take_half(new_stat_ref[...], first))
    product = flat_of(scratch, dot(b, take_half(a, first)))
    new_other = [0.5 * u + 0.5 * v for u, v in zip(thirds(other_ref), product)]
    put_thirds(new_left_ref, pick(left, new_own, new_other))
    put_thirds(new_right_ref, pick(left, new_other, new_own))


def call(kernel, outs, scratch, products, full, name, copies=0, kind=jax.ShapeDtypeStruct, **specs):
    size = full * full
    scratch = [pltpu.VMEM(s, F32) for s in scratch]
    if copies:
        scratch.append(pltpu.SemaphoreType.DMA((copies,)))
    return pl.pallas_call(
        kernel,
        out_shape=[kind(s, F32) for s in outs],
        scratch_shapes=scratch,
        compiler_params=pltpu.CompilerParams(vmem_limit_bytes=40 * 1024 * 1024),
        cost_estimate=pl.CostEstimate(flops=int(products * 6 * full * size), bytes_accessed=16 * size, transcendentals=0),
        name=name,
        **specs,
    )


def anywhere(count):
    return [pl.BlockSpec(memory_space=pl.ANY)] * count


def after(x, *others):
    return lax.optimization_barrier((x, *others))[0]


def local(grads, moment_one, moment_two, left_stat, right_stat, left_basis, right_basis):
    tiles_here, rows_here, full = grads.shape
    size = lax.axis_size("shard")
    flat_rows = full * (full // 2) // LANES
    flat = (flat_rows, LANES)
    square = (full, full)
    block = (rows_here, full)
    parity = lax.axis_index("shard") % 2
    pairs = [(i, i ^ 1) for i in range(size)]
    sides = [list(range(k, size, 2)) for k in range(2)]
    near = size in (4, 8) and rows_here % 8 == 0
    hops = {4: (1,), 8: (2, 3, 1)}[size] if near else ()
    strips = (tiles_here, *block) if near else (1, full, full)

    def exchange(x):
        return lax.all_to_all(x, "shard", split_axis=0, concat_axis=0, axis_index_groups=sides, tiled=True)

    def hop_by(x, hop):
        return lax.ppermute(x, "shard", [(i, i ^ (2 * hop)) for i in range(size)])

    def partner(x):
        return lax.ppermute(x, "shard", pairs)

    one, two, l_stat, r_stat, l_basis, r_basis = (
        x.reshape(flat) for x in (moment_one, moment_two, left_stat, right_stat, left_basis, right_basis)
    )
    count = corner_rows(flat_rows)
    outgoing_rows = flat_rows + (rows_here * (full // LANES) if near else 0)
    outgoing, corner, *pieces = call(
        functools.partial(pack_kernel, hops),
        [(outgoing_rows, LANES), (count, LANES)] + [block] * len(hops),
        [(flat_rows // 2, LANES)],
        0.1,
        full,
        "pack",
        copies=2 + len(hops) + full // LANES,
        kind=pltpu.VMEM,
        in_specs=anywhere(5),
        out_specs=anywhere(1) + [pl.BlockSpec(memory_space=pltpu.VMEM)] + anywhere(len(hops)),
    )(*(pltpu.with_memory_space_constraint(x, pltpu.HBM) for x in (l_stat, r_stat, l_basis, r_basis, grads)))
    got = partner(outgoing)
    if near:
        mine = [hop_by(piece, hop) for hop, piece in zip(hops, pieces)]
        theirs = [partner(x) for x in mine]
        rows = (grads, *mine, *theirs)
    else:
        mine = exchange(grads)
        theirs = partner(mine)
        even, odd = jnp.where(parity == 0, mine, theirs), jnp.where(parity == 0, theirs, mine)
        rows = (jnp.stack([even, odd], axis=1).reshape(square),)
        mine = [mine]
    got_corner = partner(after(corner, theirs[0] if near else mine[0]))
    wide = (full, 2 * LANES)
    tall = (2 * LANES, full)
    basis, known, right, turned, other, left = call(
        prepare_kernel, [square, square, wide, tall, flat, flat], [(3, full, LANES)], 0.1, full, "prepare"
    )(l_stat, r_stat, l_basis, r_basis, got)
    grad, new_stat, power, inner = call(
        functools.partial(products_kernel, hops), [square, square, square, tall], [], 3, full, "products"
    )(basis, known, turned, got, *rows)
    tensors = lax.axis_size("tensor")
    place = lambda t, i: i * tensors + t
    cycle = []
    for t in range(0, tensors - tensors % 2, 2):
        for i in range(0, size, 2):
            cycle += [(place(t, i), place(t, i + 1)), (place(t, i + 1), place(t + 1, i + 1))]
            cycle += [(place(t + 1, i + 1), place(t + 1, i)), (place(t + 1, i), place(t, i))]
    cycle += [(place(t, i), place(t, i ^ 1)) for t in range(tensors - tensors % 2, tensors) for i in range(size)]
    other_left = lax.ppermute(after(l_basis, basis, *(theirs if near else mine)), ("shard", "tensor"), cycle)
    (x,) = call(begin_kernel, [square], [(2, full // 2, LANES)], 7, full, "begin")(got_corner, power, basis)
    new_one, new_two, other_rows, outer, x = call(
        functools.partial(update_kernel, hops), [flat, flat, strips, wide, square], [(3, full, LANES)], 5, full, "update"
    )(inner, basis, left, right, other_left, one, two, x)
    if not near:
        partial = other_rows.reshape(tiles_here, 2, rows_here, full)
        other_rows = lax.dynamic_index_in_dim(partial, 1 - parity, 1, keepdims=False)
    got_rows = partner(other_rows)
    x, poly, send, own_rows = call(
        functools.partial(end_kernel, hops, NS_ITERS - 2),
        [square, square, flat, strips],
        [(3, full, LANES)],
        9,
        full,
        "end",
    )(after(x, other_rows), outer, right)
    back = partner(send)
    keep, new_left, new_right = call(rest_kernel, [flat, flat, flat], [(3, full, LANES)], 1.5, full, "rest")(
        x, poly, grad, new_stat, other
    )
    if near:
        kept, *sums = call(add_kernel, [block] * (1 + len(hops)), [], 0.1, full, "add")(
            after(own_rows, send), after(got_rows, send)
        )
        returned = [hop_by(x, hop) for hop, x in zip(hops, sums)]
        update = call(
            functools.partial(rows_kernel, hops),
            [grads.shape],
            [],
            0.1,
            full,
            "rows",
            copies=1 + len(hops),
            in_specs=anywhere(1 + len(hops)),
            out_specs=anywhere(1),
        )(kept, *returned)[0]
    else:
        own_rows = lax.dynamic_index_in_dim(partial, parity, 1, keepdims=False)
        update = exchange(after(own_rows, send) + after(got_rows, send))
    new_l_basis, new_r_basis = call(
        bases_kernel, [flat, flat], [], 0.1, full, "bases", copies=2, in_specs=anywhere(2), out_specs=anywhere(2)
    )(keep, back)
    halves = (new_one, new_two, new_left, new_right, new_l_basis, new_r_basis)
    return (update, *(x.reshape(1, flat_rows * LANES) for x in halves))


def solution(mesh):
    halves = P(("tensor", "shard"), None)
    rows = P("tensor", "shard", None)
    return jax.shard_map(
        local, mesh=mesh, in_specs=(rows,) + (halves,) * 6, out_specs=(rows,) + (halves,) * 6, check_vma=False
    )
```

```python
import functools

import jax
import jax.numpy as jnp
from jax import lax
from jax.experimental import pallas as pl
from jax.experimental.pallas import tpu as pltpu
from jax.sharding import PartitionSpec as P

NS_ITERS = 5
BETA_ONE = 0.9
BETA_TWO = 0.95
ADAM_EPS = 1e-08
NORM_EPS = 1e-06
LINEAR_COEFF = 3.4445
CUBIC_COEFF = -4.775
QUINTIC_COEFF = 2.0315
LANES = 128
F32 = jnp.float32


def split(x):
    high = x.astype(jnp.bfloat16)
    return high, (x - high.astype(F32)).astype(jnp.bfloat16)


def dot(a, b, dims=((1,), (0,))):
    return dot_parts(split(a), split(b), dims)


def dot_parts(a, b, dims=((1,), (0,))):
    (ka,), (kb,) = dims
    left = jnp.concatenate([a[0], a[0], a[1]], axis=ka)
    right = jnp.concatenate([b[0], b[1], b[0]], axis=kb)
    return lax.dot_general(left, right, (dims, ((), ())), preferred_element_type=F32)


def symmetric_dot(a, b, dims=((1,), (0,))):
    (ka,), (kb,) = dims
    cut = a[0].shape[0] - LANES
    head = lambda x, axis: lax.slice_in_dim(x, 0, cut, axis=axis)
    tail = lambda x, axis: lax.slice_in_dim(x, cut, cut + LANES, axis=axis)
    left = dot_parts(a, [head(x, 1 - kb) for x in b], dims)
    corner = dot_parts([tail(x, 1 - ka) for x in a], [tail(x, 1 - kb) for x in b], dims)
    right = jnp.concatenate([left[cut:].T, corner], axis=0)
    return jnp.concatenate([left, right], axis=1)


def swap(x):
    return pltpu.roll(x, LANES // 2, 1)


def low_lanes(shape):
    return lax.broadcasted_iota(jnp.int32, shape, 1) < LANES // 2


def pick(flag, x, y):
    return [jnp.where(flag, u, v) for u, v in zip(x, y)]


def thirds(ref, start=0, rows=None):
    rows = ref.shape[0] if rows is None else rows
    return [ref[pl.ds(start + k, rows // 3, stride=3), :] for k in range(3)]


def put_thirds(ref, parts):
    for k in range(3):
        ref[pl.ds(k, parts[k].shape[0], stride=3), :] = parts[k]


def interleave(scratch, index, even, odd):
    scratch[index, pl.ds(0, even.shape[0], stride=2), :] = even
    scratch[index, pl.ds(1, odd.shape[0], stride=2), :] = odd


def whole_of(scratch, first, second):
    a, b, c = first
    d, e, f = second
    low = low_lanes(a.shape)
    sb, sc, sd, se = swap(b), swap(c), swap(d), swap(e)
    interleave(scratch, 0, a, jnp.where(low, sb, sc))
    interleave(scratch, 1, jnp.where(low, b, sd), jnp.where(low, sc, e))
    interleave(scratch, 2, jnp.where(low, sd, se), f)
    return jnp.concatenate([scratch[0], scratch[1], scratch[2]], axis=1)


def half_of(scratch, flat):
    a, b, c = flat
    low = low_lanes(a.shape)
    sb, sc = swap(b), swap(c)
    interleave(scratch, 0, a, jnp.where(low, sb, sc))
    interleave(scratch, 1, jnp.where(low, b, 0.0), jnp.where(low, sc, 0.0))
    return jnp.concatenate([scratch[0], scratch[1]], axis=1)


def flat_of(scratch, half):
    scratch[0] = half[:, :LANES]
    scratch[1] = half[:, LANES:]
    pairs = half.shape[0] // 2
    even0 = scratch[0, pl.ds(0, pairs, stride=2), :]
    odd0 = swap(scratch[0, pl.ds(1, pairs, stride=2), :])
    even1 = scratch[1, pl.ds(0, pairs, stride=2), :]
    odd1 = swap(scratch[1, pl.ds(1, pairs, stride=2), :])
    low = low_lanes(even0.shape)
    return [even0, jnp.where(low, even1, odd0), jnp.where(low, odd0, odd1)]


def take_half(whole, first):
    one, two, three = whole[:, :LANES], whole[:, LANES : 2 * LANES], whole[:, 2 * LANES :]
    low = low_lanes(one.shape)
    s2, s3 = swap(two), swap(three)
    head = jnp.where(first, one, jnp.where(low, s2, s3))
    tail = jnp.where(low, jnp.where(first, two, s3), 0.0)
    return jnp.concatenate([head, tail], axis=1)


def is_first():
    return lax.rem(lax.axis_index("shard"), 2) == 0


def is_left():
    return lax.rem(lax.axis_index("shard") + lax.axis_index("tensor"), 2) == 0


def pack_kernel(hops, l_stat_ref, r_stat_ref, l_basis_ref, r_basis_ref, grads_ref, *refs):
    out_ref, small_ref, *refs = refs
    piece_refs, (corner, sems) = refs[: len(hops)], refs[len(hops) :]
    left = is_left()
    flat_rows = l_basis_ref.shape[0]
    half_rows = flat_rows // 2
    rows = grads_ref.shape[1]
    here = lax.axis_index("shard") // 2

    start = pl.multiple_of(jnp.where(is_first(), 0, half_rows), 8)

    def copies(basis_ref, stat_ref):
        return [
            pltpu.make_async_copy(stat_ref.at[pl.ds(start, half_rows)], corner, sems.at[0]),
            pltpu.make_async_copy(basis_ref, out_ref.at[pl.ds(0, flat_rows)], sems.at[1]),
        ]

    @pl.when(left)
    def _():
        for copy in copies(r_basis_ref, r_stat_ref):
            copy.start()

    @pl.when(jnp.logical_not(left))
    def _():
        for copy in copies(l_basis_ref, l_stat_ref):
            copy.start()

    more = []
    for number, (hop, piece_ref) in enumerate(zip(hops, piece_refs)):
        more.append(pltpu.make_async_copy(grads_ref.at[here ^ hop], piece_ref, sems.at[2 + number]))
    if hops:
        for k in range(grads_ref.shape[2] // LANES):
            source = grads_ref.at[here, :, pl.ds(k * LANES, LANES)]
            target = out_ref.at[pl.ds(flat_rows + k * rows, rows)]
            more.append(pltpu.make_async_copy(source, target, sems.at[2 + len(hops) + k]))
    for copy in more:
        copy.start()
    first, second = copies(l_basis_ref, l_stat_ref)
    first.wait()
    third = half_rows // 9
    a, b, c = thirds(corner)
    low = low_lanes((third, LANES))
    middle = slice(third, 2 * third)
    small_ref[pl.ds(0, third)] = jnp.where(low, a[:third], b[:third])
    small_ref[pl.ds(third, third)] = a[middle]
    small_ref[pl.ds(2 * third, third)] = jnp.where(low, swap(b[middle]), swap(c[middle]))
    small_ref[pl.ds(3 * third, 3 * third)] = corner[pl.ds(6 * third, 3 * third)]
    for copy in [second, *more]:
        copy.wait()


def corner_rows(flat_rows):
    return flat_rows // 3


def unpack_corner(got_ref):
    third = got_ref.shape[0] // 6
    small = got_ref[pl.ds(0, third), :]
    even = got_ref[pl.ds(third, third), :]
    odd = swap(got_ref[pl.ds(2 * third, third), :])
    a, b, c = thirds(got_ref, 3 * third, 3 * third)
    low = low_lanes(small.shape)
    zero = jnp.zeros_like(small)
    return [
        jnp.concatenate([jnp.where(low, small, zero), even, a], axis=0),
        jnp.concatenate([jnp.where(low, zero, small), jnp.where(low, zero, odd), b], axis=0),
        jnp.concatenate([zero, jnp.where(low, odd, zero), c], axis=0),
    ]


def known_part(first, own, scratch):
    zeros = [jnp.zeros_like(x) for x in own]
    known = whole_of(scratch, pick(first, own, zeros), pick(first, zeros, own))
    half = known.shape[0] // 2
    row = lax.broadcasted_iota(jnp.int32, known.shape, 0)
    column = lax.broadcasted_iota(jnp.int32, known.shape, 1)
    missing = (jnp.where(first, row, column) < half) & (jnp.where(first, column, row) >= half)
    return jnp.where(missing, known.T, known)


def corner_part(corner_ref, scratch):
    corner = half_of(scratch, unpack_corner(corner_ref))
    rows, wide = corner.shape
    turned = jnp.concatenate([corner, jnp.zeros((wide - rows, wide), F32)], axis=0).T[:rows]
    part = rows // 3
    row = lax.broadcasted_iota(jnp.int32, corner.shape, 0)
    column = lax.broadcasted_iota(jnp.int32, corner.shape, 1)
    missing = (row < 2 * part) & (column >= jnp.where(row < part, part, 2 * part))
    return jnp.where(missing, turned, corner)


def place_rows(grad_ref, block, rows, value):
    grad_ref[pl.ds(pl.multiple_of(block * rows, 8), rows), :] = value


def polynomial(parts):
    gram = dot_parts(parts, parts, ((1,), (1,)))
    gram_parts = split(gram)
    return CUBIC_COEFF * gram + QUINTIC_COEFF * dot_parts(gram_parts, gram_parts)


def iterate(x, steps):
    for _ in range(steps):
        parts = split(x)
        x = LINEAR_COEFF * x + dot_parts(split(polynomial(parts)), parts)
    return x


def prepare_kernel(
    l_stat_ref,
    r_stat_ref,
    l_basis_ref,
    r_basis_ref,
    got_ref,
    basis_ref,
    known_ref,
    right_ref,
    turned_ref,
    other_ref,
    copy_ref,
    scratch,
):
    left, first = is_left(), is_first()
    own = pick(left, thirds(l_basis_ref), thirds(r_basis_ref))
    got = thirds(got_ref, 0, l_basis_ref.shape[0])
    basis_ref[...] = whole_of(scratch, pick(first, own, got), pick(first, got, own))
    known_ref[...] = 0.5 * known_part(first, pick(left, thirds(l_stat_ref), thirds(r_stat_ref)), scratch)
    right = half_of(scratch, thirds(r_basis_ref))
    right_ref[...] = right
    turned_ref[...] = right.T
    other_ref[...] = jnp.where(left, r_stat_ref[...], l_stat_ref[...])
    copy_ref[...] = l_basis_ref[...]


def products_kernel(hops, basis_ref, known_ref, turned_ref, got_ref, *refs):
    left = is_left()
    grad_ref, stat_ref, power_ref, inner_ref = refs[-4:]
    if hops:
        grads_ref, mine_refs, theirs_refs = refs[0], refs[1 : 1 + len(hops)], refs[1 + len(hops) : 1 + 2 * len(hops)]
        rows = grads_ref.shape[1]
        here = lax.axis_index("shard") // 2
        parity = lax.axis_index("shard") % 2
        blocks = grad_ref.shape[1] // LANES
        start = got_ref.shape[0] - blocks * rows
        received = [got_ref[pl.ds(start + k * rows, rows), :] for k in range(blocks)]
        place_rows(grad_ref, 2 * here + parity, rows, grads_ref[here])
        place_rows(grad_ref, 2 * here + 1 - parity, rows, jnp.concatenate(received, axis=1))
        for hop, mine, theirs in zip(hops, mine_refs, theirs_refs):
            place_rows(grad_ref, 2 * (here ^ hop) + parity, rows, mine[...])
            place_rows(grad_ref, 2 * (here ^ hop) + 1 - parity, rows, theirs[...])
    else:
        grad_ref[...] = refs[0][...]
    grad = grad_ref[...]
    parts = split(jnp.where(left, grad, grad.T))
    stat = known_ref[...] + 0.5 * symmetric_dot(parts, parts, ((1,), (1,)))
    stat_ref[...] = stat
    power_ref[...] = dot(stat, basis_ref[...])
    inner_ref[...] = dot(turned_ref[...], grad, ((1,), (1,)))


def begin_kernel(corner_ref, power_ref, basis_ref, x_ref, scratch):
    first = is_first()
    corner = corner_part(corner_ref, scratch)
    rows, wide = corner.shape
    basis = jnp.where(first, basis_ref[pl.ds(rows, rows), :], basis_ref[pl.ds(0, rows), :])
    basis = jnp.concatenate([basis, jnp.zeros((wide - rows, 2 * rows), F32)], axis=0)
    term = 0.5 * dot(corner, basis)
    power = power_ref[...] + jnp.concatenate([jnp.where(first, 0.0, term), jnp.where(first, term, 0.0)], axis=0)
    x_ref[...] = iterate(power * (1.0 / jnp.sqrt(jnp.sum(power * power) + NORM_EPS)), 1)


def rows_for(hops, outer_ref, right_parts, out_ref, offset):
    rows = out_ref.shape[1]
    here = lax.axis_index("shard") // 2
    starts = [pl.multiple_of((2 * (here ^ hop) + offset) * rows, 8) if hops else 0 for hop in (0, *hops)]
    outer = [outer_ref[pl.ds(start, rows), :] for start in starts]
    partial = dot_parts(split(jnp.concatenate(outer, axis=0)), right_parts, ((1,), (1,)))
    for k in range(len(starts)):
        out_ref[k] = partial[k * rows : (k + 1) * rows]


def update_kernel(
    hops,
    inner_ref,
    basis_ref,
    left_ref,
    right_ref,
    other_left_ref,
    one_ref,
    two_ref,
    start_ref,
    new_one_ref,
    new_two_ref,
    theirs_ref,
    outer_ref,
    x_ref,
    scratch,
):
    left, first = is_left(), is_first()
    x = start_ref[...]
    parts = split(x)
    gram = symmetric_dot(parts, parts, ((1,), (1,)))
    own, got = thirds(left_ref), thirds(other_left_ref)
    basis_left = jnp.where(left, basis_ref[...], whole_of(scratch, pick(first, own, got), pick(first, got, own)))
    left_parts = split(basis_left)
    rotated = dot_parts(split(inner_ref[...]), left_parts).T
    gram_parts = split(gram)
    square = symmetric_dot(gram_parts, gram_parts)
    rotated = flat_of(scratch, rotated)
    ones = thirds(one_ref)
    twos = thirds(two_ref)
    new_one = [BETA_ONE * m + (1.0 - BETA_ONE) * r for m, r in zip(ones, rotated)]
    new_two = [BETA_TWO * v + (1.0 - BETA_TWO) * r * r for v, r in zip(twos, rotated)]
    put_thirds(new_one_ref, new_one)
    put_thirds(new_two_ref, new_two)
    direction = [m / (jnp.sqrt(v) + ADAM_EPS) for m, v in zip(new_one, new_two)]
    outer_ref[...] = dot_parts(left_parts, split(half_of(scratch, direction)))
    poly_parts = split(CUBIC_COEFF * gram + QUINTIC_COEFF * square)
    moved = dot_parts(poly_parts, parts)
    rows_for(hops, outer_ref, split(right_ref[...]), theirs_ref, 1 - lax.axis_index("shard") % 2)
    x_ref[...] = LINEAR_COEFF * x + moved


def end_kernel(hops, steps, start_ref, outer_ref, right_ref, x_ref, poly_ref, send_ref, mine_ref, scratch):
    x = iterate(start_ref[...], steps - 1)
    x_ref[...] = x
    rows_for(hops, outer_ref, split(right_ref[...]), mine_ref, lax.axis_index("shard") % 2)
    poly = polynomial(split(x))
    poly_ref[...] = poly
    half = take_half(x, jnp.logical_not(is_first()))
    put_thirds(send_ref, flat_of(scratch, LINEAR_COEFF * half + dot(poly, half)))


def add_kernel(mine_ref, theirs_ref, *out_refs):
    for k, out_ref in enumerate(out_refs):
        out_ref[...] = mine_ref[k] + theirs_ref[k]


def bases_kernel(keep_ref, back_ref, new_left_ref, new_right_ref, sems):
    left = is_left()

    def copies(own_ref, other_ref):
        return [
            pltpu.make_async_copy(keep_ref, own_ref, sems.at[0]),
            pltpu.make_async_copy(back_ref, other_ref, sems.at[1]),
        ]

    @pl.when(left)
    def _():
        for copy in copies(new_left_ref, new_right_ref):
            copy.start()

    @pl.when(jnp.logical_not(left))
    def _():
        for copy in copies(new_right_ref, new_left_ref):
            copy.start()

    for copy in copies(new_left_ref, new_right_ref):
        copy.wait()


def rows_kernel(hops, *refs):
    rows_refs, (update_ref, sems) = refs[:-2], refs[-2:]
    here = lax.axis_index("shard") // 2
    copies = [
        pltpu.make_async_copy(rows_refs[k], update_ref.at[here ^ hop], sems.at[k]) for k, hop in enumerate((0, *hops))
    ]
    for copy in copies:
        copy.start()
    for copy in copies:
        copy.wait()


def rest_kernel(x_ref, poly_ref, grad_ref, new_stat_ref, other_ref, keep_ref, new_left_ref, new_right_ref, scratch):
    left = is_left()
    first = is_first()
    half = take_half(x_ref[...], first)
    put_thirds(keep_ref, flat_of(scratch, LINEAR_COEFF * half + dot(poly_ref[...], half)))
    grad = grad_ref[...]
    turned = grad.T
    a = jnp.where(left, grad, turned)
    b = jnp.where(left, turned, grad)
    new_own = flat_of(scratch, take_half(new_stat_ref[...], first))
    product = flat_of(scratch, dot(b, take_half(a, first)))
    new_other = [0.5 * u + 0.5 * v for u, v in zip(thirds(other_ref), product)]
    put_thirds(new_left_ref, pick(left, new_own, new_other))
    put_thirds(new_right_ref, pick(left, new_other, new_own))


def call(kernel, outs, scratch, products, full, name, copies=0, kind=jax.ShapeDtypeStruct, **specs):
    size = full * full
    scratch = [pltpu.VMEM(s, F32) for s in scratch]
    if copies:
        scratch.append(pltpu.SemaphoreType.DMA((copies,)))
    return pl.pallas_call(
        kernel,
        out_shape=[kind(s, F32) for s in outs],
        scratch_shapes=scratch,
        compiler_params=pltpu.CompilerParams(vmem_limit_bytes=40 * 1024 * 1024),
        cost_estimate=pl.CostEstimate(flops=int(products * 6 * full * size), bytes_accessed=16 * size, transcendentals=0),
        name=name,
        **specs,
    )


def anywhere(count):
    return [pl.BlockSpec(memory_space=pl.ANY)] * count


def after(x, *others):
    return lax.optimization_barrier((x, *others))[0]


def local(grads, moment_one, moment_two, left_stat, right_stat, left_basis, right_basis):
    tiles_here, rows_here, full = grads.shape
    size = lax.axis_size("shard")
    flat_rows = full * (full // 2) // LANES
    flat = (flat_rows, LANES)
    square = (full, full)
    block = (rows_here, full)
    parity = lax.axis_index("shard") % 2
    pairs = [(i, i ^ 1) for i in range(size)]
    sides = [list(range(k, size, 2)) for k in range(2)]
    near = size in (4, 8) and rows_here % 8 == 0
    hops = {4: (1,), 8: (2, 3, 1)}[size] if near else ()
    strips = (tiles_here, *block) if near else (1, full, full)

    def exchange(x):
        return lax.all_to_all(x, "shard", split_axis=0, concat_axis=0, axis_index_groups=sides, tiled=True)

    def hop_by(x, hop):
        return lax.ppermute(x, "shard", [(i, i ^ (2 * hop)) for i in range(size)])

    def partner(x):
        return lax.ppermute(x, "shard", pairs)

    one, two, l_stat, r_stat, l_basis, r_basis = (
        x.reshape(flat) for x in (moment_one, moment_two, left_stat, right_stat, left_basis, right_basis)
    )
    count = corner_rows(flat_rows)
    outgoing_rows = flat_rows + (rows_here * (full // LANES) if near else 0)
    outgoing, corner, *pieces = call(
        functools.partial(pack_kernel, hops),
        [(outgoing_rows, LANES), (count, LANES)] + [block] * len(hops),
        [(flat_rows // 2, LANES)],
        0.1,
        full,
        "pack",
        copies=2 + len(hops) + full // LANES,
        kind=pltpu.VMEM,
        in_specs=anywhere(5),
        out_specs=anywhere(1) + [pl.BlockSpec(memory_space=pltpu.VMEM)] + anywhere(len(hops)),
    )(*(pltpu.with_memory_space_constraint(x, pltpu.HBM) for x in (l_stat, r_stat, l_basis, r_basis, grads)))
    got = partner(outgoing)
    if near:
        mine = [hop_by(piece, hop) for hop, piece in zip(hops, pieces)]
        theirs = [partner(x) for x in mine]
        rows = (grads, *mine, *theirs)
    else:
        mine = exchange(grads)
        theirs = partner(mine)
        even, odd = jnp.where(parity == 0, mine, theirs), jnp.where(parity == 0, theirs, mine)
        rows = (jnp.stack([even, odd], axis=1).reshape(square),)
        mine = [mine]
    got_corner = partner(after(corner, theirs[0] if near else mine[0]))
    wide = (full, 2 * LANES)
    tall = (2 * LANES, full)
    basis, known, right, turned, other, left = call(
        prepare_kernel, [square, square, wide, tall, flat, flat], [(3, full, LANES)], 0.1, full, "prepare"
    )(l_stat, r_stat, l_basis, r_basis, got)
    grad, new_stat, power, inner = call(
        functools.partial(products_kernel, hops), [square, square, square, tall], [], 3, full, "products"
    )(basis, known, turned, got, *rows)
    tensors = lax.axis_size("tensor")
    place = lambda t, i: i * tensors + t
    cycle = []
    for t in range(0, tensors - tensors % 2, 2):
        for i in range(0, size, 2):
            cycle += [(place(t, i), place(t, i + 1)), (place(t, i + 1), place(t + 1, i + 1))]
            cycle += [(place(t + 1, i + 1), place(t + 1, i)), (place(t + 1, i), place(t, i))]
    cycle += [(place(t, i), place(t, i ^ 1)) for t in range(tensors - tensors % 2, tensors) for i in range(size)]
    other_left = lax.ppermute(after(l_basis, basis, *(theirs[:2] if near else mine)), ("shard", "tensor"), cycle)
    (x,) = call(begin_kernel, [square], [(2, full // 2, LANES)], 7, full, "begin")(got_corner, power, basis)
    new_one, new_two, other_rows, outer, x = call(
        functools.partial(update_kernel, hops), [flat, flat, strips, wide, square], [(3, full, LANES)], 5, full, "update"
    )(inner, basis, left, right, other_left, one, two, x)
    if not near:
        partial = other_rows.reshape(tiles_here, 2, rows_here, full)
        other_rows = lax.dynamic_index_in_dim(partial, 1 - parity, 1, keepdims=False)
    got_rows = partner(other_rows)
    x, poly, send, own_rows = call(
        functools.partial(end_kernel, hops, NS_ITERS - 2),
        [square, square, flat, strips],
        [(3, full, LANES)],
        9,
        full,
        "end",
    )(after(x, other_rows), outer, right)
    back = partner(send)
    keep, new_left, new_right = call(rest_kernel, [flat, flat, flat], [(3, full, LANES)], 1.5, full, "rest")(
        x, poly, grad, new_stat, other
    )
    if near:
        kept, *sums = call(add_kernel, [block] * (1 + len(hops)), [], 0.1, full, "add")(
            after(own_rows, send), after(got_rows, send)
        )
        returned = [hop_by(x, hop) for hop, x in zip(hops, sums)]
        update = call(
            functools.partial(rows_kernel, hops),
            [grads.shape],
            [],
            0.1,
            full,
            "rows",
            copies=1 + len(hops),
            in_specs=anywhere(1 + len(hops)),
            out_specs=anywhere(1),
        )(kept, *returned)[0]
    else:
        own_rows = lax.dynamic_index_in_dim(partial, parity, 1, keepdims=False)
        update = exchange(after(own_rows, send) + after(got_rows, send))
    new_l_basis, new_r_basis = call(
        bases_kernel, [flat, flat], [], 0.1, full, "bases", copies=2, in_specs=anywhere(2), out_specs=anywhere(2)
    )(keep, back)
    halves = (new_one, new_two, new_left, new_right, new_l_basis, new_r_basis)
    return (update, *(x.reshape(1, flat_rows * LANES) for x in halves))


def solution(mesh):
    halves = P(("tensor", "shard"), None)
    rows = P("tensor", "shard", None)
    return jax.shard_map(
        local, mesh=mesh, in_specs=(rows,) + (halves,) * 6, out_specs=(rows,) + (halves,) * 6, check_vma=False
    )
```

```python
import functools

import jax
import jax.numpy as jnp
from jax import lax
from jax.experimental import pallas as pl
from jax.experimental.pallas import tpu as pltpu
from jax.sharding import PartitionSpec as P

NS_ITERS = 5
BETA_ONE = 0.9
BETA_TWO = 0.95
ADAM_EPS = 1e-08
NORM_EPS = 1e-06
LINEAR_COEFF = 3.4445
CUBIC_COEFF = -4.775
QUINTIC_COEFF = 2.0315
LANES = 128
F32 = jnp.float32


def split(x):
    high = x.astype(jnp.bfloat16)
    return high, (x - high.astype(F32)).astype(jnp.bfloat16)


def dot(a, b, dims=((1,), (0,))):
    return dot_parts(split(a), split(b), dims)


def dot_parts(a, b, dims=((1,), (0,))):
    (ka,), (kb,) = dims
    left = jnp.concatenate([a[0], a[0], a[1]], axis=ka)
    right = jnp.concatenate([b[0], b[1], b[0]], axis=kb)
    return lax.dot_general(left, right, (dims, ((), ())), preferred_element_type=F32)


def symmetric_dot(a, b, dims=((1,), (0,))):
    (ka,), (kb,) = dims
    cut = a[0].shape[0] - LANES
    head = lambda x, axis: lax.slice_in_dim(x, 0, cut, axis=axis)
    tail = lambda x, axis: lax.slice_in_dim(x, cut, cut + LANES, axis=axis)
    left = dot_parts(a, [head(x, 1 - kb) for x in b], dims)
    corner = dot_parts([tail(x, 1 - ka) for x in a], [tail(x, 1 - kb) for x in b], dims)
    right = jnp.concatenate([left[cut:].T, corner], axis=0)
    return jnp.concatenate([left, right], axis=1)


def swap(x):
    return pltpu.roll(x, LANES // 2, 1)


def low_lanes(shape):
    return lax.broadcasted_iota(jnp.int32, shape, 1) < LANES // 2


def pick(flag, x, y):
    return [jnp.where(flag, u, v) for u, v in zip(x, y)]


def thirds(ref, start=0, rows=None):
    rows = ref.shape[0] if rows is None else rows
    return [ref[pl.ds(start + k, rows // 3, stride=3), :] for k in range(3)]


def put_thirds(ref, parts):
    for k in range(3):
        ref[pl.ds(k, parts[k].shape[0], stride=3), :] = parts[k]


def interleave(scratch, index, even, odd):
    scratch[index, pl.ds(0, even.shape[0], stride=2), :] = even
    scratch[index, pl.ds(1, odd.shape[0], stride=2), :] = odd


def whole_of(scratch, first, second):
    a, b, c = first
    d, e, f = second
    low = low_lanes(a.shape)
    sb, sc, sd, se = swap(b), swap(c), swap(d), swap(e)
    interleave(scratch, 0, a, jnp.where(low, sb, sc))
    interleave(scratch, 1, jnp.where(low, b, sd), jnp.where(low, sc, e))
    interleave(scratch, 2, jnp.where(low, sd, se), f)
    return jnp.concatenate([scratch[0], scratch[1], scratch[2]], axis=1)


def half_of(scratch, flat):
    a, b, c = flat
    low = low_lanes(a.shape)
    sb, sc = swap(b), swap(c)
    interleave(scratch, 0, a, jnp.where(low, sb, sc))
    interleave(scratch, 1, jnp.where(low, b, 0.0), jnp.where(low, sc, 0.0))
    return jnp.concatenate([scratch[0], scratch[1]], axis=1)


def flat_of(scratch, half):
    scratch[0] = half[:, :LANES]
    scratch[1] = half[:, LANES:]
    pairs = half.shape[0] // 2
    even0 = scratch[0, pl.ds(0, pairs, stride=2), :]
    odd0 = swap(scratch[0, pl.ds(1, pairs, stride=2), :])
    even1 = scratch[1, pl.ds(0, pairs, stride=2), :]
    odd1 = swap(scratch[1, pl.ds(1, pairs, stride=2), :])
    low = low_lanes(even0.shape)
    return [even0, jnp.where(low, even1, odd0), jnp.where(low, odd0, odd1)]


def take_half(whole, first):
    one, two, three = whole[:, :LANES], whole[:, LANES : 2 * LANES], whole[:, 2 * LANES :]
    low = low_lanes(one.shape)
    s2, s3 = swap(two), swap(three)
    head = jnp.where(first, one, jnp.where(low, s2, s3))
    tail = jnp.where(low, jnp.where(first, two, s3), 0.0)
    return jnp.concatenate([head, tail], axis=1)


def is_first():
    return lax.rem(lax.axis_index("shard"), 2) == 0


def is_left():
    return lax.rem(lax.axis_index("shard") + lax.axis_index("tensor"), 2) == 0


def pack_kernel(hops, l_stat_ref, r_stat_ref, l_basis_ref, r_basis_ref, grads_ref, *refs):
    out_ref, small_ref, *refs = refs
    piece_refs, (corner, sems) = refs[: len(hops)], refs[len(hops) :]
    left = is_left()
    flat_rows = l_basis_ref.shape[0]
    half_rows = flat_rows // 2
    rows = grads_ref.shape[1]
    here = lax.axis_index("shard") // 2

    start = pl.multiple_of(jnp.where(is_first(), 0, half_rows), 8)

    def copies(basis_ref, stat_ref):
        return [
            pltpu.make_async_copy(stat_ref.at[pl.ds(start, half_rows)], corner, sems.at[0]),
            pltpu.make_async_copy(basis_ref, out_ref.at[pl.ds(0, flat_rows)], sems.at[1]),
        ]

    @pl.when(left)
    def _():
        for copy in copies(r_basis_ref, r_stat_ref):
            copy.start()

    @pl.when(jnp.logical_not(left))
    def _():
        for copy in copies(l_basis_ref, l_stat_ref):
            copy.start()

    more = []
    for number, (hop, piece_ref) in enumerate(zip(hops, piece_refs)):
        more.append(pltpu.make_async_copy(grads_ref.at[here ^ hop], piece_ref, sems.at[2 + number]))
    if hops:
        for k in range(grads_ref.shape[2] // LANES):
            source = grads_ref.at[here, :, pl.ds(k * LANES, LANES)]
            target = out_ref.at[pl.ds(flat_rows + k * rows, rows)]
            more.append(pltpu.make_async_copy(source, target, sems.at[2 + len(hops) + k]))
    for copy in more:
        copy.start()
    first, second = copies(l_basis_ref, l_stat_ref)
    first.wait()
    third = half_rows // 9
    a, b, c = thirds(corner)
    low = low_lanes((third, LANES))
    middle = slice(third, 2 * third)
    small_ref[pl.ds(0, third)] = jnp.where(low, a[:third], b[:third])
    small_ref[pl.ds(third, third)] = a[middle]
    small_ref[pl.ds(2 * third, third)] = jnp.where(low, swap(b[middle]), swap(c[middle]))
    small_ref[pl.ds(3 * third, 3 * third)] = corner[pl.ds(6 * third, 3 * third)]
    for copy in [second, *more]:
        copy.wait()


def corner_rows(flat_rows):
    return flat_rows // 3


def unpack_corner(got_ref):
    third = got_ref.shape[0] // 6
    small = got_ref[pl.ds(0, third), :]
    even = got_ref[pl.ds(third, third), :]
    odd = swap(got_ref[pl.ds(2 * third, third), :])
    a, b, c = thirds(got_ref, 3 * third, 3 * third)
    low = low_lanes(small.shape)
    zero = jnp.zeros_like(small)
    return [
        jnp.concatenate([jnp.where(low, small, zero), even, a], axis=0),
        jnp.concatenate([jnp.where(low, zero, small), jnp.where(low, zero, odd), b], axis=0),
        jnp.concatenate([zero, jnp.where(low, odd, zero), c], axis=0),
    ]


def known_part(first, own, scratch):
    zeros = [jnp.zeros_like(x) for x in own]
    known = whole_of(scratch, pick(first, own, zeros), pick(first, zeros, own))
    half = known.shape[0] // 2
    row = lax.broadcasted_iota(jnp.int32, known.shape, 0)
    column = lax.broadcasted_iota(jnp.int32, known.shape, 1)
    missing = (jnp.where(first, row, column) < half) & (jnp.where(first, column, row) >= half)
    return jnp.where(missing, known.T, known)


def corner_part(corner_ref, scratch):
    corner = half_of(scratch, unpack_corner(corner_ref))
    rows, wide = corner.shape
    turned = jnp.concatenate([corner, jnp.zeros((wide - rows, wide), F32)], axis=0).T[:rows]
    part = rows // 3
    row = lax.broadcasted_iota(jnp.int32, corner.shape, 0)
    column = lax.broadcasted_iota(jnp.int32, corner.shape, 1)
    missing = (row < 2 * part) & (column >= jnp.where(row < part, part, 2 * part))
    return jnp.where(missing, turned, corner)


def place_rows(grad_ref, block, rows, value):
    grad_ref[pl.ds(pl.multiple_of(block * rows, 8), rows), :] = value


def polynomial(parts):
    gram = dot_parts(parts, parts, ((1,), (1,)))
    gram_parts = split(gram)
    return CUBIC_COEFF * gram + QUINTIC_COEFF * dot_parts(gram_parts, gram_parts)


def iterate(x, steps):
    for _ in range(steps):
        parts = split(x)
        x = LINEAR_COEFF * x + dot_parts(split(polynomial(parts)), parts)
    return x


def prepare_kernel(
    l_stat_ref,
    r_stat_ref,
    l_basis_ref,
    r_basis_ref,
    got_ref,
    basis_ref,
    known_ref,
    right_ref,
    turned_ref,
    other_ref,
    copy_ref,
    scratch,
):
    left, first = is_left(), is_first()
    own = pick(left, thirds(l_basis_ref), thirds(r_basis_ref))
    got = thirds(got_ref, 0, l_basis_ref.shape[0])
    basis_ref[...] = whole_of(scratch, pick(first, own, got), pick(first, got, own))
    known_ref[...] = 0.5 * known_part(first, pick(left, thirds(l_stat_ref), thirds(r_stat_ref)), scratch)
    right = half_of(scratch, thirds(r_basis_ref))
    right_ref[...] = right
    turned_ref[...] = right.T
    other_ref[...] = jnp.where(left, r_stat_ref[...], l_stat_ref[...])
    copy_ref[...] = l_basis_ref[...]


def products_kernel(hops, basis_ref, known_ref, turned_ref, got_ref, *refs):
    left = is_left()
    grad_ref, stat_ref, power_ref, inner_ref = refs[-4:]
    if hops:
        grads_ref, mine_refs, theirs_refs = refs[0], refs[1 : 1 + len(hops)], refs[1 + len(hops) : 1 + 2 * len(hops)]
        rows = grads_ref.shape[1]
        here = lax.axis_index("shard") // 2
        parity = lax.axis_index("shard") % 2
        blocks = grad_ref.shape[1] // LANES
        start = got_ref.shape[0] - blocks * rows
        received = [got_ref[pl.ds(start + k * rows, rows), :] for k in range(blocks)]
        place_rows(grad_ref, 2 * here + parity, rows, grads_ref[here])
        place_rows(grad_ref, 2 * here + 1 - parity, rows, jnp.concatenate(received, axis=1))
        for hop, mine, theirs in zip(hops, mine_refs, theirs_refs):
            place_rows(grad_ref, 2 * (here ^ hop) + parity, rows, mine[...])
            place_rows(grad_ref, 2 * (here ^ hop) + 1 - parity, rows, theirs[...])
    else:
        grad_ref[...] = refs[0][...]
    grad = grad_ref[...]
    parts = split(jnp.where(left, grad, grad.T))
    stat = known_ref[...] + 0.5 * symmetric_dot(parts, parts, ((1,), (1,)))
    stat_ref[...] = stat
    power_ref[...] = dot(stat, basis_ref[...])
    inner_ref[...] = dot(turned_ref[...], grad, ((1,), (1,)))


def begin_kernel(corner_ref, power_ref, basis_ref, x_ref, scratch):
    first = is_first()
    corner = corner_part(corner_ref, scratch)
    rows, wide = corner.shape
    basis = jnp.where(first, basis_ref[pl.ds(rows, rows), :], basis_ref[pl.ds(0, rows), :])
    basis = jnp.concatenate([basis, jnp.zeros((wide - rows, 2 * rows), F32)], axis=0)
    term = 0.5 * dot(corner, basis)
    power = power_ref[...] + jnp.concatenate([jnp.where(first, 0.0, term), jnp.where(first, term, 0.0)], axis=0)
    x_ref[...] = iterate(power * (1.0 / jnp.sqrt(jnp.sum(power * power) + NORM_EPS)), 1)


def rows_for(hops, outer_ref, right_parts, out_ref, offset):
    rows = out_ref.shape[1]
    here = lax.axis_index("shard") // 2
    starts = [pl.multiple_of((2 * (here ^ hop) + offset) * rows, 8) if hops else 0 for hop in (0, *hops)]
    outer = [outer_ref[pl.ds(start, rows), :] for start in starts]
    partial = dot_parts(split(jnp.concatenate(outer, axis=0)), right_parts, ((1,), (1,)))
    for k in range(len(starts)):
        out_ref[k] = partial[k * rows : (k + 1) * rows]


def update_kernel(
    hops,
    inner_ref,
    basis_ref,
    left_ref,
    right_ref,
    other_left_ref,
    one_ref,
    two_ref,
    start_ref,
    new_one_ref,
    new_two_ref,
    theirs_ref,
    outer_ref,
    x_ref,
    scratch,
):
    left, first = is_left(), is_first()
    x = start_ref[...]
    parts = split(x)
    gram = symmetric_dot(parts, parts, ((1,), (1,)))
    own, got = thirds(left_ref), thirds(other_left_ref)
    basis_left = jnp.where(left, basis_ref[...], whole_of(scratch, pick(first, own, got), pick(first, got, own)))
    left_parts = split(basis_left)
    rotated = dot_parts(split(inner_ref[...]), left_parts).T
    gram_parts = split(gram)
    square = symmetric_dot(gram_parts, gram_parts)
    rotated = flat_of(scratch, rotated)
    ones = thirds(one_ref)
    twos = thirds(two_ref)
    new_one = [BETA_ONE * m + (1.0 - BETA_ONE) * r for m, r in zip(ones, rotated)]
    new_two = [BETA_TWO * v + (1.0 - BETA_TWO) * r * r for v, r in zip(twos, rotated)]
    put_thirds(new_one_ref, new_one)
    put_thirds(new_two_ref, new_two)
    direction = [m / (jnp.sqrt(v) + ADAM_EPS) for m, v in zip(new_one, new_two)]
    outer_ref[...] = dot_parts(left_parts, split(half_of(scratch, direction)))
    poly_parts = split(CUBIC_COEFF * gram + QUINTIC_COEFF * square)
    moved = dot_parts(poly_parts, parts)
    rows_for(hops, outer_ref, split(right_ref[...]), theirs_ref, 1 - lax.axis_index("shard") % 2)
    x_ref[...] = LINEAR_COEFF * x + moved


def end_kernel(hops, steps, start_ref, outer_ref, right_ref, x_ref, poly_ref, send_ref, mine_ref, scratch):
    x = iterate(start_ref[...], steps - 1)
    x_ref[...] = x
    rows_for(hops, outer_ref, split(right_ref[...]), mine_ref, lax.axis_index("shard") % 2)
    parts = split(x)
    gram = symmetric_dot(parts, parts, ((1,), (1,)))
    gram_parts = split(gram)
    poly = CUBIC_COEFF * gram + QUINTIC_COEFF * symmetric_dot(gram_parts, gram_parts)
    poly_ref[...] = poly
    half = take_half(x, jnp.logical_not(is_first()))
    put_thirds(send_ref, flat_of(scratch, LINEAR_COEFF * half + dot(poly, half)))


def add_kernel(mine_ref, theirs_ref, *out_refs):
    for k, out_ref in enumerate(out_refs):
        out_ref[...] = mine_ref[k] + theirs_ref[k]


def bases_kernel(keep_ref, back_ref, new_left_ref, new_right_ref, sems):
    left = is_left()

    def copies(own_ref, other_ref):
        return [
            pltpu.make_async_copy(keep_ref, own_ref, sems.at[0]),
            pltpu.make_async_copy(back_ref, other_ref, sems.at[1]),
        ]

    @pl.when(left)
    def _():
        for copy in copies(new_left_ref, new_right_ref):
            copy.start()

    @pl.when(jnp.logical_not(left))
    def _():
        for copy in copies(new_right_ref, new_left_ref):
            copy.start()

    for copy in copies(new_left_ref, new_right_ref):
        copy.wait()


def rows_kernel(hops, *refs):
    rows_refs, (update_ref, sems) = refs[:-2], refs[-2:]
    here = lax.axis_index("shard") // 2
    copies = [
        pltpu.make_async_copy(rows_refs[k], update_ref.at[here ^ hop], sems.at[k]) for k, hop in enumerate((0, *hops))
    ]
    for copy in copies:
        copy.start()
    for copy in copies:
        copy.wait()


def rest_kernel(x_ref, poly_ref, grad_ref, new_stat_ref, other_ref, keep_ref, new_left_ref, new_right_ref, scratch):
    left = is_left()
    first = is_first()
    half = take_half(x_ref[...], first)
    put_thirds(keep_ref, flat_of(scratch, LINEAR_COEFF * half + dot(poly_ref[...], half)))
    grad = grad_ref[...]
    turned = grad.T
    a = jnp.where(left, grad, turned)
    b = jnp.where(left, turned, grad)
    new_own = flat_of(scratch, take_half(new_stat_ref[...], first))
    product = flat_of(scratch, dot(b, take_half(a, first)))
    new_other = [0.5 * u + 0.5 * v for u, v in zip(thirds(other_ref), product)]
    put_thirds(new_left_ref, pick(left, new_own, new_other))
    put_thirds(new_right_ref, pick(left, new_other, new_own))


def call(kernel, outs, scratch, products, full, name, copies=0, kind=jax.ShapeDtypeStruct, **specs):
    size = full * full
    scratch = [pltpu.VMEM(s, F32) for s in scratch]
    if copies:
        scratch.append(pltpu.SemaphoreType.DMA((copies,)))
    return pl.pallas_call(
        kernel,
        out_shape=[kind(s, F32) for s in outs],
        scratch_shapes=scratch,
        compiler_params=pltpu.CompilerParams(vmem_limit_bytes=40 * 1024 * 1024),
        cost_estimate=pl.CostEstimate(flops=int(products * 6 * full * size), bytes_accessed=16 * size, transcendentals=0),
        name=name,
        **specs,
    )


def anywhere(count):
    return [pl.BlockSpec(memory_space=pl.ANY)] * count


def after(x, *others):
    return lax.optimization_barrier((x, *others))[0]


def local(grads, moment_one, moment_two, left_stat, right_stat, left_basis, right_basis):
    tiles_here, rows_here, full = grads.shape
    size = lax.axis_size("shard")
    flat_rows = full * (full // 2) // LANES
    flat = (flat_rows, LANES)
    square = (full, full)
    block = (rows_here, full)
    parity = lax.axis_index("shard") % 2
    pairs = [(i, i ^ 1) for i in range(size)]
    sides = [list(range(k, size, 2)) for k in range(2)]
    near = size in (4, 8) and rows_here % 8 == 0
    hops = {4: (1,), 8: (2, 3, 1)}[size] if near else ()
    strips = (tiles_here, *block) if near else (1, full, full)

    def exchange(x):
        return lax.all_to_all(x, "shard", split_axis=0, concat_axis=0, axis_index_groups=sides, tiled=True)

    def hop_by(x, hop):
        return lax.ppermute(x, "shard", [(i, i ^ (2 * hop)) for i in range(size)])

    def partner(x):
        return lax.ppermute(x, "shard", pairs)

    one, two, l_stat, r_stat, l_basis, r_basis = (
        x.reshape(flat) for x in (moment_one, moment_two, left_stat, right_stat, left_basis, right_basis)
    )
    count = corner_rows(flat_rows)
    outgoing_rows = flat_rows + (rows_here * (full // LANES) if near else 0)
    outgoing, corner, *pieces = call(
        functools.partial(pack_kernel, hops),
        [(outgoing_rows, LANES), (count, LANES)] + [block] * len(hops),
        [(flat_rows // 2, LANES)],
        0.1,
        full,
        "pack",
        copies=2 + len(hops) + full // LANES,
        kind=pltpu.VMEM,
        in_specs=anywhere(5),
        out_specs=anywhere(1) + [pl.BlockSpec(memory_space=pltpu.VMEM)] + anywhere(len(hops)),
    )(*(pltpu.with_memory_space_constraint(x, pltpu.HBM) for x in (l_stat, r_stat, l_basis, r_basis, grads)))
    got = partner(outgoing)
    if near:
        mine = [hop_by(piece, hop) for hop, piece in zip(hops, pieces)]
        theirs = [partner(x) for x in mine]
        rows = (grads, *mine, *theirs)
    else:
        mine = exchange(grads)
        theirs = partner(mine)
        even, odd = jnp.where(parity == 0, mine, theirs), jnp.where(parity == 0, theirs, mine)
        rows = (jnp.stack([even, odd], axis=1).reshape(square),)
        mine = [mine]
    got_corner = partner(after(corner, theirs[0] if near else mine[0]))
    wide = (full, 2 * LANES)
    tall = (2 * LANES, full)
    basis, known, right, turned, other, left = call(
        prepare_kernel, [square, square, wide, tall, flat, flat], [(3, full, LANES)], 0.1, full, "prepare"
    )(l_stat, r_stat, l_basis, r_basis, got)
    grad, new_stat, power, inner = call(
        functools.partial(products_kernel, hops), [square, square, square, tall], [], 3, full, "products"
    )(basis, known, turned, got, *rows)
    tensors = lax.axis_size("tensor")
    place = lambda t, i: i * tensors + t
    cycle = []
    for t in range(0, tensors - tensors % 2, 2):
        for i in range(0, size, 2):
            cycle += [(place(t, i), place(t, i + 1)), (place(t, i + 1), place(t + 1, i + 1))]
            cycle += [(place(t + 1, i + 1), place(t + 1, i)), (place(t + 1, i), place(t, i))]
    cycle += [(place(t, i), place(t, i ^ 1)) for t in range(tensors - tensors % 2, tensors) for i in range(size)]
    other_left = lax.ppermute(after(l_basis, basis, *(theirs[:2] if near else mine)), ("shard", "tensor"), cycle)
    (x,) = call(begin_kernel, [square], [(2, full // 2, LANES)], 7, full, "begin")(got_corner, power, basis)
    new_one, new_two, other_rows, outer, x = call(
        functools.partial(update_kernel, hops), [flat, flat, strips, wide, square], [(3, full, LANES)], 5, full, "update"
    )(inner, basis, left, right, other_left, one, two, x)
    if not near:
        partial = other_rows.reshape(tiles_here, 2, rows_here, full)
        other_rows = lax.dynamic_index_in_dim(partial, 1 - parity, 1, keepdims=False)
    got_rows = partner(other_rows)
    x, poly, send, own_rows = call(
        functools.partial(end_kernel, hops, NS_ITERS - 2),
        [square, square, flat, strips],
        [(3, full, LANES)],
        9,
        full,
        "end",
    )(after(x, other_rows), outer, right)
    back = partner(send)
    keep, new_left, new_right = call(rest_kernel, [flat, flat, flat], [(3, full, LANES)], 1.5, full, "rest")(
        x, poly, grad, new_stat, other
    )
    if near:
        kept, *sums = call(add_kernel, [block] * (1 + len(hops)), [], 0.1, full, "add")(
            after(own_rows, send), after(got_rows, send)
        )
        returned = [hop_by(x, hop) for hop, x in zip(hops, sums)]
        update = call(
            functools.partial(rows_kernel, hops),
            [grads.shape],
            [],
            0.1,
            full,
            "rows",
            copies=1 + len(hops),
            in_specs=anywhere(1 + len(hops)),
            out_specs=anywhere(1),
        )(kept, *returned)[0]
    else:
        own_rows = lax.dynamic_index_in_dim(partial, parity, 1, keepdims=False)
        update = exchange(after(own_rows, send) + after(got_rows, send))
    new_l_basis, new_r_basis = call(
        bases_kernel, [flat, flat], [], 0.1, full, "bases", copies=2, in_specs=anywhere(2), out_specs=anywhere(2)
    )(keep, back)
    halves = (new_one, new_two, new_left, new_right, new_l_basis, new_r_basis)
    return (update, *(x.reshape(1, flat_rows * LANES) for x in halves))


def solution(mesh):
    halves = P(("tensor", "shard"), None)
    rows = P("tensor", "shard", None)
    return jax.shard_map(
        local, mesh=mesh, in_specs=(rows,) + (halves,) * 6, out_specs=(rows,) + (halves,) * 6, check_vma=False
    )
```
